32 devices in a mesh: dp: 2 (over x), seq: 4 (over z), tensor: 4 (over y, core).
Axes of the slice: x: 2, y: 2, z: 4, core: 2. Of those that a mesh axis runs over, the one named last changes fastest.
Arguments:
- inputs: bfloat16 [2, 2560, 2048], P('dp', 'seq'), may hold values from -6 to 6
- first_gain: bfloat16 [2048], P(('dp', 'seq')), may hold values from 0.099609375 to 1.8984375
- w_query: bfloat16 [2048, 2048], P(('dp', 'seq'), 'tensor'), may hold values from -0.125 to 0.125
- w_key: bfloat16 [2048, 2048], P(('dp', 'seq'), 'tensor'), may hold values from -0.125 to 0.125
- w_value: bfloat16 [2048, 2048], P(('dp', 'seq'), 'tensor'), may hold values from -0.125 to 0.125
- w_out: bfloat16 [2048, 2048], P('tensor', ('dp', 'seq')), may hold values from -6 to 6
- second_gain: bfloat16 [2048], P(('dp', 'seq')), may hold values from 0.099609375 to 1.8984375
- w_up: bfloat16 [2048, 8192], P(('dp', 'seq'), 'tensor'), may hold values from -0.125 to 0.125
- w_down: bfloat16 [8192, 2048], P('tensor', ('dp', 'seq')), may hold values from -0.0625 to 0.0625
- frame_mask: int32 [2, 4], P('dp'), may hold values from 0 to 1, as said below
- cotangent: bfloat16 [2, 2560, 2048], P('dp', 'seq'), may hold values from -6 to 6
Outputs:
- result: bfloat16 [2, 2560, 2048], P('dp', 'seq')
- grad_inputs: bfloat16 [2, 2560, 2048], P('dp', 'seq')
- grad_first_gain: float32 [2048], P(('dp', 'seq'))
- grad_query: float32 [2048, 2048], P(('dp', 'seq'), 'tensor')
- grad_key: float32 [2048, 2048], P(('dp', 'seq'), 'tensor')
- grad_value: float32 [2048, 2048], P(('dp', 'seq'), 'tensor')
- grad_out: float32 [2048, 2048], P('tensor', ('dp', 'seq'))
- grad_second_gain: float32 [2048], P(('dp', 'seq'))
- grad_up: float32 [2048, 8192], P(('dp', 'seq'), 'tensor')
- grad_down: float32 [8192, 2048], P('tensor', ('dp', 'seq'))
The draws below stay inside these ranges and needn't reach their ends.
Inputs may be any that keep to these rules, and one draw needn't show every extreme that they name: `frame_mask`: frame 0 of every clip is valid. One clip, drawn from the seed, has all 4 frames valid; the other has exactly 1 invalid frame.
All inputs are finite; a program needn't handle non-finite values.
Results may differ from the reference program's by a relative error of at most 0.024.
Values may be sent and summed in bfloat16 or wider, within the bound.
A program may use at most 256 MiB of HBM per device.

```python
import jax
import jax.numpy as jnp
from jax import lax

D = 2048
HEADS = 16
HEAD_DIM = 128
FF = 8192
FRAME_TOK = 640
INNER = 2048
FRAMES = 4
CLIP_LEN = 2560
CLIPS = 2


def draw_frame_mask(key, part):
    key = jax.random.fold_in(key, 11)
    key_full, key_count, key_order = jax.random.split(key, 3)
    full_clip = jax.random.randint(key_full, (), 0, CLIPS)
    hole_count = jax.random.randint(key_count, (CLIPS, 1), 1, FRAMES // 4 + 1)
    ranking = jax.random.randint(key_order, (CLIPS, FRAMES - 1), 0, 1 << 20) * FRAMES + jnp.arange(FRAMES - 1, dtype=jnp.int32)[None, :]
    hole_rank = jnp.argsort(jnp.argsort(ranking, axis=1, stable=True), axis=1, stable=True)
    later_frames = jnp.where(hole_rank < hole_count, 0, 1).astype(jnp.int32)
    valid = jnp.concatenate([jnp.ones((CLIPS, 1), jnp.int32), later_frames], axis=1)
    clip_rows = jnp.arange(CLIPS, dtype=jnp.int32)[:, None]
    return jnp.where(clip_rows == full_clip, 1, valid).astype(jnp.int32)


def shard_levels(stream_key, dims, shards, low, high):
    gain, own = 1.0, jax.random.fold_in(stream_key, 6)
    for position, shards_of in shards:
        heights = jnp.exp(jax.random.uniform(jax.random.fold_in(own, position), (shards_of,), jnp.float32, low / len(shards), high / len(shards)))
        gain = gain * jnp.repeat(heights, dims[position] // shards_of).reshape([-1 if axis == position else 1 for axis in range(len(dims))])
    return gain


def normal_values(rng, extent, deviation, most, pieces=(), held_as=jnp.bfloat16):
    values = jax.random.normal(rng, extent, jnp.float32) * deviation
    if len(pieces) > 0:
        values = shard_levels(rng, extent, pieces, -0.22, 0.18) * values
    return jnp.clip(values, min=-most, max=most).astype(held_as)


def setup_inputs(seed: int = 0) -> dict:
    key_list = jax.random.split(jax.random.key(seed), 12)
    inputs = normal_values(key_list[0], (CLIPS, CLIP_LEN, D), 1.0, 6.0, ((0, 2), (1, 4)))
    first_gain = jnp.clip(1.0 + 0.18 * jax.random.normal(key_list[1], (D,), jnp.float32), 0.099609375, 1.8984375).astype(jnp.bfloat16)
    w_query = normal_values(key_list[2], (D, INNER), D ** -0.5, 0.125, ((0, 8), (1, 4)))
    w_key = normal_values(key_list[3], (D, INNER), D ** -0.5, 0.125, ((0, 8), (1, 4)))
    w_value = normal_values(key_list[4], (D, INNER), D ** -0.5, 0.125, ((0, 8), (1, 4)))
    w_out = normal_values(key_list[5], (INNER, D), (max(1, 2 * INNER // CLIP_LEN)) ** -0.5, 6.0, ((0, 4), (1, 8)))
    second_gain = jnp.clip(1.0 + 0.18 * jax.random.normal(key_list[6], (D,), jnp.float32), 0.099609375, 1.8984375).astype(jnp.bfloat16)
    w_up = normal_values(key_list[7], (D, FF), D ** -0.5, 0.125, ((0, 8), (1, 4)))
    w_down = normal_values(key_list[8], (FF, D), FF ** -0.5, 0.0625, ((0, 4), (1, 8)))
    frame_mask = draw_frame_mask(jax.random.fold_in(key_list[11], 71), 0)
    cotangent = normal_values(key_list[10], (CLIPS, CLIP_LEN, D), 1.0, 6.0, ((0, 2), (1, 4)))
    return dict(inputs=inputs, first_gain=first_gain, w_query=w_query, w_key=w_key, w_value=w_value, w_out=w_out, second_gain=second_gain, w_up=w_up, w_down=w_down, frame_mask=frame_mask, cotangent=cotangent)


NORM_EPS = 1e-05
MASK_FILL = -1e+30
HIGHEST = lax.Precision.HIGHEST

@jax.custom_vjp
def low(v):
    return lax.optimization_barrier(v.astype(jnp.bfloat16)).astype(jnp.float32)

@jax.custom_vjp
def low_back(v):
    return v

def low_keep(v):
    return (low(v), None)

def low_pass(kept, grad):
    return (grad,)

def back_keep(v):
    return (v, None)

def back_low(kept, grad):
    return (low(grad),)
low.defvjp(low_keep, low_pass)
low_back.defvjp(back_keep, back_low)

def layer_norm(values):
    center = values - lax.optimization_barrier(jnp.mean(values, axis=-1, keepdims=True))
    spread = lax.optimization_barrier(jnp.mean(center * center, axis=-1, keepdims=True))
    return center * lax.rsqrt(spread + NORM_EPS)

def matmul_hi(left, right):
    return jnp.dot(left, right, precision=HIGHEST, preferred_element_type=jnp.float32)

def clip_forward(clip_in, valid, first_gain, w_query, w_key, w_value, w_out, second_gain, w_up, w_down):
    first_in = low(layer_norm(clip_in) * first_gain)
    query = low_back(low(matmul_hi(first_in, w_query))).reshape(CLIP_LEN, HEADS, HEAD_DIM)
    keys = low_back(low(matmul_hi(first_in, w_key))).reshape(CLIP_LEN, HEADS, HEAD_DIM)
    values = low_back(low(matmul_hi(first_in, w_value))).reshape(CLIP_LEN, HEADS, HEAD_DIM)
    key_frame = jnp.arange(CLIP_LEN, dtype=jnp.int32) // FRAME_TOK
    key_valid = valid[key_frame] == 1
    score_scale = HEAD_DIM ** (-0.5)

    def one_frame(frame_args):
        query_block, frame_pos = frame_args
        scores = low_back(jnp.einsum('qhd,khd->hqk', query_block, keys, precision=HIGHEST) * score_scale)
        allowed = ((key_frame <= frame_pos) & key_valid)[None, None, :]
        scores = jnp.where(allowed, scores, MASK_FILL)
        row_max = lax.optimization_barrier(jnp.max(scores, axis=-1, keepdims=True))
        exp_terms = jnp.where(allowed, jnp.exp(scores - row_max), 0.0)
        attn_prob = low(exp_terms / lax.optimization_barrier(jnp.sum(exp_terms, axis=-1, keepdims=True)))
        return jnp.einsum('hqk,khd->qhd', attn_prob, values, precision=HIGHEST)
    attended = lax.map(jax.checkpoint(one_frame), (query.reshape(FRAMES, FRAME_TOK, HEADS, HEAD_DIM), jnp.arange(FRAMES, dtype=jnp.int32)))
    attended = low_back(low(attended.reshape(CLIP_LEN, HEADS * HEAD_DIM)))
    resid_mid = clip_in + low_back(matmul_hi(attended, w_out))
    second_in = low(layer_norm(resid_mid) * second_gain)
    up_pre = low_back(matmul_hi(second_in, w_up))
    up_act = low(jax.nn.gelu(up_pre, approximate=False))
    return resid_mid + low_back(matmul_hi(up_act, w_down))

def reference(inputs, first_gain, w_query, w_key, w_value, w_out, second_gain, w_up, w_down, frame_mask, cotangent):

    def whole(inputs_f, gain_one, query_w, key_w, value_w, out_w, gain_two, up_w, down_w):

        def per_clip(clip_pair):
            return clip_forward(clip_pair[0], clip_pair[1], gain_one, query_w, key_w, value_w, out_w, gain_two, up_w, down_w)
        return lax.map(per_clip, (inputs_f, frame_mask))
    result, pull = jax.vjp(whole, inputs.astype(jnp.float32), first_gain.astype(jnp.float32), w_query.astype(jnp.float32), w_key.astype(jnp.float32), w_value.astype(jnp.float32), w_out.astype(jnp.float32), second_gain.astype(jnp.float32), w_up.astype(jnp.float32), w_down.astype(jnp.float32))
    grads = pull(cotangent.astype(jnp.float32))
    return (result.astype(jnp.bfloat16), grads[0].astype(jnp.bfloat16), grads[1], grads[2], grads[3], grads[4], grads[5], grads[6], grads[7], grads[8])
```

```python
import functools

import jax
import jax.numpy as jnp
from jax import lax
from jax.experimental import pallas as pl
from jax.experimental.pallas import tpu as pltpu
from jax.sharding import PartitionSpec as P

HEAD_DIM = 128
FRAME_TOK = 640


NORM_EPS = 1e-05
MASK_FILL = -1e30


def norm_rows(values):
    center = values - jnp.mean(values, axis=-1, keepdims=True)
    spread = jnp.mean(center * center, axis=-1, keepdims=True)
    return center * lax.rsqrt(spread + NORM_EPS)


def gelu_exact(values):
    return jax.nn.gelu(values, approximate=False)


def heads_total(values):
    return lax.psum(values.astype(jnp.bfloat16), "tensor").astype(jnp.float32)


def local(
    inputs,
    first_gain,
    w_query,
    w_key,
    w_value,
    w_out,
    second_gain,
    w_up,
    w_down,
    frame_mask,
    cotangent,
):
    seq_pos = lax.axis_index("seq")
    gain_one, query_w, key_w, value_w, gain_two, up_w = (
        lax.all_gather(first_gain, ("dp", "seq"), axis=0, tiled=True),
        lax.all_gather(w_query, ("dp", "seq"), axis=0, tiled=True),
        lax.all_gather(w_key, ("dp", "seq"), axis=0, tiled=True),
        lax.all_gather(w_value, ("dp", "seq"), axis=0, tiled=True),
        lax.all_gather(second_gain, ("dp", "seq"), axis=0, tiled=True),
        lax.all_gather(w_up, ("dp", "seq"), axis=0, tiled=True),
    )
    out_w, down_w = (
        lax.all_gather(w_out, ("dp", "seq"), axis=1, tiled=True),
        lax.all_gather(w_down, ("dp", "seq"), axis=1, tiled=True),
    )
    tok_rows = inputs.shape[1]
    local_inner = query_w.shape[1]
    local_heads = local_inner // HEAD_DIM
    frames_dev = tok_rows // FRAME_TOK
    score_scale = HEAD_DIM ** (-0.5)
    clip_valid = frame_mask[0]
    frame_count = clip_valid.shape[0]
    resid_in = inputs[0].astype(jnp.float32)
    dout_rows = cotangent[0]
    row_frame = seq_pos * frames_dev + jnp.arange(tok_rows, dtype=jnp.int32) // FRAME_TOK
    frame_limit = (seq_pos + 1) * frames_dev
    normed_one = norm_rows(resid_in)
    first_in = (normed_one * gain_one.astype(jnp.float32)).astype(jnp.bfloat16)
    query = jnp.dot(first_in, query_w, preferred_element_type=jnp.float32).astype(jnp.bfloat16)
    key_local = jnp.dot(first_in, key_w, preferred_element_type=jnp.float32).astype(jnp.bfloat16)
    value_local = jnp.dot(first_in, value_w, preferred_element_type=jnp.float32).astype(
        jnp.bfloat16
    )
    key_all, value_all = (
        lax.all_gather(key_local, "seq", axis=0, tiled=True),
        lax.all_gather(value_local, "seq", axis=0, tiled=True),
    )
    query_heads = query.reshape(tok_rows, local_heads, HEAD_DIM)
    key_frames = key_all.reshape(frame_count, FRAME_TOK, local_heads, HEAD_DIM)
    value_frames = value_all.reshape(frame_count, FRAME_TOK, local_heads, HEAD_DIM)

    def frame_scores(frame_idx):
        key_block = lax.dynamic_index_in_dim(key_frames, frame_idx, 0, keepdims=False)
        value_block = lax.dynamic_index_in_dim(value_frames, frame_idx, 0, keepdims=False)
        scores = (
            jnp.einsum("qhd,khd->hqk", query_heads, key_block, preferred_element_type=jnp.float32)
            * score_scale
        )
        frame_ok = lax.dynamic_index_in_dim(clip_valid, frame_idx, 0, keepdims=False) == 1
        allowed = ((frame_idx <= row_frame) & frame_ok)[None, :, None]
        return (scores, allowed, key_block, value_block)

    def stats_step(frame_idx, running):
        row_max, row_sum = running
        scores, allowed, key_block, value_block = frame_scores(frame_idx)
        masked = jnp.where(allowed, scores, MASK_FILL)
        new_max = jnp.maximum(row_max, jnp.max(masked, axis=2))
        exp_terms = jnp.where(allowed, jnp.exp(masked - new_max[:, :, None]), 0.0)
        return (new_max, row_sum * jnp.exp(row_max - new_max) + jnp.sum(exp_terms, axis=2))

    start_stats = (
        jnp.full((local_heads, tok_rows), MASK_FILL, jnp.float32),
        jnp.zeros((local_heads, tok_rows), jnp.float32),
    )
    row_max, row_sum = lax.fori_loop(0, frame_limit, stats_step, start_stats)

    def soft_weights(scores, allowed):
        return jnp.where(allowed, jnp.exp(scores - row_max[:, :, None]) / row_sum[:, :, None], 0.0)

    def output_step(frame_idx, running):
        scores, allowed, key_block, value_block = frame_scores(frame_idx)
        attn_prob = soft_weights(scores, allowed).astype(jnp.bfloat16)
        return running + jnp.einsum(
            "hqk,khd->qhd", attn_prob, value_block, preferred_element_type=jnp.float32
        )

    attended = lax.fori_loop(
        0, frame_limit, output_step, jnp.zeros((tok_rows, local_heads, HEAD_DIM), jnp.float32)
    )
    attended_low = attended.reshape(tok_rows, local_inner).astype(jnp.bfloat16)
    resid_mid = resid_in + heads_total(
        jnp.dot(attended_low, out_w, preferred_element_type=jnp.float32)
    )
    normed_two = norm_rows(resid_mid)
    second_in = (normed_two * gain_two.astype(jnp.float32)).astype(jnp.bfloat16)
    up_pre = jnp.dot(second_in, up_w, preferred_element_type=jnp.float32)
    up_act = gelu_exact(up_pre).astype(jnp.bfloat16)
    resid_out = resid_mid + heads_total(jnp.dot(up_act, down_w, preferred_element_type=jnp.float32))
    result = resid_out.astype(jnp.bfloat16)[None]
    grad_down = jnp.einsum("tf,td->fd", up_act, dout_rows, preferred_element_type=jnp.float32)
    d_act = jnp.einsum("td,fd->tf", dout_rows, down_w, preferred_element_type=jnp.float32)
    gelu_pull = jax.vjp(gelu_exact, up_pre)[1]
    d_up_pre = gelu_pull(d_act)[0].astype(jnp.bfloat16)
    grad_up = jnp.einsum("td,tf->df", second_in, d_up_pre, preferred_element_type=jnp.float32)
    d_second = heads_total(
        jnp.einsum("tf,df->td", d_up_pre, up_w, preferred_element_type=jnp.float32)
    )
    grad_second_gain = jnp.sum(d_second * normed_two, axis=0)
    norm_pull_two = jax.vjp(norm_rows, resid_mid)[1]
    d_mid = (
        dout_rows.astype(jnp.float32) + norm_pull_two(d_second * gain_two.astype(jnp.float32))[0]
    )
    d_mix = d_mid.astype(jnp.bfloat16)
    grad_out = jnp.einsum("ti,td->id", attended_low, d_mix, preferred_element_type=jnp.float32)
    d_attended = jnp.einsum("td,id->ti", d_mix, out_w, preferred_element_type=jnp.float32).astype(
        jnp.bfloat16
    )
    dout_heads = d_attended.reshape(tok_rows, local_heads, HEAD_DIM)
    row_delta = jnp.sum(dout_heads.astype(jnp.float32) * attended, axis=2).T

    def query_step(frame_idx, running):
        scores, allowed, key_block, value_block = frame_scores(frame_idx)
        attn_prob = soft_weights(scores, allowed)
        d_prob = jnp.einsum(
            "qhd,khd->hqk", dout_heads, value_block, preferred_element_type=jnp.float32
        )
        d_scores = (attn_prob * (d_prob - row_delta[:, :, None])).astype(jnp.bfloat16)
        return running + jnp.einsum(
            "hqk,khd->qhd", d_scores, key_block, preferred_element_type=jnp.float32
        )

    query_sum = lax.fori_loop(
        0, frame_limit, query_step, jnp.zeros((tok_rows, local_heads, HEAD_DIM), jnp.float32)
    )
    d_query = (query_sum * score_scale).reshape(tok_rows, local_inner).astype(jnp.bfloat16)

    def one_frame(frame_step):
        scores, allowed, key_block, value_block = frame_scores(frame_step)
        attn_prob = soft_weights(scores, allowed)
        d_prob = jnp.einsum(
            "qhd,khd->hqk", dout_heads, value_block, preferred_element_type=jnp.float32
        )
        d_scores = (attn_prob * (d_prob - row_delta[:, :, None])).astype(jnp.bfloat16)
        key_term = (
            jnp.einsum("hqk,qhd->khd", d_scores, query_heads, preferred_element_type=jnp.float32)
            * score_scale
        )
        value_term = jnp.einsum(
            "hqk,qhd->khd",
            attn_prob.astype(jnp.bfloat16),
            dout_heads,
            preferred_element_type=jnp.float32,
        )
        return jnp.concatenate(
            [key_term.reshape(FRAME_TOK, local_inner), value_term.reshape(FRAME_TOK, local_inner)],
            axis=1,
        )

    blocks = lax.map(
        one_frame, jnp.arange(tok_rows * lax.axis_size("seq") // FRAME_TOK, dtype=jnp.int32)
    )
    kv_grad = lax.psum_scatter(
        blocks.reshape(tok_rows * lax.axis_size("seq"), 2 * local_inner).astype(jnp.bfloat16),
        "seq",
        scatter_dimension=0,
        tiled=True,
    ).astype(jnp.float32)
    d_key = kv_grad[:, :local_inner].astype(jnp.bfloat16)
    d_value = kv_grad[:, local_inner:].astype(jnp.bfloat16)
    grad_query = jnp.einsum("td,ti->di", first_in, d_query, preferred_element_type=jnp.float32)
    grad_key = jnp.einsum("td,ti->di", first_in, d_key, preferred_element_type=jnp.float32)
    grad_value = jnp.einsum("td,ti->di", first_in, d_value, preferred_element_type=jnp.float32)
    first_local = jnp.einsum("ti,di->td", d_query, query_w, preferred_element_type=jnp.float32)
    first_local = first_local + jnp.einsum(
        "ti,di->td", d_key, key_w, preferred_element_type=jnp.float32
    )
    first_local = first_local + jnp.einsum(
        "ti,di->td", d_value, value_w, preferred_element_type=jnp.float32
    )
    d_first = heads_total(first_local)
    grad_first_gain = jnp.sum(d_first * normed_one, axis=0)
    norm_pull_one = jax.vjp(norm_rows, resid_in)[1]
    grad_inputs = (d_mid + norm_pull_one(d_first * gain_one.astype(jnp.float32))[0]).astype(
        jnp.bfloat16
    )[None]
    summed_in = (
        lax.psum_scatter(
            grad_first_gain.astype(jnp.bfloat16), ("dp", "seq"), scatter_dimension=0, tiled=True
        ).astype(jnp.float32),
        lax.psum_scatter(
            grad_query.astype(jnp.bfloat16), ("dp", "seq"), scatter_dimension=0, tiled=True
        ).astype(jnp.float32),
        lax.psum_scatter(
            grad_key.astype(jnp.bfloat16), ("dp", "seq"), scatter_dimension=0, tiled=True
        ).astype(jnp.float32),
        lax.psum_scatter(
            grad_value.astype(jnp.bfloat16), ("dp", "seq"), scatter_dimension=0, tiled=True
        ).astype(jnp.float32),
        lax.psum_scatter(
            grad_second_gain.astype(jnp.bfloat16), ("dp", "seq"), scatter_dimension=0, tiled=True
        ).astype(jnp.float32),
        lax.psum_scatter(
            grad_up.astype(jnp.bfloat16), ("dp", "seq"), scatter_dimension=0, tiled=True
        ).astype(jnp.float32),
    )
    summed_out = (
        lax.psum_scatter(
            grad_out.astype(jnp.bfloat16), ("dp", "seq"), scatter_dimension=1, tiled=True
        ).astype(jnp.float32),
        lax.psum_scatter(
            grad_down.astype(jnp.bfloat16), ("dp", "seq"), scatter_dimension=1, tiled=True
        ).astype(jnp.float32),
    )
    return (
        result,
        grad_inputs,
        summed_in[0],
        summed_in[1],
        summed_in[2],
        summed_in[3],
        summed_out[0],
        summed_in[4],
        summed_in[5],
        summed_out[1],
    )


def shift(values, k):
    return lax.ppermute(values, "seq", [(i, (i + k) % SEQ) for i in range(SEQ)])


def swap_dp(values):
    return lax.ppermute(values, "dp", [(0, 1), (1, 0)])


def swap_chip(values):
    return lax.ppermute(values, "tensor", [(i, i ^ 2) for i in range(4)])


def swap_core(values):
    return lax.ppermute(values, "tensor", [(i, i ^ 1) for i in range(4)])


def tied(value, *others):
    return lax.optimization_barrier((value, *others))[0]


def gather_tensor(own):
    half = jnp.concatenate([own, swap_chip(own)], axis=0)
    return jnp.concatenate([half, swap_core(half)], axis=0)


def scatter_tensor(part):
    n = part.shape[0] // 4
    low = part.astype(jnp.bfloat16)
    half = part[: 2 * n].astype(jnp.float32) + swap_core(low[2 * n :]).astype(jnp.float32)
    other = swap_chip(half[n:].astype(jnp.bfloat16))
    return half[:n] + other.astype(jnp.float32)


def gather_blocks(own):
    mine = [own]
    for _ in range(SEQ - 1):
        mine.append(shift(mine[-1], 1))
    return mine, [swap_dp(block) for block in mine]


def scatter_blocks(parts):
    running = None
    for k in (1, 2, 3, 0):
        total = parts[k].astype(jnp.float32) + swap_dp(parts[SEQ + k]).astype(jnp.float32)
        if running is not None:
            total = total + running.astype(jnp.float32)
        if k:
            running = shift(total.astype(jnp.bfloat16), 1)
    return total


def dyn(stack, index):
    return lax.dynamic_index_in_dim(stack, index, 0, keepdims=False)


def attend_kernel(place_ref, valid_ref, q_ref, k_ref, v_ref, out_ref, lse_ref, peak, total, acc):
    place = place_ref[0]
    scale = HEAD_DIM ** (-0.5)

    def query_frame(i, carry):
        at = lax.rem(place - i + SEQ, SEQ)
        query = q_ref[at]
        peak[...] = jnp.full_like(peak, MASK_FILL)
        total[...] = jnp.zeros_like(total)
        acc[...] = jnp.zeros_like(acc)

        def key_frame(j, inner):
            @pl.when(valid_ref[j] == 1)
            def _():
                here = lax.rem(place - j + SEQ, SEQ)
                scores = lax.dot_general(k_ref[here], query, (((1,), (1,)), ((), ())), preferred_element_type=jnp.float32) * scale
                before = peak[...]
                after = jnp.maximum(before, jnp.max(scores, axis=0, keepdims=True))
                terms = jnp.exp(scores - after)
                fix = jnp.exp(before - after)
                peak[...] = after
                total[...] = total[...] * fix + jnp.sum(terms, axis=0, keepdims=True)
                acc[...] = acc[...] * fix + lax.dot_general(v_ref[here], terms.astype(jnp.bfloat16), (((0,), (0,)), ((), ())), preferred_element_type=jnp.float32)

            return inner

        lax.fori_loop(0, i + 1, key_frame, 0)
        out_ref[at] = (acc[...] / total[...]).T
        lse_ref[at] = peak[...] + jnp.log(total[...])
        return carry

    lax.fori_loop(0, SEQ, query_frame, 0)


def attend(place, valid, query, key, value):
    rows = query.shape[1]
    smem = pl.BlockSpec(memory_space=pltpu.SMEM)
    vmem = pl.BlockSpec(memory_space=pltpu.VMEM)
    return pl.pallas_call(
        attend_kernel,
        out_shape=(jax.ShapeDtypeStruct(query.shape, jnp.float32), jax.ShapeDtypeStruct((SEQ, 1, rows), jnp.float32)),
        in_specs=[smem, smem, vmem, vmem, vmem],
        out_specs=(vmem, vmem),
        scratch_shapes=[pltpu.VMEM((1, rows), jnp.float32), pltpu.VMEM((1, rows), jnp.float32), pltpu.VMEM((HEAD_DIM, rows), jnp.float32)],
        compiler_params=pltpu.CompilerParams(vmem_limit_bytes=40 * 2**20),
        cost_estimate=pl.CostEstimate(flops=4 * 10 * rows * rows * HEAD_DIM * 2, bytes_accessed=6 * query.size, transcendentals=10 * rows * rows),
    )(place, valid, query, key, value)


def attend_back_kernel(place_ref, valid_ref, q_ref, k_ref, v_ref, out_ref, lse_ref, do_ref, grad_ref, delta, dq, dk, dv):
    place = place_ref[0]
    scale = HEAD_DIM ** (-0.5)
    dq[...] = jnp.zeros_like(dq)
    for f in range(SEQ):
        delta[f] = jnp.sum((do_ref[f].astype(jnp.float32) * out_ref[f]).T, axis=0, keepdims=True)

    def key_frame(j, carry):
        here = lax.rem(place - j + SEQ, SEQ)
        dk[...] = jnp.zeros_like(dk)
        dv[...] = jnp.zeros_like(dv)

        @pl.when(valid_ref[j] == 1)
        def _():
            def query_frame(i, inner):
                at = lax.rem(place - i + SEQ, SEQ)
                query, key, value, d_out = q_ref[at], k_ref[here], v_ref[here], do_ref[at]
                scores = lax.dot_general(key, query, (((1,), (1,)), ((), ())), preferred_element_type=jnp.float32) * scale
                prob = jnp.exp(scores - lse_ref[at])
                d_prob = lax.dot_general(value, d_out, (((1,), (1,)), ((), ())), preferred_element_type=jnp.float32)
                d_scores = (prob * (d_prob - delta[at])).astype(jnp.bfloat16)
                dv[...] += jnp.dot(prob.astype(jnp.bfloat16), d_out, preferred_element_type=jnp.float32)
                dk[...] += jnp.dot(d_scores, query, preferred_element_type=jnp.float32)
                dq[at] += lax.dot_general(key, d_scores, (((0,), (0,)), ((), ())), preferred_element_type=jnp.float32)
                return inner

            lax.fori_loop(j, SEQ, query_frame, 0)

        grad_ref[here, :, HEAD_DIM : 2 * HEAD_DIM] = (dk[...] * scale).astype(jnp.bfloat16)
        grad_ref[here, :, 2 * HEAD_DIM :] = dv[...].astype(jnp.bfloat16)
        return carry

    lax.fori_loop(0, SEQ, key_frame, 0)
    for f in range(SEQ):
        grad_ref[f, :, :HEAD_DIM] = (dq[f] * scale).T.astype(jnp.bfloat16)


def attend_back(place, valid, query, key, value, out, lse, d_out):
    rows = query.shape[1]
    smem = pl.BlockSpec(memory_space=pltpu.SMEM)
    vmem = pl.BlockSpec(memory_space=pltpu.VMEM)
    return pl.pallas_call(
        attend_back_kernel,
        out_shape=jax.ShapeDtypeStruct((SEQ, rows, 3 * HEAD_DIM), jnp.bfloat16),
        in_specs=[smem, smem] + [vmem] * 6,
        out_specs=vmem,
        scratch_shapes=[
            pltpu.VMEM((SEQ, 1, rows), jnp.float32),
            pltpu.VMEM((SEQ, HEAD_DIM, rows), jnp.float32),
            pltpu.VMEM((rows, HEAD_DIM), jnp.float32),
            pltpu.VMEM((rows, HEAD_DIM), jnp.float32),
        ],
        compiler_params=pltpu.CompilerParams(vmem_limit_bytes=48 * 2**20),
        cost_estimate=pl.CostEstimate(flops=10 * 10 * rows * rows * HEAD_DIM * 2, bytes_accessed=12 * query.size, transcendentals=10 * rows * rows),
    )(place, valid, query, key, value, out, lse, d_out)


def norm_parts(values):
    center = values - jnp.mean(values, axis=-1, keepdims=True)
    rate = lax.rsqrt(jnp.mean(center * center, axis=-1, keepdims=True) + NORM_EPS)
    return center * rate, rate


def norm_back(normed, rate, grad):
    return rate * (grad - jnp.mean(grad, axis=-1, keepdims=True) - normed * jnp.mean(grad * normed, axis=-1, keepdims=True))


def mm(left, right, dims=((1,), (0,)), out=jnp.bfloat16):
    return lax.dot_general(left, right, (dims, ((), ())), preferred_element_type=jnp.float32).astype(out)


def local_fast(inputs, first_gain, w_query, w_key, w_value, w_out, second_gain, w_up, w_down, frame_mask, cotangent):
    dp, z, t = lax.axis_index("dp"), lax.axis_index("seq"), lax.axis_index("tensor")
    rows = inputs.shape[1]
    quarter = rows // 4
    width = inputs.shape[2]
    part = width // (2 * SEQ)
    heads = w_query.shape[1] // HEAD_DIM
    f32, bf16 = jnp.float32, jnp.bfloat16

    def rel_block(b):
        return (dp ^ (b // SEQ)) * SEQ + lax.rem(z - b % SEQ + SEQ, SEQ)

    def rel_cols(values):
        return jnp.concatenate([lax.dynamic_slice_in_dim(values, rel_block(b) * part, part, 1) for b in range(2 * SEQ)], axis=1)

    def can_cols(values):
        picks = []
        for c in range(2 * SEQ):
            b = (dp ^ (c // SEQ)) * SEQ + lax.rem(z - c % SEQ + SEQ, SEQ)
            picks.append(lax.dynamic_slice_in_dim(values, b * part, part, 1))
        return jnp.concatenate(picks, axis=1)

    def rel_rows(values):
        return jnp.concatenate([lax.dynamic_slice_in_dim(values, (t ^ p) * quarter, quarter, 0) for p in (0, 2, 1, 3)], axis=0)

    def can_rows(values):
        picks = []
        for c in range(4):
            d = t ^ c
            p = (d % 2) * 2 + d // 2
            picks.append(lax.dynamic_slice_in_dim(values, p * quarter, quarter, 0))
        return jnp.concatenate(picks, axis=0)

    own_in = inputs[0]
    normed_one_all = norm_parts(own_in.astype(f32))[0].astype(bf16)
    frame0 = rel_rows(normed_one_all)
    first = [frame0[:quarter]]
    for _ in range(SEQ - 1):
        first.append(shift(first[-1], 1))
    frames = [frame0] + [gather_tensor(first[k]) for k in range(1, SEQ)]

    w_three = jnp.stack([w_query, w_key, w_value], axis=1).reshape(part, 3, heads, HEAD_DIM)
    w_three = (w_three.astype(f32) * first_gain.astype(f32)[:, None, None, None]).astype(bf16)
    w_three = w_three.transpose(2, 0, 1, 3).reshape(heads, part, 3 * HEAD_DIM)
    mine = [dyn(w_three, z)] + [shift(dyn(w_three, lax.rem(z + k, SEQ)), k) for k in range(1, SEQ)]
    mine = jnp.stack(mine)
    both = jnp.concatenate([mine, swap_dp(mine)], axis=0)
    w_head = jnp.concatenate([dyn(both, (dp ^ (c // SEQ)) * SEQ + lax.rem(z - c % SEQ + SEQ, SEQ)) for c in range(2 * SEQ)], axis=0)

    out_mine, out_other = gather_blocks(w_out)
    out_rel = jnp.concatenate(out_mine + out_other, axis=1)
    w_up_scaled = (w_up.astype(f32) * second_gain.astype(f32)[:, None]).astype(bf16)
    up_mine, up_other = gather_blocks(w_up_scaled)
    up_rel = jnp.concatenate(up_mine + up_other, axis=0)
    down_mine, down_other = gather_blocks(w_down)
    down_rel = jnp.concatenate(down_mine + down_other, axis=1)

    qkv = [mm(frame, w_head) for frame in frames]
    query, key, value = (jnp.stack([one[:, n * HEAD_DIM : (n + 1) * HEAD_DIM] for one in qkv]) for n in range(3))
    place = z.reshape(1)
    valid = frame_mask[0]
    attended_f, lse = attend(place, valid, query, key, value)
    attended_low = attended_f.astype(bf16)
    came = jnp.stack([attended_low[0]] + [shift(attended_low[k], -k) for k in range(1, SEQ)])
    attended = jnp.concatenate([dyn(came, lax.rem(h - z + SEQ, SEQ)) for h in range(heads)], axis=1)

    own_rel = rel_cols(lax.dynamic_slice_in_dim(own_in, t * quarter, quarter, 0)).astype(f32)
    resid_mid = own_rel + scatter_tensor(mm(attended, out_rel))
    normed_two, rate_two = norm_parts(resid_mid)
    second_in = gather_tensor(normed_two.astype(bf16))

    cot_rel = rel_cols(rel_rows(cotangent[0]))
    up_pre = mm(second_in, up_rel, out=f32)
    cdf = 0.5 * (1.0 + lax.erf(up_pre * (0.5**0.5)))
    up_act = (up_pre * cdf).astype(bf16)
    slope = cdf + up_pre * jnp.exp(-0.5 * up_pre * up_pre) * ((2.0 * jnp.pi) ** -0.5)
    grad_down = mm(up_act, cot_rel, ((0,), (0,)))
    d_up = (mm(cot_rel, down_rel, ((1,), (1,)), f32) * slope).astype(bf16)
    result = resid_mid + scatter_tensor(mm(up_act, down_rel))
    result = can_rows(gather_tensor(can_cols(result.astype(bf16))))[None]
    grad_up = mm(second_in, d_up, ((0,), (0,)))
    d_normed_two = scatter_tensor(mm(d_up, up_rel, ((1,), (1,))))
    cot_own = cot_rel[:quarter].astype(f32)
    d_mid = cot_own + norm_back(normed_two, rate_two, d_normed_two)
    d_mix = gather_tensor(d_mid.astype(bf16))
    grad_out = mm(attended, d_mix, ((0,), (0,)))
    d_attended = mm(d_mix, out_rel, ((1,), (1,)))
    d_heads = jnp.stack([d_attended[:, h * HEAD_DIM : (h + 1) * HEAD_DIM] for h in range(heads)])
    d_out = jnp.stack([dyn(d_heads, z)] + [shift(dyn(d_heads, lax.rem(z + k, SEQ)), k) for k in range(1, SEQ)])

    d_three = attend_back(place, valid, query, key, value, attended_f, lse, d_out)
    whole = jnp.concatenate(frames, axis=0)
    grad_head = mm(whole, d_three.reshape(SEQ * rows, 3 * HEAD_DIM), ((0,), (0,)))
    grad_head = grad_head.reshape(2, SEQ * part, 3 * HEAD_DIM)
    grad_rows = dyn(grad_head, dp).astype(f32) + swap_dp(dyn(grad_head, 1 - dp)).astype(f32)
    grad_rows = grad_rows.astype(bf16).reshape(SEQ, part, 3 * HEAD_DIM)
    arrived = jnp.stack([dyn(grad_rows, z)] + [shift(dyn(grad_rows, lax.rem(z + k, SEQ)), k) for k in range(1, SEQ)])
    by_head = [dyn(arrived, lax.rem(z - h + SEQ, SEQ)).astype(f32) for h in range(heads)]
    gain_one = first_gain.astype(f32)[:, None]
    raw = [jnp.concatenate([one[:, n * HEAD_DIM : (n + 1) * HEAD_DIM] for one in by_head], axis=1) for n in range(3)]
    d_gain_one = sum(jnp.sum(weight.astype(f32) * one, axis=1) for weight, one in zip((w_query, w_key, w_value), raw))

    running = None
    for k in (1, 2, 3, 0):
        total = scatter_tensor(mm(d_three[k], w_head, ((1,), (1,))))
        if running is not None:
            total = total + running.astype(f32)
        if k:
            running = shift(total.astype(bf16), 1)
    own_quarter = lax.dynamic_slice_in_dim(own_in, t * quarter, quarter, 0).astype(f32)
    normed_one, rate_one = norm_parts(own_quarter)
    d_in = can_cols(d_mid) + norm_back(normed_one, rate_one, total)
    grad_inputs = can_rows(gather_tensor(d_in.astype(bf16)))[None]

    down_sum = scatter_blocks([grad_down[:, b * part : (b + 1) * part] for b in range(2 * SEQ)])
    up_raw = scatter_blocks([grad_up[b * part : (b + 1) * part] for b in range(2 * SEQ)])
    out_sum = scatter_blocks([grad_out[:, b * part : (b + 1) * part] for b in range(2 * SEQ)])
    d_gain_two = jnp.sum(w_up.astype(f32) * up_raw, axis=1)
    gains = jnp.stack([d_gain_one, d_gain_two])
    gains = gains + swap_core(gains)
    gains = gains + swap_chip(gains)
    return (
        result,
        grad_inputs,
        gains[0],
        raw[0] * gain_one,
        raw[1] * gain_one,
        raw[2] * gain_one,
        out_sum,
        gains[1],
        up_raw * second_gain.astype(f32)[:, None],
        down_sum,
    )


SEQ = 4


def solution(mesh):
    placed = (
        P("dp", "seq", None),
        P(("dp", "seq")),
        P(("dp", "seq"), "tensor"),
        P(("dp", "seq"), "tensor"),
        P(("dp", "seq"), "tensor"),
        P("tensor", ("dp", "seq")),
        P(("dp", "seq")),
        P(("dp", "seq"), "tensor"),
        P("tensor", ("dp", "seq")),
        P("dp", None),
        P("dp", "seq", None),
    )
    sizes = dict(mesh.shape)
    spread = sizes == {"dp": 2, "seq": SEQ, "tensor": 4}
    return jax.shard_map(
        local_fast if spread else local,
        mesh=mesh,
        in_specs=placed,
        out_specs=(
            P("dp", "seq", None),
            P("dp", "seq", None),
            P(("dp", "seq")),
            P(("dp", "seq"), "tensor"),
            P(("dp", "seq"), "tensor"),
            P(("dp", "seq"), "tensor"),
            P("tensor", ("dp", "seq")),
            P(("dp", "seq")),
            P(("dp", "seq"), "tensor"),
            P("tensor", ("dp", "seq")),
        ),
        check_vma=False,
    )
```

```python
import functools

import jax
import jax.numpy as jnp
from jax import lax
from jax.experimental import pallas as pl
from jax.experimental.pallas import tpu as pltpu
from jax.sharding import PartitionSpec as P

HEAD_DIM = 128
FRAME_TOK = 640


NORM_EPS = 1e-05
MASK_FILL = -1e30
MESH = pl.DeviceIdType.MESH


def norm_rows(values):
    center = values - jnp.mean(values, axis=-1, keepdims=True)
    spread = jnp.mean(center * center, axis=-1, keepdims=True)
    return center * lax.rsqrt(spread + NORM_EPS)


def gelu_exact(values):
    return jax.nn.gelu(values, approximate=False)


def heads_total(values):
    return lax.psum(values.astype(jnp.bfloat16), "tensor").astype(jnp.float32)


def local(
    inputs,
    first_gain,
    w_query,
    w_key,
    w_value,
    w_out,
    second_gain,
    w_up,
    w_down,
    frame_mask,
    cotangent,
):
    seq_pos = lax.axis_index("seq")
    gain_one, query_w, key_w, value_w, gain_two, up_w = (
        lax.all_gather(first_gain, ("dp", "seq"), axis=0, tiled=True),
        lax.all_gather(w_query, ("dp", "seq"), axis=0, tiled=True),
        lax.all_gather(w_key, ("dp", "seq"), axis=0, tiled=True),
        lax.all_gather(w_value, ("dp", "seq"), axis=0, tiled=True),
        lax.all_gather(second_gain, ("dp", "seq"), axis=0, tiled=True),
        lax.all_gather(w_up, ("dp", "seq"), axis=0, tiled=True),
    )
    out_w, down_w = (
        lax.all_gather(w_out, ("dp", "seq"), axis=1, tiled=True),
        lax.all_gather(w_down, ("dp", "seq"), axis=1, tiled=True),
    )
    tok_rows = inputs.shape[1]
    local_inner = query_w.shape[1]
    local_heads = local_inner // HEAD_DIM
    frames_dev = tok_rows // FRAME_TOK
    score_scale = HEAD_DIM ** (-0.5)
    clip_valid = frame_mask[0]
    frame_count = clip_valid.shape[0]
    resid_in = inputs[0].astype(jnp.float32)
    dout_rows = cotangent[0]
    row_frame = seq_pos * frames_dev + jnp.arange(tok_rows, dtype=jnp.int32) // FRAME_TOK
    frame_limit = (seq_pos + 1) * frames_dev
    normed_one = norm_rows(resid_in)
    first_in = (normed_one * gain_one.astype(jnp.float32)).astype(jnp.bfloat16)
    query = jnp.dot(first_in, query_w, preferred_element_type=jnp.float32).astype(jnp.bfloat16)
    key_local = jnp.dot(first_in, key_w, preferred_element_type=jnp.float32).astype(jnp.bfloat16)
    value_local = jnp.dot(first_in, value_w, preferred_element_type=jnp.float32).astype(
        jnp.bfloat16
    )
    key_all, value_all = (
        lax.all_gather(key_local, "seq", axis=0, tiled=True),
        lax.all_gather(value_local, "seq", axis=0, tiled=True),
    )
    query_heads = query.reshape(tok_rows, local_heads, HEAD_DIM)
    key_frames = key_all.reshape(frame_count, FRAME_TOK, local_heads, HEAD_DIM)
    value_frames = value_all.reshape(frame_count, FRAME_TOK, local_heads, HEAD_DIM)

    def frame_scores(frame_idx):
        key_block = lax.dynamic_index_in_dim(key_frames, frame_idx, 0, keepdims=False)
        value_block = lax.dynamic_index_in_dim(value_frames, frame_idx, 0, keepdims=False)
        scores = (
            jnp.einsum("qhd,khd->hqk", query_heads, key_block, preferred_element_type=jnp.float32)
            * score_scale
        )
        frame_ok = lax.dynamic_index_in_dim(clip_valid, frame_idx, 0, keepdims=False) == 1
        allowed = ((frame_idx <= row_frame) & frame_ok)[None, :, None]
        return (scores, allowed, key_block, value_block)

    def stats_step(frame_idx, running):
        row_max, row_sum = running
        scores, allowed, key_block, value_block = frame_scores(frame_idx)
        masked = jnp.where(allowed, scores, MASK_FILL)
        new_max = jnp.maximum(row_max, jnp.max(masked, axis=2))
        exp_terms = jnp.where(allowed, jnp.exp(masked - new_max[:, :, None]), 0.0)
        return (new_max, row_sum * jnp.exp(row_max - new_max) + jnp.sum(exp_terms, axis=2))

    start_stats = (
        jnp.full((local_heads, tok_rows), MASK_FILL, jnp.float32),
        jnp.zeros((local_heads, tok_rows), jnp.float32),
    )
    row_max, row_sum = lax.fori_loop(0, frame_limit, stats_step, start_stats)

    def soft_weights(scores, allowed):
        return jnp.where(allowed, jnp.exp(scores - row_max[:, :, None]) / row_sum[:, :, None], 0.0)

    def output_step(frame_idx, running):
        scores, allowed, key_block, value_block = frame_scores(frame_idx)
        attn_prob = soft_weights(scores, allowed).astype(jnp.bfloat16)
        return running + jnp.einsum(
            "hqk,khd->qhd", attn_prob, value_block, preferred_element_type=jnp.float32
        )

    attended = lax.fori_loop(
        0, frame_limit, output_step, jnp.zeros((tok_rows, local_heads, HEAD_DIM), jnp.float32)
    )
    attended_low = attended.reshape(tok_rows, local_inner).astype(jnp.bfloat16)
    resid_mid = resid_in + heads_total(
        jnp.dot(attended_low, out_w, preferred_element_type=jnp.float32)
    )
    normed_two = norm_rows(resid_mid)
    second_in = (normed_two * gain_two.astype(jnp.float32)).astype(jnp.bfloat16)
    up_pre = jnp.dot(second_in, up_w, preferred_element_type=jnp.float32)
    up_act = gelu_exact(up_pre).astype(jnp.bfloat16)
    resid_out = resid_mid + heads_total(jnp.dot(up_act, down_w, preferred_element_type=jnp.float32))
    result = resid_out.astype(jnp.bfloat16)[None]
    grad_down = jnp.einsum("tf,td->fd", up_act, dout_rows, preferred_element_type=jnp.float32)
    d_act = jnp.einsum("td,fd->tf", dout_rows, down_w, preferred_element_type=jnp.float32)
    gelu_pull = jax.vjp(gelu_exact, up_pre)[1]
    d_up_pre = gelu_pull(d_act)[0].astype(jnp.bfloat16)
    grad_up = jnp.einsum("td,tf->df", second_in, d_up_pre, preferred_element_type=jnp.float32)
    d_second = heads_total(
        jnp.einsum("tf,df->td", d_up_pre, up_w, preferred_element_type=jnp.float32)
    )
    grad_second_gain = jnp.sum(d_second * normed_two, axis=0)
    norm_pull_two = jax.vjp(norm_rows, resid_mid)[1]
    d_mid = (
        dout_rows.astype(jnp.float32) + norm_pull_two(d_second * gain_two.astype(jnp.float32))[0]
    )
    d_mix = d_mid.astype(jnp.bfloat16)
    grad_out = jnp.einsum("ti,td->id", attended_low, d_mix, preferred_element_type=jnp.float32)
    d_attended = jnp.einsum("td,id->ti", d_mix, out_w, preferred_element_type=jnp.float32).astype(
        jnp.bfloat16
    )
    dout_heads = d_attended.reshape(tok_rows, local_heads, HEAD_DIM)
    row_delta = jnp.sum(dout_heads.astype(jnp.float32) * attended, axis=2).T

    def query_step(frame_idx, running):
        scores, allowed, key_block, value_block = frame_scores(frame_idx)
        attn_prob = soft_weights(scores, allowed)
        d_prob = jnp.einsum(
            "qhd,khd->hqk", dout_heads, value_block, preferred_element_type=jnp.float32
        )
        d_scores = (attn_prob * (d_prob - row_delta[:, :, None])).astype(jnp.bfloat16)
        return running + jnp.einsum(
            "hqk,khd->qhd", d_scores, key_block, preferred_element_type=jnp.float32
        )

    query_sum = lax.fori_loop(
        0, frame_limit, query_step, jnp.zeros((tok_rows, local_heads, HEAD_DIM), jnp.float32)
    )
    d_query = (query_sum * score_scale).reshape(tok_rows, local_inner).astype(jnp.bfloat16)

    def one_frame(frame_step):
        scores, allowed, key_block, value_block = frame_scores(frame_step)
        attn_prob = soft_weights(scores, allowed)
        d_prob = jnp.einsum(
            "qhd,khd->hqk", dout_heads, value_block, preferred_element_type=jnp.float32
        )
        d_scores = (attn_prob * (d_prob - row_delta[:, :, None])).astype(jnp.bfloat16)
        key_term = (
            jnp.einsum("hqk,qhd->khd", d_scores, query_heads, preferred_element_type=jnp.float32)
            * score_scale
        )
        value_term = jnp.einsum(
            "hqk,qhd->khd",
            attn_prob.astype(jnp.bfloat16),
            dout_heads,
            preferred_element_type=jnp.float32,
        )
        return jnp.concatenate(
            [key_term.reshape(FRAME_TOK, local_inner), value_term.reshape(FRAME_TOK, local_inner)],
            axis=1,
        )

    blocks = lax.map(
        one_frame, jnp.arange(tok_rows * lax.axis_size("seq") // FRAME_TOK, dtype=jnp.int32)
    )
    kv_grad = lax.psum_scatter(
        blocks.reshape(tok_rows * lax.axis_size("seq"), 2 * local_inner).astype(jnp.bfloat16),
        "seq",
        scatter_dimension=0,
        tiled=True,
    ).astype(jnp.float32)
    d_key = kv_grad[:, :local_inner].astype(jnp.bfloat16)
    d_value = kv_grad[:, local_inner:].astype(jnp.bfloat16)
    grad_query = jnp.einsum("td,ti->di", first_in, d_query, preferred_element_type=jnp.float32)
    grad_key = jnp.einsum("td,ti->di", first_in, d_key, preferred_element_type=jnp.float32)
    grad_value = jnp.einsum("td,ti->di", first_in, d_value, preferred_element_type=jnp.float32)
    first_local = jnp.einsum("ti,di->td", d_query, query_w, preferred_element_type=jnp.float32)
    first_local = first_local + jnp.einsum(
        "ti,di->td", d_key, key_w, preferred_element_type=jnp.float32
    )
    first_local = first_local + jnp.einsum(
        "ti,di->td", d_value, value_w, preferred_element_type=jnp.float32
    )
    d_first = heads_total(first_local)
    grad_first_gain = jnp.sum(d_first * normed_one, axis=0)
    norm_pull_one = jax.vjp(norm_rows, resid_in)[1]
    grad_inputs = (d_mid + norm_pull_one(d_first * gain_one.astype(jnp.float32))[0]).astype(
        jnp.bfloat16
    )[None]
    summed_in = (
        lax.psum_scatter(
            grad_first_gain.astype(jnp.bfloat16), ("dp", "seq"), scatter_dimension=0, tiled=True
        ).astype(jnp.float32),
        lax.psum_scatter(
            grad_query.astype(jnp.bfloat16), ("dp", "seq"), scatter_dimension=0, tiled=True
        ).astype(jnp.float32),
        lax.psum_scatter(
            grad_key.astype(jnp.bfloat16), ("dp", "seq"), scatter_dimension=0, tiled=True
        ).astype(jnp.float32),
        lax.psum_scatter(
            grad_value.astype(jnp.bfloat16), ("dp", "seq"), scatter_dimension=0, tiled=True
        ).astype(jnp.float32),
        lax.psum_scatter(
            grad_second_gain.astype(jnp.bfloat16), ("dp", "seq"), scatter_dimension=0, tiled=True
        ).astype(jnp.float32),
        lax.psum_scatter(
            grad_up.astype(jnp.bfloat16), ("dp", "seq"), scatter_dimension=0, tiled=True
        ).astype(jnp.float32),
    )
    summed_out = (
        lax.psum_scatter(
            grad_out.astype(jnp.bfloat16), ("dp", "seq"), scatter_dimension=1, tiled=True
        ).astype(jnp.float32),
        lax.psum_scatter(
            grad_down.astype(jnp.bfloat16), ("dp", "seq"), scatter_dimension=1, tiled=True
        ).astype(jnp.float32),
    )
    return (
        result,
        grad_inputs,
        summed_in[0],
        summed_in[1],
        summed_in[2],
        summed_in[3],
        summed_out[0],
        summed_in[4],
        summed_in[5],
        summed_out[1],
    )


def shift(values, k):
    return lax.ppermute(values, "seq", [(i, (i + k) % SEQ) for i in range(SEQ)])


def swap_dp(values):
    return lax.ppermute(values, "dp", [(0, 1), (1, 0)])


def swap_chip(values):
    return lax.ppermute(values, "tensor", [(i, i ^ 2) for i in range(4)])


def swap_core(values):
    return lax.ppermute(values, "tensor", [(i, i ^ 1) for i in range(4)])


def tied(value, *others):
    return lax.optimization_barrier((value, *others))[0]


def gather_tensor(own):
    half = jnp.concatenate([own, swap_chip(own)], axis=0)
    return jnp.concatenate([half, swap_core(half)], axis=0)


def scatter_tensor(part):
    n = part.shape[0] // 4
    low = part.astype(jnp.bfloat16)
    half = part[: 2 * n].astype(jnp.float32) + swap_core(low[2 * n :]).astype(jnp.float32)
    other = swap_chip(half[n:].astype(jnp.bfloat16))
    return half[:n] + other.astype(jnp.float32)


def gather_blocks(own):
    mine = [own]
    for _ in range(SEQ - 1):
        mine.append(shift(mine[-1], 1))
    return mine, [swap_dp(block) for block in mine]


def scatter_blocks(parts):
    running = None
    for k in (1, 2, 3, 0):
        total = parts[k].astype(jnp.float32) + swap_dp(parts[SEQ + k]).astype(jnp.float32)
        if running is not None:
            total = total + running.astype(jnp.float32)
        if k:
            running = shift(total.astype(jnp.bfloat16), 1)
    return total


def dyn(stack, index):
    return lax.dynamic_index_in_dim(stack, index, 0, keepdims=False)


def front_kernel(
    f0_ref, w_three_ref, w_out_ref, w_up_ref, w_down_ref, own_ref, bias_ref,
    whole_ref, w_head_ref, qkv_ref, att_ref, lse_ref, attended_ref, out_ref, resid_ref, normed_ref, rate_ref, second_ref, up_ref, down_ref,
    frames, w_stack, out_all, att_low, came, part_low, core_in, half_low, chip_in, second, peak, total, acc, send, recv, local_sem,
):
    dp, z, t = lax.axis_index("dp"), lax.axis_index("seq"), lax.axis_index("tensor")
    other_dp, chip, core = {"dp": 1 - dp}, {"tensor": lax.rem(t + 2, 4)}, {"tensor": t + 1 - 2 * lax.rem(t, 2)}

    def along(k):
        return {"seq": lax.rem(z + k + SEQ, SEQ)}

    rows, width = f0_ref.shape
    quarter = rows // 4
    half = rows // 2
    part = w_out_ref.shape[1]
    used = []

    def remote(src, dst, device):
        i = len(used)
        copy = pltpu.make_async_remote_copy(src_ref=src, dst_ref=dst, send_sem=send.at[i], recv_sem=recv.at[i], device_id=device, device_id_type=MESH)
        used.append(copy)
        return copy

    kept = []

    def keep(src, dst):
        copy = pltpu.make_async_copy(src, dst, local_sem.at[len(kept)])
        kept.append(copy)
        copy.start()
        return copy

    barrier = pltpu.get_barrier_semaphore()
    peers = [other_dp, chip, core] + [along(k) for k in range(1, SEQ)]
    for peer in peers:
        pl.semaphore_signal(barrier, inc=1, device_id=peer, device_id_type=MESH)
    pl.semaphore_wait(barrier, len(peers))

    def out_at(b):
        return out_all.at[:, pl.ds(b * part, part)]

    def up_at(b):
        return up_ref.at[pl.ds(b * part, part), :]

    def down_at(b):
        return down_ref.at[:, pl.ds(b * part, part)]

    ring = along(1)
    token = [None] + [remote(f0_ref.at[pl.ds(0, quarter), :] if k == 1 else frames.at[k - 1, pl.ds(0, quarter), :], frames.at[k, pl.ds(0, quarter), :], ring) for k in range(1, SEQ)]
    token_chip = [None] + [remote(frames.at[k, pl.ds(0, quarter), :], frames.at[k, pl.ds(quarter, quarter), :], chip) for k in range(1, SEQ)]
    token_core = [None] + [remote(frames.at[k, pl.ds(0, half), :], frames.at[k, pl.ds(half, half), :], core) for k in range(1, SEQ)]
    head = [None] + [remote(w_three_ref.at[lax.rem(z + k, SEQ)], w_stack.at[k], along(k)) for k in range(1, SEQ)]
    head_dp = remote(w_stack.at[pl.ds(0, SEQ)], w_stack.at[pl.ds(SEQ, SEQ)], other_dp)

    def gather(shard, at):
        step = [None] + [remote(shard if k == 1 else at(k - 1), at(k), ring) for k in range(1, SEQ)]
        cross = [remote(shard if k == 0 else at(k), at(SEQ + k), other_dp) for k in range(SEQ)]
        return step, cross

    out_step, out_dp = gather(w_out_ref, out_at)
    up_step, up_dp = gather(w_up_ref, up_at)
    down_step, down_dp = gather(w_down_ref, down_at)
    first_back = len(used) - 1
    back = [None] + [remote(att_low.at[k], came.at[k], along(-k)) for k in range(1, SEQ)]
    sum_core = remote(part_low.at[pl.ds(half, half), :], core_in, core)
    sum_chip = remote(half_low, chip_in, chip)
    second_chip = remote(second.at[pl.ds(0, quarter), :], second.at[pl.ds(quarter, quarter), :], chip)
    second_core = remote(second.at[pl.ds(0, half), :], second.at[pl.ds(half, half), :], core)

    def pass_on(steps, cross, k):
        steps[k].wait_recv()
        if k + 1 < SEQ:
            steps[k + 1].start()
        cross[k].start()

    token[1].start()
    for k in range(1, SEQ):
        head[k].start()
    up_dp[0].start()
    out_dp[0].start()
    own_frame = keep(f0_ref, frames.at[0])
    own_head = keep(w_three_ref.at[z], w_stack.at[0])
    own_out = keep(w_out_ref, out_at(0))
    keep(w_up_ref, up_at(0))
    keep(w_down_ref, down_at(0))
    own_head.wait()
    own_frame.wait()
    token[1].wait_recv()
    token[2].start()
    token_chip[1].start()
    for k in range(1, SEQ):
        head[k].wait_recv()
    head_dp.start()
    token[2].wait_recv()
    token[3].start()
    token_chip[2].start()
    token_chip[1].wait_recv()
    token_core[1].start()
    out_step[1].start()
    up_step[1].start()
    head_dp.wait_recv()
    down_dp[0].start()
    for c in range(2 * SEQ):
        b = lax.rem(dp + c // SEQ, 2) * SEQ + lax.rem(z - c % SEQ + SEQ, SEQ)
        w_head_ref[c * part : (c + 1) * part, :] = w_stack[b]

    def project(k):
        def piece(n, carry):
            at = pl.ds(n * quarter, quarter)
            qkv_ref[k, at, :] = jnp.dot(frames[k, at, :], w_head_ref[...], preferred_element_type=jnp.float32).astype(jnp.bfloat16)
            return carry

        lax.fori_loop(0, 4, piece, 0)

    project(0)
    token_core[1].wait_recv()
    keep(frames.at[1], whole_ref.at[1])
    project(1)
    token_chip[2].wait_recv()
    token_core[2].start()
    token[3].wait_recv()
    token_chip[3].start()
    token_core[2].wait_recv()
    keep(frames.at[2], whole_ref.at[2])
    project(2)
    pass_on(out_step, out_dp, 1)
    token_chip[3].wait_recv()
    token_core[3].start()
    token_core[3].wait_recv()
    keep(frames.at[0], whole_ref.at[0])
    keep(frames.at[3], whole_ref.at[3])
    project(3)

    scale = HEAD_DIM ** (-0.5)

    def query_frame(i):
        at = lax.rem(z - i + SEQ, SEQ)
        query = qkv_ref[at, :, 0:HEAD_DIM]
        peak[...] = jnp.full_like(peak, MASK_FILL)
        total[...] = jnp.zeros_like(total)
        acc[...] = jnp.zeros_like(acc)

        def key_frame(j, inner):
            here = lax.rem(z - j + SEQ, SEQ)
            scores = lax.dot_general(qkv_ref[here, :, HEAD_DIM : 2 * HEAD_DIM], query, (((1,), (1,)), ((), ())), preferred_element_type=jnp.float32) * scale + bias_ref[j]
            before = peak[...]
            after = jnp.maximum(before, jnp.max(scores, axis=0, keepdims=True))
            terms = jnp.exp(scores - after)
            fix = jnp.exp(before - after)
            peak[...] = after
            total[...] = total[...] * fix + jnp.sum(terms, axis=0, keepdims=True)
            acc[...] = acc[...] * fix + lax.dot_general(qkv_ref[here, :, 2 * HEAD_DIM :], terms.astype(jnp.bfloat16), (((0,), (0,)), ((), ())), preferred_element_type=jnp.float32)
            return inner

        lax.fori_loop(0, i + 1, key_frame, 0)
        outcome = (acc[...] / total[...]).T
        att_ref[at] = outcome
        att_low[at] = outcome.astype(jnp.bfloat16)
        lse_ref[at] = peak[...] + jnp.log(total[...])

        @pl.when(at != 0)
        def _():
            pltpu.make_async_remote_copy(
                src_ref=att_low.at[at], dst_ref=came.at[at], send_sem=send.at[first_back + at], recv_sem=recv.at[first_back + at],
                device_id={"seq": i}, device_id_type=MESH,
            ).start()

    query_frame(0)
    query_frame(1)
    pass_on(out_step, out_dp, 2)
    query_frame(2)
    pass_on(up_step, up_dp, 1)
    query_frame(3)
    pass_on(out_step, out_dp, 3)
    came[0] = att_low[0]
    for k in range(1, SEQ):
        back[k].wait_recv()
    for h in range(SEQ):
        attended_ref[:, h * HEAD_DIM : (h + 1) * HEAD_DIM] = came[lax.rem(h - z + SEQ, SEQ)]
    own_out.wait()
    for k in range(SEQ):
        out_dp[k].wait_recv()
    keep(out_all, out_ref)

    def mix(start):
        def piece(n, carry):
            at = pl.ds(pl.multiple_of(n * 512, 512), 512)
            part_low[pl.ds(start, half), at] = jnp.dot(attended_ref[pl.ds(start, half), :], out_all[:, at], preferred_element_type=jnp.float32).astype(jnp.bfloat16)
            return carry

        lax.fori_loop(0, width // 512, piece, 0)

    mix(half)
    sum_core.start()
    mix(0)
    sum_core.wait_recv()
    half_low[...] = (part_low[quarter:half, :].astype(jnp.float32) + core_in[quarter:half, :].astype(jnp.float32)).astype(jnp.bfloat16)
    sum_chip.start()
    pass_on(up_step, up_dp, 2)
    down_step[1].start()
    sum_chip.wait_recv()
    resid = own_ref[...] + (part_low[0:quarter, :].astype(jnp.float32) + core_in[0:quarter, :].astype(jnp.float32)) + chip_in[...].astype(jnp.float32)
    center = resid - jnp.mean(resid, axis=1, keepdims=True)
    rate = lax.rsqrt(jnp.mean(center * center, axis=1, keepdims=True) + NORM_EPS)
    normed = center * rate
    resid_ref[...] = resid
    rate_ref[...] = rate
    normed_ref[...] = normed
    second[0:quarter, :] = normed.astype(jnp.bfloat16)
    second_chip.start()
    pass_on(up_step, up_dp, 3)
    second_chip.wait_recv()
    second_core.start()
    second_core.wait_recv()
    keep(second, second_ref)
    for k in range(1, SEQ):
        pass_on(down_step, down_dp, k)
    for copy in up_dp + down_dp:
        copy.wait_recv()
    for copy in used:
        copy.wait_send()
    for copy in kept:
        if not any(copy is done for done in (own_frame, own_head, own_out)):
            copy.wait()


def front(f0, w_three, w_out, w_up, w_down, own, bias):
    rows, width = f0.shape
    quarter, half = rows // 4, rows // 2
    part = w_out.shape[1]
    inner = w_out.shape[0]
    f32, bf16 = jnp.float32, jnp.bfloat16
    any_, vmem = pl.BlockSpec(memory_space=pl.ANY), pl.BlockSpec(memory_space=pltpu.VMEM)
    shape = jax.ShapeDtypeStruct
    outs = [
        (shape((SEQ, rows, width), bf16), any_),
        (shape((width, 3 * HEAD_DIM), bf16), vmem),
        (shape((SEQ, rows, 3 * HEAD_DIM), bf16), vmem),
        (shape((SEQ, rows, HEAD_DIM), f32), vmem),
        (shape((SEQ, 1, rows), f32), vmem),
        (shape((rows, inner), bf16), vmem),
        (shape((inner, width), bf16), any_),
        (shape((quarter, width), f32), vmem),
        (shape((quarter, width), f32), vmem),
        (shape((quarter, 1), f32), vmem),
        (shape((rows, width), bf16), any_),
        (shape((width, w_up.shape[1]), bf16), any_),
        (shape((w_down.shape[0], width), bf16), any_),
    ]
    copies = 3 * (SEQ - 1) + SEQ + 3 * (2 * SEQ - 1) + (SEQ - 1) + 4
    return pl.pallas_call(
        front_kernel,
        out_shape=[o[0] for o in outs],
        in_specs=[any_] * 5 + [vmem] * 2,
        out_specs=[o[1] for o in outs],
        scratch_shapes=[
            pltpu.VMEM((SEQ, rows, width), bf16),
            pltpu.VMEM((2 * SEQ, part, 3 * HEAD_DIM), bf16),
            pltpu.VMEM((inner, width), bf16),
            pltpu.VMEM((SEQ, rows, HEAD_DIM), bf16),
            pltpu.VMEM((SEQ, rows, HEAD_DIM), bf16),
            pltpu.VMEM((rows, width), bf16),
            pltpu.VMEM((half, width), bf16),
            pltpu.VMEM((quarter, width), bf16),
            pltpu.VMEM((quarter, width), bf16),
            pltpu.VMEM((rows, width), bf16),
            pltpu.VMEM((1, rows), f32),
            pltpu.VMEM((1, rows), f32),
            pltpu.VMEM((HEAD_DIM, rows), f32),
            pltpu.SemaphoreType.DMA((copies,)),
            pltpu.SemaphoreType.DMA((copies,)),
            pltpu.SemaphoreType.DMA((16,)),
        ],
        compiler_params=pltpu.CompilerParams(collective_id=0, has_side_effects=True, vmem_limit_bytes=56 * 2**20),
        cost_estimate=pl.CostEstimate(flops=8 * 10**9, bytes_accessed=50 * 10**6, transcendentals=5 * 10**6),
    )(f0, w_three, w_out, w_up, w_down, own, bias)


def attend_back_kernel(place_ref, valid_ref, qkv_ref, out_ref, lse_ref, do_ref, grad_ref, delta, dq, dk, dv):
    place = place_ref[0]
    scale = HEAD_DIM ** (-0.5)
    dq[...] = jnp.zeros_like(dq)
    for f in range(SEQ):
        delta[f] = jnp.sum((do_ref[f].astype(jnp.float32) * out_ref[f]).T, axis=0, keepdims=True)

    def key_frame(j, carry):
        here = lax.rem(place - j + SEQ, SEQ)
        dk[...] = jnp.zeros_like(dk)
        dv[...] = jnp.zeros_like(dv)

        @pl.when(valid_ref[j] == 1)
        def _():
            def query_frame(i, inner):
                at = lax.rem(place - i + SEQ, SEQ)
                query, key, value = qkv_ref[at, :, :HEAD_DIM], qkv_ref[here, :, HEAD_DIM : 2 * HEAD_DIM], qkv_ref[here, :, 2 * HEAD_DIM :]
                d_out = do_ref[at]
                scores = lax.dot_general(key, query, (((1,), (1,)), ((), ())), preferred_element_type=jnp.float32) * scale
                prob = jnp.exp(scores - lse_ref[at])
                d_prob = lax.dot_general(value, d_out, (((1,), (1,)), ((), ())), preferred_element_type=jnp.float32)
                d_scores = (prob * (d_prob - delta[at])).astype(jnp.bfloat16)
                dv[...] += jnp.dot(prob.astype(jnp.bfloat16), d_out, preferred_element_type=jnp.float32)
                dk[...] += jnp.dot(d_scores, query, preferred_element_type=jnp.float32)
                dq[at] += lax.dot_general(key, d_scores, (((0,), (0,)), ((), ())), preferred_element_type=jnp.float32)
                return inner

            lax.fori_loop(j, SEQ, query_frame, 0)

        grad_ref[here, :, HEAD_DIM : 2 * HEAD_DIM] = (dk[...] * scale).astype(jnp.bfloat16)
        grad_ref[here, :, 2 * HEAD_DIM :] = dv[...].astype(jnp.bfloat16)
        return carry

    lax.fori_loop(0, SEQ, key_frame, 0)
    for f in range(SEQ):
        grad_ref[f, :, :HEAD_DIM] = (dq[f] * scale).T.astype(jnp.bfloat16)


def attend_back(place, valid, qkv, out, lse, d_out):
    rows = qkv.shape[1]
    smem = pl.BlockSpec(memory_space=pltpu.SMEM)
    vmem = pl.BlockSpec(memory_space=pltpu.VMEM)
    return pl.pallas_call(
        attend_back_kernel,
        out_shape=jax.ShapeDtypeStruct((SEQ, rows, 3 * HEAD_DIM), jnp.bfloat16),
        in_specs=[smem, smem] + [vmem] * 4,
        out_specs=vmem,
        scratch_shapes=[
            pltpu.VMEM((SEQ, 1, rows), jnp.float32),
            pltpu.VMEM((SEQ, HEAD_DIM, rows), jnp.float32),
            pltpu.VMEM((rows, HEAD_DIM), jnp.float32),
            pltpu.VMEM((rows, HEAD_DIM), jnp.float32),
        ],
        compiler_params=pltpu.CompilerParams(vmem_limit_bytes=48 * 2**20),
        cost_estimate=pl.CostEstimate(flops=10 * 10 * rows * rows * HEAD_DIM * 2, bytes_accessed=5 * qkv.size, transcendentals=10 * rows * rows),
    )(place, valid, qkv, out, lse, d_out)


def norm_parts(values):
    center = values - jnp.mean(values, axis=-1, keepdims=True)
    rate = lax.rsqrt(jnp.mean(center * center, axis=-1, keepdims=True) + NORM_EPS)
    return center * rate, rate


def norm_back(normed, rate, grad):
    return rate * (grad - jnp.mean(grad, axis=-1, keepdims=True) - normed * jnp.mean(grad * normed, axis=-1, keepdims=True))


def mm(left, right, dims=((1,), (0,)), out=jnp.bfloat16):
    return lax.dot_general(left, right, (dims, ((), ())), preferred_element_type=jnp.float32).astype(out)


def local_fast(inputs, first_gain, w_query, w_key, w_value, w_out, second_gain, w_up, w_down, frame_mask, cotangent):
    dp, z, t = lax.axis_index("dp"), lax.axis_index("seq"), lax.axis_index("tensor")
    rows = inputs.shape[1]
    quarter = rows // 4
    width = inputs.shape[2]
    part = width // (2 * SEQ)
    heads = w_query.shape[1] // HEAD_DIM
    f32, bf16 = jnp.float32, jnp.bfloat16

    def rel_block(b):
        return (dp ^ (b // SEQ)) * SEQ + lax.rem(z - b % SEQ + SEQ, SEQ)

    def rel_cols(values):
        return jnp.concatenate([lax.dynamic_slice_in_dim(values, rel_block(b) * part, part, 1) for b in range(2 * SEQ)], axis=1)

    def can_cols(values):
        picks = []
        for c in range(2 * SEQ):
            b = (dp ^ (c // SEQ)) * SEQ + lax.rem(z - c % SEQ + SEQ, SEQ)
            picks.append(lax.dynamic_slice_in_dim(values, b * part, part, 1))
        return jnp.concatenate(picks, axis=1)

    def rel_rows(values):
        return jnp.concatenate([lax.dynamic_slice_in_dim(values, (t ^ p) * quarter, quarter, 0) for p in (0, 2, 1, 3)], axis=0)

    def can_rows(values):
        picks = []
        for c in range(4):
            d = t ^ c
            p = (d % 2) * 2 + d // 2
            picks.append(lax.dynamic_slice_in_dim(values, p * quarter, quarter, 0))
        return jnp.concatenate(picks, axis=0)

    own_in = inputs[0]
    normed_one_all = norm_parts(own_in.astype(f32))[0].astype(bf16)
    frame0 = rel_rows(normed_one_all)
    w_three = jnp.stack([w_query, w_key, w_value], axis=1).reshape(part, 3, heads, HEAD_DIM)
    w_three = (w_three.astype(f32) * first_gain.astype(f32)[:, None, None, None]).astype(bf16)
    w_three = w_three.transpose(2, 0, 1, 3).reshape(heads, part, 3 * HEAD_DIM)
    w_up_scaled = (w_up.astype(f32) * second_gain.astype(f32)[:, None]).astype(bf16)
    own_rel = rel_cols(lax.dynamic_slice_in_dim(own_in, t * quarter, quarter, 0)).astype(f32)
    place = z.reshape(1)
    valid = frame_mask[0]
    bias = jnp.broadcast_to(jnp.where(valid == 1, 0.0, MASK_FILL).astype(f32)[:, None, None], (SEQ, 1, rows))
    whole, w_head, qkv, attended_f, lse, attended, out_rel, resid_mid, normed_two, rate_two, second_in, up_rel, down_rel = front(
        frame0, w_three, w_out, w_up_scaled, w_down, own_rel, bias
    )

    cot_rel = rel_cols(rel_rows(cotangent[0]))
    up_pre = mm(second_in, up_rel, out=f32)
    cdf = 0.5 * (1.0 + lax.erf(up_pre * (0.5**0.5)))
    up_act = (up_pre * cdf).astype(bf16)
    slope = cdf + up_pre * jnp.exp(-0.5 * up_pre * up_pre) * ((2.0 * jnp.pi) ** -0.5)
    grad_down = mm(up_act, cot_rel, ((0,), (0,)))
    d_up = (mm(cot_rel, down_rel, ((1,), (1,)), f32) * slope).astype(bf16)
    result = resid_mid + scatter_tensor(mm(up_act, down_rel))
    result = can_rows(gather_tensor(can_cols(result.astype(bf16))))[None]
    grad_up = mm(second_in, d_up, ((0,), (0,)))
    d_normed_two = scatter_tensor(mm(d_up, up_rel, ((1,), (1,))))
    cot_own = cot_rel[:quarter].astype(f32)
    d_mid = cot_own + norm_back(normed_two, rate_two, d_normed_two)
    d_mix = gather_tensor(d_mid.astype(bf16))
    grad_out = mm(attended, d_mix, ((0,), (0,)))
    d_attended = mm(d_mix, out_rel, ((1,), (1,)))
    d_heads = jnp.stack([d_attended[:, h * HEAD_DIM : (h + 1) * HEAD_DIM] for h in range(heads)])
    d_out = jnp.stack([dyn(d_heads, z)] + [shift(dyn(d_heads, lax.rem(z + k, SEQ)), k) for k in range(1, SEQ)])

    d_three = attend_back(place, valid, qkv, attended_f, lse, d_out)
    grad_head = mm(whole.reshape(SEQ * rows, width), d_three.reshape(SEQ * rows, 3 * HEAD_DIM), ((0,), (0,)))
    grad_head = grad_head.reshape(2, SEQ * part, 3 * HEAD_DIM)
    grad_rows = dyn(grad_head, dp).astype(f32) + swap_dp(dyn(grad_head, 1 - dp)).astype(f32)
    grad_rows = grad_rows.astype(bf16).reshape(SEQ, part, 3 * HEAD_DIM)
    arrived = jnp.stack([dyn(grad_rows, z)] + [shift(dyn(grad_rows, lax.rem(z + k, SEQ)), k) for k in range(1, SEQ)])
    by_head = [dyn(arrived, lax.rem(z - h + SEQ, SEQ)).astype(f32) for h in range(heads)]
    gain_one = first_gain.astype(f32)[:, None]
    raw = [jnp.concatenate([one[:, n * HEAD_DIM : (n + 1) * HEAD_DIM] for one in by_head], axis=1) for n in range(3)]
    d_gain_one = sum(jnp.sum(weight.astype(f32) * one, axis=1) for weight, one in zip((w_query, w_key, w_value), raw))

    running = None
    for k in (1, 2, 3, 0):
        total = scatter_tensor(mm(d_three[k], w_head, ((1,), (1,))))
        if running is not None:
            total = total + running.astype(f32)
        if k:
            running = shift(total.astype(bf16), 1)
    own_quarter = lax.dynamic_slice_in_dim(own_in, t * quarter, quarter, 0).astype(f32)
    normed_one, rate_one = norm_parts(own_quarter)
    d_in = can_cols(d_mid) + norm_back(normed_one, rate_one, total)
    grad_inputs = can_rows(gather_tensor(d_in.astype(bf16)))[None]

    down_sum = scatter_blocks([grad_down[:, b * part : (b + 1) * part] for b in range(2 * SEQ)])
    up_raw = scatter_blocks([grad_up[b * part : (b + 1) * part] for b in range(2 * SEQ)])
    out_sum = scatter_blocks([grad_out[:, b * part : (b + 1) * part] for b in range(2 * SEQ)])
    d_gain_two = jnp.sum(w_up.astype(f32) * up_raw, axis=1)
    gains = jnp.stack([d_gain_one, d_gain_two])
    gains = gains + swap_core(gains)
    gains = gains + swap_chip(gains)
    return (
        result,
        grad_inputs,
        gains[0],
        raw[0] * gain_one,
        raw[1] * gain_one,
        raw[2] * gain_one,
        out_sum,
        gains[1],
        up_raw * second_gain.astype(f32)[:, None],
        down_sum,
    )


SEQ = 4


def solution(mesh):
    placed = (
        P("dp", "seq", None),
        P(("dp", "seq")),
        P(("dp", "seq"), "tensor"),
        P(("dp", "seq"), "tensor"),
        P(("dp", "seq"), "tensor"),
        P("tensor", ("dp", "seq")),
        P(("dp", "seq")),
        P(("dp", "seq"), "tensor"),
        P("tensor", ("dp", "seq")),
        P("dp", None),
        P("dp", "seq", None),
    )
    sizes = dict(mesh.shape)
    spread = sizes == {"dp": 2, "seq": SEQ, "tensor": 4}
    return jax.shard_map(
        local_fast if spread else local,
        mesh=mesh,
        in_specs=placed,
        out_specs=(
            P("dp", "seq", None),
            P("dp", "seq", None),
            P(("dp", "seq")),
            P(("dp", "seq"), "tensor"),
            P(("dp", "seq"), "tensor"),
            P(("dp", "seq"), "tensor"),
            P("tensor", ("dp", "seq")),
            P(("dp", "seq")),
            P(("dp", "seq"), "tensor"),
            P("tensor", ("dp", "seq")),
        ),
        check_vma=False,
    )
```

```python
import functools

import jax
import jax.numpy as jnp
from jax import lax
from jax.experimental import pallas as pl
from jax.experimental.pallas import tpu as pltpu
from jax.sharding import PartitionSpec as P

HEAD_DIM = 128
FRAME_TOK = 640


NORM_EPS = 1e-05
MASK_FILL = -1e30
MESH = pl.DeviceIdType.MESH


def norm_rows(values):
    center = values - jnp.mean(values, axis=-1, keepdims=True)
    spread = jnp.mean(center * center, axis=-1, keepdims=True)
    return center * lax.rsqrt(spread + NORM_EPS)


def gelu_exact(values):
    return jax.nn.gelu(values, approximate=False)


def heads_total(values):
    return lax.psum(values.astype(jnp.bfloat16), "tensor").astype(jnp.float32)


def local(
    inputs,
    first_gain,
    w_query,
    w_key,
    w_value,
    w_out,
    second_gain,
    w_up,
    w_down,
    frame_mask,
    cotangent,
):
    seq_pos = lax.axis_index("seq")
    gain_one, query_w, key_w, value_w, gain_two, up_w = (
        lax.all_gather(first_gain, ("dp", "seq"), axis=0, tiled=True),
        lax.all_gather(w_query, ("dp", "seq"), axis=0, tiled=True),
        lax.all_gather(w_key, ("dp", "seq"), axis=0, tiled=True),
        lax.all_gather(w_value, ("dp", "seq"), axis=0, tiled=True),
        lax.all_gather(second_gain, ("dp", "seq"), axis=0, tiled=True),
        lax.all_gather(w_up, ("dp", "seq"), axis=0, tiled=True),
    )
    out_w, down_w = (
        lax.all_gather(w_out, ("dp", "seq"), axis=1, tiled=True),
        lax.all_gather(w_down, ("dp", "seq"), axis=1, tiled=True),
    )
    tok_rows = inputs.shape[1]
    local_inner = query_w.shape[1]
    local_heads = local_inner // HEAD_DIM
    frames_dev = tok_rows // FRAME_TOK
    score_scale = HEAD_DIM ** (-0.5)
    clip_valid = frame_mask[0]
    frame_count = clip_valid.shape[0]
    resid_in = inputs[0].astype(jnp.float32)
    dout_rows = cotangent[0]
    row_frame = seq_pos * frames_dev + jnp.arange(tok_rows, dtype=jnp.int32) // FRAME_TOK
    frame_limit = (seq_pos + 1) * frames_dev
    normed_one = norm_rows(resid_in)
    first_in = (normed_one * gain_one.astype(jnp.float32)).astype(jnp.bfloat16)
    query = jnp.dot(first_in, query_w, preferred_element_type=jnp.float32).astype(jnp.bfloat16)
    key_local = jnp.dot(first_in, key_w, preferred_element_type=jnp.float32).astype(jnp.bfloat16)
    value_local = jnp.dot(first_in, value_w, preferred_element_type=jnp.float32).astype(
        jnp.bfloat16
    )
    key_all, value_all = (
        lax.all_gather(key_local, "seq", axis=0, tiled=True),
        lax.all_gather(value_local, "seq", axis=0, tiled=True),
    )
    query_heads = query.reshape(tok_rows, local_heads, HEAD_DIM)
    key_frames = key_all.reshape(frame_count, FRAME_TOK, local_heads, HEAD_DIM)
    value_frames = value_all.reshape(frame_count, FRAME_TOK, local_heads, HEAD_DIM)

    def frame_scores(frame_idx):
        key_block = lax.dynamic_index_in_dim(key_frames, frame_idx, 0, keepdims=False)
        value_block = lax.dynamic_index_in_dim(value_frames, frame_idx, 0, keepdims=False)
        scores = (
            jnp.einsum("qhd,khd->hqk", query_heads, key_block, preferred_element_type=jnp.float32)
            * score_scale
        )
        frame_ok = lax.dynamic_index_in_dim(clip_valid, frame_idx, 0, keepdims=False) == 1
        allowed = ((frame_idx <= row_frame) & frame_ok)[None, :, None]
        return (scores, allowed, key_block, value_block)

    def stats_step(frame_idx, running):
        row_max, row_sum = running
        scores, allowed, key_block, value_block = frame_scores(frame_idx)
        masked = jnp.where(allowed, scores, MASK_FILL)
        new_max = jnp.maximum(row_max, jnp.max(masked, axis=2))
        exp_terms = jnp.where(allowed, jnp.exp(masked - new_max[:, :, None]), 0.0)
        return (new_max, row_sum * jnp.exp(row_max - new_max) + jnp.sum(exp_terms, axis=2))

    start_stats = (
        jnp.full((local_heads, tok_rows), MASK_FILL, jnp.float32),
        jnp.zeros((local_heads, tok_rows), jnp.float32),
    )
    row_max, row_sum = lax.fori_loop(0, frame_limit, stats_step, start_stats)

    def soft_weights(scores, allowed):
        return jnp.where(allowed, jnp.exp(scores - row_max[:, :, None]) / row_sum[:, :, None], 0.0)

    def output_step(frame_idx, running):
        scores, allowed, key_block, value_block = frame_scores(frame_idx)
        attn_prob = soft_weights(scores, allowed).astype(jnp.bfloat16)
        return running + jnp.einsum(
            "hqk,khd->qhd", attn_prob, value_block, preferred_element_type=jnp.float32
        )

    attended = lax.fori_loop(
        0, frame_limit, output_step, jnp.zeros((tok_rows, local_heads, HEAD_DIM), jnp.float32)
    )
    attended_low = attended.reshape(tok_rows, local_inner).astype(jnp.bfloat16)
    resid_mid = resid_in + heads_total(
        jnp.dot(attended_low, out_w, preferred_element_type=jnp.float32)
    )
    normed_two = norm_rows(resid_mid)
    second_in = (normed_two * gain_two.astype(jnp.float32)).astype(jnp.bfloat16)
    up_pre = jnp.dot(second_in, up_w, preferred_element_type=jnp.float32)
    up_act = gelu_exact(up_pre).astype(jnp.bfloat16)
    resid_out = resid_mid + heads_total(jnp.dot(up_act, down_w, preferred_element_type=jnp.float32))
    result = resid_out.astype(jnp.bfloat16)[None]
    grad_down = jnp.einsum("tf,td->fd", up_act, dout_rows, preferred_element_type=jnp.float32)
    d_act = jnp.einsum("td,fd->tf", dout_rows, down_w, preferred_element_type=jnp.float32)
    gelu_pull = jax.vjp(gelu_exact, up_pre)[1]
    d_up_pre = gelu_pull(d_act)[0].astype(jnp.bfloat16)
    grad_up = jnp.einsum("td,tf->df", second_in, d_up_pre, preferred_element_type=jnp.float32)
    d_second = heads_total(
        jnp.einsum("tf,df->td", d_up_pre, up_w, preferred_element_type=jnp.float32)
    )
    grad_second_gain = jnp.sum(d_second * normed_two, axis=0)
    norm_pull_two = jax.vjp(norm_rows, resid_mid)[1]
    d_mid = (
        dout_rows.astype(jnp.float32) + norm_pull_two(d_second * gain_two.astype(jnp.float32))[0]
    )
    d_mix = d_mid.astype(jnp.bfloat16)
    grad_out = jnp.einsum("ti,td->id", attended_low, d_mix, preferred_element_type=jnp.float32)
    d_attended = jnp.einsum("td,id->ti", d_mix, out_w, preferred_element_type=jnp.float32).astype(
        jnp.bfloat16
    )
    dout_heads = d_attended.reshape(tok_rows, local_heads, HEAD_DIM)
    row_delta = jnp.sum(dout_heads.astype(jnp.float32) * attended, axis=2).T

    def query_step(frame_idx, running):
        scores, allowed, key_block, value_block = frame_scores(frame_idx)
        attn_prob = soft_weights(scores, allowed)
        d_prob = jnp.einsum(
            "qhd,khd->hqk", dout_heads, value_block, preferred_element_type=jnp.float32
        )
        d_scores = (attn_prob * (d_prob - row_delta[:, :, None])).astype(jnp.bfloat16)
        return running + jnp.einsum(
            "hqk,khd->qhd", d_scores, key_block, preferred_element_type=jnp.float32
        )

    query_sum = lax.fori_loop(
        0, frame_limit, query_step, jnp.zeros((tok_rows, local_heads, HEAD_DIM), jnp.float32)
    )
    d_query = (query_sum * score_scale).reshape(tok_rows, local_inner).astype(jnp.bfloat16)

    def one_frame(frame_step):
        scores, allowed, key_block, value_block = frame_scores(frame_step)
        attn_prob = soft_weights(scores, allowed)
        d_prob = jnp.einsum(
            "qhd,khd->hqk", dout_heads, value_block, preferred_element_type=jnp.float32
        )
        d_scores = (attn_prob * (d_prob - row_delta[:, :, None])).astype(jnp.bfloat16)
        key_term = (
            jnp.einsum("hqk,qhd->khd", d_scores, query_heads, preferred_element_type=jnp.float32)
            * score_scale
        )
        value_term = jnp.einsum(
            "hqk,qhd->khd",
            attn_prob.astype(jnp.bfloat16),
            dout_heads,
            preferred_element_type=jnp.float32,
        )
        return jnp.concatenate(
            [key_term.reshape(FRAME_TOK, local_inner), value_term.reshape(FRAME_TOK, local_inner)],
            axis=1,
        )

    blocks = lax.map(
        one_frame, jnp.arange(tok_rows * lax.axis_size("seq") // FRAME_TOK, dtype=jnp.int32)
    )
    kv_grad = lax.psum_scatter(
        blocks.reshape(tok_rows * lax.axis_size("seq"), 2 * local_inner).astype(jnp.bfloat16),
        "seq",
        scatter_dimension=0,
        tiled=True,
    ).astype(jnp.float32)
    d_key = kv_grad[:, :local_inner].astype(jnp.bfloat16)
    d_value = kv_grad[:, local_inner:].astype(jnp.bfloat16)
    grad_query = jnp.einsum("td,ti->di", first_in, d_query, preferred_element_type=jnp.float32)
    grad_key = jnp.einsum("td,ti->di", first_in, d_key, preferred_element_type=jnp.float32)
    grad_value = jnp.einsum("td,ti->di", first_in, d_value, preferred_element_type=jnp.float32)
    first_local = jnp.einsum("ti,di->td", d_query, query_w, preferred_element_type=jnp.float32)
    first_local = first_local + jnp.einsum(
        "ti,di->td", d_key, key_w, preferred_element_type=jnp.float32
    )
    first_local = first_local + jnp.einsum(
        "ti,di->td", d_value, value_w, preferred_element_type=jnp.float32
    )
    d_first = heads_total(first_local)
    grad_first_gain = jnp.sum(d_first * normed_one, axis=0)
    norm_pull_one = jax.vjp(norm_rows, resid_in)[1]
    grad_inputs = (d_mid + norm_pull_one(d_first * gain_one.astype(jnp.float32))[0]).astype(
        jnp.bfloat16
    )[None]
    summed_in = (
        lax.psum_scatter(
            grad_first_gain.astype(jnp.bfloat16), ("dp", "seq"), scatter_dimension=0, tiled=True
        ).astype(jnp.float32),
        lax.psum_scatter(
            grad_query.astype(jnp.bfloat16), ("dp", "seq"), scatter_dimension=0, tiled=True
        ).astype(jnp.float32),
        lax.psum_scatter(
            grad_key.astype(jnp.bfloat16), ("dp", "seq"), scatter_dimension=0, tiled=True
        ).astype(jnp.float32),
        lax.psum_scatter(
            grad_value.astype(jnp.bfloat16), ("dp", "seq"), scatter_dimension=0, tiled=True
        ).astype(jnp.float32),
        lax.psum_scatter(
            grad_second_gain.astype(jnp.bfloat16), ("dp", "seq"), scatter_dimension=0, tiled=True
        ).astype(jnp.float32),
        lax.psum_scatter(
            grad_up.astype(jnp.bfloat16), ("dp", "seq"), scatter_dimension=0, tiled=True
        ).astype(jnp.float32),
    )
    summed_out = (
        lax.psum_scatter(
            grad_out.astype(jnp.bfloat16), ("dp", "seq"), scatter_dimension=1, tiled=True
        ).astype(jnp.float32),
        lax.psum_scatter(
            grad_down.astype(jnp.bfloat16), ("dp", "seq"), scatter_dimension=1, tiled=True
        ).astype(jnp.float32),
    )
    return (
        result,
        grad_inputs,
        summed_in[0],
        summed_in[1],
        summed_in[2],
        summed_in[3],
        summed_out[0],
        summed_in[4],
        summed_in[5],
        summed_out[1],
    )


def shift(values, k):
    return lax.ppermute(values, "seq", [(i, (i + k) % SEQ) for i in range(SEQ)])


def swap_dp(values):
    return lax.ppermute(values, "dp", [(0, 1), (1, 0)])


def swap_chip(values):
    return lax.ppermute(values, "tensor", [(i, i ^ 2) for i in range(4)])


def swap_core(values):
    return lax.ppermute(values, "tensor", [(i, i ^ 1) for i in range(4)])


def tied(value, *others):
    return lax.optimization_barrier((value, *others))[0]


def gather_tensor(own):
    half = jnp.concatenate([own, swap_chip(own)], axis=0)
    return jnp.concatenate([half, swap_core(half)], axis=0)


def scatter_tensor(part):
    n = part.shape[0] // 4
    low = part.astype(jnp.bfloat16)
    half = part[: 2 * n].astype(jnp.float32) + swap_core(low[2 * n :]).astype(jnp.float32)
    other = swap_chip(half[n:].astype(jnp.bfloat16))
    return half[:n] + other.astype(jnp.float32)


def dyn(stack, index):
    return lax.dynamic_index_in_dim(stack, index, 0, keepdims=False)


def front_kernel(
    f0_ref, w_three_ref, w_out_ref, w_up_ref, w_down_ref, own_ref, bias_ref,
    whole_ref, w_head_ref, qkv_ref, att_ref, lse_ref, attended_ref, out_ref, resid_ref, normed_ref, rate_ref, second_ref, up_ref, down_ref,
    frames, w_stack, out_all, att_low, came, part_low, core_in, half_low, chip_in, second, peak, total, acc, send, recv, local_sem,
):
    dp, z, t = lax.axis_index("dp"), lax.axis_index("seq"), lax.axis_index("tensor")
    other_dp, chip, core = {"dp": 1 - dp}, {"tensor": lax.rem(t + 2, 4)}, {"tensor": t + 1 - 2 * lax.rem(t, 2)}

    def along(k):
        return {"seq": lax.rem(z + k + SEQ, SEQ)}

    rows, width = f0_ref.shape
    quarter = rows // 4
    half = rows // 2
    part = w_out_ref.shape[1]
    used = []

    def remote(src, dst, device):
        i = len(used)
        copy = pltpu.make_async_remote_copy(src_ref=src, dst_ref=dst, send_sem=send.at[i], recv_sem=recv.at[i], device_id=device, device_id_type=MESH)
        used.append(copy)
        return copy

    kept = []

    def keep(src, dst):
        copy = pltpu.make_async_copy(src, dst, local_sem.at[len(kept)])
        kept.append(copy)
        copy.start()
        return copy

    barrier = pltpu.get_barrier_semaphore()
    peers = [other_dp, chip, core] + [along(k) for k in range(1, SEQ)]
    for peer in peers:
        pl.semaphore_signal(barrier, inc=1, device_id=peer, device_id_type=MESH)
    pl.semaphore_wait(barrier, len(peers))

    def out_at(b):
        return out_all.at[:, pl.ds(b * part, part)]

    def up_at(b):
        return up_ref.at[pl.ds(b * part, part), :]

    def down_at(b):
        return down_ref.at[:, pl.ds(b * part, part)]

    ring = along(1)
    token = [None] + [remote(f0_ref.at[pl.ds(0, quarter), :] if k == 1 else frames.at[k - 1, pl.ds(0, quarter), :], frames.at[k, pl.ds(0, quarter), :], ring) for k in range(1, SEQ)]
    token_chip = [None] + [remote(frames.at[k, pl.ds(0, quarter), :], frames.at[k, pl.ds(quarter, quarter), :], chip) for k in range(1, SEQ)]
    token_core = [None] + [remote(frames.at[k, pl.ds(0, half), :], frames.at[k, pl.ds(half, half), :], core) for k in range(1, SEQ)]
    head = [None] + [remote(w_three_ref.at[lax.rem(z + k, SEQ)], w_stack.at[k], along(k)) for k in range(1, SEQ)]
    head_dp = remote(w_stack.at[pl.ds(0, SEQ)], w_stack.at[pl.ds(SEQ, SEQ)], other_dp)

    def gather(shard, at):
        step = [None] + [remote(shard if k == 1 else at(k - 1), at(k), ring) for k in range(1, SEQ)]
        cross = [remote(shard if k == 0 else at(k), at(SEQ + k), other_dp) for k in range(SEQ)]
        return step, cross

    out_step, out_dp = gather(w_out_ref, out_at)
    up_step, up_dp = gather(w_up_ref, up_at)
    down_step, down_dp = gather(w_down_ref, down_at)
    first_back = len(used) - 1
    back = [None] + [remote(att_low.at[k], came.at[k], along(-k)) for k in range(1, SEQ)]
    sum_core = remote(part_low.at[pl.ds(half, half), :], core_in, core)
    sum_chip = remote(half_low, chip_in, chip)
    second_chip = remote(second.at[pl.ds(0, quarter), :], second.at[pl.ds(quarter, quarter), :], chip)
    second_core = remote(second.at[pl.ds(0, half), :], second.at[pl.ds(half, half), :], core)

    def pass_on(steps, cross, k):
        steps[k].wait_recv()
        if k + 1 < SEQ:
            steps[k + 1].start()
        cross[k].start()

    token[1].start()
    for k in range(1, SEQ):
        head[k].start()
    up_dp[0].start()
    out_dp[0].start()
    own_frame = keep(f0_ref, frames.at[0])
    own_head = keep(w_three_ref.at[z], w_stack.at[0])
    own_out = keep(w_out_ref, out_at(0))
    keep(w_up_ref, up_at(0))
    keep(w_down_ref, down_at(0))
    own_head.wait()
    own_frame.wait()
    token[1].wait_recv()
    token[2].start()
    token_chip[1].start()
    for k in range(1, SEQ):
        head[k].wait_recv()
    head_dp.start()
    token[2].wait_recv()
    token[3].start()
    token_chip[2].start()
    token_chip[1].wait_recv()
    token_core[1].start()
    out_step[1].start()
    up_step[1].start()
    head_dp.wait_recv()
    down_dp[0].start()
    for c in range(2 * SEQ):
        b = lax.rem(dp + c // SEQ, 2) * SEQ + lax.rem(z - c % SEQ + SEQ, SEQ)
        w_head_ref[c * part : (c + 1) * part, :] = w_stack[b]

    def project(k):
        def piece(n, carry):
            at = pl.ds(n * quarter, quarter)
            qkv_ref[k, at, :] = jnp.dot(frames[k, at, :], w_head_ref[...], preferred_element_type=jnp.float32).astype(jnp.bfloat16)
            return carry

        lax.fori_loop(0, 4, piece, 0)

    project(0)
    token_core[1].wait_recv()
    keep(frames.at[1], whole_ref.at[1])
    project(1)
    token_chip[2].wait_recv()
    token_core[2].start()
    token[3].wait_recv()
    token_chip[3].start()
    token_core[2].wait_recv()
    keep(frames.at[2], whole_ref.at[2])
    project(2)
    pass_on(out_step, out_dp, 1)
    token_chip[3].wait_recv()
    token_core[3].start()
    token_core[3].wait_recv()
    keep(frames.at[0], whole_ref.at[0])
    keep(frames.at[3], whole_ref.at[3])
    project(3)

    scale = HEAD_DIM ** (-0.5)

    def query_frame(i):
        at = lax.rem(z - i + SEQ, SEQ)
        query = qkv_ref[at, :, 0:HEAD_DIM]
        peak[...] = jnp.full_like(peak, MASK_FILL)
        total[...] = jnp.zeros_like(total)
        acc[...] = jnp.zeros_like(acc)

        def key_frame(j, inner):
            here = lax.rem(z - j + SEQ, SEQ)
            scores = lax.dot_general(qkv_ref[here, :, HEAD_DIM : 2 * HEAD_DIM], query, (((1,), (1,)), ((), ())), preferred_element_type=jnp.float32) * scale + bias_ref[j]
            before = peak[...]
            after = jnp.maximum(before, jnp.max(scores, axis=0, keepdims=True))
            terms = jnp.exp(scores - after)
            fix = jnp.exp(before - after)
            peak[...] = after
            total[...] = total[...] * fix + jnp.sum(terms, axis=0, keepdims=True)
            acc[...] = acc[...] * fix + lax.dot_general(qkv_ref[here, :, 2 * HEAD_DIM :], terms.astype(jnp.bfloat16), (((0,), (0,)), ((), ())), preferred_element_type=jnp.float32)
            return inner

        lax.fori_loop(0, i + 1, key_frame, 0)
        outcome = (acc[...] / total[...]).T
        att_ref[at] = outcome
        att_low[at] = outcome.astype(jnp.bfloat16)
        lse_ref[at] = peak[...] + jnp.log(total[...])

        @pl.when(at != 0)
        def _():
            pltpu.make_async_remote_copy(
                src_ref=att_low.at[at], dst_ref=came.at[at], send_sem=send.at[first_back + at], recv_sem=recv.at[first_back + at],
                device_id={"seq": i}, device_id_type=MESH,
            ).start()

    query_frame(0)
    query_frame(1)
    pass_on(out_step, out_dp, 2)
    query_frame(2)
    pass_on(up_step, up_dp, 1)
    query_frame(3)
    pass_on(out_step, out_dp, 3)
    came[0] = att_low[0]
    for k in range(1, SEQ):
        back[k].wait_recv()
    for h in range(SEQ):
        attended_ref[:, h * HEAD_DIM : (h + 1) * HEAD_DIM] = came[lax.rem(h - z + SEQ, SEQ)]
    own_out.wait()
    for k in range(SEQ):
        out_dp[k].wait_recv()
    keep(out_all, out_ref)

    def mix(start):
        def piece(n, carry):
            at = pl.ds(pl.multiple_of(n * 512, 512), 512)
            part_low[pl.ds(start, half), at] = jnp.dot(attended_ref[pl.ds(start, half), :], out_all[:, at], preferred_element_type=jnp.float32).astype(jnp.bfloat16)
            return carry

        lax.fori_loop(0, width // 512, piece, 0)

    mix(half)
    sum_core.start()
    mix(0)
    sum_core.wait_recv()
    half_low[...] = (part_low[quarter:half, :].astype(jnp.float32) + core_in[quarter:half, :].astype(jnp.float32)).astype(jnp.bfloat16)
    sum_chip.start()
    pass_on(up_step, up_dp, 2)
    down_step[1].start()
    sum_chip.wait_recv()
    resid = own_ref[...] + (part_low[0:quarter, :].astype(jnp.float32) + core_in[0:quarter, :].astype(jnp.float32)) + chip_in[...].astype(jnp.float32)
    center = resid - jnp.mean(resid, axis=1, keepdims=True)
    rate = lax.rsqrt(jnp.mean(center * center, axis=1, keepdims=True) + NORM_EPS)
    normed = center * rate
    resid_ref[...] = resid
    rate_ref[...] = rate
    normed_ref[...] = normed
    second[0:quarter, :] = normed.astype(jnp.bfloat16)
    second_chip.start()
    pass_on(up_step, up_dp, 3)
    second_chip.wait_recv()
    second_core.start()
    second_core.wait_recv()
    keep(second, second_ref)
    for k in range(1, SEQ):
        pass_on(down_step, down_dp, k)
    for copy in up_dp + down_dp:
        copy.wait_recv()
    for copy in used:
        copy.wait_send()
    for copy in kept:
        if not any(copy is done for done in (own_frame, own_head, own_out)):
            copy.wait()


def front(f0, w_three, w_out, w_up, w_down, own, bias):
    rows, width = f0.shape
    quarter, half = rows // 4, rows // 2
    part = w_out.shape[1]
    inner = w_out.shape[0]
    f32, bf16 = jnp.float32, jnp.bfloat16
    any_, vmem = pl.BlockSpec(memory_space=pl.ANY), pl.BlockSpec(memory_space=pltpu.VMEM)
    shape = jax.ShapeDtypeStruct
    outs = [
        (shape((SEQ, rows, width), bf16), any_),
        (shape((width, 3 * HEAD_DIM), bf16), vmem),
        (shape((SEQ, rows, 3 * HEAD_DIM), bf16), vmem),
        (shape((SEQ, rows, HEAD_DIM), f32), vmem),
        (shape((SEQ, 1, rows), f32), vmem),
        (shape((rows, inner), bf16), vmem),
        (shape((inner, width), bf16), any_),
        (shape((quarter, width), f32), vmem),
        (shape((quarter, width), f32), vmem),
        (shape((quarter, 1), f32), vmem),
        (shape((rows, width), bf16), any_),
        (shape((width, w_up.shape[1]), bf16), any_),
        (shape((w_down.shape[0], width), bf16), any_),
    ]
    copies = 3 * (SEQ - 1) + SEQ + 3 * (2 * SEQ - 1) + (SEQ - 1) + 4
    return pl.pallas_call(
        front_kernel,
        out_shape=[o[0] for o in outs],
        in_specs=[any_] * 5 + [vmem] * 2,
        out_specs=[o[1] for o in outs],
        scratch_shapes=[
            pltpu.VMEM((SEQ, rows, width), bf16),
            pltpu.VMEM((2 * SEQ, part, 3 * HEAD_DIM), bf16),
            pltpu.VMEM((inner, width), bf16),
            pltpu.VMEM((SEQ, rows, HEAD_DIM), bf16),
            pltpu.VMEM((SEQ, rows, HEAD_DIM), bf16),
            pltpu.VMEM((rows, width), bf16),
            pltpu.VMEM((half, width), bf16),
            pltpu.VMEM((quarter, width), bf16),
            pltpu.VMEM((quarter, width), bf16),
            pltpu.VMEM((rows, width), bf16),
            pltpu.VMEM((1, rows), f32),
            pltpu.VMEM((1, rows), f32),
            pltpu.VMEM((HEAD_DIM, rows), f32),
            pltpu.SemaphoreType.DMA((copies,)),
            pltpu.SemaphoreType.DMA((copies,)),
            pltpu.SemaphoreType.DMA((16,)),
        ],
        compiler_params=pltpu.CompilerParams(collective_id=0, has_side_effects=True, vmem_limit_bytes=56 * 2**20),
        cost_estimate=pl.CostEstimate(flops=8 * 10**9, bytes_accessed=50 * 10**6, transcendentals=5 * 10**6),
    )(f0, w_three, w_out, w_up, w_down, own, bias)


def back_kernel(
    gd_ref, gd_came_ref, gu_ref, dn_ref, cot_ref, normed_two_ref, rate_two_ref, attended_ref, out_ref, qkv_ref, att_ref, lse_ref, bias_ref, w_head_ref, whole_ref,
    normed_one_ref, rate_one_ref,
    down_sum_ref, up_sum_ref, out_sum_ref, arrived_ref, grad_in_ref, cross_down_ref, cross_up_ref, ring_down_ref, ring_up_ref, first_core_ref, first_chip_ref, first_ring_ref,
    frames, t_cross, t_own, t_ring, outbox, mix, d_head, d_out, dq, dk, dv, delta, d_three, out_send, out_cross, out_ring, out_box,
    head_acc, head_low, head_cross, head_sum, dn_own, dn_core, half_low, dn_chip, mid, quart_box, in_box,
    send, recv, keep_sem, load_sem,
):
    dp, z, t = lax.axis_index("dp"), lax.axis_index("seq"), lax.axis_index("tensor")
    other_dp, chip, core = {"dp": 1 - dp}, {"tensor": lax.rem(t + 2, 4)}, {"tensor": t + 1 - 2 * lax.rem(t, 2)}
    f32, bf16 = jnp.float32, jnp.bfloat16

    def along(k):
        return {"seq": lax.rem(z + k + SEQ, SEQ)}

    rows, width = dn_ref.shape
    quarter, half = rows // 4, rows // 2
    part, hidden = gd_came_ref.shape
    inner = attended_ref.shape[1]
    half_inner = inner // 2
    ring = along(1)
    scale = HEAD_DIM ** (-0.5)
    used, sent = [], []

    def remote(src, dst, device):
        i = len(used)
        copy = pltpu.make_async_remote_copy(src_ref=src, dst_ref=dst, send_sem=send.at[i], recv_sem=recv.at[i], device_id=device, device_id_type=MESH)
        used.append(copy)
        return copy

    def flush(copy):
        if not any(copy is done for done in sent):
            copy.wait_send()
            sent.append(copy)

    def load(*pairs):
        copies = [pltpu.make_async_copy(src, dst, load_sem.at[i]) for i, (src, dst) in enumerate(pairs)]
        for copy in copies:
            copy.start()
        for copy in copies:
            copy.wait()

    barrier = pltpu.get_barrier_semaphore()
    peers = [other_dp, chip, core] + [along(k) for k in range(1, SEQ)]
    for peer in peers:
        pl.semaphore_signal(barrier, inc=1, device_id=peer, device_id_type=MESH)
    pl.semaphore_wait(barrier, len(peers))

    def block(ref, b):
        return ref.at[pl.ds(b * part, part), :]

    dn_core_copy = remote(dn_ref.at[pl.ds(half, half), :], dn_core, core)
    dn_chip_copy = remote(half_low, dn_chip, chip)
    mix_chip = remote(mix.at[pl.ds(0, quarter), :], mix.at[pl.ds(quarter, quarter), :], chip)
    mix_core = remote(mix.at[pl.ds(0, half), :], mix.at[pl.ds(half, half), :], core)
    spread = [None] + [remote(d_head.at[lax.rem(z + k, SEQ)], d_out.at[k], along(k)) for k in range(1, SEQ)]
    cross_down = {k: remote(block(gd_ref, SEQ + k), cross_down_ref.at[k], other_dp) for k in (2, 3, 0)}
    cross_up = {k: remote(block(gu_ref, SEQ + k), cross_up_ref.at[k], other_dp) for k in (1, 2, 3, 0)}
    cross_out = {k: remote(out_send.at[k], out_cross.at[k], other_dp) for k in (1, 2, 3, 0)}
    ring_down = {k: remote(outbox.at[k - 1], ring_down_ref.at[k - 1], ring) for k in (1, 2, 3)}
    ring_up = {k: remote(outbox.at[k - 1], ring_up_ref.at[k - 1], ring) for k in (1, 2, 3)}
    ring_out = {k: remote(out_box.at[k - 1], out_ring.at[k - 1], ring) for k in (1, 2, 3)}
    first_core = {k: remote(frames.at[k, pl.ds(half, half), :], first_core_ref.at[k], core) for k in (1, 2, 3, 0)}
    first_chip = {k: remote(quart_box.at[k], first_chip_ref.at[k], chip) for k in (1, 2, 3, 0)}
    first_ring = {k: remote(in_box.at[k - 1], first_ring_ref.at[k - 1], ring) for k in (1, 2, 3)}
    head_dp = remote(head_low.at[1 - dp], head_cross, other_dp)
    head_out = [None] + [remote(head_sum.at[lax.rem(z + k, SEQ)], arrived_ref.at[k], along(k)) for k in range(1, SEQ)]
    mine = grad_in_ref.at[pl.ds(t * quarter, quarter), :]
    mate = grad_in_ref.at[pl.ds(lax.rem(t + 2, 4) * quarter, quarter), :]
    in_chip = remote(in_box.at[3], mine, chip)
    in_core = [remote(in_box.at[3], mine, core), remote(mate, mate, core)]

    def scatter(k, own_ref, cross_at, crossing, ring_ref, rings, out, turned):
        pairs = [(cross_at, t_cross), (block(own_ref, k), t_own)]
        if crossing is not None and k != 2:
            crossing.wait_recv()
        if k != 1:
            came = (k - 1) % SEQ
            rings[came].wait_recv()
            pairs.append((ring_ref.at[came - 1], t_ring))
        load(*pairs)
        if k:
            for copies in (ring_down, ring_up):
                if copies is not rings and any(copies[k] is one for one in busy):
                    flush(copies[k])
            busy.append(rings[k])

        def piece(n, carry):
            at = pl.ds(pl.multiple_of(n * 256, 256), 256)
            sum_ = t_cross[:, at].astype(f32) + t_own[:, at].astype(f32)
            if k != 1:
                sum_ = sum_ + t_ring[:, at].astype(f32)
            if k:
                outbox[k - 1, :, at] = sum_.astype(bf16)
            elif turned:
                out[at, :] = sum_.T
            else:
                out[:, at] = sum_
            return carry

        lax.fori_loop(0, hidden // 256, piece, 0)
        if k:
            rings[k].start()

    busy = []

    def scatter_down(k):
        scatter(k, gd_ref, gd_came_ref if k == 1 else cross_down_ref.at[k], cross_down.get(k), ring_down_ref, ring_down, down_sum_ref, True)

    def scatter_up(k):
        if k == 2:
            cross_up[k].wait_recv()
        scatter(k, gu_ref, cross_up_ref.at[k], cross_up[k], ring_up_ref, ring_up, up_sum_ref, False)

    def out_block(b):
        return lax.dot_general(attended_ref[...], mix[:, b * part : (b + 1) * part], (((0,), (0,)), ((), ())), preferred_element_type=f32)

    def scatter_out(k):
        cross_out[k].wait_recv()
        sum_ = out_block(k) + out_cross[k].astype(f32)
        if k != 1:
            came = (k - 1) % SEQ
            ring_out[came].wait_recv()
            sum_ = sum_ + out_ring[came - 1].astype(f32)
        if k:
            out_box[k - 1] = sum_.astype(bf16)
            ring_out[k].start()
        else:
            out_sum_ref[...] = sum_

    dn_core_copy.start()
    cross_down[2].start()
    cross_down[3].start()
    fetch = [pltpu.make_async_copy(whole_ref.at[k], frames.at[k], keep_sem.at[k]) for k in range(SEQ)]
    spare = head_acc.at[pl.ds(0, quarter), :]
    load((dn_ref.at[pl.ds(0, half), :], dn_own), (normed_two_ref, spare), (out_ref.at[pl.ds(0, half_inner), :], outbox.at[1]), (out_ref.at[pl.ds(half_inner, half_inner), :], outbox.at[2]))
    for copy in fetch:
        copy.start()
    dn_core_copy.wait_recv()
    half_low[...] = (dn_own[quarter:half, :].astype(f32) + dn_core[quarter:half, :].astype(f32)).astype(bf16)
    dn_chip_copy.start()
    scatter_down(1)
    dn_chip_copy.wait_recv()
    grad = (dn_own[0:quarter, :].astype(f32) + dn_core[0:quarter, :].astype(f32)) + dn_chip[...].astype(f32)
    normed = spare[...]
    grad = rate_two_ref[...] * (grad - jnp.mean(grad, axis=1, keepdims=True) - normed * jnp.mean(grad * normed, axis=1, keepdims=True))
    grad = cot_ref[...].astype(f32) + grad
    mid[...] = grad
    mix[0:quarter, :] = grad.astype(bf16)
    mix_chip.start()
    cross_down[2].wait_recv()
    cross_down[0].start()
    mix_chip.wait_recv()
    mix_core.start()
    mix_core.wait_recv()

    for n in range(4):
        at = slice(n * quarter, (n + 1) * quarter)
        for side in range(2):
            piece = lax.dot_general(mix[at, :], outbox[side + 1], (((1,), (1,)), ((), ())), preferred_element_type=f32).astype(bf16)
            for h in range(SEQ // 2):
                d_head[side * (SEQ // 2) + h, at, :] = piece[:, h * HEAD_DIM : (h + 1) * HEAD_DIM]
    for k in range(1, SEQ):
        spread[k].start()
    d_out[0] = d_head[z]
    for k in (1, 2, 3, 0):
        out_send[k] = out_block(SEQ + k).astype(bf16)
        cross_out[k].start()
    scatter_down(2)
    cross_up[1].start()
    for k in range(1, SEQ):
        spread[k].wait_recv()
    dq[...] = jnp.zeros_like(dq)
    for f in range(SEQ):
        delta[f] = jnp.sum((d_out[f].astype(f32) * att_ref[f]).T, axis=0, keepdims=True)

    def key_frame(j):
        here = lax.rem(z - j + SEQ, SEQ)
        dk[...] = jnp.zeros_like(dk)
        dv[...] = jnp.zeros_like(dv)

        def query_frame(i, inner_):
            at = lax.rem(z - i + SEQ, SEQ)
            query, key, value = qkv_ref[at, :, :HEAD_DIM], qkv_ref[here, :, HEAD_DIM : 2 * HEAD_DIM], qkv_ref[here, :, 2 * HEAD_DIM :]
            grad_out = d_out[at]
            scores = lax.dot_general(key, query, (((1,), (1,)), ((), ())), preferred_element_type=f32) * scale + bias_ref[j]
            prob = jnp.exp(scores - lse_ref[at])
            d_prob = lax.dot_general(value, grad_out, (((1,), (1,)), ((), ())), preferred_element_type=f32)
            d_scores = (prob * (d_prob - delta[at])).astype(bf16)
            dv[...] += jnp.dot(prob.astype(bf16), grad_out, preferred_element_type=f32)
            dk[...] += jnp.dot(d_scores, query, preferred_element_type=f32)
            dq[at] += lax.dot_general(key, d_scores, (((0,), (0,)), ((), ())), preferred_element_type=f32)
            return inner_

        lax.fori_loop(j, SEQ, query_frame, 0)
        d_three[here, :, HEAD_DIM : 2 * HEAD_DIM] = (dk[...] * scale).astype(bf16)
        d_three[here, :, 2 * HEAD_DIM :] = dv[...].astype(bf16)

    key_frame(0)
    scatter_out(1)
    key_frame(1)
    scatter_down(3)
    cross_up[2].start()
    key_frame(2)
    scatter_out(2)
    key_frame(3)
    for f in range(SEQ):
        d_three[f, :, :HEAD_DIM] = (dq[f] * scale).T.astype(bf16)

    def project_back(k):
        fetch[k].wait()

        def piece(n, carry):
            at = pl.ds(pl.multiple_of(n * 512, 512), 512)
            term = lax.dot_general(d_three[k], frames[k, :, at], (((0,), (0,)), ((), ())), preferred_element_type=f32)
            head_acc[:, at] = term if k == 1 else head_acc[:, at] + term
            return carry

        lax.fori_loop(0, width // 512, piece, 0)

        def back_piece(n, carry):
            at = pl.ds(pl.multiple_of(n * 512, 512), 512)
            frames[k, :, at] = lax.dot_general(d_three[k], w_head_ref[at, :], (((1,), (1,)), ((), ())), preferred_element_type=f32).astype(bf16)
            return carry

        lax.fori_loop(0, width // 512, back_piece, 0)
        first_core[k].start()

    def half_sum(k):
        first_core[k].wait_recv()
        load((first_core_ref.at[k], dn_own))
        quart_box[k] = (frames[k, quarter:half, :].astype(f32) + dn_own[quarter:half, :].astype(f32)).astype(bf16)
        first_chip[k].start()
        frames[k, 0:quarter, :] = (frames[k, 0:quarter, :].astype(f32) + dn_own[0:quarter, :].astype(f32)).astype(bf16)

    def quarter_sum(k):
        first_chip[k].wait_recv()
        pairs = [(first_chip_ref.at[k], dn_own.at[pl.ds(0, quarter), :])]
        if k != 1:
            came = (k - 1) % SEQ
            first_ring[came].wait_recv()
            pairs.append((first_ring_ref.at[came - 1], dn_own.at[pl.ds(quarter, quarter), :]))
        load(*pairs)
        sum_ = frames[k, 0:quarter, :].astype(f32) + dn_own[0:quarter, :].astype(f32)
        if k != 1:
            sum_ = sum_ + dn_own[quarter:half, :].astype(f32)
        return sum_

    project_back(1)
    project_back(2)
    half_sum(1)
    project_back(3)
    half_sum(2)
    project_back(0)
    half_sum(3)
    half_sum(0)
    for side in range(2):
        head_low[side] = head_acc[:, side * (width // 2) : (side + 1) * (width // 2)].astype(bf16)
    head_dp.start()
    scatter_out(3)
    in_box[0] = quarter_sum(1).astype(bf16)
    first_ring[1].start()
    scatter_down(0)
    cross_up[3].start()
    in_box[1] = quarter_sum(2).astype(bf16)
    first_ring[2].start()
    scatter_up(1)
    in_box[2] = quarter_sum(3).astype(bf16)
    first_ring[3].start()
    head_dp.wait_recv()
    cross_up[0].start()
    for j in range(SEQ):
        at = slice(j * part, (j + 1) * part)
        head_sum[j] = (head_low[dp, :, at].astype(f32) + head_cross[:, at].astype(f32)).astype(bf16)
    for k in range(1, SEQ):
        head_out[k].start()
    own_head = pltpu.make_async_copy(head_sum.at[z], arrived_ref.at[0], keep_sem.at[0])
    own_head.start()
    scatter_out(0)
    scatter_up(2)
    grad = quarter_sum(0)
    load((normed_one_ref, spare))
    normed = spare[...]
    grad = rate_one_ref[...] * (grad - jnp.mean(grad, axis=1, keepdims=True) - normed * jnp.mean(grad * normed, axis=1, keepdims=True))
    for c in range(2 * SEQ):
        b = lax.rem(dp + c // SEQ, 2) * SEQ + lax.rem(z - c % SEQ + SEQ, SEQ)
        at = slice(c * part, (c + 1) * part)
        in_box[3, :, at] = (mid[:, pl.ds(pl.multiple_of(b * part, part), part)] + grad[:, at]).astype(bf16)
    in_chip.start()
    in_core[0].start()
    own_in = pltpu.make_async_copy(in_box.at[3], mine, keep_sem.at[1])
    own_in.start()
    in_chip.wait_recv()
    in_core[1].start()
    scatter_up(3)
    scatter_up(0)
    for copy in in_core + head_out[1:]:
        copy.wait_recv()
    for copy in used:
        flush(copy)
    own_head.wait()
    own_in.wait()


def back(gd, gd_came, gu, dn, cot, normed_two, rate_two, attended, out_rel, qkv, att, lse, bias, w_head, whole, normed_one, rate_one):
    rows, width = dn.shape
    quarter, half = rows // 4, rows // 2
    part = gd_came.shape[0]
    inner = attended.shape[1]
    hidden = gd.shape[1]
    three = 3 * HEAD_DIM
    f32, bf16 = jnp.float32, jnp.bfloat16
    any_, vmem = pl.BlockSpec(memory_space=pl.ANY), pl.BlockSpec(memory_space=pltpu.VMEM)
    shape = jax.ShapeDtypeStruct
    outs = [
        (shape((hidden, part), f32), vmem),
        (shape((part, hidden), f32), vmem),
        (shape((inner, part), f32), vmem),
        (shape((SEQ, three, part), bf16), any_),
        (shape((rows, width), bf16), any_),
        (shape((SEQ, part, hidden), bf16), any_),
        (shape((SEQ, part, hidden), bf16), any_),
        (shape((SEQ - 1, part, hidden), bf16), any_),
        (shape((SEQ - 1, part, hidden), bf16), any_),
        (shape((SEQ, half, width), bf16), any_),
        (shape((SEQ, quarter, width), bf16), any_),
        (shape((SEQ - 1, quarter, width), bf16), any_),
    ]
    copies = 4 + 3 + 3 + 4 + 4 + 9 + 4 + 4 + 3 + 1 + 3 + 3
    scratch = [
        ((SEQ, rows, width), bf16),
        ((part, hidden), bf16),
        ((part, hidden), bf16),
        ((part, hidden), bf16),
        ((SEQ - 1, part, hidden), bf16),
        ((rows, width), bf16),
        ((SEQ, rows, HEAD_DIM), bf16),
        ((SEQ, rows, HEAD_DIM), bf16),
        ((SEQ, HEAD_DIM, rows), f32),
        ((rows, HEAD_DIM), f32),
        ((rows, HEAD_DIM), f32),
        ((SEQ, 1, rows), f32),
        ((SEQ, rows, three), bf16),
        ((SEQ, inner, part), bf16),
        ((SEQ, inner, part), bf16),
        ((SEQ - 1, inner, part), bf16),
        ((SEQ - 1, inner, part), bf16),
        ((three, width), f32),
        ((2, three, width // 2), bf16),
        ((three, width // 2), bf16),
        ((SEQ, three, part), bf16),
        ((half, width), bf16),
        ((half, width), bf16),
        ((quarter, width), bf16),
        ((quarter, width), bf16),
        ((quarter, width), f32),
        ((SEQ, quarter, width), bf16),
        ((SEQ, quarter, width), bf16),
    ]
    return pl.pallas_call(
        back_kernel,
        out_shape=[o[0] for o in outs],
        in_specs=[any_] * 4 + [vmem, any_, vmem, vmem, any_] + [vmem] * 5 + [any_] * 2 + [vmem],
        out_specs=[o[1] for o in outs],
        scratch_shapes=[pltpu.VMEM(*one) for one in scratch]
        + [pltpu.SemaphoreType.DMA((copies,)), pltpu.SemaphoreType.DMA((copies,)), pltpu.SemaphoreType.DMA((SEQ,)), pltpu.SemaphoreType.DMA((4,))],
        compiler_params=pltpu.CompilerParams(collective_id=1, has_side_effects=True, vmem_limit_bytes=62 * 2**20),
        cost_estimate=pl.CostEstimate(flops=20 * 10**9, bytes_accessed=60 * 10**6, transcendentals=5 * 10**6),
    )(gd, gd_came, gu, dn, cot, normed_two, rate_two, attended, out_rel, qkv, att, lse, bias, w_head, whole, normed_one, rate_one)[:5]


def norm_parts(values):
    center = values - jnp.mean(values, axis=-1, keepdims=True)
    rate = lax.rsqrt(jnp.mean(center * center, axis=-1, keepdims=True) + NORM_EPS)
    return center * rate, rate


def norm_back(normed, rate, grad):
    return rate * (grad - jnp.mean(grad, axis=-1, keepdims=True) - normed * jnp.mean(grad * normed, axis=-1, keepdims=True))


def mm(left, right, dims=((1,), (0,)), out=jnp.bfloat16):
    return lax.dot_general(left, right, (dims, ((), ())), preferred_element_type=jnp.float32).astype(out)


def local_fast(inputs, first_gain, w_query, w_key, w_value, w_out, second_gain, w_up, w_down, frame_mask, cotangent):
    dp, z, t = lax.axis_index("dp"), lax.axis_index("seq"), lax.axis_index("tensor")
    rows = inputs.shape[1]
    quarter = rows // 4
    width = inputs.shape[2]
    part = width // (2 * SEQ)
    heads = w_query.shape[1] // HEAD_DIM
    f32, bf16 = jnp.float32, jnp.bfloat16

    def rel_block(b):
        return (dp ^ (b // SEQ)) * SEQ + lax.rem(z - b % SEQ + SEQ, SEQ)

    def rel_cols(values):
        return jnp.concatenate([lax.dynamic_slice_in_dim(values, rel_block(b) * part, part, 1) for b in range(2 * SEQ)], axis=1)

    def can_cols(values):
        picks = []
        for c in range(2 * SEQ):
            b = (dp ^ (c // SEQ)) * SEQ + lax.rem(z - c % SEQ + SEQ, SEQ)
            picks.append(lax.dynamic_slice_in_dim(values, b * part, part, 1))
        return jnp.concatenate(picks, axis=1)

    def rel_rows(values):
        return jnp.concatenate([lax.dynamic_slice_in_dim(values, (t ^ p) * quarter, quarter, 0) for p in (0, 2, 1, 3)], axis=0)

    def can_rows(values):
        picks = []
        for c in range(4):
            d = t ^ c
            p = (d % 2) * 2 + d // 2
            picks.append(lax.dynamic_slice_in_dim(values, p * quarter, quarter, 0))
        return jnp.concatenate(picks, axis=0)

    own_in = inputs[0]
    normed_one_all = norm_parts(own_in.astype(f32))[0].astype(bf16)
    frame0 = rel_rows(normed_one_all)
    w_three = jnp.stack([w_query, w_key, w_value], axis=1).reshape(part, 3, heads, HEAD_DIM)
    w_three = (w_three.astype(f32) * first_gain.astype(f32)[:, None, None, None]).astype(bf16)
    w_three = w_three.transpose(2, 0, 1, 3).reshape(heads, part, 3 * HEAD_DIM)
    w_up_scaled = (w_up.astype(f32) * second_gain.astype(f32)[:, None]).astype(bf16)
    own_rel = rel_cols(lax.dynamic_slice_in_dim(own_in, t * quarter, quarter, 0)).astype(f32)
    place = z.reshape(1)
    valid = frame_mask[0]
    bias = jnp.broadcast_to(jnp.where(valid == 1, 0.0, MASK_FILL).astype(f32)[:, None, None], (SEQ, 1, rows))
    whole, w_head, qkv, attended_f, lse, attended, out_rel, resid_mid, normed_two, rate_two, second_in, up_rel, down_rel = front(
        frame0, w_three, w_out, w_up_scaled, w_down, own_rel, bias
    )

    cot_rel = rel_cols(rel_rows(cotangent[0]))
    up_pre = mm(second_in, up_rel, out=f32)
    cdf = 0.5 * (1.0 + lax.erf(up_pre * (0.5**0.5)))
    up_act = (up_pre * cdf).astype(bf16)
    slope = cdf + up_pre * jnp.exp(-0.5 * up_pre * up_pre) * ((2.0 * jnp.pi) ** -0.5)
    grad_down = mm(cot_rel, up_act, ((0,), (0,)))
    down_came = swap_dp(grad_down[(SEQ + 1) * part : (SEQ + 2) * part])
    result = resid_mid + scatter_tensor(mm(up_act, down_rel))
    result = can_rows(gather_tensor(can_cols(result.astype(bf16))))[None]
    d_up = (mm(cot_rel, down_rel, ((1,), (1,)), f32) * slope).astype(bf16)
    grad_up = mm(second_in, d_up, ((0,), (0,)))
    d_normed_two = mm(d_up, up_rel, ((1,), (1,)))

    own_quarter = lax.dynamic_slice_in_dim(own_in, t * quarter, quarter, 0).astype(f32)
    normed_one, rate_one = norm_parts(own_quarter)
    down_sum, up_raw, out_sum, arrived, grad_in = back(
        grad_down, down_came, grad_up, d_normed_two, cot_rel[:quarter], normed_two, rate_two, attended, out_rel, qkv, attended_f, lse, bias, w_head, whole, normed_one, rate_one
    )
    grad_inputs = grad_in[None]
    by_head = [dyn(arrived, lax.rem(z - h + SEQ, SEQ)).astype(f32).T for h in range(heads)]
    gain_one = first_gain.astype(f32)[:, None]
    raw = [jnp.concatenate([one[:, n * HEAD_DIM : (n + 1) * HEAD_DIM] for one in by_head], axis=1) for n in range(3)]
    d_gain_one = sum(jnp.sum(weight.astype(f32) * one, axis=1) for weight, one in zip((w_query, w_key, w_value), raw))
    d_gain_two = jnp.sum(w_up.astype(f32) * up_raw, axis=1)
    gains = jnp.stack([d_gain_one, d_gain_two])
    gains = gains + swap_core(gains)
    gains = gains + swap_chip(gains)
    return (
        result,
        grad_inputs,
        gains[0],
        raw[0] * gain_one,
        raw[1] * gain_one,
        raw[2] * gain_one,
        out_sum,
        gains[1],
        up_raw * second_gain.astype(f32)[:, None],
        down_sum,
    )


SEQ = 4


def solution(mesh):
    placed = (
        P("dp", "seq", None),
        P(("dp", "seq")),
        P(("dp", "seq"), "tensor"),
        P(("dp", "seq"), "tensor"),
        P(("dp", "seq"), "tensor"),
        P("tensor", ("dp", "seq")),
        P(("dp", "seq")),
        P(("dp", "seq"), "tensor"),
        P("tensor", ("dp", "seq")),
        P("dp", None),
        P("dp", "seq", None),
    )
    sizes = dict(mesh.shape)
    spread = sizes == {"dp": 2, "seq": SEQ, "tensor": 4}
    return jax.shard_map(
        local_fast if spread else local,
        mesh=mesh,
        in_specs=placed,
        out_specs=(
            P("dp", "seq", None),
            P("dp", "seq", None),
            P(("dp", "seq")),
            P(("dp", "seq"), "tensor"),
            P(("dp", "seq"), "tensor"),
            P(("dp", "seq"), "tensor"),
            P("tensor", ("dp", "seq")),
            P(("dp", "seq")),
            P(("dp", "seq"), "tensor"),
            P("tensor", ("dp", "seq")),
        ),
        check_vma=False,
    )
```

```python
import functools

import jax
import jax.numpy as jnp
from jax import lax
from jax.experimental import pallas as pl
from jax.experimental.pallas import tpu as pltpu
from jax.sharding import PartitionSpec as P

HEAD_DIM = 128
FRAME_TOK = 640


NORM_EPS = 1e-05
MASK_FILL = -1e30
MESH = pl.DeviceIdType.MESH


def norm_rows(values):
    center = values - jnp.mean(values, axis=-1, keepdims=True)
    spread = jnp.mean(center * center, axis=-1, keepdims=True)
    return center * lax.rsqrt(spread + NORM_EPS)


def gelu_exact(values):
    return jax.nn.gelu(values, approximate=False)


def heads_total(values):
    return lax.psum(values.astype(jnp.bfloat16), "tensor").astype(jnp.float32)


def local(
    inputs,
    first_gain,
    w_query,
    w_key,
    w_value,
    w_out,
    second_gain,
    w_up,
    w_down,
    frame_mask,
    cotangent,
):
    seq_pos = lax.axis_index("seq")
    gain_one, query_w, key_w, value_w, gain_two, up_w = (
        lax.all_gather(first_gain, ("dp", "seq"), axis=0, tiled=True),
        lax.all_gather(w_query, ("dp", "seq"), axis=0, tiled=True),
        lax.all_gather(w_key, ("dp", "seq"), axis=0, tiled=True),
        lax.all_gather(w_value, ("dp", "seq"), axis=0, tiled=True),
        lax.all_gather(second_gain, ("dp", "seq"), axis=0, tiled=True),
        lax.all_gather(w_up, ("dp", "seq"), axis=0, tiled=True),
    )
    out_w, down_w = (
        lax.all_gather(w_out, ("dp", "seq"), axis=1, tiled=True),
        lax.all_gather(w_down, ("dp", "seq"), axis=1, tiled=True),
    )
    tok_rows = inputs.shape[1]
    local_inner = query_w.shape[1]
    local_heads = local_inner // HEAD_DIM
    frames_dev = tok_rows // FRAME_TOK
    score_scale = HEAD_DIM ** (-0.5)
    clip_valid = frame_mask[0]
    frame_count = clip_valid.shape[0]
    resid_in = inputs[0].astype(jnp.float32)
    dout_rows = cotangent[0]
    row_frame = seq_pos * frames_dev + jnp.arange(tok_rows, dtype=jnp.int32) // FRAME_TOK
    frame_limit = (seq_pos + 1) * frames_dev
    normed_one = norm_rows(resid_in)
    first_in = (normed_one * gain_one.astype(jnp.float32)).astype(jnp.bfloat16)
    query = jnp.dot(first_in, query_w, preferred_element_type=jnp.float32).astype(jnp.bfloat16)
    key_local = jnp.dot(first_in, key_w, preferred_element_type=jnp.float32).astype(jnp.bfloat16)
    value_local = jnp.dot(first_in, value_w, preferred_element_type=jnp.float32).astype(
        jnp.bfloat16
    )
    key_all, value_all = (
        lax.all_gather(key_local, "seq", axis=0, tiled=True),
        lax.all_gather(value_local, "seq", axis=0, tiled=True),
    )
    query_heads = query.reshape(tok_rows, local_heads, HEAD_DIM)
    key_frames = key_all.reshape(frame_count, FRAME_TOK, local_heads, HEAD_DIM)
    value_frames = value_all.reshape(frame_count, FRAME_TOK, local_heads, HEAD_DIM)

    def frame_scores(frame_idx):
        key_block = lax.dynamic_index_in_dim(key_frames, frame_idx, 0, keepdims=False)
        value_block = lax.dynamic_index_in_dim(value_frames, frame_idx, 0, keepdims=False)
        scores = (
            jnp.einsum("qhd,khd->hqk", query_heads, key_block, preferred_element_type=jnp.float32)
            * score_scale
        )
        frame_ok = lax.dynamic_index_in_dim(clip_valid, frame_idx, 0, keepdims=False) == 1
        allowed = ((frame_idx <= row_frame) & frame_ok)[None, :, None]
        return (scores, allowed, key_block, value_block)

    def stats_step(frame_idx, running):
        row_max, row_sum = running
        scores, allowed, key_block, value_block = frame_scores(frame_idx)
        masked = jnp.where(allowed, scores, MASK_FILL)
        new_max = jnp.maximum(row_max, jnp.max(masked, axis=2))
        exp_terms = jnp.where(allowed, jnp.exp(masked - new_max[:, :, None]), 0.0)
        return (new_max, row_sum * jnp.exp(row_max - new_max) + jnp.sum(exp_terms, axis=2))

    start_stats = (
        jnp.full((local_heads, tok_rows), MASK_FILL, jnp.float32),
        jnp.zeros((local_heads, tok_rows), jnp.float32),
    )
    row_max, row_sum = lax.fori_loop(0, frame_limit, stats_step, start_stats)

    def soft_weights(scores, allowed):
        return jnp.where(allowed, jnp.exp(scores - row_max[:, :, None]) / row_sum[:, :, None], 0.0)

    def output_step(frame_idx, running):
        scores, allowed, key_block, value_block = frame_scores(frame_idx)
        attn_prob = soft_weights(scores, allowed).astype(jnp.bfloat16)
        return running + jnp.einsum(
            "hqk,khd->qhd", attn_prob, value_block, preferred_element_type=jnp.float32
        )

    attended = lax.fori_loop(
        0, frame_limit, output_step, jnp.zeros((tok_rows, local_heads, HEAD_DIM), jnp.float32)
    )
    attended_low = attended.reshape(tok_rows, local_inner).astype(jnp.bfloat16)
    resid_mid = resid_in + heads_total(
        jnp.dot(attended_low, out_w, preferred_element_type=jnp.float32)
    )
    normed_two = norm_rows(resid_mid)
    second_in = (normed_two * gain_two.astype(jnp.float32)).astype(jnp.bfloat16)
    up_pre = jnp.dot(second_in, up_w, preferred_element_type=jnp.float32)
    up_act = gelu_exact(up_pre).astype(jnp.bfloat16)
    resid_out = resid_mid + heads_total(jnp.dot(up_act, down_w, preferred_element_type=jnp.float32))
    result = resid_out.astype(jnp.bfloat16)[None]
    grad_down = jnp.einsum("tf,td->fd", up_act, dout_rows, preferred_element_type=jnp.float32)
    d_act = jnp.einsum("td,fd->tf", dout_rows, down_w, preferred_element_type=jnp.float32)
    gelu_pull = jax.vjp(gelu_exact, up_pre)[1]
    d_up_pre = gelu_pull(d_act)[0].astype(jnp.bfloat16)
    grad_up = jnp.einsum("td,tf->df", second_in, d_up_pre, preferred_element_type=jnp.float32)
    d_second = heads_total(
        jnp.einsum("tf,df->td", d_up_pre, up_w, preferred_element_type=jnp.float32)
    )
    grad_second_gain = jnp.sum(d_second * normed_two, axis=0)
    norm_pull_two = jax.vjp(norm_rows, resid_mid)[1]
    d_mid = (
        dout_rows.astype(jnp.float32) + norm_pull_two(d_second * gain_two.astype(jnp.float32))[0]
    )
    d_mix = d_mid.astype(jnp.bfloat16)
    grad_out = jnp.einsum("ti,td->id", attended_low, d_mix, preferred_element_type=jnp.float32)
    d_attended = jnp.einsum("td,id->ti", d_mix, out_w, preferred_element_type=jnp.float32).astype(
        jnp.bfloat16
    )
    dout_heads = d_attended.reshape(tok_rows, local_heads, HEAD_DIM)
    row_delta = jnp.sum(dout_heads.astype(jnp.float32) * attended, axis=2).T

    def query_step(frame_idx, running):
        scores, allowed, key_block, value_block = frame_scores(frame_idx)
        attn_prob = soft_weights(scores, allowed)
        d_prob = jnp.einsum(
            "qhd,khd->hqk", dout_heads, value_block, preferred_element_type=jnp.float32
        )
        d_scores = (attn_prob * (d_prob - row_delta[:, :, None])).astype(jnp.bfloat16)
        return running + jnp.einsum(
            "hqk,khd->qhd", d_scores, key_block, preferred_element_type=jnp.float32
        )

    query_sum = lax.fori_loop(
        0, frame_limit, query_step, jnp.zeros((tok_rows, local_heads, HEAD_DIM), jnp.float32)
    )
    d_query = (query_sum * score_scale).reshape(tok_rows, local_inner).astype(jnp.bfloat16)

    def one_frame(frame_step):
        scores, allowed, key_block, value_block = frame_scores(frame_step)
        attn_prob = soft_weights(scores, allowed)
        d_prob = jnp.einsum(
            "qhd,khd->hqk", dout_heads, value_block, preferred_element_type=jnp.float32
        )
        d_scores = (attn_prob * (d_prob - row_delta[:, :, None])).astype(jnp.bfloat16)
        key_term = (
            jnp.einsum("hqk,qhd->khd", d_scores, query_heads, preferred_element_type=jnp.float32)
            * score_scale
        )
        value_term = jnp.einsum(
            "hqk,qhd->khd",
            attn_prob.astype(jnp.bfloat16),
            dout_heads,
            preferred_element_type=jnp.float32,
        )
        return jnp.concatenate(
            [key_term.reshape(FRAME_TOK, local_inner), value_term.reshape(FRAME_TOK, local_inner)],
            axis=1,
        )

    blocks = lax.map(
        one_frame, jnp.arange(tok_rows * lax.axis_size("seq") // FRAME_TOK, dtype=jnp.int32)
    )
    kv_grad = lax.psum_scatter(
        blocks.reshape(tok_rows * lax.axis_size("seq"), 2 * local_inner).astype(jnp.bfloat16),
        "seq",
        scatter_dimension=0,
        tiled=True,
    ).astype(jnp.float32)
    d_key = kv_grad[:, :local_inner].astype(jnp.bfloat16)
    d_value = kv_grad[:, local_inner:].astype(jnp.bfloat16)
    grad_query = jnp.einsum("td,ti->di", first_in, d_query, preferred_element_type=jnp.float32)
    grad_key = jnp.einsum("td,ti->di", first_in, d_key, preferred_element_type=jnp.float32)
    grad_value = jnp.einsum("td,ti->di", first_in, d_value, preferred_element_type=jnp.float32)
    first_local = jnp.einsum("ti,di->td", d_query, query_w, preferred_element_type=jnp.float32)
    first_local = first_local + jnp.einsum(
        "ti,di->td", d_key, key_w, preferred_element_type=jnp.float32
    )
    first_local = first_local + jnp.einsum(
        "ti,di->td", d_value, value_w, preferred_element_type=jnp.float32
    )
    d_first = heads_total(first_local)
    grad_first_gain = jnp.sum(d_first * normed_one, axis=0)
    norm_pull_one = jax.vjp(norm_rows, resid_in)[1]
    grad_inputs = (d_mid + norm_pull_one(d_first * gain_one.astype(jnp.float32))[0]).astype(
        jnp.bfloat16
    )[None]
    summed_in = (
        lax.psum_scatter(
            grad_first_gain.astype(jnp.bfloat16), ("dp", "seq"), scatter_dimension=0, tiled=True
        ).astype(jnp.float32),
        lax.psum_scatter(
            grad_query.astype(jnp.bfloat16), ("dp", "seq"), scatter_dimension=0, tiled=True
        ).astype(jnp.float32),
        lax.psum_scatter(
            grad_key.astype(jnp.bfloat16), ("dp", "seq"), scatter_dimension=0, tiled=True
        ).astype(jnp.float32),
        lax.psum_scatter(
            grad_value.astype(jnp.bfloat16), ("dp", "seq"), scatter_dimension=0, tiled=True
        ).astype(jnp.float32),
        lax.psum_scatter(
            grad_second_gain.astype(jnp.bfloat16), ("dp", "seq"), scatter_dimension=0, tiled=True
        ).astype(jnp.float32),
        lax.psum_scatter(
            grad_up.astype(jnp.bfloat16), ("dp", "seq"), scatter_dimension=0, tiled=True
        ).astype(jnp.float32),
    )
    summed_out = (
        lax.psum_scatter(
            grad_out.astype(jnp.bfloat16), ("dp", "seq"), scatter_dimension=1, tiled=True
        ).astype(jnp.float32),
        lax.psum_scatter(
            grad_down.astype(jnp.bfloat16), ("dp", "seq"), scatter_dimension=1, tiled=True
        ).astype(jnp.float32),
    )
    return (
        result,
        grad_inputs,
        summed_in[0],
        summed_in[1],
        summed_in[2],
        summed_in[3],
        summed_out[0],
        summed_in[4],
        summed_in[5],
        summed_out[1],
    )


def axes_of():
    dp, z, t = lax.axis_index("dp"), lax.axis_index("seq"), lax.axis_index("tensor")
    other_dp, chip, core = {"dp": 1 - dp}, {"tensor": lax.rem(t + 2, 4)}, {"tensor": t + 1 - 2 * lax.rem(t, 2)}
    pair = {"seq": z + 1 - 2 * lax.rem(z, 2)}
    return dp, z, t, other_dp, chip, core, pair


class Copies:
    def __init__(self, send, recv):
        self.send, self.recv, self.all, self.came, self.left = send, recv, [], [], []

    def make(self, src, dst, device):
        i = len(self.all)
        copy = pltpu.make_async_remote_copy(src_ref=src, dst_ref=dst, send_sem=self.send.at[i], recv_sem=self.recv.at[i], device_id=device, device_id_type=MESH)
        self.all.append(copy)
        return copy

    def wait(self, *copies):
        for copy in copies:
            if not any(copy is done for done in self.came):
                copy.wait_recv()
                self.came.append(copy)

    def finish(self):
        self.wait(*self.all)
        for copy in self.all:
            copy.wait_send()


def greet(peers):
    barrier = pltpu.get_barrier_semaphore()
    for peer in peers:
        pl.semaphore_signal(barrier, inc=1, device_id=peer, device_id_type=MESH)
    pl.semaphore_wait(barrier, len(peers))


def front_kernel(
    x_ref, w_query_ref, w_key_ref, w_value_ref, w_out_ref, w_up_ref, w_down_ref, gain_one_ref, gain_two_ref, cot_ref, bias_ref,
    whole_ref, w_head_ref, qkv_ref, att_ref, lse_ref, attended_ref, out_ref, resid_ref, normed_ref, rate_ref, second_ref, up_ref, down_ref, cots_ref,
    tokens, frames, w_own, w_head, up_own, out_all, att_low, came, part_low, core_in, half_low, chip_in, second, peak, total, acc, send, recv, local_sem,
):
    f32, bf16 = jnp.float32, jnp.bfloat16
    dp, z, t, other_dp, chip, core, pair = axes_of()
    rows, width = x_ref.shape
    quarter, half = rows // 4, rows // 2
    part, hidden = w_up_ref.shape
    side = hidden // 2
    copies = Copies(send, recv)
    kept = []

    def keep(src, dst):
        copy = pltpu.make_async_copy(src, dst, local_sem.at[len(kept)])
        kept.append(copy)
        copy.start()
        return copy

    def along(k):
        return {"seq": lax.rem(z + k + SEQ, SEQ)}

    def owner(k):
        return (dp * SEQ + lax.rem(z - k + SEQ, SEQ)) * part

    mate = t + 1 - 2 * lax.rem(t, 2)
    quarters = [t, lax.rem(t + 2, 4), mate, lax.rem(mate + 2, 4)]
    load_tokens = [keep(x_ref.at[pl.ds(quarters[n] * quarter, quarter), :], tokens.at[pl.ds(n * quarter, quarter), :]) for n in range(4)]
    keep_cots = [keep(cot_ref.at[pl.ds(quarters[n] * quarter, quarter), :], cots_ref.at[pl.ds(n * quarter, quarter), :]) for n in range(4)]
    own_out = keep(w_out_ref, out_all.at[:, pl.ds(owner(0), part)])
    keep(w_down_ref.at[pl.ds(lax.rem(z, 2) * side, side), :], down_ref.at[:, pl.ds(owner(0), part)])
    greet([other_dp, chip, core] + [along(k) for k in range(1, SEQ)])

    first = slice(0, quarter)

    def rows_at(n, count=1):
        return pl.ds(n * quarter, count * quarter)

    token = [None] + [copies.make(frames.at[k - 1, rows_at(0), :], frames.at[k, rows_at(0), :], along(1)) for k in range(1, SEQ)]
    token_chip = [None] + [copies.make(frames.at[k, rows_at(0), :], frames.at[k, rows_at(1), :], chip) for k in range(1, SEQ)]
    token_core = [None] + [copies.make(frames.at[k, rows_at(0, 2), :], frames.at[k, rows_at(2, 2), :], core) for k in range(1, SEQ)]
    head = [None] + [copies.make(w_own.at[lax.rem(z + k, SEQ)], w_head.at[pl.ds(owner(0), part), :], along(k)) for k in range(1, SEQ)]
    mine = pl.ds(dp * SEQ * part, SEQ * part)
    head_dp = copies.make(w_head.at[mine, :], w_head.at[mine, :], other_dp)

    def gather(source, at):
        step = [None] + [copies.make(source(lax.rem(z + k, 2)), at(owner(0)), along(k)) for k in range(1, SEQ)]
        cross = [copies.make(at(owner(k)) if k else source(lax.rem(z, 2)), at(owner(k)), other_dp) for k in range(SEQ)]
        return step, cross

    out_step, out_dp = gather(lambda h: w_out_ref, lambda c: out_all.at[:, pl.ds(c, part)])
    up_step, up_dp = gather(lambda h: up_own.at[h], lambda c: up_ref.at[pl.ds(c, part), :])
    down_step, down_dp = gather(lambda h: w_down_ref.at[pl.ds(h * side, side), :], lambda c: down_ref.at[:, pl.ds(c, part)])
    first_back = len(copies.all) - 1
    back_home = [None] + [copies.make(att_low.at[k], came.at[k], along(-k)) for k in range(1, SEQ)]
    sum_core = copies.make(part_low.at[rows_at(2, 2), :], core_in, core)
    sum_chip = copies.make(half_low, chip_in, chip)
    second_pair = copies.make(second.at[rows_at(0), :], second.at[rows_at(4), :], pair)
    second_chip = [copies.make(second.at[rows_at(4 * n), :], second.at[rows_at(4 * n + 1), :], chip) for n in range(2)]
    second_core = [copies.make(second.at[rows_at(4 * n, 2), :], second.at[rows_at(4 * n + 2, 2), :], core) for n in range(2)]
    cot_pair = copies.make(cot_ref.at[pl.ds(t * quarter, quarter), :], cots_ref.at[rows_at(4), :], pair)
    cot_chip = copies.make(cots_ref.at[rows_at(4), :], cots_ref.at[rows_at(5), :], chip)
    cot_core = copies.make(cots_ref.at[rows_at(4, 2), :], cots_ref.at[rows_at(6, 2), :], core)

    def norm_piece(n, carry):
        values = tokens[rows_at(n), :].astype(f32)
        center = values - jnp.mean(values, axis=1, keepdims=True)
        frames[0, rows_at(n), :] = (center * lax.rsqrt(jnp.mean(center * center, axis=1, keepdims=True) + NORM_EPS)).astype(bf16)
        return carry

    out_dp[0].start()
    out_step[1].start()
    down_dp[0].start()
    load_tokens[0].wait()
    lax.fori_loop(0, 1, norm_piece, 0)
    token[1].start()
    gain = gain_one_ref[...]
    for h in range(SEQ):
        at = slice(h * HEAD_DIM, (h + 1) * HEAD_DIM)
        for n, ref in enumerate((w_query_ref, w_key_ref, w_value_ref)):
            w_own[h, :, n * HEAD_DIM : (n + 1) * HEAD_DIM] = (ref[:, at].astype(f32) * gain).astype(bf16)
    for k in range(1, SEQ):
        head[k].start()
    w_head[pl.ds(owner(0), part), :] = w_own[z]
    gain = gain_two_ref[...]
    for h in range(2):
        up_own[h] = (w_up_ref[:, h * side : (h + 1) * side].astype(f32) * gain).astype(bf16)
    keep(up_own.at[lax.rem(z, 2)], up_ref.at[pl.ds(owner(0), part), :])
    for copy in load_tokens[1:]:
        copy.wait()
    lax.fori_loop(1, 4, norm_piece, 0)
    keep(frames.at[0], whole_ref.at[0])

    def arrive(copy, *then):
        copies.wait(copy)
        for one in then:
            one.start()

    def project(k):
        def piece(n, carry):
            qkv_ref[k, rows_at(n), :] = jnp.dot(frames[k, rows_at(n), :], w_head[...], preferred_element_type=f32).astype(bf16)
            return carry

        lax.fori_loop(0, 4, piece, 0)

    scale = HEAD_DIM ** (-0.5)

    def query_frame(i):
        at = lax.rem(z - i + SEQ, SEQ)
        query = qkv_ref[at, :, 0:HEAD_DIM]
        peak[...] = jnp.full_like(peak, MASK_FILL)
        total[...] = jnp.zeros_like(total)
        acc[...] = jnp.zeros_like(acc)

        def key_frame(j, inner):
            here = lax.rem(z - j + SEQ, SEQ)
            scores = lax.dot_general(qkv_ref[here, :, HEAD_DIM : 2 * HEAD_DIM], query, (((1,), (1,)), ((), ())), preferred_element_type=f32) * scale + bias_ref[j]
            before = peak[...]
            after = jnp.maximum(before, jnp.max(scores, axis=0, keepdims=True))
            terms = jnp.exp(scores - after)
            fix = jnp.exp(before - after)
            peak[...] = after
            total[...] = total[...] * fix + jnp.sum(terms, axis=0, keepdims=True)
            acc[...] = acc[...] * fix + lax.dot_general(qkv_ref[here, :, 2 * HEAD_DIM :], terms.astype(bf16), (((0,), (0,)), ((), ())), preferred_element_type=f32)
            return inner

        lax.fori_loop(0, i + 1, key_frame, 0)
        outcome = (acc[...] / total[...]).T
        att_ref[at] = outcome
        att_low[at] = outcome.astype(bf16)
        lse_ref[at] = peak[...] + jnp.log(total[...])

        @pl.when(at != 0)
        def _():
            pltpu.make_async_remote_copy(
                src_ref=att_low.at[at], dst_ref=came.at[at], send_sem=send.at[first_back + at], recv_sem=recv.at[first_back + at],
                device_id={"seq": i}, device_id_type=MESH,
            ).start()

    def mix(start):
        def piece(n, carry):
            at = pl.ds(pl.multiple_of(n * 512, 512), 512)
            part_low[pl.ds(start, half), at] = jnp.dot(attended_ref[pl.ds(start, half), :], out_all[:, at], preferred_element_type=f32).astype(bf16)
            return carry

        lax.fori_loop(0, width // 512, piece, 0)

    arrive(out_step[1], out_step[2])
    for k in range(1, SEQ):
        copies.wait(head[k])
    head_dp.start()
    arrive(token[1], token[2], token_chip[1])
    arrive(out_step[2], out_step[3])
    out_dp[1].start()
    out_dp[2].start()
    arrive(token_chip[1], token_core[1])
    copies.wait(head_dp)
    keep(w_head, w_head_ref)
    project(0)
    arrive(out_step[3], out_dp[3], up_step[1])
    up_dp[0].start()
    arrive(token_core[1])
    keep(frames.at[1], whole_ref.at[1])
    project(1)
    arrive(token[2], token[3], token_chip[2])
    arrive(token_chip[2], token_core[2])
    arrive(token_core[2])
    keep(frames.at[2], whole_ref.at[2])
    project(2)
    arrive(up_step[1], up_step[2], up_dp[1])
    arrive(token[3], token_chip[3])
    arrive(up_step[2], up_step[3], up_dp[2])
    arrive(token_chip[3], token_core[3])
    arrive(token_core[3])
    keep(frames.at[3], whole_ref.at[3])
    project(3)
    query_frame(0)
    query_frame(1)
    query_frame(2)
    query_frame(3)
    came[0] = att_low[0]
    arrive(up_step[3], up_dp[3], cot_pair)
    copies.wait(*back_home[1:])
    for h in range(SEQ):
        attended_ref[:, h * HEAD_DIM : (h + 1) * HEAD_DIM] = came[lax.rem(h - z + SEQ, SEQ)]
    own_out.wait()
    copies.wait(*out_dp)
    keep(out_all, out_ref)

    mix(half)
    sum_core.start()
    mix(0)
    arrive(cot_pair, cot_chip, down_step[1])
    copies.wait(sum_core)
    half_low[...] = (part_low[quarter:half, :].astype(f32) + core_in[quarter:half, :].astype(f32)).astype(bf16)
    sum_chip.start()
    arrive(down_step[1], down_step[2], down_dp[1])
    arrive(cot_chip, cot_core)
    copies.wait(sum_chip)
    resid = tokens[first, :].astype(f32) + (part_low[first, :].astype(f32) + core_in[first, :].astype(f32)) + chip_in[...].astype(f32)
    center = resid - jnp.mean(resid, axis=1, keepdims=True)
    rate = lax.rsqrt(jnp.mean(center * center, axis=1, keepdims=True) + NORM_EPS)
    normed = center * rate
    second[first, :] = normed.astype(bf16)
    second_pair.start()
    second_chip[0].start()
    resid_ref[...] = resid
    rate_ref[...] = rate
    normed_ref[...] = normed
    arrive(down_step[2], down_step[3], down_dp[2])
    arrive(second_chip[0], second_core[0])
    arrive(second_pair, second_chip[1])
    arrive(down_step[3], down_dp[3])
    arrive(second_chip[1], second_core[1])
    copies.wait(*second_core)
    keep(second, second_ref)
    copies.finish()
    for copy in kept:
        if not any(copy is done for done in [own_out] + load_tokens):
            copy.wait()


def front(x, w_query, w_key, w_value, w_out, w_up, w_down, gain_one, gain_two, cot, bias):
    rows, width = x.shape
    quarter, half = rows // 4, rows // 2
    part, hidden = w_up.shape
    inner = w_out.shape[0]
    three = 3 * HEAD_DIM
    f32, bf16 = jnp.float32, jnp.bfloat16
    any_, vmem = pl.BlockSpec(memory_space=pl.ANY), pl.BlockSpec(memory_space=pltpu.VMEM)
    shape = jax.ShapeDtypeStruct
    outs = [
        (shape((SEQ, rows, width), bf16), any_),
        (shape((width, three), bf16), any_),
        (shape((SEQ, rows, three), bf16), vmem),
        (shape((SEQ, rows, HEAD_DIM), f32), vmem),
        (shape((SEQ, 1, rows), f32), vmem),
        (shape((rows, inner), bf16), vmem),
        (shape((inner, width), bf16), any_),
        (shape((quarter, width), f32), vmem),
        (shape((quarter, width), f32), vmem),
        (shape((quarter, 1), f32), vmem),
        (shape((2 * rows, width), bf16), any_),
        (shape((width, hidden // 2), bf16), any_),
        (shape((hidden // 2, width), bf16), any_),
        (shape((2 * rows, width), bf16), any_),
    ]
    scratch = [
        ((rows, width), bf16),
        ((SEQ, rows, width), bf16),
        ((SEQ, part, three), bf16),
        ((width, three), bf16),
        ((2, part, hidden // 2), bf16),
        ((inner, width), bf16),
        ((SEQ, rows, HEAD_DIM), bf16),
        ((SEQ, rows, HEAD_DIM), bf16),
        ((rows, width), bf16),
        ((half, width), bf16),
        ((quarter, width), bf16),
        ((quarter, width), bf16),
        ((2 * rows, width), bf16),
        ((1, rows), f32),
        ((1, rows), f32),
        ((HEAD_DIM, rows), f32),
    ]
    count = 3 * 3 + 4 + 3 * 7 + 3 + 2 + 5 + 3
    return pl.pallas_call(
        front_kernel,
        out_shape=[o[0] for o in outs],
        in_specs=[any_] + [vmem] * 3 + [any_, vmem, any_, vmem, vmem, any_, vmem],
        out_specs=[o[1] for o in outs],
        scratch_shapes=[pltpu.VMEM(*one) for one in scratch] + [pltpu.SemaphoreType.DMA((count,)), pltpu.SemaphoreType.DMA((count,)), pltpu.SemaphoreType.DMA((24,))],
        compiler_params=pltpu.CompilerParams(collective_id=0, has_side_effects=True, vmem_limit_bytes=58 * 2**20),
        cost_estimate=pl.CostEstimate(flops=8 * 10**9, bytes_accessed=50 * 10**6, transcendentals=5 * 10**6),
    )(x, w_query, w_key, w_value, w_out, w_up, w_down, gain_one, gain_two, cot, bias)


def back_kernel(
    gd_ref, gd_came_ref, gu_ref, dn_ref, ff_ref, resid_ref, cots_ref, normed_two_ref, rate_two_ref, attended_ref, out_ref, qkv_ref, att_ref, lse_ref, bias_ref, w_head_ref, whole_ref, x_ref,
    down_sum_ref, up_sum_ref, out_sum_ref, arrived_ref, grad_in_ref, result_ref, cross_up_ref, far_down_ref, far_up_ref, dn_core_ref, dn_chip_ref, ff_core_ref, ff_chip_ref, pair_ref, first_core_ref, first_chip_ref, first_ring_ref,
    frames, temp, box_down, box_up, mix, d_head, d_out, dq, dk, dv, delta, d_three, out_send, out_cross, out_far, out_box,
    head_acc, head_low, head_cross, head_sum, held_a, held_b, half_box, pair_box, mid, quart_box, in_box, own_box,
    send, recv, keep_sem, load_sem,
):
    f32, bf16 = jnp.float32, jnp.bfloat16
    dp, z, t, other_dp, chip, core, pair = axes_of()
    rows, width = whole_ref.shape[1:]
    quarter, half = rows // 4, rows // 2
    part = width // (2 * SEQ)
    side = gd_ref.shape[1]
    copies = Copies(send, recv)
    scale = HEAD_DIM ** (-0.5)
    first, later = slice(0, quarter), slice(quarter, half)

    def along(k):
        return {"seq": lax.rem(z + k + SEQ, SEQ)}

    def load(*pairs):
        moves = [pltpu.make_async_copy(src, dst, load_sem.at[i]) for i, (src, dst) in enumerate(pairs)]
        for move in moves:
            move.start()
        for move in moves:
            move.wait()

    def block(side_dp, k):
        return pl.multiple_of((side_dp * SEQ + lax.rem(z - k + SEQ, SEQ)) * part, part)

    def rows_at(n, count=1):
        return pl.ds(n * quarter, count * quarter)

    greet([other_dp, chip, core] + [along(k) for k in range(1, SEQ)])

    def sums(part_ref, core_ref, chip_ref, n):
        to_core = [copies.make(part_ref.at[rows_at(4 * i + 2, 2), :], core_ref.at[i], core) for i in range(2)]
        to_chip = [copies.make(half_box.at[2 * n + i], chip_ref.at[i], chip) for i in range(2)]
        to_pair = copies.make(pair_box.at[n], pair_ref.at[n], pair)
        return to_core, to_chip, to_pair

    dn_core, dn_chip, dn_pair = sums(dn_ref, dn_core_ref, dn_chip_ref, 0)
    ff_core, ff_chip, ff_pair = sums(ff_ref, ff_core_ref, ff_chip_ref, 1)
    mix_chip = copies.make(mix.at[rows_at(0), :], mix.at[rows_at(1), :], chip)
    mix_core = copies.make(mix.at[rows_at(0, 2), :], mix.at[rows_at(2, 2), :], core)
    spread = [None] + [copies.make(d_head.at[lax.rem(z + k, SEQ)], d_out.at[k], along(k)) for k in range(1, SEQ)]
    cross_up = [copies.make(gu_ref.at[pl.ds(block(1 - dp, k), part), :], cross_up_ref.at[k], other_dp) for k in range(SEQ)]
    cross_out = [copies.make(out_send.at[k], out_cross.at[k], other_dp) for k in range(SEQ)]
    far_down = [None] + [copies.make(box_down.at[k - 1], far_down_ref.at[k - 1], along(-k)) for k in range(1, SEQ)]
    far_up = [None] + [copies.make(box_up.at[k - 1], far_up_ref.at[k - 1], along(-k)) for k in range(1, SEQ)]
    far_out = [None] + [copies.make(out_box.at[k - 1], out_far.at[k - 1], along(-k)) for k in range(1, SEQ)]
    first_core = [copies.make(frames.at[k, rows_at(2, 2), :], first_core_ref.at[k], core) for k in range(SEQ)]
    first_chip = [copies.make(quart_box.at[k], first_chip_ref.at[k], chip) for k in range(SEQ)]
    first_ring = [None] + [copies.make(in_box.at[k - 1], first_ring_ref.at[k - 1], along(1)) for k in range(1, SEQ)]
    head_dp = copies.make(head_low.at[1 - dp], head_cross, other_dp)
    head_out = [None] + [copies.make(head_sum.at[lax.rem(z + k, SEQ)], arrived_ref.at[k], along(k)) for k in range(1, SEQ)]
    kept = []

    def publish(n, ref):
        mine = ref.at[pl.ds(t * quarter, quarter), :]
        mate = ref.at[pl.ds(lax.rem(t + 2, 4) * quarter, quarter), :]
        return [copies.make(own_box.at[n], mine, chip), copies.make(own_box.at[n], mine, core), copies.make(mate, mate, core)], (own_box.at[n], mine)

    result_out, result_own = publish(0, result_ref)
    grad_out_copies, grad_own = publish(1, grad_in_ref)

    def keep(src, dst):
        move = pltpu.make_async_copy(src, dst, keep_sem.at[SEQ + len(kept)])
        kept.append(move)
        move.start()

    def half_of(part_ref, core_ref, to_core, to_chip, i, n):
        copies.wait(to_core[i])
        load((part_ref.at[rows_at(4 * i + 1), :], held_a.at[rows_at(0), :]), (core_ref.at[i, rows_at(1), :], held_a.at[rows_at(1), :]))
        half_box[2 * n + i] = (held_a[first, :].astype(f32) + held_a[later, :].astype(f32)).astype(bf16)
        to_chip[i].start()

    def quarter_of(part_ref, core_ref, chip_ref, to_chip, i, *more):
        copies.wait(to_chip[i])
        load(
            (part_ref.at[rows_at(4 * i), :], held_a.at[rows_at(0), :]), (core_ref.at[i, rows_at(0), :], held_a.at[rows_at(1), :]), (chip_ref.at[i], held_b.at[rows_at(0), :]),
            *more,
        )
        return (held_a[first, :].astype(f32) + held_a[later, :].astype(f32)) + held_b[first, :].astype(f32)

    def pair_sum(part_ref, core_ref, chip_ref, to_chip, to_pair, n):
        pair_box[n] = quarter_of(part_ref, core_ref, chip_ref, to_chip, 1).astype(bf16)
        to_pair.start()

    def own_sum(part_ref, core_ref, chip_ref, to_chip, to_pair, n, extra):
        copies.wait(to_pair)
        total = quarter_of(part_ref, core_ref, chip_ref, to_chip, 0, (pair_ref.at[n], held_b.at[rows_at(1), :]), (extra, spare))
        return total + held_b[later, :].astype(f32)

    def scatter(k, own_ref, cross_at, crossing, box, far):
        if crossing is not None:
            copies.wait(crossing)
        load((cross_at, temp.at[0]), (own_ref.at[pl.ds(block(dp, k), part), :], temp.at[1]))
        box[k - 1] = (temp[0].astype(f32) + temp[1].astype(f32)).astype(bf16)
        far[k].start()

    def down_block(k):
        return gd_came_ref.at[pl.ds(pl.multiple_of(lax.rem(z - k + SEQ, SEQ) * part, part), part), :]

    def scatter_down(k):
        scatter(k, gd_ref, down_block(k), None, box_down, far_down)

    def scatter_up(k):
        scatter(k, gu_ref, cross_up_ref.at[k], cross_up[k], box_up, far_up)

    same = pl.multiple_of(lax.rem(z, 2) * side, side)
    unlike = pl.multiple_of((1 - lax.rem(z, 2)) * side, side)

    def total_of(own_ref, cross_at, far_ref, far, crossing, store):
        copies.wait(*far[1:])
        if crossing is not None:
            copies.wait(crossing)
        load((cross_at, temp.at[0]), (own_ref.at[pl.ds(block(dp, 0), part), :], temp.at[1]), (far_ref.at[1], temp.at[2]))
        store(same, lambda at: (temp[0, :, at].astype(f32) + temp[1, :, at].astype(f32)) + temp[2, :, at].astype(f32))
        load((far_ref.at[0], temp.at[0]), (far_ref.at[2], temp.at[1]))
        store(unlike, lambda at: temp[0, :, at].astype(f32) + temp[1, :, at].astype(f32))

    def store_turned(base, value):
        for n in range(side // 256):
            down_sum_ref[pl.ds(base + n * 256, 256), :] = value(slice(n * 256, (n + 1) * 256)).T

    def store_plain(base, value):
        up_sum_ref[:, pl.ds(base, side)] = value(slice(0, side))

    def out_block(start):
        return lax.dot_general(attended_ref[...], mix[:, pl.ds(start, part)], (((0,), (0,)), ((), ())), preferred_element_type=f32)

    def scatter_out(k):
        copies.wait(cross_out[k])
        out_box[k - 1] = (out_block(block(dp, k)) + out_cross[k].astype(f32)).astype(bf16)
        far_out[k].start()

    for copy in (dn_core[1], dn_core[0], cross_up[1], cross_up[2]):
        copy.start()
    spare = head_acc.at[pl.ds(0, quarter), :]
    scatter_down(1)
    half_of(dn_ref, dn_core_ref, dn_core, dn_chip, 1, 0)
    load(*[(out_ref.at[pl.ds(h * HEAD_DIM, HEAD_DIM), :], quart_box.at[h, pl.ds(0, HEAD_DIM), :]) for h in range(SEQ)])
    scatter_down(2)
    fetch = [pltpu.make_async_copy(whole_ref.at[k], frames.at[k], keep_sem.at[k]) for k in range(SEQ)]
    for move in fetch:
        move.start()
    copies.wait(dn_chip[1])
    half_of(dn_ref, dn_core_ref, dn_core, dn_chip, 0, 0)
    pair_sum(dn_ref, dn_core_ref, dn_chip_ref, dn_chip, dn_pair, 0)
    grad = own_sum(dn_ref, dn_core_ref, dn_chip_ref, dn_chip, dn_pair, 0, normed_two_ref)
    normed = spare[...]
    grad = rate_two_ref[...] * (grad - jnp.mean(grad, axis=1, keepdims=True) - normed * jnp.mean(grad * normed, axis=1, keepdims=True))
    load((cots_ref.at[rows_at(0), :], held_a.at[rows_at(0), :]))
    grad = held_a[first, :].astype(f32) + grad
    mid[...] = grad
    mix[first, :] = grad.astype(bf16)
    mix_chip.start()
    scatter_down(3)
    copies.wait(cross_up[1], cross_up[2])
    cross_up[3].start()
    cross_up[0].start()
    copies.wait(mix_chip)
    mix_core.start()
    copies.wait(mix_core)

    for n in range(4):
        at = slice(n * quarter, (n + 1) * quarter)
        for h in range(SEQ):
            d_head[h, at, :] = lax.dot_general(mix[at, :], quart_box[h, 0:HEAD_DIM, :], (((1,), (1,)), ((), ())), preferred_element_type=f32).astype(bf16)
    for k in range(1, SEQ):
        spread[k].start()
    ff_core[1].start()
    ff_core[0].start()
    d_out[0] = d_head[z]
    for k in (1, 2, 3, 0):
        out_send[k] = out_block(block(1 - dp, k)).astype(bf16)
        cross_out[k].start()
    half_of(ff_ref, ff_core_ref, ff_core, ff_chip, 1, 1)
    copies.wait(*spread[1:])
    dq[...] = jnp.zeros_like(dq)
    for f in range(SEQ):
        delta[f] = jnp.sum((d_out[f].astype(f32) * att_ref[f]).T, axis=0, keepdims=True)

    def key_frame(j):
        here = lax.rem(z - j + SEQ, SEQ)
        dk[...] = jnp.zeros_like(dk)
        dv[...] = jnp.zeros_like(dv)

        def query_frame(i, inner_):
            at = lax.rem(z - i + SEQ, SEQ)
            query, key, value = qkv_ref[at, :, :HEAD_DIM], qkv_ref[here, :, HEAD_DIM : 2 * HEAD_DIM], qkv_ref[here, :, 2 * HEAD_DIM :]
            grad_out = d_out[at]
            scores = lax.dot_general(key, query, (((1,), (1,)), ((), ())), preferred_element_type=f32) * scale + bias_ref[j]
            prob = jnp.exp(scores - lse_ref[at])
            d_prob = lax.dot_general(value, grad_out, (((1,), (1,)), ((), ())), preferred_element_type=f32)
            d_scores = (prob * (d_prob - delta[at])).astype(bf16)
            dv[...] += jnp.dot(prob.astype(bf16), grad_out, preferred_element_type=f32)
            dk[...] += jnp.dot(d_scores, query, preferred_element_type=f32)
            dq[at] += lax.dot_general(key, d_scores, (((0,), (0,)), ((), ())), preferred_element_type=f32)
            return inner_

        lax.fori_loop(j, SEQ, query_frame, 0)
        d_three[here, :, HEAD_DIM : 2 * HEAD_DIM] = (dk[...] * scale).astype(bf16)
        d_three[here, :, 2 * HEAD_DIM :] = dv[...].astype(bf16)

    key_frame(0)
    scatter_up(1)
    key_frame(1)
    half_of(ff_ref, ff_core_ref, ff_core, ff_chip, 0, 1)
    scatter_up(2)
    key_frame(2)
    key_frame(3)
    for f in range(SEQ):
        d_three[f, :, :HEAD_DIM] = (dq[f] * scale).T.astype(bf16)

    def project_back(k):
        fetch[k].wait()

        def piece(n, carry):
            at = pl.ds(pl.multiple_of(n * 512, 512), 512)
            term = lax.dot_general(d_three[k], frames[k, :, at], (((0,), (0,)), ((), ())), preferred_element_type=f32)
            head_acc[:, at] = term if k == 1 else head_acc[:, at] + term
            return carry

        lax.fori_loop(0, width // 512, piece, 0)

        def back_piece(n, carry):
            at = pl.ds(pl.multiple_of(n * 512, 512), 512)
            frames[k, :, at] = lax.dot_general(d_three[k], w_head_ref[at, :], (((1,), (1,)), ((), ())), preferred_element_type=f32).astype(bf16)
            return carry

        lax.fori_loop(0, width // 512, back_piece, 0)
        first_core[k].start()

    def half_sum(k):
        copies.wait(first_core[k])
        load((first_core_ref.at[k], held_a))
        quart_box[k] = (frames[k, later, :].astype(f32) + held_a[later, :].astype(f32)).astype(bf16)
        first_chip[k].start()
        frames[k, first, :] = (frames[k, first, :].astype(f32) + held_a[first, :].astype(f32)).astype(bf16)

    def quarter_sum(k):
        copies.wait(first_chip[k])
        pairs = [(first_chip_ref.at[k], held_a.at[rows_at(0), :])]
        if k != 1:
            before = (k - 1) % SEQ
            copies.wait(first_ring[before])
            pairs.append((first_ring_ref.at[before - 1], held_a.at[rows_at(1), :]))
        load(*pairs)
        sum_ = frames[k, first, :].astype(f32) + held_a[first, :].astype(f32)
        if k != 1:
            sum_ = sum_ + held_a[later, :].astype(f32)
        return sum_

    project_back(1)
    project_back(2)
    half_sum(1)
    project_back(3)
    project_back(0)
    for n in range(2):
        head_low[n] = head_acc[:, n * (width // 2) : (n + 1) * (width // 2)].astype(bf16)
    head_dp.start()
    scatter_up(3)
    copies.wait(first_chip[1])
    half_sum(2)
    in_box[0] = quarter_sum(1).astype(bf16)
    first_ring[1].start()
    total_of(gd_ref, down_block(0), far_down_ref, far_down, None, store_turned)
    scatter_out(1)
    copies.wait(first_chip[2])
    half_sum(3)
    in_box[1] = quarter_sum(2).astype(bf16)
    first_ring[2].start()
    copies.wait(head_dp)
    for j in range(SEQ):
        at = slice(j * part, (j + 1) * part)
        head_sum[j] = (head_low[dp, :, at].astype(f32) + head_cross[:, at].astype(f32)).astype(bf16)
    for k in range(1, SEQ):
        head_out[k].start()
    keep(head_sum.at[z], arrived_ref.at[0])
    scatter_out(2)
    copies.wait(first_chip[3])
    half_sum(0)
    in_box[2] = quarter_sum(3).astype(bf16)
    first_ring[3].start()
    scatter_out(3)
    pair_sum(ff_ref, ff_core_ref, ff_chip_ref, ff_chip, ff_pair, 1)
    total_of(gu_ref, cross_up_ref.at[0], far_up_ref, far_up, cross_up[0], store_plain)
    grad = quarter_sum(0)
    load((x_ref.at[pl.ds(t * quarter, quarter), :], held_a.at[rows_at(0), :]))
    center = held_a[first, :].astype(f32)
    center = center - jnp.mean(center, axis=1, keepdims=True)
    rate = lax.rsqrt(jnp.mean(center * center, axis=1, keepdims=True) + NORM_EPS)
    normed = center * rate
    grad = rate * (grad - jnp.mean(grad, axis=1, keepdims=True) - normed * jnp.mean(grad * normed, axis=1, keepdims=True))
    own_box[1] = (mid[...] + grad).astype(bf16)
    grad_out_copies[0].start()
    grad_out_copies[1].start()
    keep(*grad_own)
    total = own_sum(ff_ref, ff_core_ref, ff_chip_ref, ff_chip, ff_pair, 1, resid_ref)
    own_box[0] = (spare[...] + total).astype(bf16)
    result_out[0].start()
    result_out[1].start()
    keep(*result_own)
    copies.wait(cross_out[0], *far_out[1:])
    sum_ = out_block(block(dp, 0)) + out_cross[0].astype(f32)
    for k in range(1, SEQ):
        sum_ = sum_ + out_far[k - 1].astype(f32)
    out_sum_ref[...] = sum_
    copies.wait(grad_out_copies[0])
    grad_out_copies[2].start()
    copies.wait(result_out[0])
    result_out[2].start()
    copies.finish()
    for move in kept:
        move.wait()


def back(gd, gd_came, gu, dn, ff, resid, cots, normed_two, rate_two, attended, out_rel, qkv, att, lse, bias, w_head, whole, x):
    rows, width = x.shape
    quarter, half = rows // 4, rows // 2
    part = width // (2 * SEQ)
    inner = attended.shape[1]
    side = gd.shape[1]
    three = 3 * HEAD_DIM
    f32, bf16 = jnp.float32, jnp.bfloat16
    any_, vmem = pl.BlockSpec(memory_space=pl.ANY), pl.BlockSpec(memory_space=pltpu.VMEM)
    shape = jax.ShapeDtypeStruct
    outs = [
        (shape((2 * side, part), f32), vmem),
        (shape((part, 2 * side), f32), vmem),
        (shape((inner, part), f32), vmem),
        (shape((SEQ, three, part), bf16), any_),
        (shape((rows, width), bf16), any_),
        (shape((rows, width), bf16), any_),
        (shape((SEQ, part, side), bf16), any_),
        (shape((SEQ - 1, part, side), bf16), any_),
        (shape((SEQ - 1, part, side), bf16), any_),
        (shape((2, half, width), bf16), any_),
        (shape((2, quarter, width), bf16), any_),
        (shape((2, half, width), bf16), any_),
        (shape((2, quarter, width), bf16), any_),
        (shape((2, quarter, width), bf16), any_),
        (shape((SEQ, half, width), bf16), any_),
        (shape((SEQ, quarter, width), bf16), any_),
        (shape((SEQ - 1, quarter, width), bf16), any_),
    ]
    count = 10 + 2 + 3 + 4 + 4 + 9 + 8 + 3 + 4 + 6
    scratch = [
        ((SEQ, rows, width), bf16),
        ((3, part, side), bf16),
        ((SEQ - 1, part, side), bf16),
        ((SEQ - 1, part, side), bf16),
        ((rows, width), bf16),
        ((SEQ, rows, HEAD_DIM), bf16),
        ((SEQ, rows, HEAD_DIM), bf16),
        ((SEQ, HEAD_DIM, rows), f32),
        ((rows, HEAD_DIM), f32),
        ((rows, HEAD_DIM), f32),
        ((SEQ, 1, rows), f32),
        ((SEQ, rows, three), bf16),
        ((SEQ, inner, part), bf16),
        ((SEQ, inner, part), bf16),
        ((SEQ - 1, inner, part), bf16),
        ((SEQ - 1, inner, part), bf16),
        ((three, width), f32),
        ((2, three, width // 2), bf16),
        ((three, width // 2), bf16),
        ((SEQ, three, part), bf16),
        ((half, width), bf16),
        ((half, width), bf16),
        ((4, quarter, width), bf16),
        ((2, quarter, width), bf16),
        ((quarter, width), f32),
        ((SEQ, quarter, width), bf16),
        ((SEQ - 1, quarter, width), bf16),
        ((2, quarter, width), bf16),
    ]
    return pl.pallas_call(
        back_kernel,
        out_shape=[o[0] for o in outs],
        in_specs=[any_] * 8 + [vmem, vmem, any_] + [vmem] * 5 + [any_] * 2,
        out_specs=[o[1] for o in outs],
        scratch_shapes=[pltpu.VMEM(*one) for one in scratch]
        + [pltpu.SemaphoreType.DMA((count,)), pltpu.SemaphoreType.DMA((count,)), pltpu.SemaphoreType.DMA((SEQ + 3,)), pltpu.SemaphoreType.DMA((6,))],
        compiler_params=pltpu.CompilerParams(collective_id=1, has_side_effects=True, vmem_limit_bytes=62 * 2**20),
        cost_estimate=pl.CostEstimate(flops=20 * 10**9, bytes_accessed=60 * 10**6, transcendentals=5 * 10**6),
    )(gd, gd_came, gu, dn, ff, resid, cots, normed_two, rate_two, attended, out_rel, qkv, att, lse, bias, w_head, whole, x)[:6]


def swap_dp(values):
    return lax.ppermute(values, "dp", [(0, 1), (1, 0)])


def swap_chip(values):
    return lax.ppermute(values, "tensor", [(i, i ^ 2) for i in range(4)])


def swap_core(values):
    return lax.ppermute(values, "tensor", [(i, i ^ 1) for i in range(4)])


def dyn(stack, index):
    return lax.dynamic_index_in_dim(stack, index, 0, keepdims=False)


def mm(left, right, dims=((1,), (0,)), out=jnp.bfloat16):
    return lax.dot_general(left, right, (dims, ((), ())), preferred_element_type=jnp.float32).astype(out)


def local_fast(inputs, first_gain, w_query, w_key, w_value, w_out, second_gain, w_up, w_down, frame_mask, cotangent):
    dp, z = lax.axis_index("dp"), lax.axis_index("seq")
    rows, width = inputs.shape[1:]
    heads = w_query.shape[1] // HEAD_DIM
    f32, bf16 = jnp.float32, jnp.bfloat16
    gain_one, gain_two = first_gain.astype(f32)[:, None], second_gain.astype(f32)[:, None]
    bias = jnp.broadcast_to(jnp.where(frame_mask[0] == 1, 0.0, MASK_FILL).astype(f32)[:, None, None], (SEQ, 1, rows))
    whole, w_head, qkv, attended_f, lse, attended, out_all, resid_mid, normed_two, rate_two, second_in, up_side, down_side, cots = front(
        inputs[0], w_query, w_key, w_value, w_out, w_up, w_down, gain_one, gain_two, cotangent[0], bias
    )
    up_pre = mm(second_in, up_side, out=f32)
    cdf = 0.5 * (1.0 + lax.erf(up_pre * (0.5**0.5)))
    up_act = (up_pre * cdf).astype(bf16)
    slope = cdf + up_pre * jnp.exp(-0.5 * up_pre * up_pre) * ((2.0 * jnp.pi) ** -0.5)
    grad_down = mm(cots, up_act, ((0,), (0,)))
    down_came = swap_dp(lax.dynamic_slice_in_dim(grad_down, (1 - dp) * (width // 2), width // 2, 0))
    d_up = (mm(cots, down_side, ((1,), (1,)), f32) * slope).astype(bf16)
    grad_up = mm(second_in, d_up, ((0,), (0,)))
    d_normed_two = mm(d_up, up_side, ((1,), (1,)))
    ff_part = mm(up_act, down_side)
    down_sum, up_raw, out_sum, arrived, grad_in, result = back(
        grad_down, down_came, grad_up, d_normed_two, ff_part, resid_mid, cots, normed_two, rate_two, attended, out_all, qkv, attended_f, lse, bias, w_head, whole, inputs[0]
    )
    by_head = [dyn(arrived, lax.rem(z - h + SEQ, SEQ)).astype(f32).T for h in range(heads)]
    raw = [jnp.concatenate([one[:, n * HEAD_DIM : (n + 1) * HEAD_DIM] for one in by_head], axis=1) for n in range(3)]
    d_gain_one = sum(jnp.sum(weight.astype(f32) * one, axis=1) for weight, one in zip((w_query, w_key, w_value), raw))
    d_gain_two = jnp.sum(w_up.astype(f32) * up_raw, axis=1)
    gains = jnp.stack([d_gain_one, d_gain_two])
    gains = gains + swap_core(gains)
    gains = gains + swap_chip(gains)
    return (result[None], grad_in[None], gains[0], raw[0] * gain_one, raw[1] * gain_one, raw[2] * gain_one, out_sum, gains[1], up_raw * gain_two, down_sum)


SEQ = 4


def solution(mesh):
    placed = (
        P("dp", "seq", None),
        P(("dp", "seq")),
        P(("dp", "seq"), "tensor"),
        P(("dp", "seq"), "tensor"),
        P(("dp", "seq"), "tensor"),
        P("tensor", ("dp", "seq")),
        P(("dp", "seq")),
        P(("dp", "seq"), "tensor"),
        P("tensor", ("dp", "seq")),
        P("dp", None),
        P("dp", "seq", None),
    )
    sizes = dict(mesh.shape)
    spread = sizes == {"dp": 2, "seq": SEQ, "tensor": 4}
    return jax.shard_map(
        local_fast if spread else local,
        mesh=mesh,
        in_specs=placed,
        out_specs=(
            P("dp", "seq", None),
            P("dp", "seq", None),
            P(("dp", "seq")),
            P(("dp", "seq"), "tensor"),
            P(("dp", "seq"), "tensor"),
            P(("dp", "seq"), "tensor"),
            P("tensor", ("dp", "seq")),
            P(("dp", "seq")),
            P(("dp", "seq"), "tensor"),
            P("tensor", ("dp", "seq")),
        ),
        check_vma=False,
    )
```

```python
import functools

import jax
import jax.numpy as jnp
from jax import lax
from jax.experimental import pallas as pl
from jax.experimental.pallas import tpu as pltpu
from jax.sharding import PartitionSpec as P

HEAD_DIM = 128
FRAME_TOK = 640


NORM_EPS = 1e-05
MASK_FILL = -1e30
MESH = pl.DeviceIdType.MESH


def norm_rows(values):
    center = values - jnp.mean(values, axis=-1, keepdims=True)
    spread = jnp.mean(center * center, axis=-1, keepdims=True)
    return center * lax.rsqrt(spread + NORM_EPS)


def gelu_exact(values):
    return jax.nn.gelu(values, approximate=False)


def heads_total(values):
    return lax.psum(values.astype(jnp.bfloat16), "tensor").astype(jnp.float32)


def local(
    inputs,
    first_gain,
    w_query,
    w_key,
    w_value,
    w_out,
    second_gain,
    w_up,
    w_down,
    frame_mask,
    cotangent,
):
    seq_pos = lax.axis_index("seq")
    gain_one, query_w, key_w, value_w, gain_two, up_w = (
        lax.all_gather(first_gain, ("dp", "seq"), axis=0, tiled=True),
        lax.all_gather(w_query, ("dp", "seq"), axis=0, tiled=True),
        lax.all_gather(w_key, ("dp", "seq"), axis=0, tiled=True),
        lax.all_gather(w_value, ("dp", "seq"), axis=0, tiled=True),
        lax.all_gather(second_gain, ("dp", "seq"), axis=0, tiled=True),
        lax.all_gather(w_up, ("dp", "seq"), axis=0, tiled=True),
    )
    out_w, down_w = (
        lax.all_gather(w_out, ("dp", "seq"), axis=1, tiled=True),
        lax.all_gather(w_down, ("dp", "seq"), axis=1, tiled=True),
    )
    tok_rows = inputs.shape[1]
    local_inner = query_w.shape[1]
    local_heads = local_inner // HEAD_DIM
    frames_dev = tok_rows // FRAME_TOK
    score_scale = HEAD_DIM ** (-0.5)
    clip_valid = frame_mask[0]
    frame_count = clip_valid.shape[0]
    resid_in = inputs[0].astype(jnp.float32)
    dout_rows = cotangent[0]
    row_frame = seq_pos * frames_dev + jnp.arange(tok_rows, dtype=jnp.int32) // FRAME_TOK
    frame_limit = (seq_pos + 1) * frames_dev
    normed_one = norm_rows(resid_in)
    first_in = (normed_one * gain_one.astype(jnp.float32)).astype(jnp.bfloat16)
    query = jnp.dot(first_in, query_w, preferred_element_type=jnp.float32).astype(jnp.bfloat16)
    key_local = jnp.dot(first_in, key_w, preferred_element_type=jnp.float32).astype(jnp.bfloat16)
    value_local = jnp.dot(first_in, value_w, preferred_element_type=jnp.float32).astype(
        jnp.bfloat16
    )
    key_all, value_all = (
        lax.all_gather(key_local, "seq", axis=0, tiled=True),
        lax.all_gather(value_local, "seq", axis=0, tiled=True),
    )
    query_heads = query.reshape(tok_rows, local_heads, HEAD_DIM)
    key_frames = key_all.reshape(frame_count, FRAME_TOK, local_heads, HEAD_DIM)
    value_frames = value_all.reshape(frame_count, FRAME_TOK, local_heads, HEAD_DIM)

    def frame_scores(frame_idx):
        key_block = lax.dynamic_index_in_dim(key_frames, frame_idx, 0, keepdims=False)
        value_block = lax.dynamic_index_in_dim(value_frames, frame_idx, 0, keepdims=False)
        scores = (
            jnp.einsum("qhd,khd->hqk", query_heads, key_block, preferred_element_type=jnp.float32)
            * score_scale
        )
        frame_ok = lax.dynamic_index_in_dim(clip_valid, frame_idx, 0, keepdims=False) == 1
        allowed = ((frame_idx <= row_frame) & frame_ok)[None, :, None]
        return (scores, allowed, key_block, value_block)

    def stats_step(frame_idx, running):
        row_max, row_sum = running
        scores, allowed, key_block, value_block = frame_scores(frame_idx)
        masked = jnp.where(allowed, scores, MASK_FILL)
        new_max = jnp.maximum(row_max, jnp.max(masked, axis=2))
        exp_terms = jnp.where(allowed, jnp.exp(masked - new_max[:, :, None]), 0.0)
        return (new_max, row_sum * jnp.exp(row_max - new_max) + jnp.sum(exp_terms, axis=2))

    start_stats = (
        jnp.full((local_heads, tok_rows), MASK_FILL, jnp.float32),
        jnp.zeros((local_heads, tok_rows), jnp.float32),
    )
    row_max, row_sum = lax.fori_loop(0, frame_limit, stats_step, start_stats)

    def soft_weights(scores, allowed):
        return jnp.where(allowed, jnp.exp(scores - row_max[:, :, None]) / row_sum[:, :, None], 0.0)

    def output_step(frame_idx, running):
        scores, allowed, key_block, value_block = frame_scores(frame_idx)
        attn_prob = soft_weights(scores, allowed).astype(jnp.bfloat16)
        return running + jnp.einsum(
            "hqk,khd->qhd", attn_prob, value_block, preferred_element_type=jnp.float32
        )

    attended = lax.fori_loop(
        0, frame_limit, output_step, jnp.zeros((tok_rows, local_heads, HEAD_DIM), jnp.float32)
    )
    attended_low = attended.reshape(tok_rows, local_inner).astype(jnp.bfloat16)
    resid_mid = resid_in + heads_total(
        jnp.dot(attended_low, out_w, preferred_element_type=jnp.float32)
    )
    normed_two = norm_rows(resid_mid)
    second_in = (normed_two * gain_two.astype(jnp.float32)).astype(jnp.bfloat16)
    up_pre = jnp.dot(second_in, up_w, preferred_element_type=jnp.float32)
    up_act = gelu_exact(up_pre).astype(jnp.bfloat16)
    resid_out = resid_mid + heads_total(jnp.dot(up_act, down_w, preferred_element_type=jnp.float32))
    result = resid_out.astype(jnp.bfloat16)[None]
    grad_down = jnp.einsum("tf,td->fd", up_act, dout_rows, preferred_element_type=jnp.float32)
    d_act = jnp.einsum("td,fd->tf", dout_rows, down_w, preferred_element_type=jnp.float32)
    gelu_pull = jax.vjp(gelu_exact, up_pre)[1]
    d_up_pre = gelu_pull(d_act)[0].astype(jnp.bfloat16)
    grad_up = jnp.einsum("td,tf->df", second_in, d_up_pre, preferred_element_type=jnp.float32)
    d_second = heads_total(
        jnp.einsum("tf,df->td", d_up_pre, up_w, preferred_element_type=jnp.float32)
    )
    grad_second_gain = jnp.sum(d_second * normed_two, axis=0)
    norm_pull_two = jax.vjp(norm_rows, resid_mid)[1]
    d_mid = (
        dout_rows.astype(jnp.float32) + norm_pull_two(d_second * gain_two.astype(jnp.float32))[0]
    )
    d_mix = d_mid.astype(jnp.bfloat16)
    grad_out = jnp.einsum("ti,td->id", attended_low, d_mix, preferred_element_type=jnp.float32)
    d_attended = jnp.einsum("td,id->ti", d_mix, out_w, preferred_element_type=jnp.float32).astype(
        jnp.bfloat16
    )
    dout_heads = d_attended.reshape(tok_rows, local_heads, HEAD_DIM)
    row_delta = jnp.sum(dout_heads.astype(jnp.float32) * attended, axis=2).T

    def query_step(frame_idx, running):
        scores, allowed, key_block, value_block = frame_scores(frame_idx)
        attn_prob = soft_weights(scores, allowed)
        d_prob = jnp.einsum(
            "qhd,khd->hqk", dout_heads, value_block, preferred_element_type=jnp.float32
        )
        d_scores = (attn_prob * (d_prob - row_delta[:, :, None])).astype(jnp.bfloat16)
        return running + jnp.einsum(
            "hqk,khd->qhd", d_scores, key_block, preferred_element_type=jnp.float32
        )

    query_sum = lax.fori_loop(
        0, frame_limit, query_step, jnp.zeros((tok_rows, local_heads, HEAD_DIM), jnp.float32)
    )
    d_query = (query_sum * score_scale).reshape(tok_rows, local_inner).astype(jnp.bfloat16)

    def one_frame(frame_step):
        scores, allowed, key_block, value_block = frame_scores(frame_step)
        attn_prob = soft_weights(scores, allowed)
        d_prob = jnp.einsum(
            "qhd,khd->hqk", dout_heads, value_block, preferred_element_type=jnp.float32
        )
        d_scores = (attn_prob * (d_prob - row_delta[:, :, None])).astype(jnp.bfloat16)
        key_term = (
            jnp.einsum("hqk,qhd->khd", d_scores, query_heads, preferred_element_type=jnp.float32)
            * score_scale
        )
        value_term = jnp.einsum(
            "hqk,qhd->khd",
            attn_prob.astype(jnp.bfloat16),
            dout_heads,
            preferred_element_type=jnp.float32,
        )
        return jnp.concatenate(
            [key_term.reshape(FRAME_TOK, local_inner), value_term.reshape(FRAME_TOK, local_inner)],
            axis=1,
        )

    blocks = lax.map(
        one_frame, jnp.arange(tok_rows * lax.axis_size("seq") // FRAME_TOK, dtype=jnp.int32)
    )
    kv_grad = lax.psum_scatter(
        blocks.reshape(tok_rows * lax.axis_size("seq"), 2 * local_inner).astype(jnp.bfloat16),
        "seq",
        scatter_dimension=0,
        tiled=True,
    ).astype(jnp.float32)
    d_key = kv_grad[:, :local_inner].astype(jnp.bfloat16)
    d_value = kv_grad[:, local_inner:].astype(jnp.bfloat16)
    grad_query = jnp.einsum("td,ti->di", first_in, d_query, preferred_element_type=jnp.float32)
    grad_key = jnp.einsum("td,ti->di", first_in, d_key, preferred_element_type=jnp.float32)
    grad_value = jnp.einsum("td,ti->di", first_in, d_value, preferred_element_type=jnp.float32)
    first_local = jnp.einsum("ti,di->td", d_query, query_w, preferred_element_type=jnp.float32)
    first_local = first_local + jnp.einsum(
        "ti,di->td", d_key, key_w, preferred_element_type=jnp.float32
    )
    first_local = first_local + jnp.einsum(
        "ti,di->td", d_value, value_w, preferred_element_type=jnp.float32
    )
    d_first = heads_total(first_local)
    grad_first_gain = jnp.sum(d_first * normed_one, axis=0)
    norm_pull_one = jax.vjp(norm_rows, resid_in)[1]
    grad_inputs = (d_mid + norm_pull_one(d_first * gain_one.astype(jnp.float32))[0]).astype(
        jnp.bfloat16
    )[None]
    summed_in = (
        lax.psum_scatter(
            grad_first_gain.astype(jnp.bfloat16), ("dp", "seq"), scatter_dimension=0, tiled=True
        ).astype(jnp.float32),
        lax.psum_scatter(
            grad_query.astype(jnp.bfloat16), ("dp", "seq"), scatter_dimension=0, tiled=True
        ).astype(jnp.float32),
        lax.psum_scatter(
            grad_key.astype(jnp.bfloat16), ("dp", "seq"), scatter_dimension=0, tiled=True
        ).astype(jnp.float32),
        lax.psum_scatter(
            grad_value.astype(jnp.bfloat16), ("dp", "seq"), scatter_dimension=0, tiled=True
        ).astype(jnp.float32),
        lax.psum_scatter(
            grad_second_gain.astype(jnp.bfloat16), ("dp", "seq"), scatter_dimension=0, tiled=True
        ).astype(jnp.float32),
        lax.psum_scatter(
            grad_up.astype(jnp.bfloat16), ("dp", "seq"), scatter_dimension=0, tiled=True
        ).astype(jnp.float32),
    )
    summed_out = (
        lax.psum_scatter(
            grad_out.astype(jnp.bfloat16), ("dp", "seq"), scatter_dimension=1, tiled=True
        ).astype(jnp.float32),
        lax.psum_scatter(
            grad_down.astype(jnp.bfloat16), ("dp", "seq"), scatter_dimension=1, tiled=True
        ).astype(jnp.float32),
    )
    return (
        result,
        grad_inputs,
        summed_in[0],
        summed_in[1],
        summed_in[2],
        summed_in[3],
        summed_out[0],
        summed_in[4],
        summed_in[5],
        summed_out[1],
    )


def axes_of():
    dp, z, t = lax.axis_index("dp"), lax.axis_index("seq"), lax.axis_index("tensor")
    other_dp, chip, core = {"dp": 1 - dp}, {"tensor": lax.rem(t + 2, 4)}, {"tensor": t + 1 - 2 * lax.rem(t, 2)}
    pair = {"seq": z + 1 - 2 * lax.rem(z, 2)}
    return dp, z, t, other_dp, chip, core, pair


class Copies:
    def __init__(self, send, recv):
        self.send, self.recv, self.all, self.came, self.left = send, recv, [], [], []

    def make(self, src, dst, device):
        i = len(self.all)
        copy = pltpu.make_async_remote_copy(src_ref=src, dst_ref=dst, send_sem=self.send.at[i], recv_sem=self.recv.at[i], device_id=device, device_id_type=MESH)
        self.all.append(copy)
        return copy

    def wait(self, *copies):
        for copy in copies:
            if not any(copy is done for done in self.came):
                copy.wait_recv()
                self.came.append(copy)

    def flush(self, *copies):
        for copy in copies:
            if not any(copy is done for done in self.left):
                copy.wait_send()
                self.left.append(copy)

    def finish(self):
        self.wait(*self.all)
        self.flush(*self.all)


def greet(peers):
    barrier = pltpu.get_barrier_semaphore()
    for peer in peers:
        pl.semaphore_signal(barrier, inc=1, device_id=peer, device_id_type=MESH)
    pl.semaphore_wait(barrier, len(peers))


def front_kernel(
    x_ref, w_query_ref, w_key_ref, w_value_ref, w_out_ref, w_up_ref, w_down_ref, gain_one_ref, gain_two_ref, cot_ref, bias_ref,
    whole_ref, w_head_ref, qkv_ref, att_ref, lse_ref, attended_ref, out_ref, resid_ref, normed_ref, rate_ref, second_ref, up_ref, down_ref, cots_ref,
    tokens, frames, w_own, w_head, up_own, out_all, att_low, came, part_low, core_in, half_low, chip_in, second, peak, total, acc, send, recv, local_sem,
):
    f32, bf16 = jnp.float32, jnp.bfloat16
    dp, z, t, other_dp, chip, core, pair = axes_of()
    rows, width = x_ref.shape
    quarter, half = rows // 4, rows // 2
    part, hidden = w_up_ref.shape
    side = hidden // 2
    copies = Copies(send, recv)
    kept = []

    def keep(src, dst):
        copy = pltpu.make_async_copy(src, dst, local_sem.at[len(kept)])
        kept.append(copy)
        copy.start()
        return copy

    def along(k):
        return {"seq": lax.rem(z + k + SEQ, SEQ)}

    def owner(k):
        return (dp * SEQ + lax.rem(z - k + SEQ, SEQ)) * part

    mate = t + 1 - 2 * lax.rem(t, 2)
    quarters = [t, lax.rem(t + 2, 4), mate, lax.rem(mate + 2, 4)]
    load_tokens = [keep(x_ref.at[pl.ds(quarters[n] * quarter, quarter), :], tokens.at[pl.ds(n * quarter, quarter), :]) for n in range(4)]
    keep_cots = [keep(cot_ref.at[pl.ds(quarters[n] * quarter, quarter), :], cots_ref.at[pl.ds(n * quarter, quarter), :]) for n in range(4)]
    own_out = keep(w_out_ref, out_all.at[:, pl.ds(owner(0), part)])
    keep(w_down_ref.at[pl.ds(lax.rem(z, 2) * side, side), :], down_ref.at[:, pl.ds(owner(0), part)])
    greet([other_dp, chip, core] + [along(k) for k in range(1, SEQ)])

    first = slice(0, quarter)

    def rows_at(n, count=1):
        return pl.ds(n * quarter, count * quarter)

    token = [None] + [copies.make(frames.at[k - 1, rows_at(0), :], frames.at[k, rows_at(0), :], along(1)) for k in range(1, SEQ)]
    token_chip = [None] + [copies.make(frames.at[k, rows_at(0), :], frames.at[k, rows_at(1), :], chip) for k in range(1, SEQ)]
    token_core = [None] + [copies.make(frames.at[k, rows_at(0, 2), :], frames.at[k, rows_at(2, 2), :], core) for k in range(1, SEQ)]
    head = [None] + [copies.make(w_own.at[lax.rem(z + k, SEQ)], w_head.at[pl.ds(owner(0), part), :], along(k)) for k in range(1, SEQ)]
    mine = pl.ds(dp * SEQ * part, SEQ * part)
    head_dp = copies.make(w_head.at[mine, :], w_head.at[mine, :], other_dp)

    def gather(source, at):
        step = [None] + [copies.make(source(lax.rem(z + k, 2)), at(owner(0)), along(k)) for k in range(1, SEQ)]
        cross = [copies.make(at(owner(k)) if k else source(lax.rem(z, 2)), at(owner(k)), other_dp) for k in range(SEQ)]
        return step, cross

    out_step, out_dp = gather(lambda h: w_out_ref, lambda c: out_all.at[:, pl.ds(c, part)])
    up_step, up_dp = gather(lambda h: up_own.at[h], lambda c: up_ref.at[pl.ds(c, part), :])
    down_step, down_dp = gather(lambda h: w_down_ref.at[pl.ds(h * side, side), :], lambda c: down_ref.at[:, pl.ds(c, part)])
    first_back = len(copies.all) - 1
    back_home = [None] + [copies.make(att_low.at[k], came.at[k], along(-k)) for k in range(1, SEQ)]
    sum_core = copies.make(part_low.at[rows_at(2, 2), :], core_in, core)
    sum_chip = copies.make(half_low, chip_in, chip)
    second_pair = copies.make(second.at[rows_at(0), :], second.at[rows_at(4), :], pair)
    second_chip = [copies.make(second.at[rows_at(4 * n), :], second.at[rows_at(4 * n + 1), :], chip) for n in range(2)]
    second_core = [copies.make(second.at[rows_at(4 * n, 2), :], second.at[rows_at(4 * n + 2, 2), :], core) for n in range(2)]
    cot_pair = copies.make(cot_ref.at[pl.ds(t * quarter, quarter), :], cots_ref.at[rows_at(4), :], pair)
    cot_chip = copies.make(cots_ref.at[rows_at(4), :], cots_ref.at[rows_at(5), :], chip)
    cot_core = copies.make(cots_ref.at[rows_at(4, 2), :], cots_ref.at[rows_at(6, 2), :], core)

    def norm_piece(n, carry):
        values = tokens[rows_at(n), :].astype(f32)
        center = values - jnp.mean(values, axis=1, keepdims=True)
        frames[0, rows_at(n), :] = (center * lax.rsqrt(jnp.mean(center * center, axis=1, keepdims=True) + NORM_EPS)).astype(bf16)
        return carry

    out_dp[0].start()
    down_dp[0].start()
    load_tokens[0].wait()
    lax.fori_loop(0, 1, norm_piece, 0)
    token[1].start()
    gain = gain_one_ref[...]
    for h in range(SEQ):
        at = slice(h * HEAD_DIM, (h + 1) * HEAD_DIM)
        for n, ref in enumerate((w_query_ref, w_key_ref, w_value_ref)):
            w_own[h, :, n * HEAD_DIM : (n + 1) * HEAD_DIM] = (ref[:, at].astype(f32) * gain).astype(bf16)
    for k in range(1, SEQ):
        head[k].start()
    w_head[pl.ds(owner(0), part), :] = w_own[z]
    gain = gain_two_ref[...]
    for h in range(2):
        up_own[h] = (w_up_ref[:, h * side : (h + 1) * side].astype(f32) * gain).astype(bf16)
    keep(up_own.at[lax.rem(z, 2)], up_ref.at[pl.ds(owner(0), part), :])
    for copy in load_tokens[1:]:
        copy.wait()
    lax.fori_loop(1, 4, norm_piece, 0)
    keep(frames.at[0], whole_ref.at[0])

    def arrive(copy, *then):
        copies.wait(copy)
        for one in then:
            one.start()

    def project(k):
        def piece(n, carry):
            qkv_ref[k, rows_at(n), :] = jnp.dot(frames[k, rows_at(n), :], w_head[...], preferred_element_type=f32).astype(bf16)
            return carry

        lax.fori_loop(0, 4, piece, 0)

    scale = HEAD_DIM ** (-0.5)

    def query_frame(i):
        at = lax.rem(z - i + SEQ, SEQ)
        query = qkv_ref[at, :, 0:HEAD_DIM]
        peak[...] = jnp.full_like(peak, MASK_FILL)
        total[...] = jnp.zeros_like(total)
        acc[...] = jnp.zeros_like(acc)

        def key_frame(j, inner):
            here = lax.rem(z - j + SEQ, SEQ)
            scores = lax.dot_general(qkv_ref[here, :, HEAD_DIM : 2 * HEAD_DIM], query, (((1,), (1,)), ((), ())), preferred_element_type=f32) * scale + bias_ref[j]
            before = peak[...]
            after = jnp.maximum(before, jnp.max(scores, axis=0, keepdims=True))
            terms = jnp.exp(scores - after)
            fix = jnp.exp(before - after)
            peak[...] = after
            total[...] = total[...] * fix + jnp.sum(terms, axis=0, keepdims=True)
            acc[...] = acc[...] * fix + lax.dot_general(qkv_ref[here, :, 2 * HEAD_DIM :], terms.astype(bf16), (((0,), (0,)), ((), ())), preferred_element_type=f32)
            return inner

        lax.fori_loop(0, i + 1, key_frame, 0)
        outcome = (acc[...] / total[...]).T
        att_ref[at] = outcome
        att_low[at] = outcome.astype(bf16)
        lse_ref[at] = peak[...] + jnp.log(total[...])

        @pl.when(at != 0)
        def _():
            pltpu.make_async_remote_copy(
                src_ref=att_low.at[at], dst_ref=came.at[at], send_sem=send.at[first_back + at], recv_sem=recv.at[first_back + at],
                device_id={"seq": i}, device_id_type=MESH,
            ).start()

    def mix(start):
        def piece(n, carry):
            at = pl.ds(pl.multiple_of(n * 512, 512), 512)
            part_low[pl.ds(start, half), at] = jnp.dot(attended_ref[pl.ds(start, half), :], out_all[:, at], preferred_element_type=f32).astype(bf16)
            return carry

        lax.fori_loop(0, width // 512, piece, 0)

    for k in range(1, SEQ):
        copies.wait(head[k])
    head_dp.start()
    arrive(token[1], token[2], token_chip[1])
    up_dp[0].start()
    arrive(token[2], token[3], token_chip[2])
    arrive(token_chip[1], token_core[1])
    copies.wait(head_dp)
    keep(w_head, w_head_ref)
    project(0)
    arrive(token_core[1])
    keep(frames.at[1], whole_ref.at[1])
    project(1)
    arrive(token_chip[2], token_core[2])
    arrive(token[3], token_chip[3], out_step[1], out_step[2], cot_pair)
    arrive(token_core[2])
    keep(frames.at[2], whole_ref.at[2])
    project(2)
    arrive(token_chip[3], token_core[3])
    arrive(token_core[3])
    keep(frames.at[3], whole_ref.at[3])
    project(3)
    query_frame(0)
    arrive(out_step[1], out_step[3], out_dp[1])
    query_frame(1)
    arrive(out_step[2], up_step[1], out_dp[2])
    arrive(cot_pair, cot_chip)
    query_frame(2)
    query_frame(3)
    came[0] = att_low[0]
    arrive(out_step[3], out_dp[3], up_step[2])
    copies.wait(*back_home[1:])
    for h in range(SEQ):
        attended_ref[:, h * HEAD_DIM : (h + 1) * HEAD_DIM] = came[lax.rem(h - z + SEQ, SEQ)]
    own_out.wait()
    copies.wait(*out_dp)
    keep(out_all, out_ref)

    mix(half)
    sum_core.start()
    mix(0)
    copies.wait(sum_core)
    half_low[...] = (part_low[quarter:half, :].astype(f32) + core_in[quarter:half, :].astype(f32)).astype(bf16)
    sum_chip.start()
    arrive(up_step[1], up_step[3], up_dp[1])
    arrive(cot_chip, cot_core)
    copies.wait(sum_chip)
    resid = tokens[first, :].astype(f32) + (part_low[first, :].astype(f32) + core_in[first, :].astype(f32)) + chip_in[...].astype(f32)
    center = resid - jnp.mean(resid, axis=1, keepdims=True)
    rate = lax.rsqrt(jnp.mean(center * center, axis=1, keepdims=True) + NORM_EPS)
    normed = center * rate
    second[first, :] = normed.astype(bf16)
    second_pair.start()
    second_chip[0].start()
    resid_ref[...] = resid
    rate_ref[...] = rate
    normed_ref[...] = normed
    arrive(up_step[2], down_step[1], up_dp[2])
    arrive(second_chip[0], second_core[0])
    arrive(second_pair, second_chip[1], down_step[2])
    arrive(up_step[3], up_dp[3], down_step[3])
    arrive(down_step[1], down_dp[1])
    arrive(second_chip[1], second_core[1])
    arrive(down_step[2], down_dp[2])
    arrive(down_step[3], down_dp[3])
    copies.wait(*second_core)
    keep(second, second_ref)
    copies.finish()
    for copy in kept:
        if not any(copy is done for done in [own_out] + load_tokens):
            copy.wait()


def front(x, w_query, w_key, w_value, w_out, w_up, w_down, gain_one, gain_two, cot, bias):
    rows, width = x.shape
    quarter, half = rows // 4, rows // 2
    part, hidden = w_up.shape
    inner = w_out.shape[0]
    three = 3 * HEAD_DIM
    f32, bf16 = jnp.float32, jnp.bfloat16
    any_, vmem = pl.BlockSpec(memory_space=pl.ANY), pl.BlockSpec(memory_space=pltpu.VMEM)
    shape = jax.ShapeDtypeStruct
    outs = [
        (shape((SEQ, rows, width), bf16), any_),
        (shape((width, three), bf16), any_),
        (shape((SEQ, rows, three), bf16), vmem),
        (shape((SEQ, rows, HEAD_DIM), f32), vmem),
        (shape((SEQ, 1, rows), f32), vmem),
        (shape((rows, inner), bf16), vmem),
        (shape((inner, width), bf16), any_),
        (shape((quarter, width), f32), vmem),
        (shape((quarter, width), f32), vmem),
        (shape((quarter, 1), f32), vmem),
        (shape((2 * rows, width), bf16), any_),
        (shape((width, hidden // 2), bf16), any_),
        (shape((hidden // 2, width), bf16), any_),
        (shape((2 * rows, width), bf16), any_),
    ]
    scratch = [
        ((rows, width), bf16),
        ((SEQ, rows, width), bf16),
        ((SEQ, part, three), bf16),
        ((width, three), bf16),
        ((2, part, hidden // 2), bf16),
        ((inner, width), bf16),
        ((SEQ, rows, HEAD_DIM), bf16),
        ((SEQ, rows, HEAD_DIM), bf16),
        ((rows, width), bf16),
        ((half, width), bf16),
        ((quarter, width), bf16),
        ((quarter, width), bf16),
        ((2 * rows, width), bf16),
        ((1, rows), f32),
        ((1, rows), f32),
        ((HEAD_DIM, rows), f32),
    ]
    count = 3 * 3 + 4 + 3 * 7 + 3 + 2 + 5 + 3
    return pl.pallas_call(
        front_kernel,
        out_shape=[o[0] for o in outs],
        in_specs=[any_] + [vmem] * 3 + [any_, vmem, any_, vmem, vmem, any_, vmem],
        out_specs=[o[1] for o in outs],
        scratch_shapes=[pltpu.VMEM(*one) for one in scratch] + [pltpu.SemaphoreType.DMA((count,)), pltpu.SemaphoreType.DMA((count,)), pltpu.SemaphoreType.DMA((24,))],
        compiler_params=pltpu.CompilerParams(collective_id=0, has_side_effects=True, vmem_limit_bytes=58 * 2**20),
        cost_estimate=pl.CostEstimate(flops=8 * 10**9, bytes_accessed=50 * 10**6, transcendentals=5 * 10**6),
    )(x, w_query, w_key, w_value, w_out, w_up, w_down, gain_one, gain_two, cot, bias)


def back_kernel(
    gd_ref, d_up_ref, second_ref, act_ref, down_ref, dn_ref, resid_ref, cots_ref, normed_two_ref, rate_two_ref, attended_ref, out_ref, qkv_ref, att_ref, lse_ref, bias_ref, w_head_ref, whole_ref, x_ref,
    w_query_ref, w_key_ref, w_value_ref, w_up_ref, gain_one_ref, gain_two_ref,
    down_sum_ref, up_sum_ref, out_sum_ref, grad_query_ref, grad_key_ref, grad_value_ref, gains_ref, grad_in_ref, result_ref,
    gu_ref, ff_ref, arrived_ref, cross_down_ref, cross_up_ref, far_down_ref, far_up_ref, dn_core_ref, dn_chip_ref, ff_core_ref, ff_chip_ref, pair_ref, first_core_ref, first_chip_ref, first_ring_ref,
    frames, temp, box_down, box_up, mix, d_head, d_out, dq, dk, dv, delta, d_three, out_send, out_cross, out_far, out_box,
    head_acc, head_low, head_cross, head_sum, held_a, held_b, half_box, pair_box, mid, quart_box, in_box, gain_box, gain_came,
    send, recv, keep_sem, load_sem, arena_sem, stage_sem,
):
    f32, bf16 = jnp.float32, jnp.bfloat16
    dp, z, t, other_dp, chip, core, pair = axes_of()
    rows, width = whole_ref.shape[1:]
    quarter, half = rows // 4, rows // 2
    part = width // (2 * SEQ)
    side = gd_ref.shape[1]
    inner = attended_ref.shape[1]
    copies = Copies(send, recv)
    scale = HEAD_DIM ** (-0.5)
    first, later = slice(0, quarter), slice(quarter, half)

    def along(k):
        return {"seq": lax.rem(z + k + SEQ, SEQ)}

    def load(*pairs):
        moves = [pltpu.make_async_copy(src, dst, load_sem.at[i]) for i, (src, dst) in enumerate(pairs)]
        for move in moves:
            move.start()
        for move in moves:
            move.wait()

    def block(side_dp, k):
        return pl.multiple_of((side_dp * SEQ + lax.rem(z - k + SEQ, SEQ)) * part, part)

    def rows_at(n, count=1):
        return pl.ds(n * quarter, count * quarter)

    greet([other_dp, chip, core] + [along(k) for k in range(1, SEQ)])

    def sums(part_ref, core_ref, chip_ref, n):
        to_core = [copies.make(part_ref.at[rows_at(4 * i + 2, 2), :], core_ref.at[i], core) for i in range(2)]
        to_chip = [copies.make(half_box.at[2 * n + i], chip_ref.at[i], chip) for i in range(2)]
        to_pair = copies.make(pair_box.at[n], pair_ref.at[n], pair)
        return to_core, to_chip, to_pair

    dn_core, dn_chip, dn_pair = sums(dn_ref, dn_core_ref, dn_chip_ref, 0)
    ff_core, ff_chip, ff_pair = sums(ff_ref, ff_core_ref, ff_chip_ref, 1)
    mix_chip = copies.make(mix.at[rows_at(0), :], mix.at[rows_at(1), :], chip)
    mix_core = copies.make(mix.at[rows_at(0, 2), :], mix.at[rows_at(2, 2), :], core)
    spread = [None] + [copies.make(d_head.at[lax.rem(z + k, SEQ)], d_out.at[k], along(k)) for k in range(1, SEQ)]
    cross_down = [copies.make(gd_ref.at[pl.ds(block(1 - dp, k), part), :], cross_down_ref.at[k], other_dp) for k in range(SEQ)]
    cross_up = [copies.make(gu_ref.at[pl.ds(block(1 - dp, k), part), :], cross_up_ref.at[k], other_dp) for k in range(SEQ)]
    cross_out = [copies.make(out_send.at[k], out_cross.at[k], other_dp) for k in range(SEQ)]
    far_down = [None] + [copies.make(box_down.at[k - 1], far_down_ref.at[k - 1], along(-k)) for k in range(1, SEQ)]
    far_up = [None] + [copies.make(box_up.at[k - 1], far_up_ref.at[k - 1], along(-k)) for k in range(1, SEQ)]
    far_out = [None] + [copies.make(out_box.at[k - 1], out_far.at[k - 1], along(-k)) for k in range(1, SEQ)]
    first_core = [copies.make(frames.at[k, rows_at(2, 2), :], first_core_ref.at[k], core) for k in range(SEQ)]
    first_chip = [copies.make(quart_box.at[k], first_chip_ref.at[k], chip) for k in range(SEQ)]
    first_ring = [None] + [copies.make(in_box.at[k - 1], first_ring_ref.at[k - 1], along(1)) for k in range(1, SEQ)]
    head_dp = copies.make(head_low.at[1 - dp], head_cross, other_dp)
    head_out = [None] + [copies.make(head_sum.at[lax.rem(z + k, SEQ)], arrived_ref.at[k], along(k)) for k in range(1, SEQ)]
    kept, numbered = [], []

    def publish(n, ref):
        mine = ref.at[pl.ds(t * quarter, quarter), :]
        mate = ref.at[pl.ds(lax.rem(t + 2, 4) * quarter, quarter), :]
        return [copies.make(half_box.at[n], mine, chip), copies.make(half_box.at[n], mine, core), copies.make(mate, mate, core)], (half_box.at[n], mine)

    gain_core = copies.make(gain_box.at[0], gain_came.at[0], core)
    gain_chip = copies.make(gain_box.at[1], gain_came.at[1], chip)
    result_out, result_own = publish(0, result_ref)
    grad_out_copies, grad_own = publish(1, grad_in_ref)

    def keep(src, dst):
        move = pltpu.make_async_copy(src, dst, keep_sem.at[SEQ + len(numbered)])
        numbered.append(move)
        kept.append(move)
        move.start()

    def half_of(part_ref, core_ref, to_core, to_chip, i, n):
        copies.wait(to_core[i])
        load((part_ref.at[rows_at(4 * i + 1), :], held_a.at[rows_at(0), :]), (core_ref.at[i, rows_at(1), :], held_a.at[rows_at(1), :]))
        half_box[2 * n + i] = (held_a[first, :].astype(f32) + held_a[later, :].astype(f32)).astype(bf16)
        to_chip[i].start()

    def quarter_of(part_ref, core_ref, chip_ref, to_chip, i, *more):
        copies.wait(to_chip[i])
        load(
            (part_ref.at[rows_at(4 * i), :], held_a.at[rows_at(0), :]), (core_ref.at[i, rows_at(0), :], held_a.at[rows_at(1), :]), (chip_ref.at[i], held_b.at[rows_at(0), :]),
            *more,
        )
        return (held_a[first, :].astype(f32) + held_a[later, :].astype(f32)) + held_b[first, :].astype(f32)

    def pair_sum(part_ref, core_ref, chip_ref, to_chip, to_pair, n):
        pair_box[n] = quarter_of(part_ref, core_ref, chip_ref, to_chip, 1).astype(bf16)
        to_pair.start()

    def own_sum(part_ref, core_ref, chip_ref, to_chip, to_pair, n, extra):
        copies.wait(to_pair)
        total = quarter_of(part_ref, core_ref, chip_ref, to_chip, 0, (pair_ref.at[n], held_b.at[rows_at(1), :]), (extra, spare))
        return total + held_b[later, :].astype(f32)

    def scatter(k, own_ref, cross_at, crossing, box, far):
        copies.wait(crossing)
        load((cross_at, temp.at[0]), (own_ref.at[pl.ds(block(dp, k), part), :], temp.at[1]))
        box[k - 1] = (temp[0].astype(f32) + temp[1].astype(f32)).astype(bf16)
        far[k].start()

    def scatter_down(k):
        scatter(k, gd_ref, cross_down_ref.at[k], cross_down[k], box_down, far_down)

    def scatter_up(k):
        scatter(k, gu_ref, cross_up_ref.at[k], cross_up[k], box_up, far_up)

    same = pl.multiple_of(lax.rem(z, 2) * side, side)
    unlike = pl.multiple_of((1 - lax.rem(z, 2)) * side, side)

    def total_of(own_ref, cross_at, far_ref, far, crossing, store):
        copies.wait(crossing, *far[1:])
        load((cross_at, temp.at[0]), (own_ref.at[pl.ds(block(dp, 0), part), :], temp.at[1]), (far_ref.at[1], temp.at[2]))
        store(same, lambda at: (temp[0, :, at].astype(f32) + temp[1, :, at].astype(f32)) + temp[2, :, at].astype(f32))
        load((far_ref.at[0], temp.at[0]), (far_ref.at[2], temp.at[1]))
        store(unlike, lambda at: temp[0, :, at].astype(f32) + temp[1, :, at].astype(f32))

    def store_turned(base, value):
        for n in range(side // 256):
            down_sum_ref[pl.ds(base + n * 256, 256), :] = value(slice(n * 256, (n + 1) * 256)).T

    gain_sums = []

    def store_plain(base, value):
        raw = value(slice(0, side))
        gain_sums.append(jnp.sum(held_a[0:part, pl.ds(base, side)].astype(f32) * raw, axis=1, keepdims=True))
        up_sum_ref[:, pl.ds(base, side)] = raw * gain_two_ref[...]

    def out_block(start):
        return lax.dot_general(attended_ref[...], mix[:, pl.ds(start, part)], (((0,), (0,)), ((), ())), preferred_element_type=f32)

    def scatter_out(k):
        copies.wait(cross_out[k])
        out_box[k - 1] = (out_block(block(dp, k)) + out_cross[k].astype(f32)).astype(bf16)
        far_out[k].start()

    for copy in (dn_core[1], dn_core[0], cross_down[1], cross_down[2]):
        copy.start()

    def place(*pairs):
        moves = [pltpu.make_async_copy(src, dst, arena_sem.at[i]) for i, (src, dst) in enumerate(pairs)]
        for move in moves:
            move.start()
        return moves

    def sides(ref, at):
        return [(ref.at[pl.ds(n * rows, rows), :], frames.at[at, :, pl.ds(n * side, side)]) for n in range(2)]

    arena = place(*sides(d_up_ref, 0), *sides(act_ref, 3), *[(second_ref.at[pl.ds(n * rows, rows), :], frames.at[1 + n]) for n in range(2)])
    spare = head_acc.at[pl.ds(0, quarter), :]
    half_of(dn_ref, dn_core_ref, dn_core, dn_chip, 1, 0)
    load(*[(out_ref.at[pl.ds(h * HEAD_DIM, HEAD_DIM), :], quart_box.at[h, pl.ds(0, HEAD_DIM), :]) for h in range(SEQ)])
    for move in arena:
        move.wait()

    def up_piece(b, carry):
        at = pl.ds(pl.multiple_of(b * part, part), part)
        slot = lax.rem(b, 2)
        move = pltpu.make_async_copy(temp.at[slot], gu_ref.at[at, :], stage_sem.at[slot])

        @pl.when(b >= 2)
        def _():
            move.wait()

        turned = (((0,), (0,)), ((), ()))
        value = lax.dot_general(frames[1, :, at], frames[0, :, 0:side], turned, preferred_element_type=f32)
        value = value + lax.dot_general(frames[2, :, at], frames[0, :, side:], turned, preferred_element_type=f32)
        temp[slot] = value.astype(bf16)
        move.start()
        return carry

    lax.fori_loop(0, 2 * SEQ, up_piece, 0)
    for slot in range(2):
        pltpu.make_async_copy(temp.at[slot], gu_ref.at[pl.ds(0, part), :], stage_sem.at[slot]).wait()
    arena = place((down_ref.at[pl.ds(0, rows), :], frames.at[1]), (down_ref.at[pl.ds(rows, side - rows), :], frames.at[2, pl.ds(0, side - rows), :]))
    scatter_down(1)
    copies.wait(dn_chip[1])
    half_of(dn_ref, dn_core_ref, dn_core, dn_chip, 0, 0)
    pair_sum(dn_ref, dn_core_ref, dn_chip_ref, dn_chip, dn_pair, 0)
    cross_down[3].start()
    cross_up[1].start()
    scatter_down(2)
    grad = own_sum(dn_ref, dn_core_ref, dn_chip_ref, dn_chip, dn_pair, 0, normed_two_ref)
    normed = spare[...]
    grad = rate_two_ref[...] * (grad - jnp.mean(grad, axis=1, keepdims=True) - normed * jnp.mean(grad * normed, axis=1, keepdims=True))
    load((cots_ref.at[rows_at(0), :], held_a.at[rows_at(0), :]))
    grad = held_a[first, :].astype(f32) + grad
    mid[...] = grad
    mix[first, :] = grad.astype(bf16)
    mix_chip.start()
    scatter_down(3)
    for copy in (cross_up[2], cross_up[3], cross_up[0], cross_down[0]):
        copy.start()
    scatter_up(1)
    copies.wait(mix_chip)
    mix_core.start()
    copies.wait(mix_core)

    for n in range(4):
        at = slice(n * quarter, (n + 1) * quarter)
        for h in range(SEQ):
            d_head[h, at, :] = lax.dot_general(mix[at, :], quart_box[h, 0:HEAD_DIM, :], (((1,), (1,)), ((), ())), preferred_element_type=f32).astype(bf16)
    for k in range(1, SEQ):
        spread[k].start()
    d_out[0] = d_head[z]
    for move in arena:
        move.wait()

    def ff_piece(n, carry):
        at = pl.ds(n * quarter, quarter)
        slot = lax.rem(n, 2)
        stage = held_b.at[pl.ds(slot * quarter, quarter), :]
        move = pltpu.make_async_copy(stage, ff_ref.at[at, :], stage_sem.at[slot])

        @pl.when(n >= 2)
        def _():
            move.wait()

        left = frames[3, pl.ds(lax.rem(n, 4) * quarter, quarter), pl.ds(pl.multiple_of(n // 4 * side, side), side)]
        value = jnp.dot(left[:, 0:rows], frames[1], preferred_element_type=f32)
        value = value + jnp.dot(left[:, rows:], frames[2, 0 : side - rows, :], preferred_element_type=f32)
        held_b[pl.ds(slot * quarter, quarter), :] = value.astype(bf16)
        move.start()
        return carry

    lax.fori_loop(0, 8, ff_piece, 0)
    for slot in range(2):
        pltpu.make_async_copy(held_b.at[pl.ds(slot * quarter, quarter), :], ff_ref.at[pl.ds(0, quarter), :], stage_sem.at[slot]).wait()
    ff_core[1].start()
    ff_core[0].start()
    fetch = [pltpu.make_async_copy(whole_ref.at[k], frames.at[k], keep_sem.at[k]) for k in range(SEQ)]
    for move in fetch:
        move.start()
    for k in (1, 2, 3, 0):
        out_send[k] = out_block(block(1 - dp, k)).astype(bf16)
        cross_out[k].start()
    half_of(ff_ref, ff_core_ref, ff_core, ff_chip, 1, 1)
    high = head_acc.shape[0]
    pieces = [(f, slice(0, high) if n == 0 else slice(high, rows), slice((2 * f + n) * HEAD_DIM, (2 * f + n + 1) * HEAD_DIM)) for f in range(SEQ) for n in range(2)]
    load(*[(att_ref.at[f, pl.ds(at.start, at.stop - at.start), :], head_acc.at[pl.ds(0, at.stop - at.start), pl.ds(lanes.start, HEAD_DIM)]) for f, at, lanes in pieces])
    copies.wait(*spread[1:])
    dq[...] = jnp.zeros_like(dq)
    for f, at, lanes in pieces:
        delta[f, :, at] = jnp.sum((d_out[f, at, :].astype(f32) * head_acc[0 : at.stop - at.start, lanes]).T, axis=0, keepdims=True)

    def key_frame(j):
        here = lax.rem(z - j + SEQ, SEQ)
        dk[...] = jnp.zeros_like(dk)
        dv[...] = jnp.zeros_like(dv)

        def query_frame(i, inner_):
            at = lax.rem(z - i + SEQ, SEQ)
            query, key, value = qkv_ref[at, :, :HEAD_DIM], qkv_ref[here, :, HEAD_DIM : 2 * HEAD_DIM], qkv_ref[here, :, 2 * HEAD_DIM :]
            grad_out = d_out[at]
            scores = lax.dot_general(key, query, (((1,), (1,)), ((), ())), preferred_element_type=f32) * scale + bias_ref[j]
            prob = jnp.exp(scores - lse_ref[at])
            d_prob = lax.dot_general(value, grad_out, (((1,), (1,)), ((), ())), preferred_element_type=f32)
            d_scores = (prob * (d_prob - delta[at])).astype(bf16)
            dv[...] += jnp.dot(prob.astype(bf16), grad_out, preferred_element_type=f32)
            dk[...] += jnp.dot(d_scores, query, preferred_element_type=f32)
            dq[at] += lax.dot_general(key, d_scores, (((0,), (0,)), ((), ())), preferred_element_type=f32)
            return inner_

        lax.fori_loop(j, SEQ, query_frame, 0)
        d_three[here, :, HEAD_DIM : 2 * HEAD_DIM] = (dk[...] * scale).astype(bf16)
        d_three[here, :, 2 * HEAD_DIM :] = dv[...].astype(bf16)

    key_frame(0)
    scatter_up(2)
    key_frame(1)
    half_of(ff_ref, ff_core_ref, ff_core, ff_chip, 0, 1)
    scatter_up(3)
    key_frame(2)
    scatter_out(1)
    key_frame(3)
    pair_sum(ff_ref, ff_core_ref, ff_chip_ref, ff_chip, ff_pair, 1)
    for f in range(SEQ):
        d_three[f, :, :HEAD_DIM] = (dq[f] * scale).T.astype(bf16)

    def project_back(k):
        fetch[k].wait()

        def piece(n, carry):
            at = pl.ds(pl.multiple_of(n * 512, 512), 512)
            term = lax.dot_general(d_three[k], frames[k, :, at], (((0,), (0,)), ((), ())), preferred_element_type=f32)
            head_acc[:, at] = term if k == 1 else head_acc[:, at] + term
            return carry

        lax.fori_loop(0, width // 512, piece, 0)

        def back_piece(n, carry):
            at = pl.ds(pl.multiple_of(n * 512, 512), 512)
            frames[k, :, at] = lax.dot_general(d_three[k], w_head_ref[at, :], (((1,), (1,)), ((), ())), preferred_element_type=f32).astype(bf16)
            return carry

        lax.fori_loop(0, width // 512, back_piece, 0)
        first_core[k].start()

    def half_sum(k):
        copies.wait(first_core[k])
        load((first_core_ref.at[k], held_a))
        quart_box[k] = (frames[k, later, :].astype(f32) + held_a[later, :].astype(f32)).astype(bf16)
        first_chip[k].start()
        frames[k, first, :] = (frames[k, first, :].astype(f32) + held_a[first, :].astype(f32)).astype(bf16)

    def quarter_sum(k):
        copies.wait(first_chip[k])
        pairs = [(first_chip_ref.at[k], held_a.at[rows_at(0), :])]
        if k != 1:
            before = (k - 1) % SEQ
            copies.wait(first_ring[before])
            pairs.append((first_ring_ref.at[before - 1], held_a.at[rows_at(1), :]))
        load(*pairs)
        sum_ = frames[k, first, :].astype(f32) + held_a[first, :].astype(f32)
        if k != 1:
            sum_ = sum_ + held_a[later, :].astype(f32)
        return sum_

    project_back(1)
    scatter_out(2)
    project_back(2)
    half_sum(1)
    scatter_out(3)
    project_back(3)
    project_back(0)
    for n in range(2):
        head_low[n] = head_acc[:, n * (width // 2) : (n + 1) * (width // 2)].astype(bf16)
    head_dp.start()
    copies.wait(first_chip[1])
    half_sum(2)
    in_box[0] = quarter_sum(1).astype(bf16)
    first_ring[1].start()
    total_of(gd_ref, cross_down_ref.at[0], far_down_ref, far_down, cross_down[0], store_turned)
    copies.wait(first_chip[2])
    half_sum(3)
    in_box[1] = quarter_sum(2).astype(bf16)
    first_ring[2].start()
    copies.wait(head_dp)
    for j in range(SEQ):
        at = slice(j * part, (j + 1) * part)
        head_sum[j] = (head_low[dp, :, at].astype(f32) + head_cross[:, at].astype(f32)).astype(bf16)
    for k in range(1, SEQ):
        head_out[k].start()
    keep(head_sum.at[z], arrived_ref.at[0])
    copies.wait(first_chip[3])
    half_sum(0)
    in_box[2] = quarter_sum(3).astype(bf16)
    first_ring[3].start()
    total = own_sum(ff_ref, ff_core_ref, ff_chip_ref, ff_chip, ff_pair, 1, resid_ref)
    copies.flush(*dn_chip)
    half_box[0] = (spare[...] + total).astype(bf16)
    result_out[0].start()
    result_out[1].start()
    keep(*result_own)
    load((w_up_ref, held_a.at[pl.ds(0, part), :]))
    total_of(gu_ref, cross_up_ref.at[0], far_up_ref, far_up, cross_up[0], store_plain)
    copies.wait(cross_out[0], *far_out[1:])
    sum_ = out_block(block(dp, 0)) + out_cross[0].astype(f32)
    for k in range(1, SEQ):
        sum_ = sum_ + out_far[k - 1].astype(f32)
    out_sum_ref[...] = sum_
    copies.wait(*head_out[1:])
    kept.pop(0).wait()
    load(
        *[(arrived_ref.at[k], head_cross.at[:, pl.ds(k * part, part)]) for k in range(SEQ)],
        *[(ref, held_a.at[pl.ds(0, part), pl.ds(n * inner, inner)]) for n, ref in enumerate((w_query_ref, w_key_ref, w_value_ref))],
    )
    gain_first = jnp.zeros((part, 1), f32)
    for h in range(SEQ):
        raw = head_cross[:, pl.ds(pl.multiple_of(lax.rem(z - h + SEQ, SEQ) * part, part), part)].astype(f32).T
        for n, ref in enumerate((grad_query_ref, grad_key_ref, grad_value_ref)):
            one = raw[:, n * HEAD_DIM : (n + 1) * HEAD_DIM]
            weight = held_a[0:part, n * inner + h * HEAD_DIM : n * inner + (h + 1) * HEAD_DIM].astype(f32)
            gain_first = gain_first + jnp.sum(weight * one, axis=1, keepdims=True)
            ref[:, h * HEAD_DIM : (h + 1) * HEAD_DIM] = one * gain_one_ref[...]
    lane = lax.broadcasted_iota(jnp.int32, (part, HEAD_DIM), 1)
    gain_box[0] = jnp.where(lane == 0, gain_first, gain_sums[0] + gain_sums[1])
    gain_core.start()
    copies.wait(gain_core)
    gain_box[1] = gain_box[0] + gain_came[0]
    gain_chip.start()
    grad = quarter_sum(0)
    load((x_ref.at[pl.ds(t * quarter, quarter), :], held_a.at[rows_at(0), :]))
    center = held_a[first, :].astype(f32)
    center = center - jnp.mean(center, axis=1, keepdims=True)
    rate = lax.rsqrt(jnp.mean(center * center, axis=1, keepdims=True) + NORM_EPS)
    normed = center * rate
    grad = rate * (grad - jnp.mean(grad, axis=1, keepdims=True) - normed * jnp.mean(grad * normed, axis=1, keepdims=True))
    half_box[1] = (mid[...] + grad).astype(bf16)
    grad_out_copies[0].start()
    grad_out_copies[1].start()
    keep(*grad_own)
    copies.wait(result_out[0], gain_chip)
    result_out[2].start()
    gains_ref[...] = gain_box[1] + gain_came[1]
    copies.wait(grad_out_copies[0])
    grad_out_copies[2].start()
    copies.finish()
    for move in kept:
        move.wait()


def back(gd, d_up, second, act, down, dn, resid, cots, normed_two, rate_two, attended, out_rel, qkv, att, lse, bias, w_head, whole, x, w_query, w_key, w_value, w_up, gain_one, gain_two):
    rows, width = x.shape
    quarter, half = rows // 4, rows // 2
    part = width // (2 * SEQ)
    inner = attended.shape[1]
    side = gd.shape[1]
    three = 3 * HEAD_DIM
    f32, bf16 = jnp.float32, jnp.bfloat16
    any_, vmem = pl.BlockSpec(memory_space=pl.ANY), pl.BlockSpec(memory_space=pltpu.VMEM)
    shape = jax.ShapeDtypeStruct
    outs = [
        (shape((2 * side, part), f32), vmem),
        (shape((part, 2 * side), f32), vmem),
        (shape((inner, part), f32), vmem),
        (shape((part, inner), f32), vmem),
        (shape((part, inner), f32), vmem),
        (shape((part, inner), f32), vmem),
        (shape((part, HEAD_DIM), f32), vmem),
        (shape((rows, width), bf16), any_),
        (shape((rows, width), bf16), any_),
        (shape((width, side), bf16), any_),
        (shape((2 * rows, width), bf16), any_),
        (shape((SEQ, three, part), bf16), any_),
        (shape((SEQ, part, side), bf16), any_),
        (shape((SEQ, part, side), bf16), any_),
        (shape((SEQ - 1, part, side), bf16), any_),
        (shape((SEQ - 1, part, side), bf16), any_),
        (shape((2, half, width), bf16), any_),
        (shape((2, quarter, width), bf16), any_),
        (shape((2, half, width), bf16), any_),
        (shape((2, quarter, width), bf16), any_),
        (shape((2, quarter, width), bf16), any_),
        (shape((SEQ, half, width), bf16), any_),
        (shape((SEQ, quarter, width), bf16), any_),
        (shape((SEQ - 1, quarter, width), bf16), any_),
    ]
    count = 10 + 2 + 3 + 4 + 4 + 4 + 9 + 8 + 3 + 4 + 6 + 2
    scratch = [
        ((SEQ, rows, width), bf16),
        ((3, part, side), bf16),
        ((SEQ - 1, part, side), bf16),
        ((SEQ - 1, part, side), bf16),
        ((rows, width), bf16),
        ((SEQ, rows, HEAD_DIM), bf16),
        ((SEQ, rows, HEAD_DIM), bf16),
        ((SEQ, HEAD_DIM, rows), f32),
        ((rows, HEAD_DIM), f32),
        ((rows, HEAD_DIM), f32),
        ((SEQ, 1, rows), f32),
        ((SEQ, rows, three), bf16),
        ((SEQ, inner, part), bf16),
        ((SEQ, inner, part), bf16),
        ((SEQ - 1, inner, part), bf16),
        ((SEQ - 1, inner, part), bf16),
        ((three, width), f32),
        ((2, three, width // 2), bf16),
        ((three, width // 2), bf16),
        ((SEQ, three, part), bf16),
        ((half, width), bf16),
        ((half, width), bf16),
        ((4, quarter, width), bf16),
        ((2, quarter, width), bf16),
        ((quarter, width), f32),
        ((SEQ, quarter, width), bf16),
        ((SEQ - 1, quarter, width), bf16),
        ((2, part, HEAD_DIM), f32),
        ((2, part, HEAD_DIM), f32),
    ]
    return pl.pallas_call(
        back_kernel,
        out_shape=[o[0] for o in outs],
        in_specs=[any_] * 9 + [vmem, vmem, any_, vmem, any_] + [vmem] * 3 + [any_] * 6 + [vmem] * 2,
        out_specs=[o[1] for o in outs],
        scratch_shapes=[pltpu.VMEM(*one) for one in scratch]
        + [pltpu.SemaphoreType.DMA((count,)), pltpu.SemaphoreType.DMA((count,)), pltpu.SemaphoreType.DMA((SEQ + 3,)), pltpu.SemaphoreType.DMA((8,)), pltpu.SemaphoreType.DMA((6,)), pltpu.SemaphoreType.DMA((2,))],
        compiler_params=pltpu.CompilerParams(collective_id=1, has_side_effects=True, vmem_limit_bytes=62 * 2**20),
        cost_estimate=pl.CostEstimate(flops=20 * 10**9, bytes_accessed=60 * 10**6, transcendentals=5 * 10**6),
    )(gd, d_up, second, act, down, dn, resid, cots, normed_two, rate_two, attended, out_rel, qkv, att, lse, bias, w_head, whole, x, w_query, w_key, w_value, w_up, gain_one, gain_two)[:9]


def mm(left, right, dims=((1,), (0,)), out=jnp.bfloat16):
    return lax.dot_general(left, right, (dims, ((), ())), preferred_element_type=jnp.float32).astype(out)


def local_fast(inputs, first_gain, w_query, w_key, w_value, w_out, second_gain, w_up, w_down, frame_mask, cotangent):
    rows = inputs.shape[1]
    f32, bf16 = jnp.float32, jnp.bfloat16
    gain_one, gain_two = first_gain.astype(f32)[:, None], second_gain.astype(f32)[:, None]
    bias = jnp.broadcast_to(jnp.where(frame_mask[0] == 1, 0.0, MASK_FILL).astype(f32)[:, None, None], (SEQ, 1, rows))
    whole, w_head, qkv, attended_f, lse, attended, out_all, resid_mid, normed_two, rate_two, second_in, up_side, down_side, cots = front(
        inputs[0], w_query, w_key, w_value, w_out, w_up, w_down, gain_one, gain_two, cotangent[0], bias
    )
    up_pre = mm(second_in, up_side, out=f32)
    cdf = 0.5 * (1.0 + lax.erf(up_pre * (0.5**0.5)))
    up_act = (up_pre * cdf).astype(bf16)
    slope = cdf + up_pre * jnp.exp(-0.5 * up_pre * up_pre) * ((2.0 * jnp.pi) ** -0.5)
    grad_down = mm(cots, up_act, ((0,), (0,)))
    d_up = (mm(cots, down_side, ((1,), (1,)), f32) * slope).astype(bf16)
    d_normed_two = mm(d_up, up_side, ((1,), (1,)))
    down_sum, up_sum, out_sum, grad_query, grad_key, grad_value, gains, grad_in, result = back(
        grad_down, d_up, second_in, up_act, down_side, d_normed_two, resid_mid, cots, normed_two, rate_two, attended, out_all, qkv, attended_f, lse, bias, w_head, whole, inputs[0],
        w_query, w_key, w_value, w_up, gain_one, gain_two,
    )
    return (result[None], grad_in[None], gains[:, 0], grad_query, grad_key, grad_value, out_sum, gains[:, 1], up_sum, down_sum)


SEQ = 4


def solution(mesh):
    placed = (
        P("dp", "seq", None),
        P(("dp", "seq")),
        P(("dp", "seq"), "tensor"),
        P(("dp", "seq"), "tensor"),
        P(("dp", "seq"), "tensor"),
        P("tensor", ("dp", "seq")),
        P(("dp", "seq")),
        P(("dp", "seq"), "tensor"),
        P("tensor", ("dp", "seq")),
        P("dp", None),
        P("dp", "seq", None),
    )
    sizes = dict(mesh.shape)
    spread = sizes == {"dp": 2, "seq": SEQ, "tensor": 4}
    return jax.shard_map(
        local_fast if spread else local,
        mesh=mesh,
        in_specs=placed,
        out_specs=(
            P("dp", "seq", None),
            P("dp", "seq", None),
            P(("dp", "seq")),
            P(("dp", "seq"), "tensor"),
            P(("dp", "seq"), "tensor"),
            P(("dp", "seq"), "tensor"),
            P("tensor", ("dp", "seq")),
            P(("dp", "seq")),
            P(("dp", "seq"), "tensor"),
            P("tensor", ("dp", "seq")),
        ),
        check_vma=False,
    )
```

```python
import functools

import jax
import jax.numpy as jnp
from jax import lax
from jax.experimental import pallas as pl
from jax.experimental.pallas import tpu as pltpu
from jax.sharding import PartitionSpec as P

HEAD_DIM = 128
FRAME_TOK = 640


NORM_EPS = 1e-05
MASK_FILL = -1e30
MESH = pl.DeviceIdType.MESH


def norm_rows(values):
    center = values - jnp.mean(values, axis=-1, keepdims=True)
    spread = jnp.mean(center * center, axis=-1, keepdims=True)
    return center * lax.rsqrt(spread + NORM_EPS)


def gelu_exact(values):
    return jax.nn.gelu(values, approximate=False)


def heads_total(values):
    return lax.psum(values.astype(jnp.bfloat16), "tensor").astype(jnp.float32)


def local(
    inputs,
    first_gain,
    w_query,
    w_key,
    w_value,
    w_out,
    second_gain,
    w_up,
    w_down,
    frame_mask,
    cotangent,
):
    seq_pos = lax.axis_index("seq")
    gain_one, query_w, key_w, value_w, gain_two, up_w = (
        lax.all_gather(first_gain, ("dp", "seq"), axis=0, tiled=True),
        lax.all_gather(w_query, ("dp", "seq"), axis=0, tiled=True),
        lax.all_gather(w_key, ("dp", "seq"), axis=0, tiled=True),
        lax.all_gather(w_value, ("dp", "seq"), axis=0, tiled=True),
        lax.all_gather(second_gain, ("dp", "seq"), axis=0, tiled=True),
        lax.all_gather(w_up, ("dp", "seq"), axis=0, tiled=True),
    )
    out_w, down_w = (
        lax.all_gather(w_out, ("dp", "seq"), axis=1, tiled=True),
        lax.all_gather(w_down, ("dp", "seq"), axis=1, tiled=True),
    )
    tok_rows = inputs.shape[1]
    local_inner = query_w.shape[1]
    local_heads = local_inner // HEAD_DIM
    frames_dev = tok_rows // FRAME_TOK
    score_scale = HEAD_DIM ** (-0.5)
    clip_valid = frame_mask[0]
    frame_count = clip_valid.shape[0]
    resid_in = inputs[0].astype(jnp.float32)
    dout_rows = cotangent[0]
    row_frame = seq_pos * frames_dev + jnp.arange(tok_rows, dtype=jnp.int32) // FRAME_TOK
    frame_limit = (seq_pos + 1) * frames_dev
    normed_one = norm_rows(resid_in)
    first_in = (normed_one * gain_one.astype(jnp.float32)).astype(jnp.bfloat16)
    query = jnp.dot(first_in, query_w, preferred_element_type=jnp.float32).astype(jnp.bfloat16)
    key_local = jnp.dot(first_in, key_w, preferred_element_type=jnp.float32).astype(jnp.bfloat16)
    value_local = jnp.dot(first_in, value_w, preferred_element_type=jnp.float32).astype(
        jnp.bfloat16
    )
    key_all, value_all = (
        lax.all_gather(key_local, "seq", axis=0, tiled=True),
        lax.all_gather(value_local, "seq", axis=0, tiled=True),
    )
    query_heads = query.reshape(tok_rows, local_heads, HEAD_DIM)
    key_frames = key_all.reshape(frame_count, FRAME_TOK, local_heads, HEAD_DIM)
    value_frames = value_all.reshape(frame_count, FRAME_TOK, local_heads, HEAD_DIM)

    def frame_scores(frame_idx):
        key_block = lax.dynamic_index_in_dim(key_frames, frame_idx, 0, keepdims=False)
        value_block = lax.dynamic_index_in_dim(value_frames, frame_idx, 0, keepdims=False)
        scores = (
            jnp.einsum("qhd,khd->hqk", query_heads, key_block, preferred_element_type=jnp.float32)
            * score_scale
        )
        frame_ok = lax.dynamic_index_in_dim(clip_valid, frame_idx, 0, keepdims=False) == 1
        allowed = ((frame_idx <= row_frame) & frame_ok)[None, :, None]
        return (scores, allowed, key_block, value_block)

    def stats_step(frame_idx, running):
        row_max, row_sum = running
        scores, allowed, key_block, value_block = frame_scores(frame_idx)
        masked = jnp.where(allowed, scores, MASK_FILL)
        new_max = jnp.maximum(row_max, jnp.max(masked, axis=2))
        exp_terms = jnp.where(allowed, jnp.exp(masked - new_max[:, :, None]), 0.0)
        return (new_max, row_sum * jnp.exp(row_max - new_max) + jnp.sum(exp_terms, axis=2))

    start_stats = (
        jnp.full((local_heads, tok_rows), MASK_FILL, jnp.float32),
        jnp.zeros((local_heads, tok_rows), jnp.float32),
    )
    row_max, row_sum = lax.fori_loop(0, frame_limit, stats_step, start_stats)

    def soft_weights(scores, allowed):
        return jnp.where(allowed, jnp.exp(scores - row_max[:, :, None]) / row_sum[:, :, None], 0.0)

    def output_step(frame_idx, running):
        scores, allowed, key_block, value_block = frame_scores(frame_idx)
        attn_prob = soft_weights(scores, allowed).astype(jnp.bfloat16)
        return running + jnp.einsum(
            "hqk,khd->qhd", attn_prob, value_block, preferred_element_type=jnp.float32
        )

    attended = lax.fori_loop(
        0, frame_limit, output_step, jnp.zeros((tok_rows, local_heads, HEAD_DIM), jnp.float32)
    )
    attended_low = attended.reshape(tok_rows, local_inner).astype(jnp.bfloat16)
    resid_mid = resid_in + heads_total(
        jnp.dot(attended_low, out_w, preferred_element_type=jnp.float32)
    )
    normed_two = norm_rows(resid_mid)
    second_in = (normed_two * gain_two.astype(jnp.float32)).astype(jnp.bfloat16)
    up_pre = jnp.dot(second_in, up_w, preferred_element_type=jnp.float32)
    up_act = gelu_exact(up_pre).astype(jnp.bfloat16)
    resid_out = resid_mid + heads_total(jnp.dot(up_act, down_w, preferred_element_type=jnp.float32))
    result = resid_out.astype(jnp.bfloat16)[None]
    grad_down = jnp.einsum("tf,td->fd", up_act, dout_rows, preferred_element_type=jnp.float32)
    d_act = jnp.einsum("td,fd->tf", dout_rows, down_w, preferred_element_type=jnp.float32)
    gelu_pull = jax.vjp(gelu_exact, up_pre)[1]
    d_up_pre = gelu_pull(d_act)[0].astype(jnp.bfloat16)
    grad_up = jnp.einsum("td,tf->df", second_in, d_up_pre, preferred_element_type=jnp.float32)
    d_second = heads_total(
        jnp.einsum("tf,df->td", d_up_pre, up_w, preferred_element_type=jnp.float32)
    )
    grad_second_gain = jnp.sum(d_second * normed_two, axis=0)
    norm_pull_two = jax.vjp(norm_rows, resid_mid)[1]
    d_mid = (
        dout_rows.astype(jnp.float32) + norm_pull_two(d_second * gain_two.astype(jnp.float32))[0]
    )
    d_mix = d_mid.astype(jnp.bfloat16)
    grad_out = jnp.einsum("ti,td->id", attended_low, d_mix, preferred_element_type=jnp.float32)
    d_attended = jnp.einsum("td,id->ti", d_mix, out_w, preferred_element_type=jnp.float32).astype(
        jnp.bfloat16
    )
    dout_heads = d_attended.reshape(tok_rows, local_heads, HEAD_DIM)
    row_delta = jnp.sum(dout_heads.astype(jnp.float32) * attended, axis=2).T

    def query_step(frame_idx, running):
        scores, allowed, key_block, value_block = frame_scores(frame_idx)
        attn_prob = soft_weights(scores, allowed)
        d_prob = jnp.einsum(
            "qhd,khd->hqk", dout_heads, value_block, preferred_element_type=jnp.float32
        )
        d_scores = (attn_prob * (d_prob - row_delta[:, :, None])).astype(jnp.bfloat16)
        return running + jnp.einsum(
            "hqk,khd->qhd", d_scores, key_block, preferred_element_type=jnp.float32
        )

    query_sum = lax.fori_loop(
        0, frame_limit, query_step, jnp.zeros((tok_rows, local_heads, HEAD_DIM), jnp.float32)
    )
    d_query = (query_sum * score_scale).reshape(tok_rows, local_inner).astype(jnp.bfloat16)

    def one_frame(frame_step):
        scores, allowed, key_block, value_block = frame_scores(frame_step)
        attn_prob = soft_weights(scores, allowed)
        d_prob = jnp.einsum(
            "qhd,khd->hqk", dout_heads, value_block, preferred_element_type=jnp.float32
        )
        d_scores = (attn_prob * (d_prob - row_delta[:, :, None])).astype(jnp.bfloat16)
        key_term = (
            jnp.einsum("hqk,qhd->khd", d_scores, query_heads, preferred_element_type=jnp.float32)
            * score_scale
        )
        value_term = jnp.einsum(
            "hqk,qhd->khd",
            attn_prob.astype(jnp.bfloat16),
            dout_heads,
            preferred_element_type=jnp.float32,
        )
        return jnp.concatenate(
            [key_term.reshape(FRAME_TOK, local_inner), value_term.reshape(FRAME_TOK, local_inner)],
            axis=1,
        )

    blocks = lax.map(
        one_frame, jnp.arange(tok_rows * lax.axis_size("seq") // FRAME_TOK, dtype=jnp.int32)
    )
    kv_grad = lax.psum_scatter(
        blocks.reshape(tok_rows * lax.axis_size("seq"), 2 * local_inner).astype(jnp.bfloat16),
        "seq",
        scatter_dimension=0,
        tiled=True,
    ).astype(jnp.float32)
    d_key = kv_grad[:, :local_inner].astype(jnp.bfloat16)
    d_value = kv_grad[:, local_inner:].astype(jnp.bfloat16)
    grad_query = jnp.einsum("td,ti->di", first_in, d_query, preferred_element_type=jnp.float32)
    grad_key = jnp.einsum("td,ti->di", first_in, d_key, preferred_element_type=jnp.float32)
    grad_value = jnp.einsum("td,ti->di", first_in, d_value, preferred_element_type=jnp.float32)
    first_local = jnp.einsum("ti,di->td", d_query, query_w, preferred_element_type=jnp.float32)
    first_local = first_local + jnp.einsum(
        "ti,di->td", d_key, key_w, preferred_element_type=jnp.float32
    )
    first_local = first_local + jnp.einsum(
        "ti,di->td", d_value, value_w, preferred_element_type=jnp.float32
    )
    d_first = heads_total(first_local)
    grad_first_gain = jnp.sum(d_first * normed_one, axis=0)
    norm_pull_one = jax.vjp(norm_rows, resid_in)[1]
    grad_inputs = (d_mid + norm_pull_one(d_first * gain_one.astype(jnp.float32))[0]).astype(
        jnp.bfloat16
    )[None]
    summed_in = (
        lax.psum_scatter(
            grad_first_gain.astype(jnp.bfloat16), ("dp", "seq"), scatter_dimension=0, tiled=True
        ).astype(jnp.float32),
        lax.psum_scatter(
            grad_query.astype(jnp.bfloat16), ("dp", "seq"), scatter_dimension=0, tiled=True
        ).astype(jnp.float32),
        lax.psum_scatter(
            grad_key.astype(jnp.bfloat16), ("dp", "seq"), scatter_dimension=0, tiled=True
        ).astype(jnp.float32),
        lax.psum_scatter(
            grad_value.astype(jnp.bfloat16), ("dp", "seq"), scatter_dimension=0, tiled=True
        ).astype(jnp.float32),
        lax.psum_scatter(
            grad_second_gain.astype(jnp.bfloat16), ("dp", "seq"), scatter_dimension=0, tiled=True
        ).astype(jnp.float32),
        lax.psum_scatter(
            grad_up.astype(jnp.bfloat16), ("dp", "seq"), scatter_dimension=0, tiled=True
        ).astype(jnp.float32),
    )
    summed_out = (
        lax.psum_scatter(
            grad_out.astype(jnp.bfloat16), ("dp", "seq"), scatter_dimension=1, tiled=True
        ).astype(jnp.float32),
        lax.psum_scatter(
            grad_down.astype(jnp.bfloat16), ("dp", "seq"), scatter_dimension=1, tiled=True
        ).astype(jnp.float32),
    )
    return (
        result,
        grad_inputs,
        summed_in[0],
        summed_in[1],
        summed_in[2],
        summed_in[3],
        summed_out[0],
        summed_in[4],
        summed_in[5],
        summed_out[1],
    )


def axes_of():
    dp, z, t = lax.axis_index("dp"), lax.axis_index("seq"), lax.axis_index("tensor")
    other_dp, chip, core = {"dp": 1 - dp}, {"tensor": lax.rem(t + 2, 4)}, {"tensor": t + 1 - 2 * lax.rem(t, 2)}
    pair = {"seq": z + 1 - 2 * lax.rem(z, 2)}
    return dp, z, t, other_dp, chip, core, pair


class Copies:
    def __init__(self, send, recv):
        self.send, self.recv, self.all, self.came, self.left = send, recv, [], [], []

    def make(self, src, dst, device):
        i = len(self.all)
        copy = pltpu.make_async_remote_copy(src_ref=src, dst_ref=dst, send_sem=self.send.at[i], recv_sem=self.recv.at[i], device_id=device, device_id_type=MESH)
        self.all.append(copy)
        return copy

    def wait(self, *copies):
        for copy in copies:
            if not any(copy is done for done in self.came):
                copy.wait_recv()
                self.came.append(copy)

    def flush(self, *copies):
        for copy in copies:
            if not any(copy is done for done in self.left):
                copy.wait_send()
                self.left.append(copy)

    def finish(self):
        self.wait(*self.all)
        self.flush(*self.all)


def column(row_ref):
    row = jnp.broadcast_to(row_ref[...].astype(jnp.float32), (8, row_ref.shape[1]))
    return row.T[:, 0:1]


def greet(peers):
    barrier = pltpu.get_barrier_semaphore()
    for peer in peers:
        pl.semaphore_signal(barrier, inc=1, device_id=peer, device_id_type=MESH)
    pl.semaphore_wait(barrier, len(peers))


def front_kernel(
    x_ref, w_query_ref, w_key_ref, w_value_ref, w_out_ref, w_up_ref, w_down_ref, gain_one_ref, gain_two_ref, cot_ref, valid_ref,
    whole_ref, w_head_ref, qkv_ref, att_ref, lse_ref, attended_ref, out_ref, resid_ref, normed_ref, rate_ref, second_ref, up_ref, down_ref, cots_ref,
    tokens, frames, w_own, w_head, up_own, out_all, att_low, came, part_low, core_in, half_low, chip_in, second, peak, total, acc, send, recv, local_sem,
):
    f32, bf16 = jnp.float32, jnp.bfloat16
    dp, z, t, other_dp, chip, core, pair = axes_of()
    rows, width = x_ref.shape
    quarter, half = rows // 4, rows // 2
    part, hidden = w_up_ref.shape
    side = hidden // 2
    copies = Copies(send, recv)
    kept = []

    def keep(src, dst):
        copy = pltpu.make_async_copy(src, dst, local_sem.at[len(kept)])
        kept.append(copy)
        copy.start()
        return copy

    def along(k):
        return {"seq": lax.rem(z + k + SEQ, SEQ)}

    def owner(k):
        return (dp * SEQ + lax.rem(z - k + SEQ, SEQ)) * part

    mate = t + 1 - 2 * lax.rem(t, 2)
    quarters = [t, lax.rem(t + 2, 4), mate, lax.rem(mate + 2, 4)]
    load_tokens = [keep(x_ref.at[pl.ds(quarters[n] * quarter, quarter), :], tokens.at[pl.ds(n * quarter, quarter), :]) for n in range(4)]
    keep_cots = [keep(cot_ref.at[pl.ds(quarters[n] * quarter, quarter), :], cots_ref.at[pl.ds(n * quarter, quarter), :]) for n in range(4)]
    own_out = keep(w_out_ref, out_all.at[:, pl.ds(owner(0), part)])
    keep(w_down_ref.at[pl.ds(lax.rem(z, 2) * side, side), :], down_ref.at[:, pl.ds(owner(0), part)])
    greet([other_dp, chip, core] + [along(k) for k in range(1, SEQ)])

    first = slice(0, quarter)

    def rows_at(n, count=1):
        return pl.ds(n * quarter, count * quarter)

    token = [None] + [copies.make(frames.at[k - 1, rows_at(0), :], frames.at[k, rows_at(0), :], along(1)) for k in range(1, SEQ)]
    token_chip = [None] + [copies.make(frames.at[k, rows_at(0), :], frames.at[k, rows_at(1), :], chip) for k in range(1, SEQ)]
    token_core = [None] + [copies.make(frames.at[k, rows_at(0, 2), :], frames.at[k, rows_at(2, 2), :], core) for k in range(1, SEQ)]
    head = [None] + [copies.make(w_own.at[lax.rem(z + k, SEQ)], w_head.at[pl.ds(owner(0), part), :], along(k)) for k in range(1, SEQ)]
    mine = pl.ds(dp * SEQ * part, SEQ * part)
    head_dp = copies.make(w_head.at[mine, :], w_head.at[mine, :], other_dp)

    def gather(source, at):
        step = [None] + [copies.make(source(lax.rem(z + k, 2)), at(owner(0)), along(k)) for k in range(1, SEQ)]
        cross = [copies.make(at(owner(k)) if k else source(lax.rem(z, 2)), at(owner(k)), other_dp) for k in range(SEQ)]
        return step, cross

    out_step, out_dp = gather(lambda h: w_out_ref, lambda c: out_all.at[:, pl.ds(c, part)])
    up_step, up_dp = gather(lambda h: up_own.at[h], lambda c: up_ref.at[pl.ds(c, part), :])
    down_step, down_dp = gather(lambda h: w_down_ref.at[pl.ds(h * side, side), :], lambda c: down_ref.at[:, pl.ds(c, part)])
    first_back = len(copies.all) - 1
    back_home = [None] + [copies.make(att_low.at[k], came.at[k], along(-k)) for k in range(1, SEQ)]
    sum_core = copies.make(part_low.at[rows_at(2, 2), :], core_in, core)
    sum_chip = copies.make(half_low, chip_in, chip)
    second_pair = copies.make(second.at[rows_at(0), :], second.at[rows_at(4), :], pair)
    second_chip = [copies.make(second.at[rows_at(4 * n), :], second.at[rows_at(4 * n + 1), :], chip) for n in range(2)]
    second_core = [copies.make(second.at[rows_at(4 * n, 2), :], second.at[rows_at(4 * n + 2, 2), :], core) for n in range(2)]
    cot_pair = copies.make(cot_ref.at[pl.ds(t * quarter, quarter), :], cots_ref.at[rows_at(4), :], pair)
    cot_chip = copies.make(cots_ref.at[rows_at(4), :], cots_ref.at[rows_at(5), :], chip)
    cot_core = copies.make(cots_ref.at[rows_at(4, 2), :], cots_ref.at[rows_at(6, 2), :], core)

    def norm_piece(n, carry):
        values = tokens[rows_at(n), :].astype(f32)
        center = values - jnp.mean(values, axis=1, keepdims=True)
        frames[0, rows_at(n), :] = (center * lax.rsqrt(jnp.mean(center * center, axis=1, keepdims=True) + NORM_EPS)).astype(bf16)
        return carry

    out_dp[0].start()
    down_dp[0].start()
    load_tokens[0].wait()
    lax.fori_loop(0, 1, norm_piece, 0)
    token[1].start()
    gain = column(gain_one_ref)
    for h in range(SEQ):
        at = slice(h * HEAD_DIM, (h + 1) * HEAD_DIM)
        for n, ref in enumerate((w_query_ref, w_key_ref, w_value_ref)):
            w_own[h, :, n * HEAD_DIM : (n + 1) * HEAD_DIM] = (ref[:, at].astype(f32) * gain).astype(bf16)
    for k in range(1, SEQ):
        head[k].start()
    w_head[pl.ds(owner(0), part), :] = w_own[z]
    gain = column(gain_two_ref)
    for h in range(2):
        up_own[h] = (w_up_ref[:, h * side : (h + 1) * side].astype(f32) * gain).astype(bf16)
    keep(up_own.at[lax.rem(z, 2)], up_ref.at[pl.ds(owner(0), part), :])
    for copy in load_tokens[1:]:
        copy.wait()
    lax.fori_loop(1, 4, norm_piece, 0)
    keep(frames.at[0], whole_ref.at[0])

    def arrive(copy, *then):
        copies.wait(copy)
        for one in then:
            one.start()

    def project(k):
        def piece(n, carry):
            qkv_ref[k, rows_at(n), :] = jnp.dot(frames[k, rows_at(n), :], w_head[...], preferred_element_type=f32).astype(bf16)
            return carry

        lax.fori_loop(0, 4, piece, 0)

    scale = HEAD_DIM ** (-0.5)

    def query_frame(i):
        at = lax.rem(z - i + SEQ, SEQ)
        query = qkv_ref[at, :, 0:HEAD_DIM]
        peak[...] = jnp.full_like(peak, MASK_FILL)
        total[...] = jnp.zeros_like(total)
        acc[...] = jnp.zeros_like(acc)

        def key_frame(j, inner):
            here = lax.rem(z - j + SEQ, SEQ)
            scores = lax.dot_general(qkv_ref[here, :, HEAD_DIM : 2 * HEAD_DIM], query, (((1,), (1,)), ((), ())), preferred_element_type=f32) * scale + (valid_ref[0, j] - 1).astype(f32) * -MASK_FILL
            before = peak[...]
            after = jnp.maximum(before, jnp.max(scores, axis=0, keepdims=True))
            terms = jnp.exp(scores - after)
            fix = jnp.exp(before - after)
            peak[...] = after
            total[...] = total[...] * fix + jnp.sum(terms, axis=0, keepdims=True)
            acc[...] = acc[...] * fix + lax.dot_general(qkv_ref[here, :, 2 * HEAD_DIM :], terms.astype(bf16), (((0,), (0,)), ((), ())), preferred_element_type=f32)
            return inner

        lax.fori_loop(0, i + 1, key_frame, 0)
        outcome = (acc[...] / total[...]).T
        att_ref[at] = outcome
        att_low[at] = outcome.astype(bf16)
        lse_ref[at] = peak[...] + jnp.log(total[...])

        @pl.when(at != 0)
        def _():
            pltpu.make_async_remote_copy(
                src_ref=att_low.at[at], dst_ref=came.at[at], send_sem=send.at[first_back + at], recv_sem=recv.at[first_back + at],
                device_id={"seq": i}, device_id_type=MESH,
            ).start()

    def mix(start):
        def piece(n, carry):
            at = pl.ds(pl.multiple_of(n * 512, 512), 512)
            part_low[pl.ds(start, half), at] = jnp.dot(attended_ref[pl.ds(start, half), :], out_all[:, at], preferred_element_type=f32).astype(bf16)
            return carry

        lax.fori_loop(0, width // 512, piece, 0)

    for k in range(1, SEQ):
        copies.wait(head[k])
    head_dp.start()
    arrive(token[1], token[2], token_chip[1])
    up_dp[0].start()
    arrive(token[2], token[3], token_chip[2], out_step[1])
    arrive(token_chip[1], token_core[1])
    copies.wait(head_dp)
    keep(w_head, w_head_ref)
    project(0)
    arrive(token_core[1])
    keep(frames.at[1], whole_ref.at[1])
    project(1)
    arrive(token_chip[2], token_core[2])
    arrive(token[3], token_chip[3], out_step[2], cot_pair)
    arrive(token_core[2])
    keep(frames.at[2], whole_ref.at[2])
    project(2)
    arrive(token_chip[3], token_core[3])
    arrive(token_core[3])
    keep(frames.at[3], whole_ref.at[3])
    project(3)
    query_frame(0)
    arrive(out_step[1], out_step[3], out_dp[1])
    query_frame(1)
    arrive(out_step[2], up_step[1], out_dp[2])
    arrive(cot_pair, cot_chip)
    query_frame(2)
    query_frame(3)
    came[0] = att_low[0]
    arrive(out_step[3], out_dp[3], up_step[2])
    copies.wait(*back_home[1:])
    for h in range(SEQ):
        attended_ref[:, h * HEAD_DIM : (h + 1) * HEAD_DIM] = came[lax.rem(h - z + SEQ, SEQ)]
    own_out.wait()
    copies.wait(*out_dp)
    keep(out_all, out_ref)

    mix(half)
    sum_core.start()
    mix(0)
    copies.wait(sum_core)
    half_low[...] = (part_low[quarter:half, :].astype(f32) + core_in[quarter:half, :].astype(f32)).astype(bf16)
    sum_chip.start()
    arrive(up_step[1], up_step[3], up_dp[1], down_step[1])
    arrive(cot_chip, cot_core)
    copies.wait(sum_chip)
    resid = tokens[first, :].astype(f32) + (part_low[first, :].astype(f32) + core_in[first, :].astype(f32)) + chip_in[...].astype(f32)
    center = resid - jnp.mean(resid, axis=1, keepdims=True)
    rate = lax.rsqrt(jnp.mean(center * center, axis=1, keepdims=True) + NORM_EPS)
    normed = center * rate
    second[first, :] = normed.astype(bf16)
    second_pair.start()
    second_chip[0].start()
    resid_ref[...] = resid
    rate_ref[...] = rate
    normed_ref[...] = normed
    arrive(up_step[2], down_step[2], up_dp[2])
    arrive(second_chip[0], second_core[0])
    arrive(second_pair, second_chip[1], down_step[3])
    arrive(up_step[3], up_dp[3])
    arrive(down_step[1], down_dp[1])
    arrive(second_chip[1], second_core[1])
    arrive(down_step[2], down_dp[2])
    arrive(down_step[3], down_dp[3])
    copies.wait(*second_core)
    keep(second, second_ref)
    copies.finish()
    for copy in kept:
        if not any(copy is done for done in [own_out] + load_tokens):
            copy.wait()


def front(x, w_query, w_key, w_value, w_out, w_up, w_down, gain_one, gain_two, cot, valid):
    rows, width = x.shape
    quarter, half = rows // 4, rows // 2
    part, hidden = w_up.shape
    inner = w_out.shape[0]
    three = 3 * HEAD_DIM
    f32, bf16 = jnp.float32, jnp.bfloat16
    any_, vmem = pl.BlockSpec(memory_space=pl.ANY), pl.BlockSpec(memory_space=pltpu.VMEM)
    shape = jax.ShapeDtypeStruct
    outs = [
        (shape((SEQ, rows, width), bf16), any_),
        (shape((width, three), bf16), any_),
        (shape((SEQ, rows, three), bf16), vmem),
        (shape((SEQ, rows, HEAD_DIM), f32), vmem),
        (shape((SEQ, 1, rows), f32), vmem),
        (shape((rows, inner), bf16), vmem),
        (shape((inner, width), bf16), any_),
        (shape((quarter, width), f32), vmem),
        (shape((quarter, width), f32), vmem),
        (shape((quarter, 1), f32), vmem),
        (shape((2 * rows, width), bf16), any_),
        (shape((width, hidden // 2), bf16), any_),
        (shape((hidden // 2, width), bf16), any_),
        (shape((2 * rows, width), bf16), any_),
    ]
    scratch = [
        ((rows, width), bf16),
        ((SEQ, rows, width), bf16),
        ((SEQ, part, three), bf16),
        ((width, three), bf16),
        ((2, part, hidden // 2), bf16),
        ((inner, width), bf16),
        ((SEQ, rows, HEAD_DIM), bf16),
        ((SEQ, rows, HEAD_DIM), bf16),
        ((rows, width), bf16),
        ((half, width), bf16),
        ((quarter, width), bf16),
        ((quarter, width), bf16),
        ((2 * rows, width), bf16),
        ((1, rows), f32),
        ((1, rows), f32),
        ((HEAD_DIM, rows), f32),
    ]
    count = 3 * 3 + 4 + 3 * 7 + 3 + 2 + 5 + 3
    return pl.pallas_call(
        front_kernel,
        out_shape=[o[0] for o in outs],
        in_specs=[any_] + [vmem] * 3 + [any_, vmem, any_, vmem, vmem, any_, pl.BlockSpec(memory_space=pltpu.SMEM)],
        out_specs=[o[1] for o in outs],
        scratch_shapes=[pltpu.VMEM(*one) for one in scratch] + [pltpu.SemaphoreType.DMA((count,)), pltpu.SemaphoreType.DMA((count,)), pltpu.SemaphoreType.DMA((24,))],
        compiler_params=pltpu.CompilerParams(collective_id=0, has_side_effects=True, vmem_limit_bytes=58 * 2**20),
        cost_estimate=pl.CostEstimate(flops=8 * 10**9, bytes_accessed=50 * 10**6, transcendentals=5 * 10**6),
    )(x, w_query, w_key, w_value, w_out, w_up, w_down, gain_one, gain_two, cot, valid)


def back_kernel(
    gd_ref, d_up_ref, second_ref, act_ref, down_ref, dn_ref, resid_ref, cots_ref, normed_two_ref, rate_two_ref, attended_ref, out_ref, qkv_ref, att_ref, lse_ref, valid_ref, w_head_ref, whole_ref, x_ref,
    w_query_ref, w_key_ref, w_value_ref, w_up_ref, gain_one_ref, gain_two_ref,
    down_sum_ref, up_sum_ref, out_sum_ref, grad_query_ref, grad_key_ref, grad_value_ref, gains_ref, grad_in_ref, result_ref,
    gu_ref, ff_ref, arrived_ref, cross_down_ref, cross_up_ref, far_down_ref, far_up_ref, dn_core_ref, dn_chip_ref, ff_core_ref, ff_chip_ref, pair_ref, first_core_ref, first_chip_ref, first_ring_ref,
    frames, temp, box_down, box_up, mix, d_head, d_out, dq, dk, dv, delta, d_three, out_send, out_cross, out_far, out_box,
    head_acc, head_low, head_cross, head_sum, held_a, held_b, half_box, pair_box, mid, quart_box, in_box, gain_box, gain_came,
    send, recv, keep_sem, load_sem, arena_sem, stage_sem,
):
    f32, bf16 = jnp.float32, jnp.bfloat16
    dp, z, t, other_dp, chip, core, pair = axes_of()
    rows, width = whole_ref.shape[1:]
    quarter, half = rows // 4, rows // 2
    part = width // (2 * SEQ)
    side = gd_ref.shape[1]
    inner = attended_ref.shape[1]
    copies = Copies(send, recv)
    scale = HEAD_DIM ** (-0.5)
    first, later = slice(0, quarter), slice(quarter, half)

    def along(k):
        return {"seq": lax.rem(z + k + SEQ, SEQ)}

    def load(*pairs):
        moves = [pltpu.make_async_copy(src, dst, load_sem.at[i]) for i, (src, dst) in enumerate(pairs)]
        for move in moves:
            move.start()
        for move in moves:
            move.wait()

    def block(side_dp, k):
        return pl.multiple_of((side_dp * SEQ + lax.rem(z - k + SEQ, SEQ)) * part, part)

    def rows_at(n, count=1):
        return pl.ds(n * quarter, count * quarter)

    greet([other_dp, chip, core] + [along(k) for k in range(1, SEQ)])

    def sums(part_ref, core_ref, chip_ref, n):
        to_core = [copies.make(part_ref.at[rows_at(4 * i + 2, 2), :], core_ref.at[i], core) for i in range(2)]
        to_chip = [copies.make(half_box.at[2 * n + i], chip_ref.at[i], chip) for i in range(2)]
        to_pair = copies.make(pair_box.at[n], pair_ref.at[n], pair)
        return to_core, to_chip, to_pair

    dn_core, dn_chip, dn_pair = sums(dn_ref, dn_core_ref, dn_chip_ref, 0)
    ff_core, ff_chip, ff_pair = sums(ff_ref, ff_core_ref, ff_chip_ref, 1)
    mix_chip = copies.make(mix.at[rows_at(0), :], mix.at[rows_at(1), :], chip)
    mix_core = copies.make(mix.at[rows_at(0, 2), :], mix.at[rows_at(2, 2), :], core)
    spread = [None] + [copies.make(d_head.at[lax.rem(z + k, SEQ)], d_out.at[k], along(k)) for k in range(1, SEQ)]
    cross_down = [copies.make(gd_ref.at[pl.ds(block(1 - dp, k), part), :], cross_down_ref.at[k], other_dp) for k in range(SEQ)]
    cross_up = [copies.make(gu_ref.at[pl.ds(block(1 - dp, k), part), :], cross_up_ref.at[k], other_dp) for k in range(SEQ)]
    cross_out = [copies.make(out_send.at[k], out_cross.at[k], other_dp) for k in range(SEQ)]
    far_down = [None] + [copies.make(box_down.at[k - 1], far_down_ref.at[k - 1], along(-k)) for k in range(1, SEQ)]
    far_up = [None] + [copies.make(box_up.at[k - 1], far_up_ref.at[k - 1], along(-k)) for k in range(1, SEQ)]
    far_out = [None] + [copies.make(out_box.at[k - 1], out_far.at[k - 1], along(-k)) for k in range(1, SEQ)]
    first_core = [copies.make(frames.at[k, rows_at(2, 2), :], first_core_ref.at[k], core) for k in range(SEQ)]
    first_chip = [copies.make(quart_box.at[k], first_chip_ref.at[k], chip) for k in range(SEQ)]
    first_ring = [None] + [copies.make(in_box.at[k - 1], first_ring_ref.at[k - 1], along(1)) for k in range(1, SEQ)]
    head_dp = copies.make(head_low.at[1 - dp], head_cross, other_dp)
    head_out = [None] + [copies.make(head_sum.at[lax.rem(z + k, SEQ)], arrived_ref.at[k], along(k)) for k in range(1, SEQ)]
    kept, numbered = [], []

    def publish(n, ref):
        mine = ref.at[pl.ds(t * quarter, quarter), :]
        mate = ref.at[pl.ds(lax.rem(t + 2, 4) * quarter, quarter), :]
        return [copies.make(half_box.at[n], mine, chip), copies.make(half_box.at[n], mine, core), copies.make(mate, mate, core)], (half_box.at[n], mine)

    gain_core = copies.make(gain_box.at[0], gain_came.at[0], core)
    gain_chip = copies.make(gain_box.at[1], gain_came.at[1], chip)
    result_out, result_own = publish(0, result_ref)
    grad_out_copies, grad_own = publish(1, grad_in_ref)

    def keep(src, dst):
        move = pltpu.make_async_copy(src, dst, keep_sem.at[SEQ + len(numbered)])
        numbered.append(move)
        kept.append(move)
        move.start()

    def half_of(part_ref, core_ref, to_core, to_chip, i, n):
        copies.wait(to_core[i])
        load((part_ref.at[rows_at(4 * i + 1), :], held_a.at[rows_at(0), :]), (core_ref.at[i, rows_at(1), :], held_a.at[rows_at(1), :]))
        half_box[2 * n + i] = (held_a[first, :].astype(f32) + held_a[later, :].astype(f32)).astype(bf16)
        to_chip[i].start()

    def quarter_of(part_ref, core_ref, chip_ref, to_chip, i, *more):
        copies.wait(to_chip[i])
        load(
            (part_ref.at[rows_at(4 * i), :], held_a.at[rows_at(0), :]), (core_ref.at[i, rows_at(0), :], held_a.at[rows_at(1), :]), (chip_ref.at[i], held_b.at[rows_at(0), :]),
            *more,
        )
        return (held_a[first, :].astype(f32) + held_a[later, :].astype(f32)) + held_b[first, :].astype(f32)

    def pair_sum(part_ref, core_ref, chip_ref, to_chip, to_pair, n):
        pair_box[n] = quarter_of(part_ref, core_ref, chip_ref, to_chip, 1).astype(bf16)
        to_pair.start()

    def own_sum(part_ref, core_ref, chip_ref, to_chip, to_pair, n, extra):
        copies.wait(to_pair)
        total = quarter_of(part_ref, core_ref, chip_ref, to_chip, 0, (pair_ref.at[n], held_b.at[rows_at(1), :]), (extra, spare))
        return total + held_b[later, :].astype(f32)

    def scatter(k, own_ref, cross_at, crossing, box, far, go=True):
        copies.wait(crossing)
        load((cross_at, temp.at[0]), (own_ref.at[pl.ds(block(dp, k), part), :], temp.at[1]))
        box[k - 1] = (temp[0].astype(f32) + temp[1].astype(f32)).astype(bf16)
        if go:
            far[k].start()

    def scatter_down(k):
        scatter(k, gd_ref, cross_down_ref.at[k], cross_down[k], box_down, far_down)

    def scatter_up(k, go=True):
        scatter(k, gu_ref, cross_up_ref.at[k], cross_up[k], box_up, far_up, go)

    same = pl.multiple_of(lax.rem(z, 2) * side, side)
    unlike = pl.multiple_of((1 - lax.rem(z, 2)) * side, side)

    def total_of(own_ref, cross_at, far_ref, far, crossing, store):
        copies.wait(crossing, *far[1:])
        load((cross_at, temp.at[0]), (own_ref.at[pl.ds(block(dp, 0), part), :], temp.at[1]), (far_ref.at[1], temp.at[2]))
        store(same, lambda at: (temp[0, :, at].astype(f32) + temp[1, :, at].astype(f32)) + temp[2, :, at].astype(f32))
        load((far_ref.at[0], temp.at[0]), (far_ref.at[2], temp.at[1]))
        store(unlike, lambda at: temp[0, :, at].astype(f32) + temp[1, :, at].astype(f32))

    def store_turned(base, value):
        for n in range(side // 256):
            down_sum_ref[pl.ds(base + n * 256, 256), :] = value(slice(n * 256, (n + 1) * 256)).T

    gain_sums = []

    def store_plain(base, value):
        raw = value(slice(0, side))
        gain_sums.append(jnp.sum(held_a[0:part, pl.ds(base, side)].astype(f32) * raw, axis=1, keepdims=True))
        up_sum_ref[:, pl.ds(base, side)] = raw * column(gain_two_ref)

    def out_block(start):
        return lax.dot_general(attended_ref[...], mix[:, pl.ds(start, part)], (((0,), (0,)), ((), ())), preferred_element_type=f32)

    def scatter_out(k):
        copies.wait(cross_out[k])
        out_box[k - 1] = (out_block(block(dp, k)) + out_cross[k].astype(f32)).astype(bf16)
        far_out[k].start()

    for copy in (dn_core[1], dn_core[0], cross_down[1]):
        copy.start()

    def place(*pairs):
        moves = [pltpu.make_async_copy(src, dst, arena_sem.at[i]) for i, (src, dst) in enumerate(pairs)]
        for move in moves:
            move.start()
        return moves

    def sides(ref, at):
        return [(ref.at[pl.ds(n * rows, rows), :], frames.at[at, :, pl.ds(n * side, side)]) for n in range(2)]

    arena = place(*sides(d_up_ref, 0), *sides(act_ref, 3), *[(second_ref.at[pl.ds(n * rows, rows), :], frames.at[1 + n]) for n in range(2)])
    spare = head_acc.at[pl.ds(0, quarter), :]
    half_of(dn_ref, dn_core_ref, dn_core, dn_chip, 1, 0)
    cross_down[2].start()
    load(*[(out_ref.at[pl.ds(h * HEAD_DIM, HEAD_DIM), :], quart_box.at[h, pl.ds(0, HEAD_DIM), :]) for h in range(SEQ)])
    for move in arena:
        move.wait()

    def up_piece(b, carry):
        at = pl.ds(pl.multiple_of(b * part, part), part)
        slot = lax.rem(b, 2)
        move = pltpu.make_async_copy(temp.at[slot], gu_ref.at[at, :], stage_sem.at[slot])

        @pl.when(lax.rem(b, SEQ) >= 2)
        def _():
            move.wait()

        turned = (((0,), (0,)), ((), ()))
        value = lax.dot_general(frames[1, :, at], frames[0, :, 0:side], turned, preferred_element_type=f32)
        value = value + lax.dot_general(frames[2, :, at], frames[0, :, side:], turned, preferred_element_type=f32)
        temp[slot] = value.astype(bf16)
        move.start()
        return carry

    lax.fori_loop(0, SEQ, up_piece, 0)
    for slot in range(2):
        pltpu.make_async_copy(temp.at[slot], gu_ref.at[pl.ds(0, part), :], stage_sem.at[slot]).wait()
    scatter_down(1)
    cross_down[3].start()
    lax.fori_loop(SEQ, 2 * SEQ, up_piece, 0)
    for slot in range(2):
        pltpu.make_async_copy(temp.at[slot], gu_ref.at[pl.ds(0, part), :], stage_sem.at[slot]).wait()
    arena = place((down_ref.at[pl.ds(0, rows), :], frames.at[1]), (down_ref.at[pl.ds(rows, side - rows), :], frames.at[2, pl.ds(0, side - rows), :]))
    copies.wait(dn_chip[1])
    half_of(dn_ref, dn_core_ref, dn_core, dn_chip, 0, 0)
    pair_sum(dn_ref, dn_core_ref, dn_chip_ref, dn_chip, dn_pair, 0)
    cross_up[1].start()
    scatter_down(2)
    grad = own_sum(dn_ref, dn_core_ref, dn_chip_ref, dn_chip, dn_pair, 0, normed_two_ref)
    normed = spare[...]
    grad = rate_two_ref[...] * (grad - jnp.mean(grad, axis=1, keepdims=True) - normed * jnp.mean(grad * normed, axis=1, keepdims=True))
    load((cots_ref.at[rows_at(0), :], held_a.at[rows_at(0), :]))
    grad = held_a[first, :].astype(f32) + grad
    mid[...] = grad
    mix[first, :] = grad.astype(bf16)
    mix_chip.start()
    scatter_down(3)
    for copy in (cross_up[2], cross_up[3], cross_up[0], cross_down[0]):
        copy.start()
    scatter_up(1)
    copies.wait(mix_chip)
    mix_core.start()

    def to_head(k, at):
        h = lax.rem(z + k, SEQ)
        d_head[h, at, :] = lax.dot_general(mix[at, :], quart_box[h, 0:HEAD_DIM, :], (((1,), (1,)), ((), ())), preferred_element_type=f32).astype(bf16)

    for k in (1, 2, 3, 0):
        to_head(k, slice(0, half))
    copies.wait(mix_core)
    for k in (1, 2, 3, 0):
        to_head(k, slice(half, rows))
        if k:
            spread[k].start()
    d_out[0] = d_head[z]
    for move in arena:
        move.wait()

    def ff_piece(n, carry):
        at = pl.ds(n * quarter, quarter)
        slot = lax.rem(n, 2)
        stage = held_b.at[pl.ds(slot * quarter, quarter), :]
        move = pltpu.make_async_copy(stage, ff_ref.at[at, :], stage_sem.at[slot])

        @pl.when(n >= 2)
        def _():
            move.wait()

        left = frames[3, pl.ds(lax.rem(n, 4) * quarter, quarter), pl.ds(pl.multiple_of(n // 4 * side, side), side)]
        value = jnp.dot(left[:, 0:rows], frames[1], preferred_element_type=f32)
        value = value + jnp.dot(left[:, rows:], frames[2, 0 : side - rows, :], preferred_element_type=f32)
        held_b[pl.ds(slot * quarter, quarter), :] = value.astype(bf16)
        move.start()
        return carry

    lax.fori_loop(0, 8, ff_piece, 0)
    for slot in range(2):
        pltpu.make_async_copy(held_b.at[pl.ds(slot * quarter, quarter), :], ff_ref.at[pl.ds(0, quarter), :], stage_sem.at[slot]).wait()
    ff_core[1].start()
    ff_core[0].start()
    fetch = [pltpu.make_async_copy(whole_ref.at[k], frames.at[k], keep_sem.at[k]) for k in range(SEQ)]
    for move in fetch:
        move.start()
    for k in (1, 2, 3, 0):
        out_send[k] = out_block(block(1 - dp, k)).astype(bf16)
        cross_out[k].start()
    half_of(ff_ref, ff_core_ref, ff_core, ff_chip, 1, 1)
    high = head_acc.shape[0]
    pieces = [(f, slice(0, high) if n == 0 else slice(high, rows), slice((2 * f + n) * HEAD_DIM, (2 * f + n + 1) * HEAD_DIM)) for f in range(SEQ) for n in range(2)]
    load(*[(att_ref.at[f, pl.ds(at.start, at.stop - at.start), :], head_acc.at[pl.ds(0, at.stop - at.start), pl.ds(lanes.start, HEAD_DIM)]) for f, at, lanes in pieces])
    scatter_up(2, False)
    scatter_up(3, False)
    copies.wait(*spread[1:])
    far_up[2].start()
    dq[...] = jnp.zeros_like(dq)
    for f, at, lanes in pieces:
        delta[f, :, at] = jnp.sum((d_out[f, at, :].astype(f32) * head_acc[0 : at.stop - at.start, lanes]).T, axis=0, keepdims=True)

    def key_frame(j):
        here = lax.rem(z - j + SEQ, SEQ)
        dk[...] = jnp.zeros_like(dk)
        dv[...] = jnp.zeros_like(dv)

        def query_frame(i, inner_):
            at = lax.rem(z - i + SEQ, SEQ)
            query, key, value = qkv_ref[at, :, :HEAD_DIM], qkv_ref[here, :, HEAD_DIM : 2 * HEAD_DIM], qkv_ref[here, :, 2 * HEAD_DIM :]
            grad_out = d_out[at]
            scores = lax.dot_general(key, query, (((1,), (1,)), ((), ())), preferred_element_type=f32) * scale + (valid_ref[0, j] - 1).astype(f32) * -MASK_FILL
            prob = jnp.exp(scores - lse_ref[at])
            d_prob = lax.dot_general(value, grad_out, (((1,), (1,)), ((), ())), preferred_element_type=f32)
            d_scores = (prob * (d_prob - delta[at])).astype(bf16)
            dv[...] += jnp.dot(prob.astype(bf16), grad_out, preferred_element_type=f32)
            dk[...] += jnp.dot(d_scores, query, preferred_element_type=f32)
            dq[at] += lax.dot_general(key, d_scores, (((0,), (0,)), ((), ())), preferred_element_type=f32)
            return inner_

        lax.fori_loop(j, SEQ, query_frame, 0)
        d_three[here, :, HEAD_DIM : 2 * HEAD_DIM] = (dk[...] * scale).astype(bf16)
        d_three[here, :, 2 * HEAD_DIM :] = dv[...].astype(bf16)

    key_frame(0)
    far_up[3].start()
    scatter_out(1)
    key_frame(1)
    half_of(ff_ref, ff_core_ref, ff_core, ff_chip, 0, 1)
    scatter_out(2)
    key_frame(2)
    key_frame(3)
    pair_sum(ff_ref, ff_core_ref, ff_chip_ref, ff_chip, ff_pair, 1)
    for f in range(SEQ):
        d_three[f, :, :HEAD_DIM] = (dq[f] * scale).T.astype(bf16)

    def project_back(k):
        fetch[k].wait()

        def piece(n, carry):
            at = pl.ds(pl.multiple_of(n * 512, 512), 512)
            term = lax.dot_general(d_three[k], frames[k, :, at], (((0,), (0,)), ((), ())), preferred_element_type=f32)
            head_acc[:, at] = term if k == 1 else head_acc[:, at] + term
            return carry

        lax.fori_loop(0, width // 512, piece, 0)

        def back_piece(n, carry):
            at = pl.ds(pl.multiple_of(n * 512, 512), 512)
            frames[k, :, at] = lax.dot_general(d_three[k], w_head_ref[at, :], (((1,), (1,)), ((), ())), preferred_element_type=f32).astype(bf16)
            return carry

        lax.fori_loop(0, width // 512, back_piece, 0)
        first_core[k].start()

    def half_sum(k):
        copies.wait(first_core[k])
        load((first_core_ref.at[k], held_a))
        quart_box[k] = (frames[k, later, :].astype(f32) + held_a[later, :].astype(f32)).astype(bf16)
        first_chip[k].start()
        frames[k, first, :] = (frames[k, first, :].astype(f32) + held_a[first, :].astype(f32)).astype(bf16)

    def quarter_sum(k):
        copies.wait(first_chip[k])
        pairs = [(first_chip_ref.at[k], held_a.at[rows_at(0), :])]
        if k != 1:
            before = (k - 1) % SEQ
            copies.wait(first_ring[before])
            pairs.append((first_ring_ref.at[before - 1], held_a.at[rows_at(1), :]))
        load(*pairs)
        sum_ = frames[k, first, :].astype(f32) + held_a[first, :].astype(f32)
        if k != 1:
            sum_ = sum_ + held_a[later, :].astype(f32)
        return sum_

    project_back(1)
    scatter_out(3)
    project_back(2)
    half_sum(1)
    project_back(3)
    project_back(0)
    for n in range(2):
        head_low[n] = head_acc[:, n * (width // 2) : (n + 1) * (width // 2)].astype(bf16)
    head_dp.start()
    half_sum(2)
    in_box[0] = quarter_sum(1).astype(bf16)
    first_ring[1].start()
    total_of(gd_ref, cross_down_ref.at[0], far_down_ref, far_down, cross_down[0], store_turned)
    half_sum(3)
    load((w_up_ref, held_a.at[pl.ds(0, part), :]))
    total_of(gu_ref, cross_up_ref.at[0], far_up_ref, far_up, cross_up[0], store_plain)
    in_box[1] = quarter_sum(2).astype(bf16)
    first_ring[2].start()
    half_sum(0)
    copies.wait(head_dp)
    for j in range(SEQ):
        at = slice(j * part, (j + 1) * part)
        head_sum[j] = (head_low[dp, :, at].astype(f32) + head_cross[:, at].astype(f32)).astype(bf16)
    keep(head_sum.at[z], arrived_ref.at[0])
    copies.wait(cross_out[0], *far_out[1:])
    sum_ = out_block(block(dp, 0)) + out_cross[0].astype(f32)
    for k in range(1, SEQ):
        sum_ = sum_ + out_far[k - 1].astype(f32)
    out_sum_ref[...] = sum_
    in_box[2] = quarter_sum(3).astype(bf16)
    first_ring[3].start()
    total = own_sum(ff_ref, ff_core_ref, ff_chip_ref, ff_chip, ff_pair, 1, resid_ref)
    copies.flush(*dn_chip)
    half_box[0] = (spare[...] + total).astype(bf16)
    result_out[0].start()
    result_out[1].start()
    keep(*result_own)
    load((x_ref.at[pl.ds(t * quarter, quarter), :], held_a.at[rows_at(0), :]))
    center = held_a[first, :].astype(f32)
    center = center - jnp.mean(center, axis=1, keepdims=True)
    rate = lax.rsqrt(jnp.mean(center * center, axis=1, keepdims=True) + NORM_EPS)
    head_acc[later, :] = center * rate
    for k in range(1, SEQ):
        head_out[k].start()
    grad = quarter_sum(0)
    normed = head_acc[later, :]
    grad = rate * (grad - jnp.mean(grad, axis=1, keepdims=True) - normed * jnp.mean(grad * normed, axis=1, keepdims=True))
    half_box[1] = (mid[...] + grad).astype(bf16)
    grad_out_copies[0].start()
    grad_out_copies[1].start()
    keep(*grad_own)
    copies.wait(result_out[0])
    result_out[2].start()
    copies.wait(*head_out[1:])
    kept.pop(0).wait()
    load(
        *[(arrived_ref.at[k], head_cross.at[:, pl.ds(k * part, part)]) for k in range(SEQ)],
        *[(ref, held_a.at[pl.ds(0, part), pl.ds(n * inner, inner)]) for n, ref in enumerate((w_query_ref, w_key_ref, w_value_ref))],
    )
    gain_first, gain = jnp.zeros((part, 1), f32), column(gain_one_ref)
    for h in range(SEQ):
        raw = head_cross[:, pl.ds(pl.multiple_of(lax.rem(z - h + SEQ, SEQ) * part, part), part)].astype(f32).T
        for n, ref in enumerate((grad_query_ref, grad_key_ref, grad_value_ref)):
            one = raw[:, n * HEAD_DIM : (n + 1) * HEAD_DIM]
            weight = held_a[0:part, n * inner + h * HEAD_DIM : n * inner + (h + 1) * HEAD_DIM].astype(f32)
            gain_first = gain_first + jnp.sum(weight * one, axis=1, keepdims=True)
            ref[:, h * HEAD_DIM : (h + 1) * HEAD_DIM] = one * gain
    lane = lax.broadcasted_iota(jnp.int32, (part, HEAD_DIM), 1)
    gain_box[0] = jnp.where(lane == 0, gain_first, gain_sums[0] + gain_sums[1])
    gain_core.start()
    copies.wait(gain_core)
    gain_box[1] = gain_box[0] + gain_came[0]
    gain_chip.start()
    copies.wait(grad_out_copies[0])
    grad_out_copies[2].start()
    copies.wait(gain_chip)
    gains_ref[...] = (gain_box[1] + gain_came[1]).T[0:8]
    copies.finish()
    for move in kept:
        move.wait()


def back(gd, d_up, second, act, down, dn, resid, cots, normed_two, rate_two, attended, out_rel, qkv, att, lse, valid, w_head, whole, x, w_query, w_key, w_value, w_up, gain_one, gain_two):
    rows, width = x.shape
    quarter, half = rows // 4, rows // 2
    part = width // (2 * SEQ)
    inner = attended.shape[1]
    side = gd.shape[1]
    three = 3 * HEAD_DIM
    f32, bf16 = jnp.float32, jnp.bfloat16
    any_, vmem = pl.BlockSpec(memory_space=pl.ANY), pl.BlockSpec(memory_space=pltpu.VMEM)
    shape = jax.ShapeDtypeStruct
    outs = [
        (shape((2 * side, part), f32), vmem),
        (shape((part, 2 * side), f32), vmem),
        (shape((inner, part), f32), vmem),
        (shape((part, inner), f32), vmem),
        (shape((part, inner), f32), vmem),
        (shape((part, inner), f32), vmem),
        (shape((8, part), f32), vmem),
        (shape((rows, width), bf16), any_),
        (shape((rows, width), bf16), any_),
        (shape((width, side), bf16), any_),
        (shape((2 * rows, width), bf16), any_),
        (shape((SEQ, three, part), bf16), any_),
        (shape((SEQ, part, side), bf16), any_),
        (shape((SEQ, part, side), bf16), any_),
        (shape((SEQ - 1, part, side), bf16), any_),
        (shape((SEQ - 1, part, side), bf16), any_),
        (shape((2, half, width), bf16), any_),
        (shape((2, quarter, width), bf16), any_),
        (shape((2, half, width), bf16), any_),
        (shape((2, quarter, width), bf16), any_),
        (shape((2, quarter, width), bf16), any_),
        (shape((SEQ, half, width), bf16), any_),
        (shape((SEQ, quarter, width), bf16), any_),
        (shape((SEQ - 1, quarter, width), bf16), any_),
    ]
    count = 10 + 2 + 3 + 4 + 4 + 4 + 9 + 8 + 3 + 4 + 6 + 2
    scratch = [
        ((SEQ, rows, width), bf16),
        ((3, part, side), bf16),
        ((SEQ - 1, part, side), bf16),
        ((SEQ - 1, part, side), bf16),
        ((rows, width), bf16),
        ((SEQ, rows, HEAD_DIM), bf16),
        ((SEQ, rows, HEAD_DIM), bf16),
        ((SEQ, HEAD_DIM, rows), f32),
        ((rows, HEAD_DIM), f32),
        ((rows, HEAD_DIM), f32),
        ((SEQ, 1, rows), f32),
        ((SEQ, rows, three), bf16),
        ((SEQ, inner, part), bf16),
        ((SEQ, inner, part), bf16),
        ((SEQ - 1, inner, part), bf16),
        ((SEQ - 1, inner, part), bf16),
        ((three, width), f32),
        ((2, three, width // 2), bf16),
        ((three, width // 2), bf16),
        ((SEQ, three, part), bf16),
        ((half, width), bf16),
        ((half, width), bf16),
        ((4, quarter, width), bf16),
        ((2, quarter, width), bf16),
        ((quarter, width), f32),
        ((SEQ, quarter, width), bf16),
        ((SEQ - 1, quarter, width), bf16),
        ((2, part, HEAD_DIM), f32),
        ((2, part, HEAD_DIM), f32),
    ]
    return pl.pallas_call(
        back_kernel,
        out_shape=[o[0] for o in outs],
        in_specs=[any_] * 9 + [vmem, vmem, any_, vmem, any_, vmem, pl.BlockSpec(memory_space=pltpu.SMEM), vmem] + [any_] * 6 + [vmem] * 2,
        out_specs=[o[1] for o in outs],
        scratch_shapes=[pltpu.VMEM(*one) for one in scratch]
        + [pltpu.SemaphoreType.DMA((count,)), pltpu.SemaphoreType.DMA((count,)), pltpu.SemaphoreType.DMA((SEQ + 3,)), pltpu.SemaphoreType.DMA((8,)), pltpu.SemaphoreType.DMA((6,)), pltpu.SemaphoreType.DMA((2,))],
        compiler_params=pltpu.CompilerParams(collective_id=1, has_side_effects=True, vmem_limit_bytes=62 * 2**20),
        cost_estimate=pl.CostEstimate(flops=20 * 10**9, bytes_accessed=60 * 10**6, transcendentals=5 * 10**6),
    )(gd, d_up, second, act, down, dn, resid, cots, normed_two, rate_two, attended, out_rel, qkv, att, lse, valid, w_head, whole, x, w_query, w_key, w_value, w_up, gain_one, gain_two)[:9]


def mm(left, right, dims=((1,), (0,)), out=jnp.bfloat16):
    return lax.dot_general(left, right, (dims, ((), ())), preferred_element_type=jnp.float32).astype(out)


def local_fast(inputs, first_gain, w_query, w_key, w_value, w_out, second_gain, w_up, w_down, frame_mask, cotangent):
    rows = inputs.shape[1]
    f32, bf16 = jnp.float32, jnp.bfloat16
    gain_one, gain_two = first_gain[None], second_gain[None]
    valid = frame_mask
    whole, w_head, qkv, attended_f, lse, attended, out_all, resid_mid, normed_two, rate_two, second_in, up_side, down_side, cots = front(
        inputs[0], w_query, w_key, w_value, w_out, w_up, w_down, gain_one, gain_two, cotangent[0], valid
    )
    up_pre = mm(second_in, up_side, out=f32)
    cdf = 0.5 * (1.0 + lax.erf(up_pre * (0.5**0.5)))
    up_act = (up_pre * cdf).astype(bf16)
    slope = cdf + up_pre * jnp.exp(-0.5 * up_pre * up_pre) * ((2.0 * jnp.pi) ** -0.5)
    grad_down = mm(cots, up_act, ((0,), (0,)))
    d_up = (mm(cots, down_side, ((1,), (1,)), f32) * slope).astype(bf16)
    d_normed_two = mm(d_up, up_side, ((1,), (1,)))
    down_sum, up_sum, out_sum, grad_query, grad_key, grad_value, gains, grad_in, result = back(
        grad_down, d_up, second_in, up_act, down_side, d_normed_two, resid_mid, cots, normed_two, rate_two, attended, out_all, qkv, attended_f, lse, valid, w_head, whole, inputs[0],
        w_query, w_key, w_value, w_up, gain_one, gain_two,
    )
    return (result[None], grad_in[None], gains[0], grad_query, grad_key, grad_value, out_sum, gains[1], up_sum, down_sum)


SEQ = 4


def solution(mesh):
    placed = (
        P("dp", "seq", None),
        P(("dp", "seq")),
        P(("dp", "seq"), "tensor"),
        P(("dp", "seq"), "tensor"),
        P(("dp", "seq"), "tensor"),
        P("tensor", ("dp", "seq")),
        P(("dp", "seq")),
        P(("dp", "seq"), "tensor"),
        P("tensor", ("dp", "seq")),
        P("dp", None),
        P("dp", "seq", None),
    )
    sizes = dict(mesh.shape)
    spread = sizes == {"dp": 2, "seq": SEQ, "tensor": 4}
    return jax.shard_map(
        local_fast if spread else local,
        mesh=mesh,
        in_specs=placed,
        out_specs=(
            P("dp", "seq", None),
            P("dp", "seq", None),
            P(("dp", "seq")),
            P(("dp", "seq"), "tensor"),
            P(("dp", "seq"), "tensor"),
            P(("dp", "seq"), "tensor"),
            P("tensor", ("dp", "seq")),
            P(("dp", "seq")),
            P(("dp", "seq"), "tensor"),
            P("tensor", ("dp", "seq")),
        ),
        check_vma=False,
    )
```

```python
import functools

import jax
import jax.numpy as jnp
from jax import lax
from jax.experimental import pallas as pl
from jax.experimental.pallas import tpu as pltpu
from jax.sharding import PartitionSpec as P

HEAD_DIM = 128
FRAME_TOK = 640


NORM_EPS = 1e-05
MASK_FILL = -1e30
MESH = pl.DeviceIdType.MESH


def norm_rows(values):
    center = values - jnp.mean(values, axis=-1, keepdims=True)
    spread = jnp.mean(center * center, axis=-1, keepdims=True)
    return center * lax.rsqrt(spread + NORM_EPS)


def gelu_exact(values):
    return jax.nn.gelu(values, approximate=False)


def heads_total(values):
    return lax.psum(values.astype(jnp.bfloat16), "tensor").astype(jnp.float32)


def local(
    inputs,
    first_gain,
    w_query,
    w_key,
    w_value,
    w_out,
    second_gain,
    w_up,
    w_down,
    frame_mask,
    cotangent,
):
    seq_pos = lax.axis_index("seq")
    gain_one, query_w, key_w, value_w, gain_two, up_w = (
        lax.all_gather(first_gain, ("dp", "seq"), axis=0, tiled=True),
        lax.all_gather(w_query, ("dp", "seq"), axis=0, tiled=True),
        lax.all_gather(w_key, ("dp", "seq"), axis=0, tiled=True),
        lax.all_gather(w_value, ("dp", "seq"), axis=0, tiled=True),
        lax.all_gather(second_gain, ("dp", "seq"), axis=0, tiled=True),
        lax.all_gather(w_up, ("dp", "seq"), axis=0, tiled=True),
    )
    out_w, down_w = (
        lax.all_gather(w_out, ("dp", "seq"), axis=1, tiled=True),
        lax.all_gather(w_down, ("dp", "seq"), axis=1, tiled=True),
    )
    tok_rows = inputs.shape[1]
    local_inner = query_w.shape[1]
    local_heads = local_inner // HEAD_DIM
    frames_dev = tok_rows // FRAME_TOK
    score_scale = HEAD_DIM ** (-0.5)
    clip_valid = frame_mask[0]
    frame_count = clip_valid.shape[0]
    resid_in = inputs[0].astype(jnp.float32)
    dout_rows = cotangent[0]
    row_frame = seq_pos * frames_dev + jnp.arange(tok_rows, dtype=jnp.int32) // FRAME_TOK
    frame_limit = (seq_pos + 1) * frames_dev
    normed_one = norm_rows(resid_in)
    first_in = (normed_one * gain_one.astype(jnp.float32)).astype(jnp.bfloat16)
    query = jnp.dot(first_in, query_w, preferred_element_type=jnp.float32).astype(jnp.bfloat16)
    key_local = jnp.dot(first_in, key_w, preferred_element_type=jnp.float32).astype(jnp.bfloat16)
    value_local = jnp.dot(first_in, value_w, preferred_element_type=jnp.float32).astype(
        jnp.bfloat16
    )
    key_all, value_all = (
        lax.all_gather(key_local, "seq", axis=0, tiled=True),
        lax.all_gather(value_local, "seq", axis=0, tiled=True),
    )
    query_heads = query.reshape(tok_rows, local_heads, HEAD_DIM)
    key_frames = key_all.reshape(frame_count, FRAME_TOK, local_heads, HEAD_DIM)
    value_frames = value_all.reshape(frame_count, FRAME_TOK, local_heads, HEAD_DIM)

    def frame_scores(frame_idx):
        key_block = lax.dynamic_index_in_dim(key_frames, frame_idx, 0, keepdims=False)
        value_block = lax.dynamic_index_in_dim(value_frames, frame_idx, 0, keepdims=False)
        scores = (
            jnp.einsum("qhd,khd->hqk", query_heads, key_block, preferred_element_type=jnp.float32)
            * score_scale
        )
        frame_ok = lax.dynamic_index_in_dim(clip_valid, frame_idx, 0, keepdims=False) == 1
        allowed = ((frame_idx <= row_frame) & frame_ok)[None, :, None]
        return (scores, allowed, key_block, value_block)

    def stats_step(frame_idx, running):
        row_max, row_sum = running
        scores, allowed, key_block, value_block = frame_scores(frame_idx)
        masked = jnp.where(allowed, scores, MASK_FILL)
        new_max = jnp.maximum(row_max, jnp.max(masked, axis=2))
        exp_terms = jnp.where(allowed, jnp.exp(masked - new_max[:, :, None]), 0.0)
        return (new_max, row_sum * jnp.exp(row_max - new_max) + jnp.sum(exp_terms, axis=2))

    start_stats = (
        jnp.full((local_heads, tok_rows), MASK_FILL, jnp.float32),
        jnp.zeros((local_heads, tok_rows), jnp.float32),
    )
    row_max, row_sum = lax.fori_loop(0, frame_limit, stats_step, start_stats)

    def soft_weights(scores, allowed):
        return jnp.where(allowed, jnp.exp(scores - row_max[:, :, None]) / row_sum[:, :, None], 0.0)

    def output_step(frame_idx, running):
        scores, allowed, key_block, value_block = frame_scores(frame_idx)
        attn_prob = soft_weights(scores, allowed).astype(jnp.bfloat16)
        return running + jnp.einsum(
            "hqk,khd->qhd", attn_prob, value_block, preferred_element_type=jnp.float32
        )

    attended = lax.fori_loop(
        0, frame_limit, output_step, jnp.zeros((tok_rows, local_heads, HEAD_DIM), jnp.float32)
    )
    attended_low = attended.reshape(tok_rows, local_inner).astype(jnp.bfloat16)
    resid_mid = resid_in + heads_total(
        jnp.dot(attended_low, out_w, preferred_element_type=jnp.float32)
    )
    normed_two = norm_rows(resid_mid)
    second_in = (normed_two * gain_two.astype(jnp.float32)).astype(jnp.bfloat16)
    up_pre = jnp.dot(second_in, up_w, preferred_element_type=jnp.float32)
    up_act = gelu_exact(up_pre).astype(jnp.bfloat16)
    resid_out = resid_mid + heads_total(jnp.dot(up_act, down_w, preferred_element_type=jnp.float32))
    result = resid_out.astype(jnp.bfloat16)[None]
    grad_down = jnp.einsum("tf,td->fd", up_act, dout_rows, preferred_element_type=jnp.float32)
    d_act = jnp.einsum("td,fd->tf", dout_rows, down_w, preferred_element_type=jnp.float32)
    gelu_pull = jax.vjp(gelu_exact, up_pre)[1]
    d_up_pre = gelu_pull(d_act)[0].astype(jnp.bfloat16)
    grad_up = jnp.einsum("td,tf->df", second_in, d_up_pre, preferred_element_type=jnp.float32)
    d_second = heads_total(
        jnp.einsum("tf,df->td", d_up_pre, up_w, preferred_element_type=jnp.float32)
    )
    grad_second_gain = jnp.sum(d_second * normed_two, axis=0)
    norm_pull_two = jax.vjp(norm_rows, resid_mid)[1]
    d_mid = (
        dout_rows.astype(jnp.float32) + norm_pull_two(d_second * gain_two.astype(jnp.float32))[0]
    )
    d_mix = d_mid.astype(jnp.bfloat16)
    grad_out = jnp.einsum("ti,td->id", attended_low, d_mix, preferred_element_type=jnp.float32)
    d_attended = jnp.einsum("td,id->ti", d_mix, out_w, preferred_element_type=jnp.float32).astype(
        jnp.bfloat16
    )
    dout_heads = d_attended.reshape(tok_rows, local_heads, HEAD_DIM)
    row_delta = jnp.sum(dout_heads.astype(jnp.float32) * attended, axis=2).T

    def query_step(frame_idx, running):
        scores, allowed, key_block, value_block = frame_scores(frame_idx)
        attn_prob = soft_weights(scores, allowed)
        d_prob = jnp.einsum(
            "qhd,khd->hqk", dout_heads, value_block, preferred_element_type=jnp.float32
        )
        d_scores = (attn_prob * (d_prob - row_delta[:, :, None])).astype(jnp.bfloat16)
        return running + jnp.einsum(
            "hqk,khd->qhd", d_scores, key_block, preferred_element_type=jnp.float32
        )

    query_sum = lax.fori_loop(
        0, frame_limit, query_step, jnp.zeros((tok_rows, local_heads, HEAD_DIM), jnp.float32)
    )
    d_query = (query_sum * score_scale).reshape(tok_rows, local_inner).astype(jnp.bfloat16)

    def one_frame(frame_step):
        scores, allowed, key_block, value_block = frame_scores(frame_step)
        attn_prob = soft_weights(scores, allowed)
        d_prob = jnp.einsum(
            "qhd,khd->hqk", dout_heads, value_block, preferred_element_type=jnp.float32
        )
        d_scores = (attn_prob * (d_prob - row_delta[:, :, None])).astype(jnp.bfloat16)
        key_term = (
            jnp.einsum("hqk,qhd->khd", d_scores, query_heads, preferred_element_type=jnp.float32)
            * score_scale
        )
        value_term = jnp.einsum(
            "hqk,qhd->khd",
            attn_prob.astype(jnp.bfloat16),
            dout_heads,
            preferred_element_type=jnp.float32,
        )
        return jnp.concatenate(
            [key_term.reshape(FRAME_TOK, local_inner), value_term.reshape(FRAME_TOK, local_inner)],
            axis=1,
        )

    blocks = lax.map(
        one_frame, jnp.arange(tok_rows * lax.axis_size("seq") // FRAME_TOK, dtype=jnp.int32)
    )
    kv_grad = lax.psum_scatter(
        blocks.reshape(tok_rows * lax.axis_size("seq"), 2 * local_inner).astype(jnp.bfloat16),
        "seq",
        scatter_dimension=0,
        tiled=True,
    ).astype(jnp.float32)
    d_key = kv_grad[:, :local_inner].astype(jnp.bfloat16)
    d_value = kv_grad[:, local_inner:].astype(jnp.bfloat16)
    grad_query = jnp.einsum("td,ti->di", first_in, d_query, preferred_element_type=jnp.float32)
    grad_key = jnp.einsum("td,ti->di", first_in, d_key, preferred_element_type=jnp.float32)
    grad_value = jnp.einsum("td,ti->di", first_in, d_value, preferred_element_type=jnp.float32)
    first_local = jnp.einsum("ti,di->td", d_query, query_w, preferred_element_type=jnp.float32)
    first_local = first_local + jnp.einsum(
        "ti,di->td", d_key, key_w, preferred_element_type=jnp.float32
    )
    first_local = first_local + jnp.einsum(
        "ti,di->td", d_value, value_w, preferred_element_type=jnp.float32
    )
    d_first = heads_total(first_local)
    grad_first_gain = jnp.sum(d_first * normed_one, axis=0)
    norm_pull_one = jax.vjp(norm_rows, resid_in)[1]
    grad_inputs = (d_mid + norm_pull_one(d_first * gain_one.astype(jnp.float32))[0]).astype(
        jnp.bfloat16
    )[None]
    summed_in = (
        lax.psum_scatter(
            grad_first_gain.astype(jnp.bfloat16), ("dp", "seq"), scatter_dimension=0, tiled=True
        ).astype(jnp.float32),
        lax.psum_scatter(
            grad_query.astype(jnp.bfloat16), ("dp", "seq"), scatter_dimension=0, tiled=True
        ).astype(jnp.float32),
        lax.psum_scatter(
            grad_key.astype(jnp.bfloat16), ("dp", "seq"), scatter_dimension=0, tiled=True
        ).astype(jnp.float32),
        lax.psum_scatter(
            grad_value.astype(jnp.bfloat16), ("dp", "seq"), scatter_dimension=0, tiled=True
        ).astype(jnp.float32),
        lax.psum_scatter(
            grad_second_gain.astype(jnp.bfloat16), ("dp", "seq"), scatter_dimension=0, tiled=True
        ).astype(jnp.float32),
        lax.psum_scatter(
            grad_up.astype(jnp.bfloat16), ("dp", "seq"), scatter_dimension=0, tiled=True
        ).astype(jnp.float32),
    )
    summed_out = (
        lax.psum_scatter(
            grad_out.astype(jnp.bfloat16), ("dp", "seq"), scatter_dimension=1, tiled=True
        ).astype(jnp.float32),
        lax.psum_scatter(
            grad_down.astype(jnp.bfloat16), ("dp", "seq"), scatter_dimension=1, tiled=True
        ).astype(jnp.float32),
    )
    return (
        result,
        grad_inputs,
        summed_in[0],
        summed_in[1],
        summed_in[2],
        summed_in[3],
        summed_out[0],
        summed_in[4],
        summed_in[5],
        summed_out[1],
    )


def axes_of():
    dp, z, t = lax.axis_index("dp"), lax.axis_index("seq"), lax.axis_index("tensor")
    other_dp, chip, core = {"dp": 1 - dp}, {"tensor": lax.rem(t + 2, 4)}, {"tensor": t + 1 - 2 * lax.rem(t, 2)}
    pair = {"seq": z + 1 - 2 * lax.rem(z, 2)}
    return dp, z, t, other_dp, chip, core, pair


class Copies:
    def __init__(self, send, recv):
        self.send, self.recv, self.all, self.came, self.left = send, recv, [], [], []

    def make(self, src, dst, device):
        i = len(self.all)
        copy = pltpu.make_async_remote_copy(src_ref=src, dst_ref=dst, send_sem=self.send.at[i], recv_sem=self.recv.at[i], device_id=device, device_id_type=MESH)
        self.all.append(copy)
        return copy

    def wait(self, *copies):
        for copy in copies:
            if not any(copy is done for done in self.came):
                copy.wait_recv()
                self.came.append(copy)

    def flush(self, *copies):
        for copy in copies:
            if not any(copy is done for done in self.left):
                copy.wait_send()
                self.left.append(copy)

    def finish(self):
        self.wait(*self.all)
        self.flush(*self.all)


def column(row_ref):
    row = jnp.broadcast_to(row_ref[...].astype(jnp.float32), (8, row_ref.shape[1]))
    return row.T[:, 0:1]


def greet(peers):
    barrier = pltpu.get_barrier_semaphore()
    for peer in peers:
        pl.semaphore_signal(barrier, inc=1, device_id=peer, device_id_type=MESH)
    pl.semaphore_wait(barrier, len(peers))


def front_kernel(
    x_ref, w_query_ref, w_key_ref, w_value_ref, w_out_ref, w_up_ref, w_down_ref, gain_one_ref, gain_two_ref, cot_ref, valid_ref,
    whole_ref, w_head_ref, qkv_out, att_out, lse_ref, attended_out, out_ref, resid_out, normed_out, rate_ref, second_ref, up_ref, down_ref, cots_ref,
    tokens, frames, w_own, w_head, up_own, out_all, att_low, came, part_low, core_in, half_low, chip_in, second, peak, total, acc, qkv_ref, att_ref, attended_ref, resid_ref, normed_ref, send, recv, local_sem,
):
    f32, bf16 = jnp.float32, jnp.bfloat16
    dp, z, t, other_dp, chip, core, pair = axes_of()
    rows, width = x_ref.shape
    quarter, half = rows // 4, rows // 2
    part, hidden = w_up_ref.shape
    side = hidden // 2
    copies = Copies(send, recv)
    kept = []

    def keep(src, dst):
        copy = pltpu.make_async_copy(src, dst, local_sem.at[len(kept)])
        kept.append(copy)
        copy.start()
        return copy

    def along(k):
        return {"seq": lax.rem(z + k + SEQ, SEQ)}

    def owner(k):
        return (dp * SEQ + lax.rem(z - k + SEQ, SEQ)) * part

    mate = t + 1 - 2 * lax.rem(t, 2)
    quarters = [t, lax.rem(t + 2, 4), mate, lax.rem(mate + 2, 4)]
    load_tokens = [keep(x_ref.at[pl.ds(quarters[n] * quarter, quarter), :], tokens.at[pl.ds(n * quarter, quarter), :]) for n in range(4)]
    keep_cots = [keep(cot_ref.at[pl.ds(quarters[n] * quarter, quarter), :], cots_ref.at[pl.ds(n * quarter, quarter), :]) for n in range(4)]
    own_out = keep(w_out_ref, out_all.at[:, pl.ds(owner(0), part)])
    keep(w_down_ref.at[pl.ds(lax.rem(z, 2) * side, side), :], down_ref.at[:, pl.ds(owner(0), part)])
    greet([other_dp, chip, core] + [along(k) for k in range(1, SEQ)])

    first = slice(0, quarter)

    def rows_at(n, count=1):
        return pl.ds(n * quarter, count * quarter)

    token = [None] + [copies.make(frames.at[k - 1, rows_at(0), :], frames.at[k, rows_at(0), :], along(1)) for k in range(1, SEQ)]
    token_chip = [None] + [copies.make(frames.at[k, rows_at(0), :], frames.at[k, rows_at(1), :], chip) for k in range(1, SEQ)]
    token_core = [None] + [copies.make(frames.at[k, rows_at(0, 2), :], frames.at[k, rows_at(2, 2), :], core) for k in range(1, SEQ)]
    head = [None] + [copies.make(w_own.at[lax.rem(z + k, SEQ)], w_head.at[pl.ds(owner(0), part), :], along(k)) for k in range(1, SEQ)]
    mine = pl.ds(dp * SEQ * part, SEQ * part)
    head_dp = copies.make(w_head.at[mine, :], w_head.at[mine, :], other_dp)

    def gather(source, at):
        step = [None] + [copies.make(source(lax.rem(z + k, 2)), at(owner(0)), along(k)) for k in range(1, SEQ)]
        cross = [copies.make(at(owner(k)) if k else source(lax.rem(z, 2)), at(owner(k)), other_dp) for k in range(SEQ)]
        return step, cross

    out_step, out_dp = gather(lambda h: w_out_ref, lambda c: out_all.at[:, pl.ds(c, part)])
    up_step, up_dp = gather(lambda h: up_own.at[h], lambda c: up_ref.at[pl.ds(c, part), :])
    down_step, down_dp = gather(lambda h: w_down_ref.at[pl.ds(h * side, side), :], lambda c: down_ref.at[:, pl.ds(c, part)])
    first_back = len(copies.all) - 1
    back_home = [None] + [copies.make(att_low.at[k], came.at[k], along(-k)) for k in range(1, SEQ)]
    sum_core = copies.make(part_low.at[rows_at(2, 2), :], core_in, core)
    sum_chip = copies.make(half_low, chip_in, chip)
    second_pair = copies.make(second.at[rows_at(0), :], second.at[rows_at(4), :], pair)
    second_chip = [copies.make(second.at[rows_at(4 * n), :], second.at[rows_at(4 * n + 1), :], chip) for n in range(2)]
    second_core = [copies.make(second.at[rows_at(4 * n, 2), :], second.at[rows_at(4 * n + 2, 2), :], core) for n in range(2)]
    cot_pair = copies.make(cot_ref.at[pl.ds(t * quarter, quarter), :], cots_ref.at[rows_at(4), :], pair)
    cot_chip = copies.make(cots_ref.at[rows_at(4), :], cots_ref.at[rows_at(5), :], chip)
    cot_core = copies.make(cots_ref.at[rows_at(4, 2), :], cots_ref.at[rows_at(6, 2), :], core)

    def norm_piece(n, carry):
        values = tokens[rows_at(n), :].astype(f32)
        center = values - jnp.mean(values, axis=1, keepdims=True)
        frames[0, rows_at(n), :] = (center * lax.rsqrt(jnp.mean(center * center, axis=1, keepdims=True) + NORM_EPS)).astype(bf16)
        return carry

    out_dp[0].start()
    down_dp[0].start()
    load_tokens[0].wait()
    lax.fori_loop(0, 1, norm_piece, 0)
    token[1].start()
    gain = column(gain_one_ref)
    for h in range(SEQ):
        at = slice(h * HEAD_DIM, (h + 1) * HEAD_DIM)
        for n, ref in enumerate((w_query_ref, w_key_ref, w_value_ref)):
            w_own[h, :, n * HEAD_DIM : (n + 1) * HEAD_DIM] = (ref[:, at].astype(f32) * gain).astype(bf16)
    for k in range(1, SEQ):
        head[k].start()
    w_head[pl.ds(owner(0), part), :] = w_own[z]
    gain = column(gain_two_ref)
    for h in range(2):
        up_own[h] = (w_up_ref[:, h * side : (h + 1) * side].astype(f32) * gain).astype(bf16)
    keep(up_own.at[lax.rem(z, 2)], up_ref.at[pl.ds(owner(0), part), :])
    for copy in load_tokens[1:]:
        copy.wait()
    lax.fori_loop(1, 4, norm_piece, 0)
    keep(frames.at[0], whole_ref.at[0])

    def arrive(copy, *then):
        copies.wait(copy)
        for one in then:
            one.start()

    def project(k):
        def piece(n, carry):
            qkv_ref[k, rows_at(n), :] = jnp.dot(frames[k, rows_at(n), :], w_head[...], preferred_element_type=f32).astype(bf16)
            return carry

        lax.fori_loop(0, 4, piece, 0)

    scale = HEAD_DIM ** (-0.5)

    def query_frame(i):
        at = lax.rem(z - i + SEQ, SEQ)
        query = qkv_ref[at, :, 0:HEAD_DIM]
        peak[...] = jnp.full_like(peak, MASK_FILL)
        total[...] = jnp.zeros_like(total)
        acc[...] = jnp.zeros_like(acc)

        def key_frame(j, inner):
            here = lax.rem(z - j + SEQ, SEQ)
            scores = lax.dot_general(qkv_ref[here, :, HEAD_DIM : 2 * HEAD_DIM], query, (((1,), (1,)), ((), ())), preferred_element_type=f32) * scale + (valid_ref[0, j] - 1).astype(f32) * -MASK_FILL
            before = peak[...]
            after = jnp.maximum(before, jnp.max(scores, axis=0, keepdims=True))
            terms = jnp.exp(scores - after)
            fix = jnp.exp(before - after)
            peak[...] = after
            total[...] = total[...] * fix + jnp.sum(terms, axis=0, keepdims=True)
            acc[...] = acc[...] * fix + lax.dot_general(qkv_ref[here, :, 2 * HEAD_DIM :], terms.astype(bf16), (((0,), (0,)), ((), ())), preferred_element_type=f32)
            return inner

        lax.fori_loop(0, i + 1, key_frame, 0)
        outcome = (acc[...] / total[...]).T
        att_ref[at] = outcome
        att_low[at] = outcome.astype(bf16)
        lse_ref[at] = peak[...] + jnp.log(total[...])

        @pl.when(at != 0)
        def _():
            pltpu.make_async_remote_copy(
                src_ref=att_low.at[at], dst_ref=came.at[at], send_sem=send.at[first_back + at], recv_sem=recv.at[first_back + at],
                device_id={"seq": i}, device_id_type=MESH,
            ).start()

    def mix(start):
        def piece(n, carry):
            at = pl.ds(pl.multiple_of(n * 512, 512), 512)
            part_low[pl.ds(start, half), at] = jnp.dot(attended_ref[pl.ds(start, half), :], out_all[:, at], preferred_element_type=f32).astype(bf16)
            return carry

        lax.fori_loop(0, width // 512, piece, 0)

    for k in range(1, SEQ):
        copies.wait(head[k])
    head_dp.start()
    arrive(token[1], token[2], token_chip[1])
    up_dp[0].start()
    arrive(token[2], token[3], token_chip[2], out_step[1])
    arrive(token_chip[1], token_core[1])
    copies.wait(head_dp)
    keep(w_head, w_head_ref)
    project(0)
    arrive(token_core[1])
    keep(frames.at[1], whole_ref.at[1])
    project(1)
    arrive(token_chip[2], token_core[2])
    arrive(token[3], token_chip[3], out_step[2], cot_pair)
    arrive(token_core[2])
    keep(frames.at[2], whole_ref.at[2])
    project(2)
    arrive(token_chip[3], token_core[3])
    arrive(token_core[3])
    keep(frames.at[3], whole_ref.at[3])
    project(3)
    keep(qkv_ref, qkv_out)
    query_frame(0)
    arrive(out_step[1], out_step[3], out_dp[1])
    query_frame(1)
    arrive(out_step[2], up_step[1], out_dp[2])
    arrive(cot_pair, cot_chip)
    query_frame(2)
    query_frame(3)
    keep(att_ref, att_out)
    came[0] = att_low[0]
    arrive(out_step[3], out_dp[3], up_step[2])
    copies.wait(*back_home[1:])
    for h in range(SEQ):
        attended_ref[:, h * HEAD_DIM : (h + 1) * HEAD_DIM] = came[lax.rem(h - z + SEQ, SEQ)]
    keep(attended_ref, attended_out)
    own_out.wait()
    copies.wait(*out_dp)
    keep(out_all, out_ref)

    mix(half)
    sum_core.start()
    mix(0)
    copies.wait(sum_core)
    half_low[...] = (part_low[quarter:half, :].astype(f32) + core_in[quarter:half, :].astype(f32)).astype(bf16)
    sum_chip.start()
    arrive(up_step[1], up_step[3], up_dp[1], down_step[1])
    arrive(cot_chip, cot_core)
    copies.wait(sum_chip)
    resid = tokens[first, :].astype(f32) + (part_low[first, :].astype(f32) + core_in[first, :].astype(f32)) + chip_in[...].astype(f32)
    center = resid - jnp.mean(resid, axis=1, keepdims=True)
    rate = lax.rsqrt(jnp.mean(center * center, axis=1, keepdims=True) + NORM_EPS)
    normed = center * rate
    second[first, :] = normed.astype(bf16)
    second_pair.start()
    second_chip[0].start()
    resid_ref[...] = resid
    rate_ref[...] = rate
    normed_ref[...] = normed
    keep(resid_ref, resid_out)
    keep(normed_ref, normed_out)
    arrive(up_step[2], down_step[2], up_dp[2])
    arrive(second_chip[0], second_core[0])
    arrive(second_pair, second_chip[1], down_step[3])
    arrive(up_step[3], up_dp[3])
    arrive(down_step[1], down_dp[1])
    arrive(second_chip[1], second_core[1])
    arrive(down_step[2], down_dp[2])
    arrive(down_step[3], down_dp[3])
    copies.wait(*second_core)
    keep(second, second_ref)
    copies.finish()
    for copy in kept:
        if not any(copy is done for done in [own_out] + load_tokens):
            copy.wait()


def front(x, w_query, w_key, w_value, w_out, w_up, w_down, gain_one, gain_two, cot, valid):
    rows, width = x.shape
    quarter, half = rows // 4, rows // 2
    part, hidden = w_up.shape
    inner = w_out.shape[0]
    three = 3 * HEAD_DIM
    f32, bf16 = jnp.float32, jnp.bfloat16
    any_, vmem = pl.BlockSpec(memory_space=pl.ANY), pl.BlockSpec(memory_space=pltpu.VMEM)
    shape = jax.ShapeDtypeStruct
    outs = [
        (shape((SEQ, rows, width), bf16), any_),
        (shape((width, three), bf16), any_),
        (shape((SEQ, rows, three), bf16), any_),
        (shape((SEQ, rows, HEAD_DIM), f32), any_),
        (shape((SEQ, 1, rows), f32), vmem),
        (shape((rows, inner), bf16), any_),
        (shape((inner, width), bf16), any_),
        (shape((quarter, width), f32), any_),
        (shape((quarter, width), f32), any_),
        (shape((quarter, 1), f32), vmem),
        (shape((2 * rows, width), bf16), any_),
        (shape((width, hidden // 2), bf16), any_),
        (shape((hidden // 2, width), bf16), any_),
        (shape((2 * rows, width), bf16), any_),
    ]
    scratch = [
        ((rows, width), bf16),
        ((SEQ, rows, width), bf16),
        ((SEQ, part, three), bf16),
        ((width, three), bf16),
        ((2, part, hidden // 2), bf16),
        ((inner, width), bf16),
        ((SEQ, rows, HEAD_DIM), bf16),
        ((SEQ, rows, HEAD_DIM), bf16),
        ((rows, width), bf16),
        ((half, width), bf16),
        ((quarter, width), bf16),
        ((quarter, width), bf16),
        ((2 * rows, width), bf16),
        ((1, rows), f32),
        ((1, rows), f32),
        ((HEAD_DIM, rows), f32),
        ((SEQ, rows, three), bf16),
        ((SEQ, rows, HEAD_DIM), f32),
        ((rows, inner), bf16),
        ((quarter, width), f32),
        ((quarter, width), f32),
    ]
    count = 3 * 3 + 4 + 3 * 7 + 3 + 2 + 5 + 3
    return pl.pallas_call(
        front_kernel,
        out_shape=[o[0] for o in outs],
        in_specs=[any_] + [vmem] * 3 + [any_, vmem, any_, vmem, vmem, any_, pl.BlockSpec(memory_space=pltpu.SMEM)],
        out_specs=[o[1] for o in outs],
        scratch_shapes=[pltpu.VMEM(*one) for one in scratch] + [pltpu.SemaphoreType.DMA((count,)), pltpu.SemaphoreType.DMA((count,)), pltpu.SemaphoreType.DMA((24,))],
        compiler_params=pltpu.CompilerParams(collective_id=0, has_side_effects=True, vmem_limit_bytes=58 * 2**20),
        cost_estimate=pl.CostEstimate(flops=8 * 10**9, bytes_accessed=50 * 10**6, transcendentals=5 * 10**6),
    )(x, w_query, w_key, w_value, w_out, w_up, w_down, gain_one, gain_two, cot, valid)


def back_kernel(
    gd_ref, d_up_ref, second_ref, act_ref, down_ref, dn_ref, resid_ref, cots_ref, normed_two_ref, rate_two_ref, attended_ref, out_ref, qkv_ref, att_ref, lse_ref, valid_ref, w_head_ref, whole_ref, x_ref,
    w_query_ref, w_key_ref, w_value_ref, w_up_ref, gain_one_ref, gain_two_ref,
    down_sum_out, up_sum_out, out_sum_out, grad_query_out, grad_key_out, grad_value_out, gains_ref, grad_in_ref, result_ref,
    gu_ref, ff_ref, arrived_ref, cross_down_ref, cross_up_ref, far_down_ref, far_up_ref, dn_core_ref, dn_chip_ref, ff_core_ref, ff_chip_ref, pair_ref, first_core_ref, first_chip_ref, first_ring_ref,
    frames, temp, box_down, box_up, mix, d_head, d_out, dq, dk, dv, delta, d_three, out_send, out_cross, out_far, out_box,
    head_acc, head_low, head_cross, head_sum, held_a, held_b, half_box, pair_box, mid, quart_box, in_box, gain_box, gain_came, down_sum_ref, up_sum_ref, out_sum_ref, grad_query_ref, grad_key_ref, grad_value_ref,
    send, recv, keep_sem, load_sem, arena_sem, stage_sem,
):
    f32, bf16 = jnp.float32, jnp.bfloat16
    dp, z, t, other_dp, chip, core, pair = axes_of()
    rows, width = whole_ref.shape[1:]
    quarter, half = rows // 4, rows // 2
    part = width // (2 * SEQ)
    side = gd_ref.shape[1]
    inner = attended_ref.shape[1]
    copies = Copies(send, recv)
    scale = HEAD_DIM ** (-0.5)
    first, later = slice(0, quarter), slice(quarter, half)

    def along(k):
        return {"seq": lax.rem(z + k + SEQ, SEQ)}

    def load(*pairs):
        moves = [pltpu.make_async_copy(src, dst, load_sem.at[i]) for i, (src, dst) in enumerate(pairs)]
        for move in moves:
            move.start()
        for move in moves:
            move.wait()

    def block(side_dp, k):
        return pl.multiple_of((side_dp * SEQ + lax.rem(z - k + SEQ, SEQ)) * part, part)

    def rows_at(n, count=1):
        return pl.ds(n * quarter, count * quarter)

    greet([other_dp, chip, core] + [along(k) for k in range(1, SEQ)])

    def sums(part_ref, core_ref, chip_ref, n):
        to_core = [copies.make(part_ref.at[rows_at(4 * i + 2, 2), :], core_ref.at[i], core) for i in range(2)]
        to_chip = [copies.make(half_box.at[2 * n + i], chip_ref.at[i], chip) for i in range(2)]
        to_pair = copies.make(pair_box.at[n], pair_ref.at[n], pair)
        return to_core, to_chip, to_pair

    dn_core, dn_chip, dn_pair = sums(dn_ref, dn_core_ref, dn_chip_ref, 0)
    ff_core, ff_chip, ff_pair = sums(ff_ref, ff_core_ref, ff_chip_ref, 1)
    mix_chip = copies.make(mix.at[rows_at(0), :], mix.at[rows_at(1), :], chip)
    mix_core = copies.make(mix.at[rows_at(0, 2), :], mix.at[rows_at(2, 2), :], core)
    spread = [None] + [copies.make(d_head.at[lax.rem(z + k, SEQ)], d_out.at[k], along(k)) for k in range(1, SEQ)]
    cross_down = [copies.make(gd_ref.at[pl.ds(block(1 - dp, k), part), :], cross_down_ref.at[k], other_dp) for k in range(SEQ)]
    cross_up = [copies.make(gu_ref.at[pl.ds(block(1 - dp, k), part), :], cross_up_ref.at[k], other_dp) for k in range(SEQ)]
    cross_out = [copies.make(out_send.at[k], out_cross.at[k], other_dp) for k in range(SEQ)]
    far_down = [None] + [copies.make(box_down.at[k - 1], far_down_ref.at[k - 1], along(-k)) for k in range(1, SEQ)]
    far_up = [None] + [copies.make(box_up.at[k - 1], far_up_ref.at[k - 1], along(-k)) for k in range(1, SEQ)]
    far_out = [None] + [copies.make(out_box.at[k - 1], out_far.at[k - 1], along(-k)) for k in range(1, SEQ)]
    first_core = [copies.make(frames.at[k, rows_at(2, 2), :], first_core_ref.at[k], core) for k in range(SEQ)]
    first_chip = [copies.make(quart_box.at[k], first_chip_ref.at[k], chip) for k in range(SEQ)]
    first_ring = [None] + [copies.make(in_box.at[k - 1], first_ring_ref.at[k - 1], along(1)) for k in range(1, SEQ)]
    head_dp = copies.make(head_low.at[1 - dp], head_cross, other_dp)
    head_out = [None] + [copies.make(head_sum.at[lax.rem(z + k, SEQ)], arrived_ref.at[k], along(k)) for k in range(1, SEQ)]
    kept = []

    def publish(n, ref):
        mine = ref.at[pl.ds(t * quarter, quarter), :]
        mate = ref.at[pl.ds(lax.rem(t + 2, 4) * quarter, quarter), :]
        return [copies.make(half_box.at[n], mine, chip), copies.make(half_box.at[n], mine, core), copies.make(mate, mate, core)], (half_box.at[n], mine)

    gain_core = copies.make(gain_box.at[0], gain_came.at[0], core)
    gain_chip = copies.make(gain_box.at[1], gain_came.at[1], chip)
    result_out, result_own = publish(0, result_ref)
    grad_out_copies, grad_own = publish(1, grad_in_ref)

    def keep(src, dst):
        move = pltpu.make_async_copy(src, dst, keep_sem.at[SEQ + len(kept)])
        kept.append(move)
        move.start()
        return move

    def half_of(part_ref, core_ref, to_core, to_chip, i, n):
        copies.wait(to_core[i])
        load((part_ref.at[rows_at(4 * i + 1), :], held_a.at[rows_at(0), :]), (core_ref.at[i, rows_at(1), :], held_a.at[rows_at(1), :]))
        half_box[2 * n + i] = (held_a[first, :].astype(f32) + held_a[later, :].astype(f32)).astype(bf16)
        to_chip[i].start()

    def quarter_of(part_ref, core_ref, chip_ref, to_chip, i, *more):
        copies.wait(to_chip[i])
        load(
            (part_ref.at[rows_at(4 * i), :], held_a.at[rows_at(0), :]), (core_ref.at[i, rows_at(0), :], held_a.at[rows_at(1), :]), (chip_ref.at[i], held_b.at[rows_at(0), :]),
            *more,
        )
        return (held_a[first, :].astype(f32) + held_a[later, :].astype(f32)) + held_b[first, :].astype(f32)

    def pair_sum(part_ref, core_ref, chip_ref, to_chip, to_pair, n):
        pair_box[n] = quarter_of(part_ref, core_ref, chip_ref, to_chip, 1).astype(bf16)
        to_pair.start()

    def own_sum(part_ref, core_ref, chip_ref, to_chip, to_pair, n, extra):
        copies.wait(to_pair)
        total = quarter_of(part_ref, core_ref, chip_ref, to_chip, 0, (pair_ref.at[n], held_b.at[rows_at(1), :]), (extra, spare))
        return total + held_b[later, :].astype(f32)

    def scatter(k, own_ref, cross_at, crossing, box, far, go=True):
        copies.wait(crossing)
        load((cross_at, temp.at[0]), (own_ref.at[pl.ds(block(dp, k), part), :], temp.at[1]))
        box[k - 1] = (temp[0].astype(f32) + temp[1].astype(f32)).astype(bf16)
        if go:
            far[k].start()

    def scatter_down(k):
        scatter(k, gd_ref, cross_down_ref.at[k], cross_down[k], box_down, far_down)

    def scatter_up(k, go=True):
        scatter(k, gu_ref, cross_up_ref.at[k], cross_up[k], box_up, far_up, go)

    same = pl.multiple_of(lax.rem(z, 2) * side, side)
    unlike = pl.multiple_of((1 - lax.rem(z, 2)) * side, side)

    def total_of(own_ref, cross_at, far_ref, far, crossing, store):
        copies.wait(crossing, *far[1:])
        load((cross_at, temp.at[0]), (own_ref.at[pl.ds(block(dp, 0), part), :], temp.at[1]), (far_ref.at[1], temp.at[2]))
        store(same, lambda at: (temp[0, :, at].astype(f32) + temp[1, :, at].astype(f32)) + temp[2, :, at].astype(f32))
        load((far_ref.at[0], temp.at[0]), (far_ref.at[2], temp.at[1]))
        store(unlike, lambda at: temp[0, :, at].astype(f32) + temp[1, :, at].astype(f32))

    def store_turned(base, value):
        for n in range(side // 256):
            down_sum_ref[pl.ds(base + n * 256, 256), :] = value(slice(n * 256, (n + 1) * 256)).T

    gain_sums = []

    def store_plain(base, value):
        raw = value(slice(0, side))
        gain_sums.append(jnp.sum(held_a[0:part, pl.ds(base, side)].astype(f32) * raw, axis=1, keepdims=True))
        up_sum_ref[:, pl.ds(base, side)] = raw * column(gain_two_ref)

    def out_block(start):
        return lax.dot_general(attended_ref[...], mix[:, pl.ds(start, part)], (((0,), (0,)), ((), ())), preferred_element_type=f32)

    def scatter_out(k):
        copies.wait(cross_out[k])
        out_box[k - 1] = (out_block(block(dp, k)) + out_cross[k].astype(f32)).astype(bf16)
        far_out[k].start()

    for copy in (dn_core[1], dn_core[0], cross_down[1]):
        copy.start()

    def place(*pairs):
        moves = [pltpu.make_async_copy(src, dst, arena_sem.at[i]) for i, (src, dst) in enumerate(pairs)]
        for move in moves:
            move.start()
        return moves

    def sides(ref, at):
        return [(ref.at[pl.ds(n * rows, rows), :], frames.at[at, :, pl.ds(n * side, side)]) for n in range(2)]

    arena = place(*sides(d_up_ref, 0), *sides(act_ref, 3), *[(second_ref.at[pl.ds(n * rows, rows), :], frames.at[1 + n]) for n in range(2)])
    spare = head_acc.at[pl.ds(0, quarter), :]
    half_of(dn_ref, dn_core_ref, dn_core, dn_chip, 1, 0)
    cross_down[2].start()
    load(*[(out_ref.at[pl.ds(h * HEAD_DIM, HEAD_DIM), :], quart_box.at[h, pl.ds(0, HEAD_DIM), :]) for h in range(SEQ)])
    for move in arena:
        move.wait()

    def up_piece(b, carry):
        at = pl.ds(pl.multiple_of(b * part, part), part)
        slot = lax.rem(b, 2)
        move = pltpu.make_async_copy(temp.at[slot], gu_ref.at[at, :], stage_sem.at[slot])

        @pl.when(lax.rem(b, SEQ) >= 2)
        def _():
            move.wait()

        turned = (((0,), (0,)), ((), ()))
        value = lax.dot_general(frames[1, :, at], frames[0, :, 0:side], turned, preferred_element_type=f32)
        value = value + lax.dot_general(frames[2, :, at], frames[0, :, side:], turned, preferred_element_type=f32)
        temp[slot] = value.astype(bf16)
        move.start()
        return carry

    lax.fori_loop(0, SEQ, up_piece, 0)
    for slot in range(2):
        pltpu.make_async_copy(temp.at[slot], gu_ref.at[pl.ds(0, part), :], stage_sem.at[slot]).wait()
    scatter_down(1)
    cross_down[3].start()
    lax.fori_loop(SEQ, 2 * SEQ, up_piece, 0)
    for slot in range(2):
        pltpu.make_async_copy(temp.at[slot], gu_ref.at[pl.ds(0, part), :], stage_sem.at[slot]).wait()
    arena = place((down_ref.at[pl.ds(0, rows), :], frames.at[1]), (down_ref.at[pl.ds(rows, side - rows), :], frames.at[2, pl.ds(0, side - rows), :]))
    copies.wait(dn_chip[1])
    half_of(dn_ref, dn_core_ref, dn_core, dn_chip, 0, 0)
    pair_sum(dn_ref, dn_core_ref, dn_chip_ref, dn_chip, dn_pair, 0)
    cross_up[1].start()
    scatter_down(2)
    grad = own_sum(dn_ref, dn_core_ref, dn_chip_ref, dn_chip, dn_pair, 0, normed_two_ref)
    normed = spare[...]
    grad = rate_two_ref[...] * (grad - jnp.mean(grad, axis=1, keepdims=True) - normed * jnp.mean(grad * normed, axis=1, keepdims=True))
    load((cots_ref.at[rows_at(0), :], held_a.at[rows_at(0), :]))
    grad = held_a[first, :].astype(f32) + grad
    mid[...] = grad
    mix[first, :] = grad.astype(bf16)
    mix_chip.start()
    scatter_down(3)
    for copy in (cross_up[2], cross_up[3], cross_up[0], cross_down[0]):
        copy.start()
    scatter_up(1)
    copies.wait(mix_chip)
    mix_core.start()

    def to_head(k, at):
        h = lax.rem(z + k, SEQ)
        d_head[h, at, :] = lax.dot_general(mix[at, :], quart_box[h, 0:HEAD_DIM, :], (((1,), (1,)), ((), ())), preferred_element_type=f32).astype(bf16)

    for k in (1, 2, 3, 0):
        to_head(k, slice(0, half))
    copies.wait(mix_core)
    for k in (1, 2, 3, 0):
        to_head(k, slice(half, rows))
        if k:
            spread[k].start()
    d_out[0] = d_head[z]
    for move in arena:
        move.wait()

    def ff_piece(n, carry):
        at = pl.ds(n * quarter, quarter)
        slot = lax.rem(n, 2)
        stage = held_b.at[pl.ds(slot * quarter, quarter), :]
        move = pltpu.make_async_copy(stage, ff_ref.at[at, :], stage_sem.at[slot])

        @pl.when(n >= 2)
        def _():
            move.wait()

        left = frames[3, pl.ds(lax.rem(n, 4) * quarter, quarter), pl.ds(pl.multiple_of(n // 4 * side, side), side)]
        value = jnp.dot(left[:, 0:rows], frames[1], preferred_element_type=f32)
        value = value + jnp.dot(left[:, rows:], frames[2, 0 : side - rows, :], preferred_element_type=f32)
        held_b[pl.ds(slot * quarter, quarter), :] = value.astype(bf16)
        move.start()
        return carry

    lax.fori_loop(0, 8, ff_piece, 0)
    for slot in range(2):
        pltpu.make_async_copy(held_b.at[pl.ds(slot * quarter, quarter), :], ff_ref.at[pl.ds(0, quarter), :], stage_sem.at[slot]).wait()
    ff_core[1].start()
    ff_core[0].start()
    fetch = [pltpu.make_async_copy(whole_ref.at[k], frames.at[k], keep_sem.at[k]) for k in range(SEQ)]
    for move in fetch:
        move.start()
    for k in (1, 2, 3, 0):
        out_send[k] = out_block(block(1 - dp, k)).astype(bf16)
        cross_out[k].start()
    half_of(ff_ref, ff_core_ref, ff_core, ff_chip, 1, 1)
    high = head_acc.shape[0]
    pieces = [(f, slice(0, high) if n == 0 else slice(high, rows), slice((2 * f + n) * HEAD_DIM, (2 * f + n + 1) * HEAD_DIM)) for f in range(SEQ) for n in range(2)]
    load(*[(att_ref.at[f, pl.ds(at.start, at.stop - at.start), :], head_acc.at[pl.ds(0, at.stop - at.start), pl.ds(lanes.start, HEAD_DIM)]) for f, at, lanes in pieces])
    scatter_up(2, False)
    scatter_up(3, False)
    copies.wait(*spread[1:])
    far_up[2].start()
    dq[...] = jnp.zeros_like(dq)
    for f, at, lanes in pieces:
        delta[f, :, at] = jnp.sum((d_out[f, at, :].astype(f32) * head_acc[0 : at.stop - at.start, lanes]).T, axis=0, keepdims=True)

    def key_frame(j):
        here = lax.rem(z - j + SEQ, SEQ)
        dk[...] = jnp.zeros_like(dk)
        dv[...] = jnp.zeros_like(dv)

        def query_frame(i, inner_):
            at = lax.rem(z - i + SEQ, SEQ)
            query, key, value = qkv_ref[at, :, :HEAD_DIM], qkv_ref[here, :, HEAD_DIM : 2 * HEAD_DIM], qkv_ref[here, :, 2 * HEAD_DIM :]
            grad_out = d_out[at]
            scores = lax.dot_general(key, query, (((1,), (1,)), ((), ())), preferred_element_type=f32) * scale + (valid_ref[0, j] - 1).astype(f32) * -MASK_FILL
            prob = jnp.exp(scores - lse_ref[at])
            d_prob = lax.dot_general(value, grad_out, (((1,), (1,)), ((), ())), preferred_element_type=f32)
            d_scores = (prob * (d_prob - delta[at])).astype(bf16)
            dv[...] += jnp.dot(prob.astype(bf16), grad_out, preferred_element_type=f32)
            dk[...] += jnp.dot(d_scores, query, preferred_element_type=f32)
            dq[at] += lax.dot_general(key, d_scores, (((0,), (0,)), ((), ())), preferred_element_type=f32)
            return inner_

        lax.fori_loop(j, SEQ, query_frame, 0)
        d_three[here, :, HEAD_DIM : 2 * HEAD_DIM] = (dk[...] * scale).astype(bf16)
        d_three[here, :, 2 * HEAD_DIM :] = dv[...].astype(bf16)

    key_frame(0)
    far_up[3].start()
    scatter_out(1)
    key_frame(1)
    half_of(ff_ref, ff_core_ref, ff_core, ff_chip, 0, 1)
    scatter_out(2)
    key_frame(2)
    key_frame(3)
    pair_sum(ff_ref, ff_core_ref, ff_chip_ref, ff_chip, ff_pair, 1)
    for f in range(SEQ):
        d_three[f, :, :HEAD_DIM] = (dq[f] * scale).T.astype(bf16)

    def project_back(k):
        fetch[k].wait()

        def piece(n, carry):
            at = pl.ds(pl.multiple_of(n * 512, 512), 512)
            term = lax.dot_general(d_three[k], frames[k, :, at], (((0,), (0,)), ((), ())), preferred_element_type=f32)
            head_acc[:, at] = term if k == 1 else head_acc[:, at] + term
            return carry

        lax.fori_loop(0, width // 512, piece, 0)

        def back_piece(n, carry):
            at = pl.ds(pl.multiple_of(n * 512, 512), 512)
            frames[k, :, at] = lax.dot_general(d_three[k], w_head_ref[at, :], (((1,), (1,)), ((), ())), preferred_element_type=f32).astype(bf16)
            return carry

        lax.fori_loop(0, width // 512, back_piece, 0)
        first_core[k].start()

    def half_sum(k):
        copies.wait(first_core[k])
        load((first_core_ref.at[k], held_a))
        quart_box[k] = (frames[k, later, :].astype(f32) + held_a[later, :].astype(f32)).astype(bf16)
        first_chip[k].start()
        frames[k, first, :] = (frames[k, first, :].astype(f32) + held_a[first, :].astype(f32)).astype(bf16)

    def quarter_sum(k):
        copies.wait(first_chip[k])
        pairs = [(first_chip_ref.at[k], held_a.at[rows_at(0), :])]
        if k != 1:
            before = (k - 1) % SEQ
            copies.wait(first_ring[before])
            pairs.append((first_ring_ref.at[before - 1], held_a.at[rows_at(1), :]))
        load(*pairs)
        sum_ = frames[k, first, :].astype(f32) + held_a[first, :].astype(f32)
        if k != 1:
            sum_ = sum_ + held_a[later, :].astype(f32)
        return sum_

    project_back(1)
    scatter_out(3)
    project_back(2)
    half_sum(1)
    project_back(3)
    project_back(0)
    for n in range(2):
        head_low[n] = head_acc[:, n * (width // 2) : (n + 1) * (width // 2)].astype(bf16)
    head_dp.start()
    half_sum(2)
    in_box[0] = quarter_sum(1).astype(bf16)
    first_ring[1].start()
    total_of(gd_ref, cross_down_ref.at[0], far_down_ref, far_down, cross_down[0], store_turned)
    keep(down_sum_ref, down_sum_out)
    half_sum(3)
    load((w_up_ref, held_a.at[pl.ds(0, part), :]))
    total_of(gu_ref, cross_up_ref.at[0], far_up_ref, far_up, cross_up[0], store_plain)
    keep(up_sum_ref, up_sum_out)
    in_box[1] = quarter_sum(2).astype(bf16)
    first_ring[2].start()
    half_sum(0)
    copies.wait(head_dp)
    for j in range(SEQ):
        at = slice(j * part, (j + 1) * part)
        head_sum[j] = (head_low[dp, :, at].astype(f32) + head_cross[:, at].astype(f32)).astype(bf16)
    own_head = keep(head_sum.at[z], arrived_ref.at[0])
    copies.wait(cross_out[0], *far_out[1:])
    sum_ = out_block(block(dp, 0)) + out_cross[0].astype(f32)
    for k in range(1, SEQ):
        sum_ = sum_ + out_far[k - 1].astype(f32)
    out_sum_ref[...] = sum_
    keep(out_sum_ref, out_sum_out)
    in_box[2] = quarter_sum(3).astype(bf16)
    first_ring[3].start()
    total = own_sum(ff_ref, ff_core_ref, ff_chip_ref, ff_chip, ff_pair, 1, resid_ref)
    copies.flush(*dn_chip)
    half_box[0] = (spare[...] + total).astype(bf16)
    result_out[0].start()
    result_out[1].start()
    keep(*result_own)
    load((x_ref.at[pl.ds(t * quarter, quarter), :], held_a.at[rows_at(0), :]))
    center = held_a[first, :].astype(f32)
    center = center - jnp.mean(center, axis=1, keepdims=True)
    rate = lax.rsqrt(jnp.mean(center * center, axis=1, keepdims=True) + NORM_EPS)
    head_acc[later, :] = center * rate
    for k in range(1, SEQ):
        head_out[k].start()
    grad = quarter_sum(0)
    normed = head_acc[later, :]
    grad = rate * (grad - jnp.mean(grad, axis=1, keepdims=True) - normed * jnp.mean(grad * normed, axis=1, keepdims=True))
    half_box[1] = (mid[...] + grad).astype(bf16)
    grad_out_copies[0].start()
    grad_out_copies[1].start()
    keep(*grad_own)
    copies.wait(result_out[0])
    result_out[2].start()
    copies.wait(*head_out[1:])
    own_head.wait()
    load(
        *[(arrived_ref.at[k], head_cross.at[:, pl.ds(k * part, part)]) for k in range(SEQ)],
        *[(ref, held_a.at[pl.ds(0, part), pl.ds(n * inner, inner)]) for n, ref in enumerate((w_query_ref, w_key_ref, w_value_ref))],
    )
    gain_first, gain = jnp.zeros((part, 1), f32), column(gain_one_ref)
    for h in range(SEQ):
        raw = head_cross[:, pl.ds(pl.multiple_of(lax.rem(z - h + SEQ, SEQ) * part, part), part)].astype(f32).T
        for n, ref in enumerate((grad_query_ref, grad_key_ref, grad_value_ref)):
            one = raw[:, n * HEAD_DIM : (n + 1) * HEAD_DIM]
            weight = held_a[0:part, n * inner + h * HEAD_DIM : n * inner + (h + 1) * HEAD_DIM].astype(f32)
            gain_first = gain_first + jnp.sum(weight * one, axis=1, keepdims=True)
            ref[:, h * HEAD_DIM : (h + 1) * HEAD_DIM] = one * gain
    keep(grad_query_ref, grad_query_out)
    keep(grad_key_ref, grad_key_out)
    keep(grad_value_ref, grad_value_out)
    lane = lax.broadcasted_iota(jnp.int32, (part, HEAD_DIM), 1)
    gain_box[0] = jnp.where(lane == 0, gain_first, gain_sums[0] + gain_sums[1])
    gain_core.start()
    copies.wait(gain_core)
    gain_box[1] = gain_box[0] + gain_came[0]
    gain_chip.start()
    copies.wait(grad_out_copies[0])
    grad_out_copies[2].start()
    copies.wait(gain_chip)
    gains_ref[...] = (gain_box[1] + gain_came[1]).T[0:8]
    copies.finish()
    for move in kept:
        if move is not own_head:
            move.wait()


def back(gd, d_up, second, act, down, dn, resid, cots, normed_two, rate_two, attended, out_rel, qkv, att, lse, valid, w_head, whole, x, w_query, w_key, w_value, w_up, gain_one, gain_two):
    rows, width = x.shape
    quarter, half = rows // 4, rows // 2
    part = width // (2 * SEQ)
    inner = attended.shape[1]
    side = gd.shape[1]
    three = 3 * HEAD_DIM
    f32, bf16 = jnp.float32, jnp.bfloat16
    any_, vmem = pl.BlockSpec(memory_space=pl.ANY), pl.BlockSpec(memory_space=pltpu.VMEM)
    shape = jax.ShapeDtypeStruct
    outs = [
        (shape((2 * side, part), f32), any_),
        (shape((part, 2 * side), f32), any_),
        (shape((inner, part), f32), any_),
        (shape((part, inner), f32), any_),
        (shape((part, inner), f32), any_),
        (shape((part, inner), f32), any_),
        (shape((8, part), f32), vmem),
        (shape((rows, width), bf16), any_),
        (shape((rows, width), bf16), any_),
        (shape((width, side), bf16), any_),
        (shape((2 * rows, width), bf16), any_),
        (shape((SEQ, three, part), bf16), any_),
        (shape((SEQ, part, side), bf16), any_),
        (shape((SEQ, part, side), bf16), any_),
        (shape((SEQ - 1, part, side), bf16), any_),
        (shape((SEQ - 1, part, side), bf16), any_),
        (shape((2, half, width), bf16), any_),
        (shape((2, quarter, width), bf16), any_),
        (shape((2, half, width), bf16), any_),
        (shape((2, quarter, width), bf16), any_),
        (shape((2, quarter, width), bf16), any_),
        (shape((SEQ, half, width), bf16), any_),
        (shape((SEQ, quarter, width), bf16), any_),
        (shape((SEQ - 1, quarter, width), bf16), any_),
    ]
    count = 10 + 2 + 3 + 4 + 4 + 4 + 9 + 8 + 3 + 4 + 6 + 2
    scratch = [
        ((SEQ, rows, width), bf16),
        ((3, part, side), bf16),
        ((SEQ - 1, part, side), bf16),
        ((SEQ - 1, part, side), bf16),
        ((rows, width), bf16),
        ((SEQ, rows, HEAD_DIM), bf16),
        ((SEQ, rows, HEAD_DIM), bf16),
        ((SEQ, HEAD_DIM, rows), f32),
        ((rows, HEAD_DIM), f32),
        ((rows, HEAD_DIM), f32),
        ((SEQ, 1, rows), f32),
        ((SEQ, rows, three), bf16),
        ((SEQ, inner, part), bf16),
        ((SEQ, inner, part), bf16),
        ((SEQ - 1, inner, part), bf16),
        ((SEQ - 1, inner, part), bf16),
        ((three, width), f32),
        ((2, three, width // 2), bf16),
        ((three, width // 2), bf16),
        ((SEQ, three, part), bf16),
        ((half, width), bf16),
        ((half, width), bf16),
        ((4, quarter, width), bf16),
        ((2, quarter, width), bf16),
        ((quarter, width), f32),
        ((SEQ, quarter, width), bf16),
        ((SEQ - 1, quarter, width), bf16),
        ((2, part, HEAD_DIM), f32),
        ((2, part, HEAD_DIM), f32),
        ((2 * side, part), f32),
        ((part, 2 * side), f32),
        ((inner, part), f32),
        ((part, inner), f32),
        ((part, inner), f32),
        ((part, inner), f32),
    ]
    return pl.pallas_call(
        back_kernel,
        out_shape=[o[0] for o in outs],
        in_specs=[any_] * 9 + [vmem, vmem, any_, vmem, any_, vmem, pl.BlockSpec(memory_space=pltpu.SMEM), vmem] + [any_] * 6 + [vmem] * 2,
        out_specs=[o[1] for o in outs],
        scratch_shapes=[pltpu.VMEM(*one) for one in scratch]
        + [pltpu.SemaphoreType.DMA((count,)), pltpu.SemaphoreType.DMA((count,)), pltpu.SemaphoreType.DMA((SEQ + 9,)), pltpu.SemaphoreType.DMA((8,)), pltpu.SemaphoreType.DMA((6,)), pltpu.SemaphoreType.DMA((2,))],
        compiler_params=pltpu.CompilerParams(collective_id=1, has_side_effects=True, vmem_limit_bytes=62 * 2**20),
        cost_estimate=pl.CostEstimate(flops=20 * 10**9, bytes_accessed=60 * 10**6, transcendentals=5 * 10**6),
    )(gd, d_up, second, act, down, dn, resid, cots, normed_two, rate_two, attended, out_rel, qkv, att, lse, valid, w_head, whole, x, w_query, w_key, w_value, w_up, gain_one, gain_two)[:9]


def mm(left, right, dims=((1,), (0,)), out=jnp.bfloat16):
    return lax.dot_general(left, right, (dims, ((), ())), preferred_element_type=jnp.float32).astype(out)


def local_fast(inputs, first_gain, w_query, w_key, w_value, w_out, second_gain, w_up, w_down, frame_mask, cotangent):
    rows = inputs.shape[1]
    f32, bf16 = jnp.float32, jnp.bfloat16
    gain_one, gain_two = first_gain[None], second_gain[None]
    valid = frame_mask
    whole, w_head, qkv, attended_f, lse, attended, out_all, resid_mid, normed_two, rate_two, second_in, up_side, down_side, cots = front(
        inputs[0], w_query, w_key, w_value, w_out, w_up, w_down, gain_one, gain_two, cotangent[0], valid
    )
    up_pre = mm(second_in, up_side, out=f32)
    cdf = 0.5 * (1.0 + lax.erf(up_pre * (0.5**0.5)))
    up_act = (up_pre * cdf).astype(bf16)
    slope = cdf + up_pre * jnp.exp(-0.5 * up_pre * up_pre) * ((2.0 * jnp.pi) ** -0.5)
    grad_down = mm(cots, up_act, ((0,), (0,)))
    d_up = (mm(cots, down_side, ((1,), (1,)), f32) * slope).astype(bf16)
    d_normed_two = mm(d_up, up_side, ((1,), (1,)))
    down_sum, up_sum, out_sum, grad_query, grad_key, grad_value, gains, grad_in, result = back(
        grad_down, d_up, second_in, up_act, down_side, d_normed_two, resid_mid, cots, normed_two, rate_two, attended, out_all, qkv, attended_f, lse, valid, w_head, whole, inputs[0],
        w_query, w_key, w_value, w_up, gain_one, gain_two,
    )
    return (result[None], grad_in[None], gains[0], grad_query, grad_key, grad_value, out_sum, gains[1], up_sum, down_sum)


SEQ = 4


def solution(mesh):
    placed = (
        P("dp", "seq", None),
        P(("dp", "seq")),
        P(("dp", "seq"), "tensor"),
        P(("dp", "seq"), "tensor"),
        P(("dp", "seq"), "tensor"),
        P("tensor", ("dp", "seq")),
        P(("dp", "seq")),
        P(("dp", "seq"), "tensor"),
        P("tensor", ("dp", "seq")),
        P("dp", None),
        P("dp", "seq", None),
    )
    sizes = dict(mesh.shape)
    spread = sizes == {"dp": 2, "seq": SEQ, "tensor": 4}
    return jax.shard_map(
        local_fast if spread else local,
        mesh=mesh,
        in_specs=placed,
        out_specs=(
            P("dp", "seq", None),
            P("dp", "seq", None),
            P(("dp", "seq")),
            P(("dp", "seq"), "tensor"),
            P(("dp", "seq"), "tensor"),
            P(("dp", "seq"), "tensor"),
            P("tensor", ("dp", "seq")),
            P(("dp", "seq")),
            P(("dp", "seq"), "tensor"),
            P("tensor", ("dp", "seq")),
        ),
        check_vma=False,
    )
```

```python
import functools

import jax
import jax.numpy as jnp
from jax import lax
from jax.experimental import pallas as pl
from jax.experimental.pallas import tpu as pltpu
from jax.sharding import PartitionSpec as P

HEAD_DIM = 128
FRAME_TOK = 640


NORM_EPS = 1e-05
MASK_FILL = -1e30
MESH = pl.DeviceIdType.MESH


def norm_rows(values):
    center = values - jnp.mean(values, axis=-1, keepdims=True)
    spread = jnp.mean(center * center, axis=-1, keepdims=True)
    return center * lax.rsqrt(spread + NORM_EPS)


def gelu_exact(values):
    return jax.nn.gelu(values, approximate=False)


def heads_total(values):
    return lax.psum(values.astype(jnp.bfloat16), "tensor").astype(jnp.float32)


def local(
    inputs,
    first_gain,
    w_query,
    w_key,
    w_value,
    w_out,
    second_gain,
    w_up,
    w_down,
    frame_mask,
    cotangent,
):
    seq_pos = lax.axis_index("seq")
    gain_one, query_w, key_w, value_w, gain_two, up_w = (
        lax.all_gather(first_gain, ("dp", "seq"), axis=0, tiled=True),
        lax.all_gather(w_query, ("dp", "seq"), axis=0, tiled=True),
        lax.all_gather(w_key, ("dp", "seq"), axis=0, tiled=True),
        lax.all_gather(w_value, ("dp", "seq"), axis=0, tiled=True),
        lax.all_gather(second_gain, ("dp", "seq"), axis=0, tiled=True),
        lax.all_gather(w_up, ("dp", "seq"), axis=0, tiled=True),
    )
    out_w, down_w = (
        lax.all_gather(w_out, ("dp", "seq"), axis=1, tiled=True),
        lax.all_gather(w_down, ("dp", "seq"), axis=1, tiled=True),
    )
    tok_rows = inputs.shape[1]
    local_inner = query_w.shape[1]
    local_heads = local_inner // HEAD_DIM
    frames_dev = tok_rows // FRAME_TOK
    score_scale = HEAD_DIM ** (-0.5)
    clip_valid = frame_mask[0]
    frame_count = clip_valid.shape[0]
    resid_in = inputs[0].astype(jnp.float32)
    dout_rows = cotangent[0]
    row_frame = seq_pos * frames_dev + jnp.arange(tok_rows, dtype=jnp.int32) // FRAME_TOK
    frame_limit = (seq_pos + 1) * frames_dev
    normed_one = norm_rows(resid_in)
    first_in = (normed_one * gain_one.astype(jnp.float32)).astype(jnp.bfloat16)
    query = jnp.dot(first_in, query_w, preferred_element_type=jnp.float32).astype(jnp.bfloat16)
    key_local = jnp.dot(first_in, key_w, preferred_element_type=jnp.float32).astype(jnp.bfloat16)
    value_local = jnp.dot(first_in, value_w, preferred_element_type=jnp.float32).astype(
        jnp.bfloat16
    )
    key_all, value_all = (
        lax.all_gather(key_local, "seq", axis=0, tiled=True),
        lax.all_gather(value_local, "seq", axis=0, tiled=True),
    )
    query_heads = query.reshape(tok_rows, local_heads, HEAD_DIM)
    key_frames = key_all.reshape(frame_count, FRAME_TOK, local_heads, HEAD_DIM)
    value_frames = value_all.reshape(frame_count, FRAME_TOK, local_heads, HEAD_DIM)

    def frame_scores(frame_idx):
        key_block = lax.dynamic_index_in_dim(key_frames, frame_idx, 0, keepdims=False)
        value_block = lax.dynamic_index_in_dim(value_frames, frame_idx, 0, keepdims=False)
        scores = (
            jnp.einsum("qhd,khd->hqk", query_heads, key_block, preferred_element_type=jnp.float32)
            * score_scale
        )
        frame_ok = lax.dynamic_index_in_dim(clip_valid, frame_idx, 0, keepdims=False) == 1
        allowed = ((frame_idx <= row_frame) & frame_ok)[None, :, None]
        return (scores, allowed, key_block, value_block)

    def stats_step(frame_idx, running):
        row_max, row_sum = running
        scores, allowed, key_block, value_block = frame_scores(frame_idx)
        masked = jnp.where(allowed, scores, MASK_FILL)
        new_max = jnp.maximum(row_max, jnp.max(masked, axis=2))
        exp_terms = jnp.where(allowed, jnp.exp(masked - new_max[:, :, None]), 0.0)
        return (new_max, row_sum * jnp.exp(row_max - new_max) + jnp.sum(exp_terms, axis=2))

    start_stats = (
        jnp.full((local_heads, tok_rows), MASK_FILL, jnp.float32),
        jnp.zeros((local_heads, tok_rows), jnp.float32),
    )
    row_max, row_sum = lax.fori_loop(0, frame_limit, stats_step, start_stats)

    def soft_weights(scores, allowed):
        return jnp.where(allowed, jnp.exp(scores - row_max[:, :, None]) / row_sum[:, :, None], 0.0)

    def output_step(frame_idx, running):
        scores, allowed, key_block, value_block = frame_scores(frame_idx)
        attn_prob = soft_weights(scores, allowed).astype(jnp.bfloat16)
        return running + jnp.einsum(
            "hqk,khd->qhd", attn_prob, value_block, preferred_element_type=jnp.float32
        )

    attended = lax.fori_loop(
        0, frame_limit, output_step, jnp.zeros((tok_rows, local_heads, HEAD_DIM), jnp.float32)
    )
    attended_low = attended.reshape(tok_rows, local_inner).astype(jnp.bfloat16)
    resid_mid = resid_in + heads_total(
        jnp.dot(attended_low, out_w, preferred_element_type=jnp.float32)
    )
    normed_two = norm_rows(resid_mid)
    second_in = (normed_two * gain_two.astype(jnp.float32)).astype(jnp.bfloat16)
    up_pre = jnp.dot(second_in, up_w, preferred_element_type=jnp.float32)
    up_act = gelu_exact(up_pre).astype(jnp.bfloat16)
    resid_out = resid_mid + heads_total(jnp.dot(up_act, down_w, preferred_element_type=jnp.float32))
    result = resid_out.astype(jnp.bfloat16)[None]
    grad_down = jnp.einsum("tf,td->fd", up_act, dout_rows, preferred_element_type=jnp.float32)
    d_act = jnp.einsum("td,fd->tf", dout_rows, down_w, preferred_element_type=jnp.float32)
    gelu_pull = jax.vjp(gelu_exact, up_pre)[1]
    d_up_pre = gelu_pull(d_act)[0].astype(jnp.bfloat16)
    grad_up = jnp.einsum("td,tf->df", second_in, d_up_pre, preferred_element_type=jnp.float32)
    d_second = heads_total(
        jnp.einsum("tf,df->td", d_up_pre, up_w, preferred_element_type=jnp.float32)
    )
    grad_second_gain = jnp.sum(d_second * normed_two, axis=0)
    norm_pull_two = jax.vjp(norm_rows, resid_mid)[1]
    d_mid = (
        dout_rows.astype(jnp.float32) + norm_pull_two(d_second * gain_two.astype(jnp.float32))[0]
    )
    d_mix = d_mid.astype(jnp.bfloat16)
    grad_out = jnp.einsum("ti,td->id", attended_low, d_mix, preferred_element_type=jnp.float32)
    d_attended = jnp.einsum("td,id->ti", d_mix, out_w, preferred_element_type=jnp.float32).astype(
        jnp.bfloat16
    )
    dout_heads = d_attended.reshape(tok_rows, local_heads, HEAD_DIM)
    row_delta = jnp.sum(dout_heads.astype(jnp.float32) * attended, axis=2).T

    def query_step(frame_idx, running):
        scores, allowed, key_block, value_block = frame_scores(frame_idx)
        attn_prob = soft_weights(scores, allowed)
        d_prob = jnp.einsum(
            "qhd,khd->hqk", dout_heads, value_block, preferred_element_type=jnp.float32
        )
        d_scores = (attn_prob * (d_prob - row_delta[:, :, None])).astype(jnp.bfloat16)
        return running + jnp.einsum(
            "hqk,khd->qhd", d_scores, key_block, preferred_element_type=jnp.float32
        )

    query_sum = lax.fori_loop(
        0, frame_limit, query_step, jnp.zeros((tok_rows, local_heads, HEAD_DIM), jnp.float32)
    )
    d_query = (query_sum * score_scale).reshape(tok_rows, local_inner).astype(jnp.bfloat16)

    def one_frame(frame_step):
        scores, allowed, key_block, value_block = frame_scores(frame_step)
        attn_prob = soft_weights(scores, allowed)
        d_prob = jnp.einsum(
            "qhd,khd->hqk", dout_heads, value_block, preferred_element_type=jnp.float32
        )
        d_scores = (attn_prob * (d_prob - row_delta[:, :, None])).astype(jnp.bfloat16)
        key_term = (
            jnp.einsum("hqk,qhd->khd", d_scores, query_heads, preferred_element_type=jnp.float32)
            * score_scale
        )
        value_term = jnp.einsum(
            "hqk,qhd->khd",
            attn_prob.astype(jnp.bfloat16),
            dout_heads,
            preferred_element_type=jnp.float32,
        )
        return jnp.concatenate(
            [key_term.reshape(FRAME_TOK, local_inner), value_term.reshape(FRAME_TOK, local_inner)],
            axis=1,
        )

    blocks = lax.map(
        one_frame, jnp.arange(tok_rows * lax.axis_size("seq") // FRAME_TOK, dtype=jnp.int32)
    )
    kv_grad = lax.psum_scatter(
        blocks.reshape(tok_rows * lax.axis_size("seq"), 2 * local_inner).astype(jnp.bfloat16),
        "seq",
        scatter_dimension=0,
        tiled=True,
    ).astype(jnp.float32)
    d_key = kv_grad[:, :local_inner].astype(jnp.bfloat16)
    d_value = kv_grad[:, local_inner:].astype(jnp.bfloat16)
    grad_query = jnp.einsum("td,ti->di", first_in, d_query, preferred_element_type=jnp.float32)
    grad_key = jnp.einsum("td,ti->di", first_in, d_key, preferred_element_type=jnp.float32)
    grad_value = jnp.einsum("td,ti->di", first_in, d_value, preferred_element_type=jnp.float32)
    first_local = jnp.einsum("ti,di->td", d_query, query_w, preferred_element_type=jnp.float32)
    first_local = first_local + jnp.einsum(
        "ti,di->td", d_key, key_w, preferred_element_type=jnp.float32
    )
    first_local = first_local + jnp.einsum(
        "ti,di->td", d_value, value_w, preferred_element_type=jnp.float32
    )
    d_first = heads_total(first_local)
    grad_first_gain = jnp.sum(d_first * normed_one, axis=0)
    norm_pull_one = jax.vjp(norm_rows, resid_in)[1]
    grad_inputs = (d_mid + norm_pull_one(d_first * gain_one.astype(jnp.float32))[0]).astype(
        jnp.bfloat16
    )[None]
    summed_in = (
        lax.psum_scatter(
            grad_first_gain.astype(jnp.bfloat16), ("dp", "seq"), scatter_dimension=0, tiled=True
        ).astype(jnp.float32),
        lax.psum_scatter(
            grad_query.astype(jnp.bfloat16), ("dp", "seq"), scatter_dimension=0, tiled=True
        ).astype(jnp.float32),
        lax.psum_scatter(
            grad_key.astype(jnp.bfloat16), ("dp", "seq"), scatter_dimension=0, tiled=True
        ).astype(jnp.float32),
        lax.psum_scatter(
            grad_value.astype(jnp.bfloat16), ("dp", "seq"), scatter_dimension=0, tiled=True
        ).astype(jnp.float32),
        lax.psum_scatter(
            grad_second_gain.astype(jnp.bfloat16), ("dp", "seq"), scatter_dimension=0, tiled=True
        ).astype(jnp.float32),
        lax.psum_scatter(
            grad_up.astype(jnp.bfloat16), ("dp", "seq"), scatter_dimension=0, tiled=True
        ).astype(jnp.float32),
    )
    summed_out = (
        lax.psum_scatter(
            grad_out.astype(jnp.bfloat16), ("dp", "seq"), scatter_dimension=1, tiled=True
        ).astype(jnp.float32),
        lax.psum_scatter(
            grad_down.astype(jnp.bfloat16), ("dp", "seq"), scatter_dimension=1, tiled=True
        ).astype(jnp.float32),
    )
    return (
        result,
        grad_inputs,
        summed_in[0],
        summed_in[1],
        summed_in[2],
        summed_in[3],
        summed_out[0],
        summed_in[4],
        summed_in[5],
        summed_out[1],
    )


def axes_of():
    dp, z, t = lax.axis_index("dp"), lax.axis_index("seq"), lax.axis_index("tensor")
    other_dp, chip, core = {"dp": 1 - dp}, {"tensor": lax.rem(t + 2, 4)}, {"tensor": t + 1 - 2 * lax.rem(t, 2)}
    pair = {"seq": z + 1 - 2 * lax.rem(z, 2)}
    return dp, z, t, other_dp, chip, core, pair


class Copies:
    def __init__(self, send, recv):
        self.send, self.recv, self.all, self.came, self.left = send, recv, [], [], []

    def make(self, src, dst, device):
        i = len(self.all)
        copy = pltpu.make_async_remote_copy(src_ref=src, dst_ref=dst, send_sem=self.send.at[i], recv_sem=self.recv.at[i], device_id=device, device_id_type=MESH)
        self.all.append(copy)
        return copy

    def wait(self, *copies):
        for copy in copies:
            if not any(copy is done for done in self.came):
                copy.wait_recv()
                self.came.append(copy)

    def flush(self, *copies):
        for copy in copies:
            if not any(copy is done for done in self.left):
                copy.wait_send()
                self.left.append(copy)

    def finish(self):
        self.wait(*self.all)
        self.flush(*self.all)


def column(row_ref):
    row = jnp.broadcast_to(row_ref[...].astype(jnp.float32)[None], (8, row_ref.shape[0]))
    return row.T[:, 0:1]


def greet(peers):
    barrier = pltpu.get_barrier_semaphore()
    for peer in peers:
        pl.semaphore_signal(barrier, inc=1, device_id=peer, device_id_type=MESH)
    pl.semaphore_wait(barrier, len(peers))


def front_kernel(
    x_ref, w_query_ref, w_key_ref, w_value_ref, w_out_ref, w_up_ref, w_down_ref, gain_one_ref, gain_two_ref, cot_ref, valid_ref,
    whole_ref, w_head_ref, qkv_out, att_out, lse_ref, attended_out, out_ref, resid_out, normed_out, rate_ref, second_ref, up_ref, down_ref, cots_ref,
    tokens, frames, w_own, w_head, up_own, out_all, att_low, came, part_low, core_in, half_low, chip_in, second, peak, total, acc, qkv_ref, att_ref, attended_ref, resid_ref, normed_ref, send, recv, local_sem,
):
    f32, bf16 = jnp.float32, jnp.bfloat16
    dp, z, t, other_dp, chip, core, pair = axes_of()
    rows, width = x_ref.shape
    quarter, half = rows // 4, rows // 2
    part, hidden = w_up_ref.shape
    side = hidden // 2
    copies = Copies(send, recv)
    kept = []

    def keep(src, dst):
        copy = pltpu.make_async_copy(src, dst, local_sem.at[len(kept)])
        kept.append(copy)
        copy.start()
        return copy

    def along(k):
        return {"seq": lax.rem(z + k + SEQ, SEQ)}

    def owner(k):
        return (dp * SEQ + lax.rem(z - k + SEQ, SEQ)) * part

    mate = t + 1 - 2 * lax.rem(t, 2)
    quarters = [t, lax.rem(t + 2, 4), mate, lax.rem(mate + 2, 4)]
    load_tokens = [keep(x_ref.at[pl.ds(quarters[n] * quarter, quarter), :], tokens.at[pl.ds(n * quarter, quarter), :]) for n in range(4)]
    keep_cots = [keep(cot_ref.at[pl.ds(quarters[n] * quarter, quarter), :], cots_ref.at[pl.ds(n * quarter, quarter), :]) for n in range(4)]
    own_out = keep(w_out_ref, out_all.at[:, pl.ds(owner(0), part)])
    keep(w_down_ref.at[pl.ds(lax.rem(z, 2) * side, side), :], down_ref.at[:, pl.ds(owner(0), part)])
    greet([other_dp, chip, core] + [along(k) for k in range(1, SEQ)])

    first = slice(0, quarter)

    def rows_at(n, count=1):
        return pl.ds(n * quarter, count * quarter)

    token = [None] + [copies.make(frames.at[k - 1, rows_at(0), :], frames.at[k, rows_at(0), :], along(1)) for k in range(1, SEQ)]
    token_chip = [None] + [copies.make(frames.at[k, rows_at(0), :], frames.at[k, rows_at(1), :], chip) for k in range(1, SEQ)]
    token_core = [None] + [copies.make(frames.at[k, rows_at(0, 2), :], frames.at[k, rows_at(2, 2), :], core) for k in range(1, SEQ)]
    head = [None] + [copies.make(w_own.at[lax.rem(z + k, SEQ)], w_head.at[pl.ds(owner(0), part), :], along(k)) for k in range(1, SEQ)]
    mine = pl.ds(dp * SEQ * part, SEQ * part)
    head_dp = copies.make(w_head.at[mine, :], w_head.at[mine, :], other_dp)

    def gather(source, at):
        step = [None] + [copies.make(source(lax.rem(z + k, 2)), at(owner(0)), along(k)) for k in range(1, SEQ)]
        cross = [copies.make(at(owner(k)) if k else source(lax.rem(z, 2)), at(owner(k)), other_dp) for k in range(SEQ)]
        return step, cross

    out_step, out_dp = gather(lambda h: w_out_ref, lambda c: out_all.at[:, pl.ds(c, part)])
    up_step, up_dp = gather(lambda h: up_own.at[h], lambda c: up_ref.at[pl.ds(c, part), :])
    down_step, down_dp = gather(lambda h: w_down_ref.at[pl.ds(h * side, side), :], lambda c: down_ref.at[:, pl.ds(c, part)])
    first_back = len(copies.all) - 1
    back_home = [None] + [copies.make(att_low.at[k], came.at[k], along(-k)) for k in range(1, SEQ)]
    sum_core = copies.make(part_low.at[rows_at(2, 2), :], core_in, core)
    sum_chip = copies.make(half_low, chip_in, chip)
    second_pair = copies.make(second.at[rows_at(0), :], second.at[rows_at(4), :], pair)
    second_chip = [copies.make(second.at[rows_at(4 * n), :], second.at[rows_at(4 * n + 1), :], chip) for n in range(2)]
    second_core = [copies.make(second.at[rows_at(4 * n, 2), :], second.at[rows_at(4 * n + 2, 2), :], core) for n in range(2)]
    cot_pair = copies.make(cot_ref.at[pl.ds(t * quarter, quarter), :], cots_ref.at[rows_at(4), :], pair)
    cot_chip = copies.make(cots_ref.at[rows_at(4), :], cots_ref.at[rows_at(5), :], chip)
    cot_core = copies.make(cots_ref.at[rows_at(4, 2), :], cots_ref.at[rows_at(6, 2), :], core)

    def norm_piece(n, carry):
        values = tokens[rows_at(n), :].astype(f32)
        center = values - jnp.mean(values, axis=1, keepdims=True)
        frames[0, rows_at(n), :] = (center * lax.rsqrt(jnp.mean(center * center, axis=1, keepdims=True) + NORM_EPS)).astype(bf16)
        return carry

    out_dp[0].start()
    down_dp[0].start()
    load_tokens[0].wait()
    lax.fori_loop(0, 1, norm_piece, 0)
    token[1].start()
    gain = column(gain_one_ref)
    for h in range(SEQ):
        at = slice(h * HEAD_DIM, (h + 1) * HEAD_DIM)
        for n, ref in enumerate((w_query_ref, w_key_ref, w_value_ref)):
            w_own[h, :, n * HEAD_DIM : (n + 1) * HEAD_DIM] = (ref[:, at].astype(f32) * gain).astype(bf16)
    for k in range(1, SEQ):
        head[k].start()
    w_head[pl.ds(owner(0), part), :] = w_own[z]
    gain = column(gain_two_ref)
    for h in range(2):
        up_own[h] = (w_up_ref[:, h * side : (h + 1) * side].astype(f32) * gain).astype(bf16)
    keep(up_own.at[lax.rem(z, 2)], up_ref.at[pl.ds(owner(0), part), :])
    for copy in load_tokens[1:]:
        copy.wait()
    lax.fori_loop(1, 4, norm_piece, 0)
    keep(frames.at[0], whole_ref.at[0])

    def arrive(copy, *then):
        copies.wait(copy)
        for one in then:
            one.start()

    def project(k):
        def piece(n, carry):
            qkv_ref[k, rows_at(n), :] = jnp.dot(frames[k, rows_at(n), :], w_head[...], preferred_element_type=f32).astype(bf16)
            return carry

        lax.fori_loop(0, 4, piece, 0)

    scale = HEAD_DIM ** (-0.5)

    def query_frame(i):
        at = lax.rem(z - i + SEQ, SEQ)
        query = qkv_ref[at, :, 0:HEAD_DIM]
        peak[...] = jnp.full_like(peak, MASK_FILL)
        total[...] = jnp.zeros_like(total)
        acc[...] = jnp.zeros_like(acc)

        def key_frame(j, inner):
            here = lax.rem(z - j + SEQ, SEQ)
            scores = lax.dot_general(qkv_ref[here, :, HEAD_DIM : 2 * HEAD_DIM], query, (((1,), (1,)), ((), ())), preferred_element_type=f32) * scale + (valid_ref[0, j] - 1).astype(f32) * -MASK_FILL
            before = peak[...]
            after = jnp.maximum(before, jnp.max(scores, axis=0, keepdims=True))
            terms = jnp.exp(scores - after)
            fix = jnp.exp(before - after)
            peak[...] = after
            total[...] = total[...] * fix + jnp.sum(terms, axis=0, keepdims=True)
            acc[...] = acc[...] * fix + lax.dot_general(qkv_ref[here, :, 2 * HEAD_DIM :], terms.astype(bf16), (((0,), (0,)), ((), ())), preferred_element_type=f32)
            return inner

        lax.fori_loop(0, i + 1, key_frame, 0)
        outcome = (acc[...] / total[...]).T
        att_ref[at] = outcome
        att_low[at] = outcome.astype(bf16)
        lse_ref[at] = peak[...] + jnp.log(total[...])

        @pl.when(at != 0)
        def _():
            pltpu.make_async_remote_copy(
                src_ref=att_low.at[at], dst_ref=came.at[at], send_sem=send.at[first_back + at], recv_sem=recv.at[first_back + at],
                device_id={"seq": i}, device_id_type=MESH,
            ).start()

    def mix(start):
        def piece(n, carry):
            at = pl.ds(pl.multiple_of(n * 512, 512), 512)
            part_low[pl.ds(start, half), at] = jnp.dot(attended_ref[pl.ds(start, half), :], out_all[:, at], preferred_element_type=f32).astype(bf16)
            return carry

        lax.fori_loop(0, width // 512, piece, 0)

    for k in range(1, SEQ):
        copies.wait(head[k])
    head_dp.start()
    arrive(token[1], token[2], token_chip[1])
    up_dp[0].start()
    arrive(token[2], token[3], token_chip[2], out_step[1])
    arrive(token_chip[1], token_core[1])
    copies.wait(head_dp)
    keep(w_head, w_head_ref)
    project(0)
    arrive(token_core[1])
    keep(frames.at[1], whole_ref.at[1])
    project(1)
    arrive(token_chip[2], token_core[2])
    arrive(token[3], token_chip[3], out_step[2], cot_pair)
    arrive(token_core[2])
    keep(frames.at[2], whole_ref.at[2])
    project(2)
    arrive(token_chip[3], token_core[3])
    arrive(token_core[3])
    keep(frames.at[3], whole_ref.at[3])
    project(3)
    keep(qkv_ref, qkv_out)
    query_frame(0)
    arrive(out_step[1], out_step[3], out_dp[1])
    query_frame(1)
    arrive(out_step[2], up_step[1], out_dp[2])
    arrive(cot_pair, cot_chip)
    query_frame(2)
    query_frame(3)
    keep(att_ref, att_out)
    came[0] = att_low[0]
    arrive(out_step[3], out_dp[3], up_step[2])
    copies.wait(*back_home[1:])
    for h in range(SEQ):
        attended_ref[:, h * HEAD_DIM : (h + 1) * HEAD_DIM] = came[lax.rem(h - z + SEQ, SEQ)]
    keep(attended_ref, attended_out)
    own_out.wait()
    copies.wait(*out_dp)
    keep(out_all, out_ref)

    mix(half)
    sum_core.start()
    mix(0)
    copies.wait(sum_core)
    half_low[...] = (part_low[quarter:half, :].astype(f32) + core_in[quarter:half, :].astype(f32)).astype(bf16)
    sum_chip.start()
    arrive(up_step[1], up_step[3], up_dp[1], down_step[1])
    arrive(cot_chip, cot_core)
    copies.wait(sum_chip)
    resid = tokens[first, :].astype(f32) + (part_low[first, :].astype(f32) + core_in[first, :].astype(f32)) + chip_in[...].astype(f32)
    center = resid - jnp.mean(resid, axis=1, keepdims=True)
    rate = lax.rsqrt(jnp.mean(center * center, axis=1, keepdims=True) + NORM_EPS)
    normed = center * rate
    second[first, :] = normed.astype(bf16)
    second_pair.start()
    second_chip[0].start()
    resid_ref[...] = resid
    rate_ref[...] = rate
    normed_ref[...] = normed
    keep(resid_ref, resid_out)
    keep(normed_ref, normed_out)
    arrive(up_step[2], down_step[2], up_dp[2])
    arrive(second_chip[0], second_core[0])
    arrive(second_pair, second_chip[1], down_step[3])
    arrive(up_step[3], up_dp[3])
    arrive(down_step[1], down_dp[1])
    arrive(second_chip[1], second_core[1])
    arrive(down_step[2], down_dp[2])
    arrive(down_step[3], down_dp[3])
    copies.wait(*second_core)
    keep(second, second_ref)
    copies.finish()
    for copy in kept:
        if not any(copy is done for done in [own_out] + load_tokens):
            copy.wait()


def front(x, w_query, w_key, w_value, w_out, w_up, w_down, gain_one, gain_two, cot, valid):
    rows, width = x.shape
    quarter, half = rows // 4, rows // 2
    part, hidden = w_up.shape
    inner = w_out.shape[0]
    three = 3 * HEAD_DIM
    f32, bf16 = jnp.float32, jnp.bfloat16
    any_, vmem = pl.BlockSpec(memory_space=pl.ANY), pl.BlockSpec(memory_space=pltpu.VMEM)
    shape = jax.ShapeDtypeStruct
    outs = [
        (shape((SEQ, rows, width), bf16), any_),
        (shape((width, three), bf16), any_),
        (shape((SEQ, rows, three), bf16), any_),
        (shape((SEQ, rows, HEAD_DIM), f32), any_),
        (shape((SEQ, 1, rows), f32), vmem),
        (shape((rows, inner), bf16), any_),
        (shape((inner, width), bf16), any_),
        (shape((quarter, width), f32), any_),
        (shape((quarter, width), f32), any_),
        (shape((quarter, 1), f32), vmem),
        (shape((2 * rows, width), bf16), any_),
        (shape((width, hidden // 2), bf16), any_),
        (shape((hidden // 2, width), bf16), any_),
        (shape((2 * rows, width), bf16), any_),
    ]
    scratch = [
        ((rows, width), bf16),
        ((SEQ, rows, width), bf16),
        ((SEQ, part, three), bf16),
        ((width, three), bf16),
        ((2, part, hidden // 2), bf16),
        ((inner, width), bf16),
        ((SEQ, rows, HEAD_DIM), bf16),
        ((SEQ, rows, HEAD_DIM), bf16),
        ((rows, width), bf16),
        ((half, width), bf16),
        ((quarter, width), bf16),
        ((quarter, width), bf16),
        ((2 * rows, width), bf16),
        ((1, rows), f32),
        ((1, rows), f32),
        ((HEAD_DIM, rows), f32),
        ((SEQ, rows, three), bf16),
        ((SEQ, rows, HEAD_DIM), f32),
        ((rows, inner), bf16),
        ((quarter, width), f32),
        ((quarter, width), f32),
    ]
    count = 3 * 3 + 4 + 3 * 7 + 3 + 2 + 5 + 3
    return pl.pallas_call(
        front_kernel,
        out_shape=[o[0] for o in outs],
        in_specs=[any_] + [vmem] * 3 + [any_, vmem, any_, vmem, vmem, any_, pl.BlockSpec(memory_space=pltpu.SMEM)],
        out_specs=[o[1] for o in outs],
        scratch_shapes=[pltpu.VMEM(*one) for one in scratch] + [pltpu.SemaphoreType.DMA((count,)), pltpu.SemaphoreType.DMA((count,)), pltpu.SemaphoreType.DMA((24,))],
        compiler_params=pltpu.CompilerParams(collective_id=0, has_side_effects=True, vmem_limit_bytes=58 * 2**20),
        cost_estimate=pl.CostEstimate(flops=8 * 10**9, bytes_accessed=50 * 10**6, transcendentals=5 * 10**6),
    )(x, w_query, w_key, w_value, w_out, w_up, w_down, gain_one, gain_two, cot, valid)


def back_kernel(
    gd_ref, d_up_ref, second_ref, act_ref, down_ref, dn_ref, resid_ref, cots_ref, normed_two_ref, rate_two_ref, attended_ref, out_ref, qkv_ref, att_ref, lse_ref, valid_ref, w_head_ref, whole_ref, x_ref,
    w_query_ref, w_key_ref, w_value_ref, w_up_ref, gain_one_ref, gain_two_ref,
    down_sum_out, up_sum_out, out_sum_out, grad_query_out, grad_key_out, grad_value_out, gains_ref, grad_in_ref, result_ref,
    gu_ref, ff_ref, arrived_ref, cross_down_ref, cross_up_ref, far_down_ref, far_up_ref, dn_core_ref, dn_chip_ref, ff_core_ref, ff_chip_ref, pair_ref, first_core_ref, first_chip_ref, first_ring_ref,
    frames, temp, box_down, box_up, mix, d_head, d_out, dq, dk, dv, delta, d_three, out_send, out_cross, out_far, out_box,
    head_acc, head_low, head_cross, head_sum, held_a, held_b, half_box, pair_box, mid, quart_box, in_box, gain_box, gain_came, down_sum_ref, up_sum_ref, out_sum_ref, grad_query_ref, grad_key_ref, grad_value_ref,
    send, recv, keep_sem, load_sem, arena_sem, stage_sem,
):
    f32, bf16 = jnp.float32, jnp.bfloat16
    dp, z, t, other_dp, chip, core, pair = axes_of()
    rows, width = whole_ref.shape[1:]
    quarter, half = rows // 4, rows // 2
    part = width // (2 * SEQ)
    side = gd_ref.shape[1]
    inner = attended_ref.shape[1]
    copies = Copies(send, recv)
    scale = HEAD_DIM ** (-0.5)
    first, later = slice(0, quarter), slice(quarter, half)

    def along(k):
        return {"seq": lax.rem(z + k + SEQ, SEQ)}

    def load(*pairs):
        moves = [pltpu.make_async_copy(src, dst, load_sem.at[i]) for i, (src, dst) in enumerate(pairs)]
        for move in moves:
            move.start()
        for move in moves:
            move.wait()

    def block(side_dp, k):
        return pl.multiple_of((side_dp * SEQ + lax.rem(z - k + SEQ, SEQ)) * part, part)

    def rows_at(n, count=1):
        return pl.ds(n * quarter, count * quarter)

    greet([other_dp, chip, core] + [along(k) for k in range(1, SEQ)])

    def sums(part_ref, core_ref, chip_ref, n):
        to_core = [copies.make(part_ref.at[rows_at(4 * i + 2, 2), :], core_ref.at[i], core) for i in range(2)]
        to_chip = [copies.make(half_box.at[2 * n + i], chip_ref.at[i], chip) for i in range(2)]
        to_pair = copies.make(pair_box.at[n], pair_ref.at[n], pair)
        return to_core, to_chip, to_pair

    dn_core, dn_chip, dn_pair = sums(dn_ref, dn_core_ref, dn_chip_ref, 0)
    ff_core, ff_chip, ff_pair = sums(ff_ref, ff_core_ref, ff_chip_ref, 1)
    mix_chip = copies.make(mix.at[rows_at(0), :], mix.at[rows_at(1), :], chip)
    mix_core = copies.make(mix.at[rows_at(0, 2), :], mix.at[rows_at(2, 2), :], core)
    spread = [None] + [copies.make(d_head.at[lax.rem(z + k, SEQ)], d_out.at[k], along(k)) for k in range(1, SEQ)]
    cross_down = [copies.make(gd_ref.at[pl.ds(block(1 - dp, k), part), :], cross_down_ref.at[k], other_dp) for k in range(SEQ)]
    cross_up = [copies.make(gu_ref.at[pl.ds(block(1 - dp, k), part), :], cross_up_ref.at[k], other_dp) for k in range(SEQ)]
    cross_out = [copies.make(out_send.at[k], out_cross.at[k], other_dp) for k in range(SEQ)]
    far_down = [None] + [copies.make(box_down.at[k - 1], far_down_ref.at[k - 1], along(-k)) for k in range(1, SEQ)]
    far_up = [None] + [copies.make(box_up.at[k - 1], far_up_ref.at[k - 1], along(-k)) for k in range(1, SEQ)]
    far_out = [None] + [copies.make(out_box.at[k - 1], out_far.at[k - 1], along(-k)) for k in range(1, SEQ)]
    first_core = [copies.make(frames.at[k, rows_at(2, 2), :], first_core_ref.at[k], core) for k in range(SEQ)]
    first_chip = [copies.make(quart_box.at[k], first_chip_ref.at[k], chip) for k in range(SEQ)]
    first_ring = [None] + [copies.make(in_box.at[k - 1], first_ring_ref.at[k - 1], along(1)) for k in range(1, SEQ)]
    head_dp = copies.make(head_low.at[1 - dp], head_cross, other_dp)
    head_out = [None] + [copies.make(head_sum.at[lax.rem(z + k, SEQ)], arrived_ref.at[k], along(k)) for k in range(1, SEQ)]
    kept = []

    def publish(n, ref):
        mine = ref.at[pl.ds(t * quarter, quarter), :]
        mate = ref.at[pl.ds(lax.rem(t + 2, 4) * quarter, quarter), :]
        return [copies.make(half_box.at[n], mine, chip), copies.make(half_box.at[n], mine, core), copies.make(mate, mate, core)], (half_box.at[n], mine)

    gain_core = copies.make(gain_box.at[0], gain_came.at[0], core)
    gain_chip = copies.make(gain_box.at[1], gain_came.at[1], chip)
    result_out, result_own = publish(0, result_ref)
    grad_out_copies, grad_own = publish(1, grad_in_ref)

    def keep(src, dst):
        move = pltpu.make_async_copy(src, dst, keep_sem.at[SEQ + len(kept)])
        kept.append(move)
        move.start()
        return move

    def half_of(part_ref, core_ref, to_core, to_chip, i, n):
        copies.wait(to_core[i])
        load((part_ref.at[rows_at(4 * i + 1), :], held_a.at[rows_at(0), :]), (core_ref.at[i, rows_at(1), :], held_a.at[rows_at(1), :]))
        half_box[2 * n + i] = (held_a[first, :].astype(f32) + held_a[later, :].astype(f32)).astype(bf16)
        to_chip[i].start()

    def quarter_of(part_ref, core_ref, chip_ref, to_chip, i, *more):
        copies.wait(to_chip[i])
        load(
            (part_ref.at[rows_at(4 * i), :], held_a.at[rows_at(0), :]), (core_ref.at[i, rows_at(0), :], held_a.at[rows_at(1), :]), (chip_ref.at[i], held_b.at[rows_at(0), :]),
            *more,
        )
        return (held_a[first, :].astype(f32) + held_a[later, :].astype(f32)) + held_b[first, :].astype(f32)

    def pair_sum(part_ref, core_ref, chip_ref, to_chip, to_pair, n):
        pair_box[n] = quarter_of(part_ref, core_ref, chip_ref, to_chip, 1).astype(bf16)
        to_pair.start()

    def own_sum(part_ref, core_ref, chip_ref, to_chip, to_pair, n, extra):
        copies.wait(to_pair)
        total = quarter_of(part_ref, core_ref, chip_ref, to_chip, 0, (pair_ref.at[n], held_b.at[rows_at(1), :]), (extra, spare))
        return total + held_b[later, :].astype(f32)

    def scatter(k, own_ref, cross_at, crossing, box, far, go=True):
        copies.wait(crossing)
        load((cross_at, temp.at[0]), (own_ref.at[pl.ds(block(dp, k), part), :], temp.at[1]))
        box[k - 1] = (temp[0].astype(f32) + temp[1].astype(f32)).astype(bf16)
        if go:
            far[k].start()

    def scatter_down(k):
        scatter(k, gd_ref, cross_down_ref.at[k], cross_down[k], box_down, far_down)

    def scatter_up(k, go=True):
        scatter(k, gu_ref, cross_up_ref.at[k], cross_up[k], box_up, far_up, go)

    same = pl.multiple_of(lax.rem(z, 2) * side, side)
    unlike = pl.multiple_of((1 - lax.rem(z, 2)) * side, side)

    def total_of(own_ref, cross_at, far_ref, far, crossing, store):
        copies.wait(crossing, *far[1:])
        load((cross_at, temp.at[0]), (own_ref.at[pl.ds(block(dp, 0), part), :], temp.at[1]), (far_ref.at[1], temp.at[2]))
        store(same, lambda at: (temp[0, :, at].astype(f32) + temp[1, :, at].astype(f32)) + temp[2, :, at].astype(f32))
        load((far_ref.at[0], temp.at[0]), (far_ref.at[2], temp.at[1]))
        store(unlike, lambda at: temp[0, :, at].astype(f32) + temp[1, :, at].astype(f32))

    def store_turned(base, value):
        for n in range(side // 256):
            down_sum_ref[pl.ds(base + n * 256, 256), :] = value(slice(n * 256, (n + 1) * 256)).T

    gain_sums = []

    def store_plain(base, value):
        raw = value(slice(0, side))
        gain_sums.append(jnp.sum(held_a[0:part, pl.ds(base, side)].astype(f32) * raw, axis=1, keepdims=True))
        up_sum_ref[:, pl.ds(base, side)] = raw * column(gain_two_ref)

    def out_block(start):
        return lax.dot_general(attended_ref[...], mix[:, pl.ds(start, part)], (((0,), (0,)), ((), ())), preferred_element_type=f32)

    def scatter_out(k):
        copies.wait(cross_out[k])
        out_box[k - 1] = (out_block(block(dp, k)) + out_cross[k].astype(f32)).astype(bf16)
        far_out[k].start()

    for copy in (dn_core[1], dn_core[0], cross_down[1]):
        copy.start()

    def place(*pairs):
        moves = [pltpu.make_async_copy(src, dst, arena_sem.at[i]) for i, (src, dst) in enumerate(pairs)]
        for move in moves:
            move.start()
        return moves

    def sides(ref, at):
        return [(ref.at[pl.ds(n * rows, rows), :], frames.at[at, :, pl.ds(n * side, side)]) for n in range(2)]

    arena = place(*sides(d_up_ref, 0), *sides(act_ref, 3), *[(second_ref.at[pl.ds(n * rows, rows), :], frames.at[1 + n]) for n in range(2)])
    spare = head_acc.at[pl.ds(0, quarter), :]
    half_of(dn_ref, dn_core_ref, dn_core, dn_chip, 1, 0)
    cross_down[2].start()
    load(*[(out_ref.at[pl.ds(h * HEAD_DIM, HEAD_DIM), :], quart_box.at[h, pl.ds(0, HEAD_DIM), :]) for h in range(SEQ)])
    for move in arena:
        move.wait()

    def up_piece(b, carry):
        at = pl.ds(pl.multiple_of(b * part, part), part)
        slot = lax.rem(b, 2)
        move = pltpu.make_async_copy(temp.at[slot], gu_ref.at[at, :], stage_sem.at[slot])

        @pl.when(lax.rem(b, SEQ) >= 2)
        def _():
            move.wait()

        turned = (((0,), (0,)), ((), ()))
        value = lax.dot_general(frames[1, :, at], frames[0, :, 0:side], turned, preferred_element_type=f32)
        value = value + lax.dot_general(frames[2, :, at], frames[0, :, side:], turned, preferred_element_type=f32)
        temp[slot] = value.astype(bf16)
        move.start()
        return carry

    lax.fori_loop(0, SEQ, up_piece, 0)
    for slot in range(2):
        pltpu.make_async_copy(temp.at[slot], gu_ref.at[pl.ds(0, part), :], stage_sem.at[slot]).wait()
    scatter_down(1)
    cross_down[3].start()
    lax.fori_loop(SEQ, 2 * SEQ, up_piece, 0)
    for slot in range(2):
        pltpu.make_async_copy(temp.at[slot], gu_ref.at[pl.ds(0, part), :], stage_sem.at[slot]).wait()
    arena = place((down_ref.at[pl.ds(0, rows), :], frames.at[1]), (down_ref.at[pl.ds(rows, side - rows), :], frames.at[2, pl.ds(0, side - rows), :]))
    copies.wait(dn_chip[1])
    half_of(dn_ref, dn_core_ref, dn_core, dn_chip, 0, 0)
    pair_sum(dn_ref, dn_core_ref, dn_chip_ref, dn_chip, dn_pair, 0)
    cross_up[1].start()
    scatter_down(2)
    grad = own_sum(dn_ref, dn_core_ref, dn_chip_ref, dn_chip, dn_pair, 0, normed_two_ref)
    normed = spare[...]
    grad = rate_two_ref[...] * (grad - jnp.mean(grad, axis=1, keepdims=True) - normed * jnp.mean(grad * normed, axis=1, keepdims=True))
    load((cots_ref.at[rows_at(0), :], held_a.at[rows_at(0), :]))
    grad = held_a[first, :].astype(f32) + grad
    mid[...] = grad
    mix[first, :] = grad.astype(bf16)
    mix_chip.start()
    scatter_down(3)
    for copy in (cross_up[2], cross_up[3], cross_up[0], cross_down[0]):
        copy.start()
    scatter_up(1)
    copies.wait(mix_chip)
    mix_core.start()

    def to_head(k, at):
        h = lax.rem(z + k, SEQ)
        d_head[h, at, :] = lax.dot_general(mix[at, :], quart_box[h, 0:HEAD_DIM, :], (((1,), (1,)), ((), ())), preferred_element_type=f32).astype(bf16)

    for k in (1, 2, 3, 0):
        to_head(k, slice(0, half))
    copies.wait(mix_core)
    for k in (1, 2, 3, 0):
        to_head(k, slice(half, rows))
        if k:
            spread[k].start()
    d_out[0] = d_head[z]
    for move in arena:
        move.wait()

    def ff_piece(n, carry):
        at = pl.ds(n * quarter, quarter)
        slot = lax.rem(n, 2)
        stage = held_b.at[pl.ds(slot * quarter, quarter), :]
        move = pltpu.make_async_copy(stage, ff_ref.at[at, :], stage_sem.at[slot])

        @pl.when(n >= 2)
        def _():
            move.wait()

        left = frames[3, pl.ds(lax.rem(n, 4) * quarter, quarter), pl.ds(pl.multiple_of(n // 4 * side, side), side)]
        value = jnp.dot(left[:, 0:rows], frames[1], preferred_element_type=f32)
        value = value + jnp.dot(left[:, rows:], frames[2, 0 : side - rows, :], preferred_element_type=f32)
        held_b[pl.ds(slot * quarter, quarter), :] = value.astype(bf16)
        move.start()
        return carry

    lax.fori_loop(0, 8, ff_piece, 0)
    for slot in range(2):
        pltpu.make_async_copy(held_b.at[pl.ds(slot * quarter, quarter), :], ff_ref.at[pl.ds(0, quarter), :], stage_sem.at[slot]).wait()
    ff_core[1].start()
    ff_core[0].start()
    fetch = [pltpu.make_async_copy(whole_ref.at[k], frames.at[k], keep_sem.at[k]) for k in range(SEQ)]
    for move in fetch:
        move.start()
    for k in (1, 2, 3, 0):
        out_send[k] = out_block(block(1 - dp, k)).astype(bf16)
        cross_out[k].start()
    half_of(ff_ref, ff_core_ref, ff_core, ff_chip, 1, 1)
    high = head_acc.shape[0]
    pieces = [(f, slice(0, high) if n == 0 else slice(high, rows), slice((2 * f + n) * HEAD_DIM, (2 * f + n + 1) * HEAD_DIM)) for f in range(SEQ) for n in range(2)]
    load(*[(att_ref.at[f, pl.ds(at.start, at.stop - at.start), :], head_acc.at[pl.ds(0, at.stop - at.start), pl.ds(lanes.start, HEAD_DIM)]) for f, at, lanes in pieces])
    scatter_up(2, False)
    scatter_up(3, False)
    copies.wait(*spread[1:])
    far_up[2].start()
    dq[...] = jnp.zeros_like(dq)
    for f, at, lanes in pieces:
        delta[f, :, at] = jnp.sum((d_out[f, at, :].astype(f32) * head_acc[0 : at.stop - at.start, lanes]).T, axis=0, keepdims=True)

    def key_frame(j):
        here = lax.rem(z - j + SEQ, SEQ)
        dk[...] = jnp.zeros_like(dk)
        dv[...] = jnp.zeros_like(dv)

        def query_frame(i, inner_):
            at = lax.rem(z - i + SEQ, SEQ)
            query, key, value = qkv_ref[at, :, :HEAD_DIM], qkv_ref[here, :, HEAD_DIM : 2 * HEAD_DIM], qkv_ref[here, :, 2 * HEAD_DIM :]
            grad_out = d_out[at]
            scores = lax.dot_general(key, query, (((1,), (1,)), ((), ())), preferred_element_type=f32) * scale + (valid_ref[0, j] - 1).astype(f32) * -MASK_FILL
            prob = jnp.exp(scores - lse_ref[at])
            d_prob = lax.dot_general(value, grad_out, (((1,), (1,)), ((), ())), preferred_element_type=f32)
            d_scores = (prob * (d_prob - delta[at])).astype(bf16)
            dv[...] += jnp.dot(prob.astype(bf16), grad_out, preferred_element_type=f32)
            dk[...] += jnp.dot(d_scores, query, preferred_element_type=f32)
            dq[at] += lax.dot_general(key, d_scores, (((0,), (0,)), ((), ())), preferred_element_type=f32)
            return inner_

        lax.fori_loop(j, SEQ, query_frame, 0)
        d_three[here, :, HEAD_DIM : 2 * HEAD_DIM] = (dk[...] * scale).astype(bf16)
        d_three[here, :, 2 * HEAD_DIM :] = dv[...].astype(bf16)

    key_frame(0)
    far_up[3].start()
    scatter_out(1)
    key_frame(1)
    half_of(ff_ref, ff_core_ref, ff_core, ff_chip, 0, 1)
    scatter_out(2)
    key_frame(2)
    key_frame(3)
    pair_sum(ff_ref, ff_core_ref, ff_chip_ref, ff_chip, ff_pair, 1)
    for f in range(SEQ):
        d_three[f, :, :HEAD_DIM] = (dq[f] * scale).T.astype(bf16)

    def project_back(k):
        fetch[k].wait()

        def piece(n, carry):
            at = pl.ds(pl.multiple_of(n * 512, 512), 512)
            term = lax.dot_general(d_three[k], frames[k, :, at], (((0,), (0,)), ((), ())), preferred_element_type=f32)
            head_acc[:, at] = term if k == 1 else head_acc[:, at] + term
            return carry

        lax.fori_loop(0, width // 512, piece, 0)

        def back_piece(n, carry):
            at = pl.ds(pl.multiple_of(n * 512, 512), 512)
            frames[k, :, at] = lax.dot_general(d_three[k], w_head_ref[at, :], (((1,), (1,)), ((), ())), preferred_element_type=f32).astype(bf16)
            return carry

        lax.fori_loop(0, width // 512, back_piece, 0)
        first_core[k].start()

    def half_sum(k):
        copies.wait(first_core[k])
        load((first_core_ref.at[k], held_a))
        quart_box[k] = (frames[k, later, :].astype(f32) + held_a[later, :].astype(f32)).astype(bf16)
        first_chip[k].start()
        frames[k, first, :] = (frames[k, first, :].astype(f32) + held_a[first, :].astype(f32)).astype(bf16)

    def quarter_sum(k):
        copies.wait(first_chip[k])
        pairs = [(first_chip_ref.at[k], held_a.at[rows_at(0), :])]
        if k != 1:
            before = (k - 1) % SEQ
            copies.wait(first_ring[before])
            pairs.append((first_ring_ref.at[before - 1], held_a.at[rows_at(1), :]))
        load(*pairs)
        sum_ = frames[k, first, :].astype(f32) + held_a[first, :].astype(f32)
        if k != 1:
            sum_ = sum_ + held_a[later, :].astype(f32)
        return sum_

    project_back(1)
    scatter_out(3)
    project_back(2)
    half_sum(1)
    project_back(3)
    project_back(0)
    for n in range(2):
        head_low[n] = head_acc[:, n * (width // 2) : (n + 1) * (width // 2)].astype(bf16)
    head_dp.start()
    half_sum(2)
    in_box[0] = quarter_sum(1).astype(bf16)
    first_ring[1].start()
    total_of(gd_ref, cross_down_ref.at[0], far_down_ref, far_down, cross_down[0], store_turned)
    keep(down_sum_ref, down_sum_out)
    half_sum(3)
    load((w_up_ref, held_a.at[pl.ds(0, part), :]))
    total_of(gu_ref, cross_up_ref.at[0], far_up_ref, far_up, cross_up[0], store_plain)
    keep(up_sum_ref, up_sum_out)
    in_box[1] = quarter_sum(2).astype(bf16)
    first_ring[2].start()
    half_sum(0)
    copies.wait(head_dp)
    for j in range(SEQ):
        at = slice(j * part, (j + 1) * part)
        head_sum[j] = (head_low[dp, :, at].astype(f32) + head_cross[:, at].astype(f32)).astype(bf16)
    own_head = keep(head_sum.at[z], arrived_ref.at[0])
    copies.wait(cross_out[0], *far_out[1:])
    sum_ = out_block(block(dp, 0)) + out_cross[0].astype(f32)
    for k in range(1, SEQ):
        sum_ = sum_ + out_far[k - 1].astype(f32)
    out_sum_ref[...] = sum_
    keep(out_sum_ref, out_sum_out)
    in_box[2] = quarter_sum(3).astype(bf16)
    first_ring[3].start()
    total = own_sum(ff_ref, ff_core_ref, ff_chip_ref, ff_chip, ff_pair, 1, resid_ref)
    copies.flush(*dn_chip)
    half_box[0] = (spare[...] + total).astype(bf16)
    result_out[0].start()
    result_out[1].start()
    keep(*result_own)
    load((x_ref.at[pl.ds(t * quarter, quarter), :], held_a.at[rows_at(0), :]))
    center = held_a[first, :].astype(f32)
    center = center - jnp.mean(center, axis=1, keepdims=True)
    rate = lax.rsqrt(jnp.mean(center * center, axis=1, keepdims=True) + NORM_EPS)
    head_acc[later, :] = center * rate
    for k in range(1, SEQ):
        head_out[k].start()
    grad = quarter_sum(0)
    normed = head_acc[later, :]
    grad = rate * (grad - jnp.mean(grad, axis=1, keepdims=True) - normed * jnp.mean(grad * normed, axis=1, keepdims=True))
    half_box[1] = (mid[...] + grad).astype(bf16)
    grad_out_copies[0].start()
    grad_out_copies[1].start()
    keep(*grad_own)
    copies.wait(result_out[0])
    result_out[2].start()
    copies.wait(*head_out[1:])
    own_head.wait()
    load(
        *[(arrived_ref.at[k], head_cross.at[:, pl.ds(k * part, part)]) for k in range(SEQ)],
        *[(ref, held_a.at[pl.ds(0, part), pl.ds(n * inner, inner)]) for n, ref in enumerate((w_query_ref, w_key_ref, w_value_ref))],
    )
    gain_first, gain = jnp.zeros((part, 1), f32), column(gain_one_ref)
    for h in range(SEQ):
        raw = head_cross[:, pl.ds(pl.multiple_of(lax.rem(z - h + SEQ, SEQ) * part, part), part)].astype(f32).T
        for n, ref in enumerate((grad_query_ref, grad_key_ref, grad_value_ref)):
            one = raw[:, n * HEAD_DIM : (n + 1) * HEAD_DIM]
            weight = held_a[0:part, n * inner + h * HEAD_DIM : n * inner + (h + 1) * HEAD_DIM].astype(f32)
            gain_first = gain_first + jnp.sum(weight * one, axis=1, keepdims=True)
            ref[:, h * HEAD_DIM : (h + 1) * HEAD_DIM] = one * gain
    keep(grad_query_ref, grad_query_out)
    keep(grad_key_ref, grad_key_out)
    keep(grad_value_ref, grad_value_out)
    lane = lax.broadcasted_iota(jnp.int32, (part, HEAD_DIM), 1)
    gain_box[0] = jnp.where(lane == 0, gain_first, gain_sums[0] + gain_sums[1])
    gain_core.start()
    copies.wait(gain_core)
    gain_box[1] = gain_box[0] + gain_came[0]
    gain_chip.start()
    copies.wait(grad_out_copies[0])
    grad_out_copies[2].start()
    copies.wait(gain_chip)
    gains_ref[...] = (gain_box[1] + gain_came[1]).T[0:8]
    copies.finish()
    for move in kept:
        if move is not own_head:
            move.wait()


def back(gd, d_up, second, act, down, dn, resid, cots, normed_two, rate_two, attended, out_rel, qkv, att, lse, valid, w_head, whole, x, w_query, w_key, w_value, w_up, gain_one, gain_two):
    rows, width = x.shape
    quarter, half = rows // 4, rows // 2
    part = width // (2 * SEQ)
    inner = attended.shape[1]
    side = gd.shape[1]
    three = 3 * HEAD_DIM
    f32, bf16 = jnp.float32, jnp.bfloat16
    any_, vmem = pl.BlockSpec(memory_space=pl.ANY), pl.BlockSpec(memory_space=pltpu.VMEM)
    shape = jax.ShapeDtypeStruct
    outs = [
        (shape((2 * side, part), f32), any_),
        (shape((part, 2 * side), f32), any_),
        (shape((inner, part), f32), any_),
        (shape((part, inner), f32), any_),
        (shape((part, inner), f32), any_),
        (shape((part, inner), f32), any_),
        (shape((8, part), f32), vmem),
        (shape((rows, width), bf16), any_),
        (shape((rows, width), bf16), any_),
        (shape((width, side), bf16), any_),
        (shape((2 * rows, width), bf16), any_),
        (shape((SEQ, three, part), bf16), any_),
        (shape((SEQ, part, side), bf16), any_),
        (shape((SEQ, part, side), bf16), any_),
        (shape((SEQ - 1, part, side), bf16), any_),
        (shape((SEQ - 1, part, side), bf16), any_),
        (shape((2, half, width), bf16), any_),
        (shape((2, quarter, width), bf16), any_),
        (shape((2, half, width), bf16), any_),
        (shape((2, quarter, width), bf16), any_),
        (shape((2, quarter, width), bf16), any_),
        (shape((SEQ, half, width), bf16), any_),
        (shape((SEQ, quarter, width), bf16), any_),
        (shape((SEQ - 1, quarter, width), bf16), any_),
    ]
    count = 10 + 2 + 3 + 4 + 4 + 4 + 9 + 8 + 3 + 4 + 6 + 2
    scratch = [
        ((SEQ, rows, width), bf16),
        ((3, part, side), bf16),
        ((SEQ - 1, part, side), bf16),
        ((SEQ - 1, part, side), bf16),
        ((rows, width), bf16),
        ((SEQ, rows, HEAD_DIM), bf16),
        ((SEQ, rows, HEAD_DIM), bf16),
        ((SEQ, HEAD_DIM, rows), f32),
        ((rows, HEAD_DIM), f32),
        ((rows, HEAD_DIM), f32),
        ((SEQ, 1, rows), f32),
        ((SEQ, rows, three), bf16),
        ((SEQ, inner, part), bf16),
        ((SEQ, inner, part), bf16),
        ((SEQ - 1, inner, part), bf16),
        ((SEQ - 1, inner, part), bf16),
        ((three, width), f32),
        ((2, three, width // 2), bf16),
        ((three, width // 2), bf16),
        ((SEQ, three, part), bf16),
        ((half, width), bf16),
        ((half, width), bf16),
        ((4, quarter, width), bf16),
        ((2, quarter, width), bf16),
        ((quarter, width), f32),
        ((SEQ, quarter, width), bf16),
        ((SEQ - 1, quarter, width), bf16),
        ((2, part, HEAD_DIM), f32),
        ((2, part, HEAD_DIM), f32),
        ((2 * side, part), f32),
        ((part, 2 * side), f32),
        ((inner, part), f32),
        ((part, inner), f32),
        ((part, inner), f32),
        ((part, inner), f32),
    ]
    return pl.pallas_call(
        back_kernel,
        out_shape=[o[0] for o in outs],
        in_specs=[any_] * 9 + [vmem, vmem, any_, vmem, any_, vmem, pl.BlockSpec(memory_space=pltpu.SMEM), vmem] + [any_] * 6 + [vmem] * 2,
        out_specs=[o[1] for o in outs],
        scratch_shapes=[pltpu.VMEM(*one) for one in scratch]
        + [pltpu.SemaphoreType.DMA((count,)), pltpu.SemaphoreType.DMA((count,)), pltpu.SemaphoreType.DMA((SEQ + 9,)), pltpu.SemaphoreType.DMA((8,)), pltpu.SemaphoreType.DMA((6,)), pltpu.SemaphoreType.DMA((2,))],
        compiler_params=pltpu.CompilerParams(collective_id=1, has_side_effects=True, vmem_limit_bytes=62 * 2**20),
        cost_estimate=pl.CostEstimate(flops=20 * 10**9, bytes_accessed=60 * 10**6, transcendentals=5 * 10**6),
    )(gd, d_up, second, act, down, dn, resid, cots, normed_two, rate_two, attended, out_rel, qkv, att, lse, valid, w_head, whole, x, w_query, w_key, w_value, w_up, gain_one, gain_two)[:9]


def mm(left, right, dims=((1,), (0,)), out=jnp.bfloat16):
    return lax.dot_general(left, right, (dims, ((), ())), preferred_element_type=jnp.float32).astype(out)


def local_fast(inputs, first_gain, w_query, w_key, w_value, w_out, second_gain, w_up, w_down, frame_mask, cotangent):
    rows = inputs.shape[1]
    f32, bf16 = jnp.float32, jnp.bfloat16
    gain_one, gain_two = first_gain, second_gain
    valid = frame_mask
    whole, w_head, qkv, attended_f, lse, attended, out_all, resid_mid, normed_two, rate_two, second_in, up_side, down_side, cots = front(
        inputs[0], w_query, w_key, w_value, w_out, w_up, w_down, gain_one, gain_two, cotangent[0], valid
    )
    up_pre = mm(second_in, up_side, out=f32)
    cdf = 0.5 * (1.0 + lax.erf(up_pre * (0.5**0.5)))
    up_act = (up_pre * cdf).astype(bf16)
    slope = cdf + up_pre * jnp.exp(-0.5 * up_pre * up_pre) * ((2.0 * jnp.pi) ** -0.5)
    grad_down = mm(cots, up_act, ((0,), (0,)))
    d_up = (mm(cots, down_side, ((1,), (1,)), f32) * slope).astype(bf16)
    d_normed_two = mm(d_up, up_side, ((1,), (1,)))
    down_sum, up_sum, out_sum, grad_query, grad_key, grad_value, gains, grad_in, result = back(
        grad_down, d_up, second_in, up_act, down_side, d_normed_two, resid_mid, cots, normed_two, rate_two, attended, out_all, qkv, attended_f, lse, valid, w_head, whole, inputs[0],
        w_query, w_key, w_value, w_up, gain_one, gain_two,
    )
    return (result[None], grad_in[None], gains[0], grad_query, grad_key, grad_value, out_sum, gains[1], up_sum, down_sum)


SEQ = 4


def solution(mesh):
    placed = (
        P("dp", "seq", None),
        P(("dp", "seq")),
        P(("dp", "seq"), "tensor"),
        P(("dp", "seq"), "tensor"),
        P(("dp", "seq"), "tensor"),
        P("tensor", ("dp", "seq")),
        P(("dp", "seq")),
        P(("dp", "seq"), "tensor"),
        P("tensor", ("dp", "seq")),
        P("dp", None),
        P("dp", "seq", None),
    )
    sizes = dict(mesh.shape)
    spread = sizes == {"dp": 2, "seq": SEQ, "tensor": 4}
    return jax.shard_map(
        local_fast if spread else local,
        mesh=mesh,
        in_specs=placed,
        out_specs=(
            P("dp", "seq", None),
            P("dp", "seq", None),
            P(("dp", "seq")),
            P(("dp", "seq"), "tensor"),
            P(("dp", "seq"), "tensor"),
            P(("dp", "seq"), "tensor"),
            P("tensor", ("dp", "seq")),
            P(("dp", "seq")),
            P(("dp", "seq"), "tensor"),
            P("tensor", ("dp", "seq")),
        ),
        check_vma=False,
    )
```
